32 devices in a mesh: dp: 4 (over x, core), fsdp: 8 (over z, y).
Axes of the slice: x: 2, y: 2, z: 4, core: 2. Of those that a mesh axis runs over, the one named last changes fastest.
Arguments:
- frames_in: bfloat16 [64, 256, 512], P(('dp', 'fsdp')), may hold values from -6 to 6
- frame_lengths: int32 [64], P(('dp', 'fsdp')), may hold values from 128 to 256, as said below
- label_ids: int32 [64, 24], P(('dp', 'fsdp')), may hold values from 1 to 1023
- label_lengths: int32 [64], P(('dp', 'fsdp')), may hold values from 12 to 24, as said below
- pred_states: bfloat16 [64, 25, 640], P(('dp', 'fsdp')), may hold values from -6 to 6
- norm_gains: bfloat16 [2, 5, 512], P(None, None, 'fsdp'), may hold values from 0.5 to 1.5
- first_in: bfloat16 [2, 512, 2048], P(None, 'fsdp'), may hold values from -0.25 to 0.25
- first_out: bfloat16 [2, 2048, 512], P(None, 'fsdp'), may hold values from -0.125 to 0.125
- attend_joint: bfloat16 [2, 512, 1536], P(None, 'fsdp'), may hold values from -0.25 to 0.25
- attend_out: bfloat16 [2, 512, 512], P(None, 'fsdp'), may hold values from -1 to 1
- point_in: bfloat16 [2, 512, 1024], P(None, 'fsdp'), may hold values from -0.25 to 0.25
- depth_taps: bfloat16 [2, 9, 512], P(None, None, 'fsdp'), may hold values from -2 to 2
- batch_gain: bfloat16 [2, 512], P(None, 'fsdp'), may hold values from 0.5 to 1.5
- batch_bias: bfloat16 [2, 512], P(None, 'fsdp'), may hold values from -3 to 3
- point_out: bfloat16 [2, 512, 512], P(None, 'fsdp'), may hold values from -0.25 to 0.25
- second_in: bfloat16 [2, 512, 2048], P(None, 'fsdp'), may hold values from -0.25 to 0.25
- second_out: bfloat16 [2, 2048, 512], P(None, 'fsdp'), may hold values from -0.125 to 0.125
- enc_weight: bfloat16 [512, 640], P('fsdp'), may hold values from -0.25 to 0.25
- pred_weight: bfloat16 [640, 640], P('fsdp'), may hold values from -0.25 to 0.25
- token_weight: bfloat16 [640, 1024], P('fsdp'), may hold values from -0.5 to 0.5
- duration_weight: bfloat16 [640, 5], P('fsdp'), may hold values from -0.5 to 0.5
Outputs:
- utt_loss: float32 [64], P(('dp', 'fsdp'))
- grad_frames: float32 [64, 256, 512], P(('dp', 'fsdp'))
- grad_norm_gains: float32 [2, 5, 512], P(None, None, 'fsdp')
- grad_first_in: float32 [2, 512, 2048], P(None, 'fsdp')
- grad_first_out: float32 [2, 2048, 512], P(None, 'fsdp')
- grad_attend_joint: float32 [2, 512, 1536], P(None, 'fsdp')
- grad_attend_out: float32 [2, 512, 512], P(None, 'fsdp')
- grad_point_in: float32 [2, 512, 1024], P(None, 'fsdp')
- grad_depth_taps: float32 [2, 9, 512], P(None, None, 'fsdp')
- grad_batch_gain: float32 [2, 512], P(None, 'fsdp')
- grad_batch_bias: float32 [2, 512], P(None, 'fsdp')
- grad_point_out: float32 [2, 512, 512], P(None, 'fsdp')
- grad_second_in: float32 [2, 512, 2048], P(None, 'fsdp')
- grad_second_out: float32 [2, 2048, 512], P(None, 'fsdp')
- grad_enc_weight: float32 [512, 640], P('fsdp')
- grad_pred_weight: float32 [640, 640], P('fsdp')
- grad_token_weight: float32 [640, 1024], P('fsdp')
- grad_duration_weight: float32 [640, 5], P('fsdp')
The draws below stay inside these ranges and needn't reach their ends.
Inputs may be any that keep to these rules, and one draw needn't show every extreme that they name: `frame_lengths`: every utterance has at least half of its 256 frames valid; the first utterance of every draw has all 256. `label_lengths`: every utterance has at least half of its 24 targets; the first utterance of every draw has all 24.
All inputs are finite; a program needn't handle non-finite values.
Results may differ from the reference program's by a relative error of at most 0.028.
Values may be sent and summed in bfloat16 or wider, within the bound.
A program may use at most 256 MiB of HBM per device.

```python
import jax
import jax.numpy as jnp
from jax import lax

D = 512
FF = 2048
HEADS = 8
KERNEL = 9
JOINT = 640
VOCAB = 1024
DURS = 5
LAYERS = 2
FRAMES = 256
LABELS = 24
SLOTS = 25
UTTS = 64


def draw_frame_lengths(key, part):
    key = jax.random.fold_in(key, 11)
    drawn = jax.random.randint(key, (UTTS,), FRAMES // 2, FRAMES + 1)
    places = lax.broadcasted_iota(jnp.int32, (UTTS,), 0)
    return jnp.where(places == 0, FRAMES, drawn).astype(jnp.int32)


def draw_label_lengths(key, part):
    key = jax.random.fold_in(key, 12)
    drawn = jax.random.randint(key, (UTTS,), max(1, LABELS // 2), LABELS + 1)
    places = lax.broadcasted_iota(jnp.int32, (UTTS,), 0)
    return jnp.where(places == 0, LABELS, drawn).astype(jnp.int32)


def place_ends(values, rng, low, top_value):
    longest = values.shape.index(max(values.shape))
    spots = []
    for shift in (0, 1):
        where = [jax.random.randint(jax.random.fold_in(rng, axis), (), 0, length) for axis, length in enumerate(values.shape)]
        where[longest] = (where[longest] + shift) % values.shape[longest]
        spots.append(tuple(where))
    return values.at[spots[0]].set(low).at[spots[1]].set(top_value)


def levels(stream_key, extent, shards, low, top_value):
    def one(axis_at, blocks):
        draws = jax.random.uniform(jax.random.fold_in(jax.random.fold_in(stream_key, 6), axis_at), (blocks,), jnp.float32, low / len(shards), top_value / len(shards))
        return jnp.repeat(jnp.exp(draws), extent[axis_at] // blocks).reshape((-1,) + (1,) * (len(extent) - axis_at - 1))

    level = one(*shards[0])
    for cut in shards[1:]:
        level = level * one(*cut)
    return level


def noise(key, shape, scale, most, shards=(), held_as=jnp.bfloat16):
    entries = jax.random.normal(key, shape, jnp.float32) * scale
    if len(shards) > 0:
        entries = levels(key, shape, shards, -0.22, 0.18) * entries
    return jnp.clip(entries, min=-most, max=most).astype(held_as)


def setup_inputs(seed: int = 0) -> dict:
    seeds = jax.random.split(jax.random.key(seed), 22)
    frames_in = noise(seeds[0], (UTTS, FRAMES, D), 1.0, 6.0, ((0, 32),))
    frame_lengths = draw_frame_lengths(jax.random.fold_in(seeds[21], 71), 0)
    label_ids = place_ends(jax.random.randint(seeds[2], (UTTS, LABELS), 1, VOCAB), jax.random.fold_in(seeds[2], 1), 1, VOCAB - 1).astype(jnp.int32)
    label_lengths = draw_label_lengths(jax.random.fold_in(seeds[21], 71), 0)
    pred_states = noise(seeds[4], (UTTS, SLOTS, JOINT), 1.0, 6.0, ((0, 32),))
    norm_gains = jnp.clip(1.0 + 0.1 * jax.random.normal(seeds[5], (LAYERS, 5, D), jnp.float32), 0.5, 1.5).astype(jnp.bfloat16)
    first_in = noise(seeds[6], (LAYERS, D, FF), D ** -0.5, 0.25, ((1, 8),))
    first_out = noise(seeds[7], (LAYERS, FF, D), FF ** -0.5, 0.125, ((1, 8),))
    attend_joint = noise(seeds[8], (LAYERS, D, 3 * D), D ** -0.5, 0.25, ((1, 8),))
    attend_out = noise(seeds[9], (LAYERS, D, D), (D // 16) ** -0.5, 1.0, ((1, 8),))
    point_in = noise(seeds[10], (LAYERS, D, 2 * D), D ** -0.5, 0.25, ((1, 8),))
    depth_taps = noise(seeds[11], (LAYERS, KERNEL, D), KERNEL ** -0.5, 2.0, ((2, 8),))
    batch_gain = jnp.clip(1.0 + 0.1 * jax.random.normal(seeds[12], (LAYERS, D), jnp.float32), 0.5, 1.5).astype(jnp.bfloat16)
    batch_bias = noise(seeds[13], (LAYERS, D), 0.5, 3.0, ((1, 8),))
    point_out = noise(seeds[14], (LAYERS, D, D), D ** -0.5, 0.25, ((1, 8),))
    second_in = noise(seeds[15], (LAYERS, D, FF), D ** -0.5, 0.25, ((1, 8),))
    second_out = noise(seeds[16], (LAYERS, FF, D), FF ** -0.5, 0.125, ((1, 8),))
    enc_weight = noise(seeds[17], (D, JOINT), D ** -0.5, 0.25, ((0, 8),))
    pred_weight = noise(seeds[18], (JOINT, JOINT), JOINT ** -0.5, 0.25, ((0, 8),))
    token_weight = noise(seeds[19], (JOINT, VOCAB), (JOINT // 4) ** -0.5, 0.5, ((0, 8),))
    duration_weight = noise(seeds[20], (JOINT, DURS), (JOINT // 4) ** -0.5, 0.5, ((0, 8),))
    return {"frames_in": frames_in, "frame_lengths": frame_lengths, "label_ids": label_ids, "label_lengths": label_lengths, "pred_states": pred_states, "norm_gains": norm_gains, "first_in": first_in, "first_out": first_out, "attend_joint": attend_joint, "attend_out": attend_out, "point_in": point_in, "depth_taps": depth_taps, "batch_gain": batch_gain, "batch_bias": batch_bias, "point_out": point_out, "second_in": second_in, "second_out": second_out, "enc_weight": enc_weight, "pred_weight": pred_weight, "token_weight": token_weight, "duration_weight": duration_weight}


@jax.custom_vjp
def low(v):
    return lax.optimization_barrier(v.astype(jnp.bfloat16)).astype(jnp.float32)

@jax.custom_vjp
def low_back(v):
    return v

def low_keep(v):
    return (low(v), None)

def low_pass(kept, grad):
    return (grad,)

def back_keep(v):
    return (v, None)

def back_low(kept, grad):
    return (low(grad),)
low.defvjp(low_keep, low_pass)
low_back.defvjp(back_keep, back_low)
EPS = 1e-05
MASKED = -1000000000.0
NEG = -1e+30
HIGH = lax.Precision.HIGHEST

def log_total(value, axis):
    top = lax.optimization_barrier(jnp.max(value, axis, keepdims=True))
    return jnp.squeeze(top, axis) + jnp.log(lax.optimization_barrier(jnp.sum(jnp.exp(value - top), axis)))

def lattice(blank, label, dur, t_len, u_len):
    utts, frames, slots = blank.shape
    reach = dur.shape[-1] - 1
    lower = lax.broadcasted_iota(jnp.int32, (slots, slots), 1) <= lax.broadcasted_iota(jnp.int32, (slots, slots), 0)
    start_row = jnp.where(lax.broadcasted_iota(jnp.int32, (utts, 1, slots), 2) == 0, 0.0, NEG).astype(jnp.float32)
    pending = jnp.concatenate([start_row, jnp.full((utts, reach - 1, slots), NEG, jnp.float32)], 1)
    edge = jnp.full((utts, 1), NEG, jnp.float32)

    def advance(waiting, inputs):
        blank_t, label_t, dur_t = inputs
        arrive = waiting[:, 0]
        emit = label_t + dur_t[:, :, 0]
        climb = jnp.cumsum(emit, -1) - emit
        table = jnp.where(lower[None], (arrive - climb)[:, None, :], NEG)
        alpha = climb + log_total(table, -1)
        moves = []
        for skip in range(1, reach + 1):
            stay = alpha + blank_t + dur_t[:, :, skip]
            rise = jnp.concatenate([edge, (alpha + label_t + dur_t[:, :, skip])[:, :-1]], 1)
            moves.append(jnp.logaddexp(stay, rise))
        later = [jnp.logaddexp(waiting[:, skip], moves[skip - 1]) for skip in range(1, reach)] + [moves[reach - 1]]
        return (jnp.stack(later, 1), alpha)
    inputs = (jnp.swapaxes(blank, 0, 1), jnp.swapaxes(label, 0, 1), jnp.swapaxes(dur, 0, 1))
    unused, alphas = lax.scan(advance, pending, inputs)
    alphas = jnp.swapaxes(alphas, 0, 1)
    times = lax.broadcasted_iota(jnp.int32, (utts, frames, slots), 1)
    places = lax.broadcasted_iota(jnp.int32, (utts, frames, slots), 2)
    at_end = places == u_len[:, None, None]
    ends = []
    for skip in range(1, reach + 1):
        hit = at_end & (times + skip == t_len[:, None, None])
        ends.append(jnp.where(hit, alphas + blank + dur[..., skip], NEG))
    return log_total(jnp.stack(ends, -1).reshape(utts, -1), -1)

def norm_rows(value, gain):
    centre = lax.optimization_barrier(jnp.mean(value, -1, keepdims=True))
    centred = value - centre
    spread = lax.optimization_barrier(jnp.mean(centred * centred, -1, keepdims=True))
    return centred * lax.rsqrt(spread + EPS) * gain

def project(value, weight):
    return low_back(jnp.dot(low(value), weight, precision=HIGH, preferred_element_type=jnp.float32))

def feed_forward(resid, gain, w_in, w_out):
    hidden = project(norm_rows(resid, gain), w_in)
    return resid + 0.5 * project(jax.nn.silu(hidden), w_out)

def attend_one(item):
    query, key, value, bias = item
    scale = query.shape[-1] ** (-0.5)
    scores = low_back(jnp.einsum('qhe,khe->hqk', query, key, precision=HIGH) * scale) + bias
    weights = jax.nn.softmax(scores, axis=-1)
    return low_back(jnp.einsum('hqk,khe->qhe', low(weights), value, precision=HIGH))

def attention(resid, gain, w_joint, w_proj, key_bias):
    rows, width = resid.shape
    utts = key_bias.shape[0]
    joint = low(project(norm_rows(resid, gain), w_joint)).reshape(utts, rows // utts, 3, HEADS, width // HEADS)
    context = lax.map(jax.checkpoint(attend_one), (joint[:, :, 0], joint[:, :, 1], joint[:, :, 2], key_bias))
    return resid + project(context.reshape(rows, width), w_proj)

def conv_inner(projected, depth, valid_rows, utts):
    rows, double = projected.shape
    width = double // 2
    frames = rows // utts
    taps = depth.shape[0]
    gated = projected[:, :width] * jax.nn.sigmoid(projected[:, width:]) * valid_rows
    padded = jnp.pad(gated.reshape(utts, frames, width), ((0, 0), (taps // 2, taps // 2), (0, 0)))
    total = padded[:, 0:frames] * depth[0]
    for tap in range(1, taps):
        total = total + padded[:, tap:tap + frames] * depth[tap]
    return total.reshape(rows, width)

def convolution(resid, gain, w_in, depth, bn_gain, bn_bias, w_out, valid_rows, utts):
    projected = project(norm_rows(resid, gain), w_in)
    depthwise = conv_inner(projected, depth, valid_rows, utts)
    count = jnp.sum(valid_rows)
    centre = lax.optimization_barrier(jnp.sum(depthwise * valid_rows, 0)) / count
    centred = depthwise - centre
    spread = lax.optimization_barrier(jnp.sum(valid_rows * centred * centred, 0)) / count
    shifted = centred * lax.rsqrt(spread + EPS) * bn_gain + bn_bias
    return resid + project(jax.nn.silu(shifted), w_out)

def reference(frames_in, frame_lengths, label_ids, label_lengths, pred_states, norm_gains, first_in, first_out, attend_joint, attend_out, point_in, depth_taps, batch_gain, batch_bias, point_out, second_in, second_out, enc_weight, pred_weight, token_weight, duration_weight):
    utts, frames, width = frames_in.shape
    slots = pred_states.shape[1]
    rows = utts * frames
    positions = lax.broadcasted_iota(jnp.int32, (utts, frames), 1)
    valid = (positions < frame_lengths[:, None]).astype(jnp.float32)
    valid_rows = valid.reshape(rows, 1)
    key_bias = ((1.0 - valid) * MASKED)[:, None, None, :]
    labels_ext = jnp.concatenate([label_ids, jnp.zeros((utts, 1), jnp.int32)], 1).astype(jnp.int32)
    pred_in = pred_states.astype(jnp.float32)
    params = tuple((w.astype(jnp.float32) for w in (norm_gains, first_in, first_out, attend_joint, attend_out, point_in, depth_taps, batch_gain, batch_bias, point_out, second_in, second_out, enc_weight, pred_weight, token_weight, duration_weight)))

    def forward(start, weights):
        gains, f_in, f_out, w_joint, w_proj, p_in, depth, bn_gain, bn_bias, p_out, s_in, s_out, w_enc, w_pred, w_tok, w_dur = weights
        resid = start
        for layer in range(gains.shape[0]):
            resid = feed_forward(resid, gains[layer, 0], f_in[layer], f_out[layer])
            resid = attention(resid, gains[layer, 1], w_joint[layer], w_proj[layer], key_bias)
            resid = convolution(resid, gains[layer, 2], p_in[layer], depth[layer], bn_gain[layer], bn_bias[layer], p_out[layer], valid_rows, utts)
            resid = feed_forward(resid, gains[layer, 3], s_in[layer], s_out[layer])
            resid = norm_rows(resid, gains[layer, 4])
        joint = w_enc.shape[1]
        enc = project(resid, w_enc).reshape(utts, frames, joint)
        pred = project(pred_in.reshape(utts * slots, joint), w_pred).reshape(utts, slots, joint)

        def joint_one(item):
            enc_u, pred_u, lab_u = item
            hidden = low(jnp.tanh(enc_u[:, None, :] + pred_u[None, :, :]))
            tok = low_back(jnp.einsum('tsj,jv->tsv', hidden, w_tok, precision=HIGH))
            durl = low_back(jnp.einsum('tsj,jv->tsv', hidden, w_dur, precision=HIGH))
            total = log_total(tok, -1)
            blank = tok[..., 0] - total
            picked = jnp.take_along_axis(tok, jnp.broadcast_to(lab_u[None, :, None], (frames, slots, 1)).astype(jnp.int32), -1)
            label = picked[..., 0] - total
            dur = durl - log_total(durl, -1)[..., None]
            return (blank, label, dur)
        blank, label, dur = lax.map(jax.checkpoint(joint_one), (enc, pred, labels_ext))
        log_prob = lattice(blank, label, dur, frame_lengths, label_lengths)
        return (-jnp.sum(log_prob), log_prob)
    start = frames_in.reshape(rows, width).astype(jnp.float32)
    objective, pullback, log_prob = jax.vjp(forward, start, params, has_aux=True)
    grad_start, grads = pullback(jnp.ones_like(objective))
    utt_loss = -log_prob / frame_lengths.astype(jnp.float32)
    return (utt_loss, grad_start.reshape(utts, frames, width), grads[0], grads[1], grads[2], grads[3], grads[4], grads[5], grads[6], grads[7], grads[8], grads[9], grads[10], grads[11], grads[12], grads[13], grads[14], grads[15])
```

```python
import functools
from functools import partial

import jax
import jax.numpy as jnp
from jax import lax
from jax.experimental import pallas as pl
from jax.experimental.pallas import tpu as pltpu
from jax.sharding import PartitionSpec as P

HEADS = 8


EPS = 1e-05
MASKED = -1000000000.0
NEG = -1e30


def lattice_kernel(slots, feats_ref, tlen_ref, ulen_ref, grads_ref, prob_ref, s_ref, l_ref, ls_ref, a_ref, b_ref, init_ref):
    utts = tlen_ref.shape[0]
    frames = feats_ref.shape[2]
    rows = feats_ref.shape[1]
    wide = frames + 128
    reach = feats_ref.shape[0] - 3
    diags = frames + slots
    pad = 8
    total = a_ref.shape[0]
    body = wide

    def skew(x, sign):
        k = lax.broadcasted_iota(jnp.int32, x.shape, 0) % 32
        for bit in range(5):
            step = 1 << bit
            x = jnp.where((k // step) % 2 == 1, pltpu.roll(x, step if sign > 0 else wide - step, 1), x)
        return x

    def to_diag(x):
        x = jnp.concatenate([x, jnp.zeros((rows, 128), jnp.float32)], 1)
        x = skew(x, 1)
        x = jnp.concatenate([x, jnp.zeros((128 - rows, wide), jnp.float32)], 0)
        return x.T

    lane = lax.broadcasted_iota(jnp.int32, (wide, 128), 1)
    diag = lax.broadcasted_iota(jnp.int32, (wide, 128), 0)
    k_of = lane % 32
    t_of = diag - k_of
    t_len = jnp.full((wide, 128), -1, jnp.int32)
    u_len = jnp.full((wide, 128), -1, jnp.int32)
    for u in range(utts):
        mine = (lane // 32) == u
        t_len = jnp.where(mine, tlen_ref[u], t_len)
        u_len = jnp.where(mine, ulen_ref[u], u_len)
    blank = to_diag(feats_ref[0])
    label = to_diag(feats_ref[1])
    edge = jnp.full((pad, 128), NEG, jnp.float32)
    real = (t_of >= 0)
    for ref in (s_ref, l_ref, ls_ref):
        for e in range(ref.shape[0]):
            ref[e, 0:pad, :] = edge
            ref[e, pad + wide:, :] = jnp.full((ref.shape[1] - pad - wide, 128), NEG, jnp.float32)
    for e in range(reach + 1):
        dur = to_diag(feats_ref[2 + e])
        if e > 0:
            keep = real & (k_of <= u_len) & ((t_of + e < t_len) | ((t_of + e == t_len) & (k_of == u_len)))
            s_ref[e - 1, pad:pad + wide, :] = jnp.where(keep, blank + dur, NEG)
        keep = real & (k_of < u_len) & (t_of + e < t_len)
        lab = jnp.where(keep, label + dur, NEG)
        l_ref[e, pad:pad + wide, :] = lab
        ls_ref[e, pad:pad + wide, :] = pltpu.roll(lab, 1, 1)
    init_ref[pad:pad + wide, :] = jnp.where((t_of == t_len) & (k_of == u_len), 0.0, NEG)
    a_ref[...] = jnp.full(a_ref.shape, NEG, jnp.float32)
    b_ref[...] = jnp.full(b_ref.shape, NEG, jnp.float32)

    first = jnp.where((lax.broadcasted_iota(jnp.int32, (1, 128), 1) % 32 == 0)
                      & (lax.broadcasted_iota(jnp.int32, (1, 128), 1) < 32 * utts), 0.0, NEG)

    def lse(terms):
        tops = list(terms)
        while len(tops) > 1:
            tops = [jnp.maximum(tops[i], tops[i + 1]) if i + 1 < len(tops) else tops[i] for i in range(0, len(tops), 2)]
        top = tops[0]
        parts = [jnp.exp(x - top) for x in terms]
        while len(parts) > 1:
            parts = [parts[i] + parts[i + 1] if i + 1 < len(parts) else parts[i] for i in range(0, len(parts), 2)]
        return jnp.maximum(top + jnp.log(parts[0]), NEG)

    a_ref[pl.ds(pad, 1), :] = first
    last = diags

    def step(i, carry):
        ha, hra, hb, hrb = carry
        row = pad + i
        terms = [ha[e - 1] + s_ref[e - 1, pl.ds(row - e, 1), :] for e in range(1, reach + 1)]
        terms += [hra[e] + ls_ref[e, pl.ds(row - e - 1, 1), :] for e in range(reach + 1)]
        a = lse(terms[::-1])
        a_ref[pl.ds(row, 1), :] = a
        ra = pltpu.roll(a, 1, 1)
        rowb = pad + last - i
        terms = [hb[e - 1] + s_ref[e - 1, pl.ds(rowb, 1), :] for e in range(1, reach + 1)]
        terms += [hrb[e] + l_ref[e, pl.ds(rowb, 1), :] for e in range(reach + 1)]
        b = jnp.maximum(lse(terms[::-1]), init_ref[pl.ds(rowb, 1), :])
        b_ref[pl.ds(rowb, 1), :] = b
        rb = pltpu.roll(b, 127, 1)
        return ((a,) + ha[:-1], (ra,) + hra[:-1], (b,) + hb[:-1], (rb,) + hrb[:-1])

    b0 = init_ref[pl.ds(pad + last, 1), :]
    b_ref[pl.ds(pad + last, 1), :] = b0
    none = a_ref[pl.ds(0, 1), :]
    first = a_ref[pl.ds(pad, 1), :]
    ha = (first,) + (none,) * (reach - 1)
    hra = (pltpu.roll(first, 1, 1),) + (none,) * reach
    hb = (b0,) + (none,) * (reach - 1)
    hrb = (pltpu.roll(b0, 127, 1),) + (none,) * reach
    lax.fori_loop(1, last + 1, step, (ha, hra, hb, hrb))

    zrow = b_ref[pl.ds(pad, 1), :]
    lane1 = lax.broadcasted_iota(jnp.int32, (1, 128), 1)
    z = jnp.zeros((1, 128), jnp.float32)
    for u in range(utts):
        zu = jnp.max(jnp.where(lane1 == 32 * u, zrow, 2 * NEG), axis=1, keepdims=True)
        z = jnp.where(lane1 // 32 == u, zu, z)
        prob_ref[pl.ds(u, 1), :] = jnp.broadcast_to(zu, (1, 128))

    def from_diag(x):
        x = x.T[:rows]
        return skew(x, -1)[:, :frames]

    a = a_ref[pad:pad + wide, :] - z
    g_blank = jnp.zeros((wide, 128), jnp.float32)
    g_label = jnp.zeros((wide, 128), jnp.float32)
    for e in range(reach + 1):
        bb = b_ref[pad + e + 1: pad + e + 1 + wide, :]
        pl_ = jnp.exp(a + l_ref[e, pad:pad + wide, :] + pltpu.roll(bb, 127, 1))
        g_label = g_label - pl_
        g = -pl_
        if e > 0:
            ps = jnp.exp(a + s_ref[e - 1, pad:pad + wide, :] + b_ref[pad + e: pad + e + wide, :])
            g_blank = g_blank - ps
            g = g - ps
        grads_ref[2 + e] = from_diag(g)
    grads_ref[0] = from_diag(g_blank)
    grads_ref[1] = from_diag(g_label)


def lattice(feats, t_len, u_len, slots):
    _, rows, frames = feats.shape
    wide = frames + 128
    total = wide + 16
    reach = feats.shape[0] - 3
    return pl.pallas_call(
        functools.partial(lattice_kernel, slots),
        out_shape=(jax.ShapeDtypeStruct(feats.shape, jnp.float32), jax.ShapeDtypeStruct((8, 128), jnp.float32)),
        in_specs=[pl.BlockSpec(memory_space=pltpu.VMEM), pl.BlockSpec(memory_space=pltpu.SMEM), pl.BlockSpec(memory_space=pltpu.SMEM)],
        out_specs=(pl.BlockSpec(memory_space=pltpu.VMEM),) * 2,
        scratch_shapes=[pltpu.VMEM((reach, total, 128), jnp.float32), pltpu.VMEM((reach + 1, total, 128), jnp.float32),
                        pltpu.VMEM((reach + 1, total, 128), jnp.float32), pltpu.VMEM((total, 128), jnp.float32),
                        pltpu.VMEM((total, 128), jnp.float32), pltpu.VMEM((total, 128), jnp.float32)],
        compiler_params=pltpu.CompilerParams(vmem_limit_bytes=48 << 20),
        name="lattice",
    )(feats, t_len, u_len)


GROUP=5
CHUNK=256

def nn(a,b): return jnp.dot(a,b,preferred_element_type=jnp.float32)
def nt(a,b): return lax.dot_general(a,b,(((1,),(1,)),((),())),preferred_element_type=jnp.float32)

def fold8(x, op):
    parts=[x[i:i+8] for i in range(0,x.shape[0],8)]
    while len(parts)>1:
        parts=[op(parts[i],parts[i+1]) if i+1<len(parts) else parts[i] for i in range(0,len(parts),2)]
    return parts[0]

def joint_fwd_kernel(groups, durs, labels_ref, enc_ref, pred_ref, wt_ref, feats_ref, p_ref, tok_ref):
    step=pl.program_id(0)
    vocab=p_ref.shape[2]
    u=step//groups
    g=step%groups
    for j in range(GROUP):
        k=g*GROUP+j
        hid=jnp.tanh(enc_ref[...]+pred_ref[0,:,j:j+1]).astype(jnp.bfloat16)
        tops=[]
        for c in range(0,vocab,CHUNK):
            t=nn(wt_ref[c:c+CHUNK,:],hid)
            tok_ref[j%2,c:c+CHUNK,:]=t
            tops.append(fold8(t,jnp.maximum))
        dl=nn(wt_ref[vocab:,:],hid)[:8]
        top=jnp.max(functools.reduce(jnp.maximum,tops),0,keepdims=True)
        sums=[]
        for c in range(0,vocab,CHUNK):
            e=jnp.exp(tok_ref[j%2,c:c+CHUNK,:]-top)
            p_ref[0,j,c:c+CHUNK,:]=e.astype(jnp.bfloat16)
            sums.append(fold8(e,jnp.add))
        total=jnp.sum(functools.reduce(jnp.add,sums),0,keepdims=True)
        lse=top+jnp.log(total)
        row=u*32+k
        feats_ref[0,pl.ds(row,1),:]=tok_ref[j%2,0:1,:]-lse
        feats_ref[1,pl.ds(row,1),:]=tok_ref[j%2,pl.ds(labels_ref[u,k],1),:]-lse
        real=lax.broadcasted_iota(jnp.int32,dl.shape,0)<durs
        dtop=jnp.max(jnp.where(real,dl,-1e30),0,keepdims=True)
        dlse=dtop+jnp.log(jnp.sum(jnp.where(real,jnp.exp(dl-dtop),0.0),0,keepdims=True))
        dlp=dl-dlse
        for e in range(durs):
            feats_ref[2+e,pl.ds(row,1),:]=dlp[e:e+1]
        feats_ref[2+durs,pl.ds(row,1),:]=1.0/total

def joint_forward(enc_t, pred_t, labels, w_t, vocab, durs, frames):
    joint, rows=enc_t.shape
    utts,slots=labels.shape
    groups=slots//GROUP
    return pl.pallas_call(
        partial(joint_fwd_kernel,groups,durs),
        grid=(utts*groups,),
        in_specs=[pl.BlockSpec(memory_space=pltpu.SMEM),
            pl.BlockSpec((joint,frames),lambda s:(0,s//groups)),
            pl.BlockSpec((1,joint,8),lambda s:(s,0,0)),
            pl.BlockSpec(w_t.shape,lambda s:(0,0))],
        out_specs=[pl.BlockSpec((3+durs,utts*32,frames),lambda s:(0,0,0)),
            pl.BlockSpec((1,GROUP,vocab,frames),lambda s:(s,0,0,0))],
        out_shape=[jax.ShapeDtypeStruct((3+durs,utts*32,frames),jnp.float32),
            jax.ShapeDtypeStruct((utts*groups,GROUP,vocab,frames),jnp.bfloat16)],
        scratch_shapes=[pltpu.VMEM((2,vocab,frames),jnp.float32)],
        compiler_params=pltpu.CompilerParams(vmem_limit_bytes=50<<20),
        name="joint_forward",
    )(labels,enc_t,pred_t,w_t)

def joint_bwd_kernel(groups, durs, labels_ref, enc_ref, pred_ref, w_ref, feats_ref, grads_ref, p_ref, genc_ref, gpred_ref, gtok_ref, gdur_ref, h_ref, d_ref, acc_ref):
    step=pl.program_id(0)
    vocab=p_ref.shape[2]
    frames=p_ref.shape[3]
    u=step//groups
    g=step%groups

    @pl.when(step==0)
    def _():
        acc_ref[...]=jnp.zeros_like(acc_ref)
    @pl.when(g==0)
    def _():
        genc_ref[...]=jnp.zeros_like(genc_ref)
    for j in range(GROUP):
        k=g*GROUP+j
        row=u*32+k
        cols=slice(j*frames,(j+1)*frames)
        th=jnp.tanh(enc_ref[...]+pred_ref[0,:,j:j+1])
        h_ref[:,cols]=th.astype(jnp.bfloat16)
        gb=grads_ref[0,pl.ds(row,1),:]
        gl=grads_ref[1,pl.ds(row,1),:]
        scale=-(gb+gl)*feats_ref[2+durs,pl.ds(row,1),:]
        for c in range(0,vocab,CHUNK):
            d_ref[c:c+CHUNK,cols]=(p_ref[0,j,c:c+CHUNK,:].astype(jnp.float32)*scale).astype(jnp.bfloat16)
        label=labels_ref[u,k]
        def fix(base):
            v=p_ref[0,j,pl.ds(base,16),:].astype(jnp.float32)*scale
            at=lax.broadcasted_iota(jnp.int32,v.shape,0)+base
            v=v+jnp.where(at==0,gb,0.0)+jnp.where(at==label,gl,0.0)
            d_ref[pl.ds(base,16),cols]=v.astype(jnp.bfloat16)
        fix(0)
        fix(pl.multiple_of((label//16)*16,16))
        gd=[grads_ref[2+e,pl.ds(row,1),:] for e in range(durs)]
        gsum=functools.reduce(jnp.add,gd)
        at=lax.broadcasted_iota(jnp.int32,(16,frames),0)
        dd=jnp.zeros((16,frames),jnp.float32)
        for e in range(durs):
            dd=jnp.where(at==e,gd[e]-gsum*jnp.exp(feats_ref[2+e,pl.ds(row,1),:]),dd)
        d_ref[vocab:vocab+16,cols]=dd.astype(jnp.bfloat16)
        d_ref[vocab+16:,cols]=jnp.zeros((d_ref.shape[0]-vocab-16,frames),jnp.bfloat16)
        dh=nn(w_ref[...],d_ref[:,cols])
        th=jnp.tanh(enc_ref[...]+pred_ref[0,:,j:j+1])
        dp=dh*(1.0-th*th)
        genc_ref[...]+=dp
        gpred_ref[0,:,j:j+1]=jnp.sum(dp,1,keepdims=True)
    for c in range(0,d_ref.shape[0],384):
        acc_ref[:,c:c+384]+=nt(h_ref[...],d_ref[c:c+384,:])
    @pl.when(step==pl.num_programs(0)-1)
    def _():
        gtok_ref[...]=acc_ref[:,:vocab].astype(jnp.bfloat16)
        gdur_ref[...]=acc_ref[:,vocab:].astype(jnp.bfloat16)

def joint_backward(enc_t, pred_t, labels, w, feats, grads, p, vocab, durs, frames):
    joint, rows=enc_t.shape
    utts,slots=labels.shape
    groups=slots//GROUP
    full=lambda a: pl.BlockSpec(a.shape,lambda s:(0,)*a.ndim)
    return pl.pallas_call(
        partial(joint_bwd_kernel,groups,durs),
        grid=(utts*groups,),
        in_specs=[pl.BlockSpec(memory_space=pltpu.SMEM),
            pl.BlockSpec((joint,frames),lambda s:(0,s//groups)),
            pl.BlockSpec((1,joint,8),lambda s:(s,0,0)),
            full(w),full(feats),full(grads),
            pl.BlockSpec((1,GROUP,vocab,frames),lambda s:(s,0,0,0))],
        out_specs=[pl.BlockSpec((joint,frames),lambda s:(0,s//groups)),
            pl.BlockSpec((1,joint,8),lambda s:(s,0,0)),
            pl.BlockSpec((joint,vocab),lambda s:(0,0)),
            pl.BlockSpec((joint,128),lambda s:(0,0))],
        out_shape=[jax.ShapeDtypeStruct((joint,rows),jnp.float32),
            jax.ShapeDtypeStruct((utts*groups,joint,8),jnp.float32),
            jax.ShapeDtypeStruct((joint,vocab),jnp.bfloat16),
            jax.ShapeDtypeStruct((joint,128),jnp.bfloat16)],
        scratch_shapes=[pltpu.VMEM((joint,GROUP*frames),jnp.bfloat16),
            pltpu.VMEM((vocab+128,GROUP*frames),jnp.bfloat16),
            pltpu.VMEM((joint,vocab+128),jnp.float32)],
        compiler_params=pltpu.CompilerParams(vmem_limit_bytes=56<<20),
        name="joint_backward",
    )(labels,enc_t,pred_t,w,feats,grads,p)


def norm_rows(value, gain):
    centre = jnp.mean(value, -1, keepdims=True)
    centred = value - centre
    spread = jnp.mean(centred * centred, -1, keepdims=True)
    return centred * lax.rsqrt(spread + EPS) * gain


def norm_back(value, gain, grad):
    result, pullback = jax.vjp(norm_rows, value, gain)
    return pullback(grad)


def matmul(left, right):
    return jnp.dot(left, right, preferred_element_type=jnp.float32)


def contract_rows(left, right):
    return lax.dot_general(
        left, right, (((0,), (0,)), ((), ())), preferred_element_type=jnp.float32
    )


def contract_cols(left, right):
    return lax.dot_general(
        left, right, (((1,), (1,)), ((), ())), preferred_element_type=jnp.float32
    )


def swish_slope(value):
    sigmoid_value = jax.nn.sigmoid(value)
    return sigmoid_value * (1.0 + value * (1.0 - sigmoid_value))


def ffn_forward(resid, gain, w_in, w_out):
    normed_low = norm_rows(resid, gain).astype(jnp.bfloat16)
    hidden = matmul(normed_low, w_in)
    active_low = jax.nn.silu(hidden).astype(jnp.bfloat16)
    return (resid + 0.5 * matmul(active_low, w_out), (normed_low, hidden, active_low))


def ffn_backward(resid, gain, w_in, w_out, saved, grad_out):
    normed_low, hidden, active_low = saved
    grad_branch = (0.5 * grad_out).astype(jnp.bfloat16)
    grad_w_out = contract_rows(active_low, grad_branch)
    grad_hidden = (contract_cols(grad_branch, w_out) * swish_slope(hidden)).astype(jnp.bfloat16)
    grad_w_in = contract_rows(normed_low, grad_hidden)
    grad_normed = contract_cols(grad_hidden, w_in)
    grad_resid, grad_gain = norm_back(resid, gain, grad_normed)
    return (grad_out + grad_resid, grad_gain, grad_w_in, grad_w_out)


def attend_forward(resid, gain, w_joint, w_proj, key_bias):
    rows, width = resid.shape
    utts = key_bias.shape[0]
    head_dim = width // HEADS
    normed_low = norm_rows(resid, gain).astype(jnp.bfloat16)
    joint_low = (
        matmul(normed_low, w_joint)
        .astype(jnp.bfloat16)
        .reshape(utts, rows // utts, 3, HEADS, head_dim)
    )
    scores = (
        jnp.einsum(
            "uqhe,ukhe->uhqk",
            joint_low[:, :, 0],
            joint_low[:, :, 1],
            preferred_element_type=jnp.float32,
        )
        * head_dim ** (-0.5)
        + key_bias
    )
    weights = jax.nn.softmax(scores, axis=-1)
    weights_low = weights.astype(jnp.bfloat16)
    context = jnp.einsum(
        "uhqk,ukhe->uqhe", weights_low, joint_low[:, :, 2], preferred_element_type=jnp.float32
    )
    context_low = context.reshape(rows, width).astype(jnp.bfloat16)
    return (
        resid + matmul(context_low, w_proj),
        (normed_low, joint_low, weights, weights_low, context_low),
    )


def attend_backward(resid, gain, w_joint, w_proj, saved, grad_out):
    normed_low, joint_low, weights, weights_low, context_low = saved
    rows, width = resid.shape
    utts, frames, three, heads, head_dim = joint_low.shape
    scale = head_dim ** (-0.5)
    query, key, value = (joint_low[:, :, 0], joint_low[:, :, 1], joint_low[:, :, 2])
    grad_branch = grad_out.astype(jnp.bfloat16)
    grad_proj = contract_rows(context_low, grad_branch)
    grad_context = (
        contract_cols(grad_branch, w_proj)
        .astype(jnp.bfloat16)
        .reshape(utts, frames, heads, head_dim)
    )
    grad_weights = jnp.einsum(
        "uqhe,ukhe->uhqk", grad_context, value, preferred_element_type=jnp.float32
    )
    grad_value = jnp.einsum(
        "uhqk,uqhe->ukhe", weights_low, grad_context, preferred_element_type=jnp.float32
    )
    grad_scores = (
        weights * (grad_weights - jnp.sum(grad_weights * weights, -1, keepdims=True))
    ).astype(jnp.bfloat16)
    grad_query = (
        jnp.einsum("uhqk,ukhe->uqhe", grad_scores, key, preferred_element_type=jnp.float32) * scale
    )
    grad_key = (
        jnp.einsum("uhqk,uqhe->ukhe", grad_scores, query, preferred_element_type=jnp.float32)
        * scale
    )
    grad_joint = (
        jnp.stack([grad_query, grad_key, grad_value], 2)
        .reshape(rows, 3 * width)
        .astype(jnp.bfloat16)
    )
    grad_w_joint = contract_rows(normed_low, grad_joint)
    grad_normed = contract_cols(grad_joint, w_joint)
    grad_resid, grad_gain = norm_back(resid, gain, grad_normed)
    return (grad_out + grad_resid, grad_gain, grad_w_joint, grad_proj)


def conv_inner(projected, depth, valid_rows, utts):
    rows, double = projected.shape
    width = double // 2
    frames = rows // utts
    taps = depth.shape[0]
    gated = projected[:, :width] * jax.nn.sigmoid(projected[:, width:]) * valid_rows
    padded = jnp.pad(gated.reshape(utts, frames, width), ((0, 0), (taps // 2, taps // 2), (0, 0)))
    total = padded[:, 0:frames] * depth[0]
    for tap in range(1, taps):
        total = total + padded[:, tap : tap + frames] * depth[tap]
    return total.reshape(rows, width)


def batch_stats(depthwise, valid_rows):
    total, count = lax.psum(
        (jnp.sum(depthwise * valid_rows, 0), jnp.sum(valid_rows)), ("dp", "fsdp")
    )
    centre = total / count
    centred = depthwise - centre
    spread = lax.psum(jnp.sum(valid_rows * centred * centred, 0), ("dp", "fsdp")) / count
    return (centre, lax.rsqrt(spread + EPS), count)


def run_layer(resid, weights, valid_rows, key_bias):
    gains, f_in, f_out, w_joint, w_proj, p_in, depth, bn_gain, bn_bias, p_out, s_in, s_out = weights
    gains = gains.astype(jnp.float32)
    utts = key_bias.shape[0]
    first, saved_first = ffn_forward(resid, gains[0], f_in, f_out)
    second, saved_attend = attend_forward(first, gains[1], w_joint, w_proj, key_bias)
    normed_low = norm_rows(second, gains[2]).astype(jnp.bfloat16)
    projected = matmul(normed_low, p_in)
    depthwise = conv_inner(projected, depth.astype(jnp.float32), valid_rows, utts)
    centre, inv_std, count = batch_stats(depthwise, valid_rows)
    normalized = (depthwise - centre) * inv_std
    shifted = normalized * bn_gain.astype(jnp.float32) + bn_bias.astype(jnp.float32)
    active_low = jax.nn.silu(shifted).astype(jnp.bfloat16)
    third = second + matmul(active_low, p_out)
    fourth, saved_fourth = ffn_forward(third, gains[3], s_in, s_out)
    output = norm_rows(fourth, gains[4])
    record = (
        resid,
        first,
        second,
        third,
        fourth,
        saved_first,
        saved_attend,
        saved_fourth,
        normed_low,
        projected,
        normalized,
        shifted,
        active_low,
        inv_std,
        count,
    )
    return (output, record)


def layer_backward(weights, record, grad_out, valid_rows, key_bias):
    gains, f_in, f_out, w_joint, w_proj, p_in, depth, bn_gain, bn_bias, p_out, s_in, s_out = weights
    gains = gains.astype(jnp.float32)
    utts = key_bias.shape[0]
    (
        resid,
        first,
        second,
        third,
        fourth,
        saved_first,
        saved_attend,
        saved_fourth,
        normed_low,
        projected,
        normalized,
        shifted,
        active_low,
        inv_std,
        count,
    ) = record
    grad_fourth, grad_gain_four = norm_back(fourth, gains[4], grad_out)
    grad_third, grad_gain_three, grad_s_in, grad_s_out = ffn_backward(
        third, gains[3], s_in, s_out, saved_fourth, grad_fourth
    )
    grad_branch = grad_third.astype(jnp.bfloat16)
    grad_p_out = contract_rows(active_low, grad_branch)
    grad_shifted = contract_cols(grad_branch, p_out) * swish_slope(shifted)
    bias_sum, gain_sum = lax.psum(
        (jnp.sum(grad_shifted, 0), jnp.sum(grad_shifted * normalized, 0)), ("dp", "fsdp")
    )
    grad_depthwise = (
        bn_gain.astype(jnp.float32)
        * inv_std
        * (grad_shifted - valid_rows * (bias_sum + normalized * gain_sum) / count)
    )
    conv_local = partial(conv_inner, valid_rows=valid_rows, utts=utts)
    result, pullback = jax.vjp(conv_local, projected, depth.astype(jnp.float32))
    grad_projected, grad_depth = pullback(grad_depthwise)
    grad_projected_low = grad_projected.astype(jnp.bfloat16)
    grad_p_in = contract_rows(normed_low, grad_projected_low)
    grad_normed = contract_cols(grad_projected_low, p_in)
    grad_conv_resid, grad_gain_two = norm_back(second, gains[2], grad_normed)
    grad_second = grad_third + grad_conv_resid
    grad_first, grad_gain_one, grad_joint, grad_proj = attend_backward(
        first, gains[1], w_joint, w_proj, saved_attend, grad_second
    )
    grad_resid, grad_gain_zero, grad_f_in, grad_f_out = ffn_backward(
        resid, gains[0], f_in, f_out, saved_first, grad_first
    )
    grad_gains = jnp.stack(
        [grad_gain_zero, grad_gain_one, grad_gain_two, grad_gain_three, grad_gain_four]
    )
    return (
        grad_resid,
        (
            grad_gains,
            grad_f_in,
            grad_f_out,
            grad_joint,
            grad_proj,
            grad_p_in,
            grad_depth,
            gain_sum,
            bias_sum,
            grad_p_out,
            grad_s_in,
            grad_s_out,
        ),
    )


def reduce_grads(stacked, joint_grads):
    shares = (
        lax.psum_scatter(
            stacked[0].astype(jnp.bfloat16), "fsdp", scatter_dimension=1, tiled=True
        ).astype(jnp.float32),
        lax.psum_scatter(
            stacked[1].astype(jnp.bfloat16), "fsdp", scatter_dimension=1, tiled=True
        ).astype(jnp.float32),
        lax.psum_scatter(
            stacked[2].astype(jnp.bfloat16), "fsdp", scatter_dimension=1, tiled=True
        ).astype(jnp.float32),
        lax.psum_scatter(
            stacked[3].astype(jnp.bfloat16), "fsdp", scatter_dimension=1, tiled=True
        ).astype(jnp.float32),
        lax.psum_scatter(
            stacked[4].astype(jnp.bfloat16), "fsdp", scatter_dimension=1, tiled=True
        ).astype(jnp.float32),
        lax.psum_scatter(
            stacked[5].astype(jnp.bfloat16), "fsdp", scatter_dimension=1, tiled=True
        ).astype(jnp.float32),
        lax.psum_scatter(
            stacked[6].astype(jnp.bfloat16), "fsdp", scatter_dimension=1, tiled=True
        ).astype(jnp.float32),
        lax.psum_scatter(
            stacked[7].astype(jnp.bfloat16), "fsdp", scatter_dimension=1, tiled=True
        ).astype(jnp.float32),
        lax.psum_scatter(
            stacked[8].astype(jnp.bfloat16), "fsdp", scatter_dimension=1, tiled=True
        ).astype(jnp.float32),
        lax.psum_scatter(
            stacked[9].astype(jnp.bfloat16), "fsdp", scatter_dimension=1, tiled=True
        ).astype(jnp.float32),
        lax.psum_scatter(
            joint_grads[0].astype(jnp.bfloat16), "fsdp", scatter_dimension=0, tiled=True
        ).astype(jnp.float32),
        lax.psum_scatter(
            joint_grads[1].astype(jnp.bfloat16), "fsdp", scatter_dimension=0, tiled=True
        ).astype(jnp.float32),
        lax.psum_scatter(
            joint_grads[2].astype(jnp.bfloat16), "fsdp", scatter_dimension=0, tiled=True
        ).astype(jnp.float32),
        lax.psum_scatter(
            joint_grads[3].astype(jnp.bfloat16), "fsdp", scatter_dimension=0, tiled=True
        ).astype(jnp.float32),
    )
    return (
        lax.psum(shares[0].astype(jnp.bfloat16), "dp").astype(jnp.float32),
        lax.psum(shares[1].astype(jnp.bfloat16), "dp").astype(jnp.float32),
        lax.psum(shares[2].astype(jnp.bfloat16), "dp").astype(jnp.float32),
        lax.psum(shares[3].astype(jnp.bfloat16), "dp").astype(jnp.float32),
        lax.psum(shares[4].astype(jnp.bfloat16), "dp").astype(jnp.float32),
        lax.psum(shares[5].astype(jnp.bfloat16), "dp").astype(jnp.float32),
        lax.psum(shares[6].astype(jnp.bfloat16), "dp").astype(jnp.float32),
        lax.psum(shares[7].astype(jnp.bfloat16), "dp").astype(jnp.float32),
        lax.psum(shares[8].astype(jnp.bfloat16), "dp").astype(jnp.float32),
        lax.psum(shares[9].astype(jnp.bfloat16), "dp").astype(jnp.float32),
        lax.psum(shares[10].astype(jnp.bfloat16), "dp").astype(jnp.float32),
        lax.psum(shares[11].astype(jnp.bfloat16), "dp").astype(jnp.float32),
        lax.psum(shares[12].astype(jnp.bfloat16), "dp").astype(jnp.float32),
        lax.psum(shares[13].astype(jnp.bfloat16), "dp").astype(jnp.float32),
    )


def local(
    frames_in,
    frame_lengths,
    label_ids,
    label_lengths,
    pred_states,
    norm_gains,
    first_in,
    first_out,
    attend_joint,
    attend_out,
    point_in,
    depth_taps,
    batch_gain,
    batch_bias,
    point_out,
    second_in,
    second_out,
    enc_weight,
    pred_weight,
    token_weight,
    duration_weight,
):
    utts, frames, width = frames_in.shape
    slots = pred_states.shape[1]
    rows = utts * frames
    positions = lax.broadcasted_iota(jnp.int32, (utts, frames), 1)
    valid = (positions < frame_lengths[:, None]).astype(jnp.float32)
    valid_rows = valid.reshape(rows, 1)
    key_bias = ((1.0 - valid) * MASKED)[:, None, None, :]
    layers = norm_gains.shape[0]
    resid = frames_in.reshape(rows, width).astype(jnp.float32)
    records = []
    for layer in range(layers):
        weights = (
            lax.all_gather(norm_gains[layer], "fsdp", axis=1, tiled=True),
            lax.all_gather(first_in[layer], "fsdp", axis=0, tiled=True),
            lax.all_gather(first_out[layer], "fsdp", axis=0, tiled=True),
            lax.all_gather(attend_joint[layer], "fsdp", axis=0, tiled=True),
            lax.all_gather(attend_out[layer], "fsdp", axis=0, tiled=True),
            lax.all_gather(point_in[layer], "fsdp", axis=0, tiled=True),
            lax.all_gather(depth_taps[layer], "fsdp", axis=1, tiled=True),
            lax.all_gather(batch_gain[layer], "fsdp", axis=0, tiled=True),
            lax.all_gather(batch_bias[layer], "fsdp", axis=0, tiled=True),
            lax.all_gather(point_out[layer], "fsdp", axis=0, tiled=True),
            lax.all_gather(second_in[layer], "fsdp", axis=0, tiled=True),
            lax.all_gather(second_out[layer], "fsdp", axis=0, tiled=True),
        )
        resid, record = run_layer(resid, weights, valid_rows, key_bias)
        kept = None
        records.append((kept, record))
    w_enc, w_pred, w_tok, w_dur = (
        lax.all_gather(enc_weight, "fsdp", axis=0, tiled=True),
        lax.all_gather(pred_weight, "fsdp", axis=0, tiled=True),
        lax.all_gather(token_weight, "fsdp", axis=0, tiled=True),
        lax.all_gather(duration_weight, "fsdp", axis=0, tiled=True),
    )
    joint = w_enc.shape[1]
    vocab = w_tok.shape[1]
    out_low = resid.astype(jnp.bfloat16)
    enc = matmul(out_low, w_enc)
    pred_low = pred_states.reshape(utts * slots, joint)
    pred = matmul(pred_low, w_pred).reshape(utts, slots, joint)
    groups = slots // GROUP
    durs = w_dur.shape[1]
    pred_t = jnp.pad(
        jnp.swapaxes(pred.reshape(utts * groups, GROUP, joint), 1, 2),
        ((0, 0), (0, 0), (0, 8 - GROUP)),
    )
    w_cat = jnp.concatenate([w_tok, jnp.pad(w_dur, ((0, 0), (0, 128 - durs)))], 1)
    enc_t = enc.T
    labels_ext = jnp.concatenate([label_ids, jnp.zeros((utts, 1), jnp.int32)], 1)
    feats, expd = joint_forward(enc_t, pred_t, labels_ext, w_cat.T, vocab, durs, frames)
    lat_grads, scores = lattice(feats[: 2 + durs], frame_lengths, label_lengths, slots)
    log_prob = scores[:utts, 0]
    utt_loss = -log_prob / frame_lengths.astype(jnp.float32)
    grad_enc_t, grad_pred_t, grad_tok, grad_dur_w = joint_backward(
        enc_t, pred_t, labels_ext, w_cat, feats, lat_grads, expd, vocab, durs, frames
    )
    grad_dur_w = grad_dur_w[:, :durs]
    grad_pred_rows = jnp.swapaxes(grad_pred_t[:, :, :GROUP], 1, 2)
    grad_enc_low = grad_enc_t.T.astype(jnp.bfloat16)
    grad_w_enc = contract_rows(out_low, grad_enc_low)
    grad = contract_cols(grad_enc_low, w_enc)
    grad_w_pred = contract_rows(
        pred_low, grad_pred_rows.reshape(utts * slots, joint).astype(jnp.bfloat16)
    )
    shard = width // lax.axis_size("fsdp")
    offset = lax.axis_index("fsdp") * shard
    collected = [None] * layers
    for layer in reversed(range(layers)):
        kept, record = records[layer]
        weights = (
            lax.all_gather(norm_gains[layer], "fsdp", axis=1, tiled=True),
            lax.all_gather(first_in[layer], "fsdp", axis=0, tiled=True),
            lax.all_gather(first_out[layer], "fsdp", axis=0, tiled=True),
            lax.all_gather(attend_joint[layer], "fsdp", axis=0, tiled=True),
            lax.all_gather(attend_out[layer], "fsdp", axis=0, tiled=True),
            lax.all_gather(point_in[layer], "fsdp", axis=0, tiled=True),
            lax.all_gather(depth_taps[layer], "fsdp", axis=1, tiled=True),
            lax.all_gather(batch_gain[layer], "fsdp", axis=0, tiled=True),
            lax.all_gather(batch_bias[layer], "fsdp", axis=0, tiled=True),
            lax.all_gather(point_out[layer], "fsdp", axis=0, tiled=True),
            lax.all_gather(second_in[layer], "fsdp", axis=0, tiled=True),
            lax.all_gather(second_out[layer], "fsdp", axis=0, tiled=True),
        )
        grad, grads = layer_backward(weights, record, grad, valid_rows, key_bias)
        collected[layer] = grads

    def stack_member(member):
        return jnp.stack([collected[layer][member] for layer in range(layers)])

    stacked = (
        jnp.swapaxes(stack_member(0), 1, 2),
        stack_member(1),
        stack_member(2),
        stack_member(3),
        stack_member(4),
        stack_member(5),
        jnp.swapaxes(stack_member(6), 1, 2),
        stack_member(9),
        stack_member(10),
        stack_member(11),
    )
    summed = reduce_grads(stacked, (grad_w_enc, grad_w_pred, grad_tok, grad_dur_w))
    gain_piece = lax.dynamic_slice_in_dim(stack_member(7), offset, shard, 1)
    bias_piece = lax.dynamic_slice_in_dim(stack_member(8), offset, shard, 1)
    grad_frames = grad.reshape(utts, frames, width)
    return (
        utt_loss,
        grad_frames,
        jnp.swapaxes(summed[0], 1, 2),
        summed[1],
        summed[2],
        summed[3],
        summed[4],
        summed[5],
        jnp.swapaxes(summed[6], 1, 2),
        gain_piece,
        bias_piece,
        summed[7],
        summed[8],
        summed[9],
        summed[10],
        summed[11],
        summed[12],
        summed[13],
    )


def solution(mesh):
    placed = (
        P(("dp", "fsdp"), None, None),
        P(("dp", "fsdp")),
        P(("dp", "fsdp"), None),
        P(("dp", "fsdp")),
        P(("dp", "fsdp"), None, None),
        P(None, None, "fsdp"),
        P(None, "fsdp", None),
        P(None, "fsdp", None),
        P(None, "fsdp", None),
        P(None, "fsdp", None),
        P(None, "fsdp", None),
        P(None, None, "fsdp"),
        P(None, "fsdp"),
        P(None, "fsdp"),
        P(None, "fsdp", None),
        P(None, "fsdp", None),
        P(None, "fsdp", None),
        P("fsdp", None),
        P("fsdp", None),
        P("fsdp", None),
        P("fsdp", None),
    )
    return jax.shard_map(
        local,
        mesh=mesh,
        in_specs=placed,
        out_specs=(
            P(("dp", "fsdp")),
            P(("dp", "fsdp"), None, None),
            P(None, None, "fsdp"),
            P(None, "fsdp", None),
            P(None, "fsdp", None),
            P(None, "fsdp", None),
            P(None, "fsdp", None),
            P(None, "fsdp", None),
            P(None, None, "fsdp"),
            P(None, "fsdp"),
            P(None, "fsdp"),
            P(None, "fsdp", None),
            P(None, "fsdp", None),
            P(None, "fsdp", None),
            P("fsdp", None),
            P("fsdp", None),
            P("fsdp", None),
            P("fsdp", None),
        ),
        check_vma=False,
    )
```

```python
from functools import partial, reduce

import jax
import jax.numpy as jnp
from jax import lax
from jax.experimental import pallas as pl
from jax.experimental.pallas import tpu as pltpu
from jax.sharding import PartitionSpec as P

HEADS = 8


EPS = 1e-05
MASKED = -1000000000.0
NEG = -1e30


def lattice_kernel(slots, feats_ref, tlen_ref, ulen_ref, grads_ref, prob_ref, s_ref, l_ref, ls_ref, a_ref, b_ref, init_ref):
    utts = tlen_ref.shape[0]
    frames = feats_ref.shape[2]
    rows = feats_ref.shape[1]
    wide = frames + 128
    reach = feats_ref.shape[0] - 3
    diags = frames + slots
    pad = 8
    total = a_ref.shape[0]
    body = wide

    def skew(x, sign):
        k = lax.broadcasted_iota(jnp.int32, x.shape, 0) % 32
        for bit in range(5):
            step = 1 << bit
            x = jnp.where((k // step) % 2 == 1, pltpu.roll(x, step if sign > 0 else wide - step, 1), x)
        return x

    def to_diag(x):
        x = jnp.concatenate([x, jnp.zeros((rows, 128), jnp.float32)], 1)
        x = skew(x, 1)
        x = jnp.concatenate([x, jnp.zeros((128 - rows, wide), jnp.float32)], 0)
        return x.T

    lane = lax.broadcasted_iota(jnp.int32, (wide, 128), 1)
    diag = lax.broadcasted_iota(jnp.int32, (wide, 128), 0)
    k_of = lane % 32
    t_of = diag - k_of
    t_len = jnp.full((wide, 128), -1, jnp.int32)
    u_len = jnp.full((wide, 128), -1, jnp.int32)
    for u in range(utts):
        mine = (lane // 32) == u
        t_len = jnp.where(mine, tlen_ref[u], t_len)
        u_len = jnp.where(mine, ulen_ref[u], u_len)
    blank = to_diag(feats_ref[0])
    label = to_diag(feats_ref[1])
    edge = jnp.full((pad, 128), NEG, jnp.float32)
    real = (t_of >= 0)
    for ref in (s_ref, l_ref, ls_ref):
        for e in range(ref.shape[0]):
            ref[e, 0:pad, :] = edge
            ref[e, pad + wide:, :] = jnp.full((ref.shape[1] - pad - wide, 128), NEG, jnp.float32)
    for e in range(reach + 1):
        dur = to_diag(feats_ref[2 + e])
        if e > 0:
            keep = real & (k_of <= u_len) & ((t_of + e < t_len) | ((t_of + e == t_len) & (k_of == u_len)))
            s_ref[e - 1, pad:pad + wide, :] = jnp.where(keep, blank + dur, NEG)
        keep = real & (k_of < u_len) & (t_of + e < t_len)
        lab = jnp.where(keep, label + dur, NEG)
        l_ref[e, pad:pad + wide, :] = lab
        ls_ref[e, pad:pad + wide, :] = pltpu.roll(lab, 1, 1)
    init_ref[pad:pad + wide, :] = jnp.where((t_of == t_len) & (k_of == u_len), 0.0, NEG)
    a_ref[...] = jnp.full(a_ref.shape, NEG, jnp.float32)
    b_ref[...] = jnp.full(b_ref.shape, NEG, jnp.float32)

    first = jnp.where((lax.broadcasted_iota(jnp.int32, (1, 128), 1) % 32 == 0)
                      & (lax.broadcasted_iota(jnp.int32, (1, 128), 1) < 32 * utts), 0.0, NEG)

    def lse(terms):
        tops = list(terms)
        while len(tops) > 1:
            tops = [jnp.maximum(tops[i], tops[i + 1]) if i + 1 < len(tops) else tops[i] for i in range(0, len(tops), 2)]
        top = tops[0]
        parts = [jnp.exp(x - top) for x in terms]
        while len(parts) > 1:
            parts = [parts[i] + parts[i + 1] if i + 1 < len(parts) else parts[i] for i in range(0, len(parts), 2)]
        return jnp.maximum(top + jnp.log(parts[0]), NEG)

    a_ref[pl.ds(pad, 1), :] = first
    last = diags

    def step(i, carry):
        ha, hra, hb, hrb = carry
        row = pad + i
        terms = [ha[e - 1] + s_ref[e - 1, pl.ds(row - e, 1), :] for e in range(1, reach + 1)]
        terms += [hra[e] + ls_ref[e, pl.ds(row - e - 1, 1), :] for e in range(reach + 1)]
        a = lse(terms[::-1])
        a_ref[pl.ds(row, 1), :] = a
        ra = pltpu.roll(a, 1, 1)
        rowb = pad + last - i
        terms = [hb[e - 1] + s_ref[e - 1, pl.ds(rowb, 1), :] for e in range(1, reach + 1)]
        terms += [hrb[e] + l_ref[e, pl.ds(rowb, 1), :] for e in range(reach + 1)]
        b = jnp.maximum(lse(terms[::-1]), init_ref[pl.ds(rowb, 1), :])
        b_ref[pl.ds(rowb, 1), :] = b
        rb = pltpu.roll(b, 127, 1)
        return ((a,) + ha[:-1], (ra,) + hra[:-1], (b,) + hb[:-1], (rb,) + hrb[:-1])

    b0 = init_ref[pl.ds(pad + last, 1), :]
    b_ref[pl.ds(pad + last, 1), :] = b0
    none = a_ref[pl.ds(0, 1), :]
    first = a_ref[pl.ds(pad, 1), :]
    ha = (first,) + (none,) * (reach - 1)
    hra = (pltpu.roll(first, 1, 1),) + (none,) * reach
    hb = (b0,) + (none,) * (reach - 1)
    hrb = (pltpu.roll(b0, 127, 1),) + (none,) * reach
    lax.fori_loop(1, last + 1, step, (ha, hra, hb, hrb))

    zrow = b_ref[pl.ds(pad, 1), :]
    lane1 = lax.broadcasted_iota(jnp.int32, (1, 128), 1)
    z = jnp.zeros((1, 128), jnp.float32)
    for u in range(utts):
        zu = jnp.max(jnp.where(lane1 == 32 * u, zrow, 2 * NEG), axis=1, keepdims=True)
        z = jnp.where(lane1 // 32 == u, zu, z)
        prob_ref[pl.ds(u, 1), :] = jnp.broadcast_to(zu, (1, 128))

    def from_diag(x):
        x = x.T[:rows]
        return skew(x, -1)[:, :frames]

    a = a_ref[pad:pad + wide, :] - z
    g_blank = jnp.zeros((wide, 128), jnp.float32)
    g_label = jnp.zeros((wide, 128), jnp.float32)
    for e in range(reach + 1):
        bb = b_ref[pad + e + 1: pad + e + 1 + wide, :]
        pl_ = jnp.exp(a + l_ref[e, pad:pad + wide, :] + pltpu.roll(bb, 127, 1))
        g_label = g_label - pl_
        g = -pl_
        if e > 0:
            ps = jnp.exp(a + s_ref[e - 1, pad:pad + wide, :] + b_ref[pad + e: pad + e + wide, :])
            g_blank = g_blank - ps
            g = g - ps
        grads_ref[2 + e] = from_diag(g)
    grads_ref[0] = from_diag(g_blank)
    grads_ref[1] = from_diag(g_label)


def lattice(feats, t_len, u_len, slots):
    _, rows, frames = feats.shape
    wide = frames + 128
    total = wide + 16
    reach = feats.shape[0] - 3
    return pl.pallas_call(
        partial(lattice_kernel, slots),
        out_shape=(jax.ShapeDtypeStruct(feats.shape, jnp.float32), jax.ShapeDtypeStruct((8, 128), jnp.float32)),
        in_specs=[pl.BlockSpec(memory_space=pltpu.VMEM), pl.BlockSpec(memory_space=pltpu.SMEM), pl.BlockSpec(memory_space=pltpu.SMEM)],
        out_specs=(pl.BlockSpec(memory_space=pltpu.VMEM),) * 2,
        scratch_shapes=[pltpu.VMEM((reach, total, 128), jnp.float32), pltpu.VMEM((reach + 1, total, 128), jnp.float32),
                        pltpu.VMEM((reach + 1, total, 128), jnp.float32), pltpu.VMEM((total, 128), jnp.float32),
                        pltpu.VMEM((total, 128), jnp.float32), pltpu.VMEM((total, 128), jnp.float32)],
        compiler_params=pltpu.CompilerParams(vmem_limit_bytes=48 << 20),
        name="lattice",
    )(feats, t_len, u_len)


GROUP=5
CHUNK=256

def nn(a,b): return jnp.dot(a,b,preferred_element_type=jnp.float32)
def nt(a,b): return lax.dot_general(a,b,(((1,),(1,)),((),())),preferred_element_type=jnp.float32)

def fold8(x, op):
    parts=[x[i:i+8] for i in range(0,x.shape[0],8)]
    while len(parts)>1:
        parts=[op(parts[i],parts[i+1]) if i+1<len(parts) else parts[i] for i in range(0,len(parts),2)]
    return parts[0]

def joint_fwd_kernel(groups, durs, labels_ref, enc_ref, pred_ref, wt_ref, feats_ref, p_ref, tok_ref):
    step=pl.program_id(0)
    vocab=p_ref.shape[2]
    u=step//groups
    g=step%groups
    for j in range(GROUP):
        k=g*GROUP+j
        hid=jnp.tanh(enc_ref[...]+pred_ref[0,:,j:j+1]).astype(jnp.bfloat16)
        tops=[]
        for c in range(0,vocab,CHUNK):
            t=nn(wt_ref[c:c+CHUNK,:],hid)
            tok_ref[j%2,c:c+CHUNK,:]=t
            tops.append(fold8(t,jnp.maximum))
        dl=nn(wt_ref[vocab:,:],hid)[:8]
        top=jnp.max(reduce(jnp.maximum,tops),0,keepdims=True)
        sums=[]
        for c in range(0,vocab,CHUNK):
            e=jnp.exp(tok_ref[j%2,c:c+CHUNK,:]-top)
            p_ref[0,j,c:c+CHUNK,:]=e.astype(jnp.bfloat16)
            sums.append(fold8(e,jnp.add))
        total=jnp.sum(reduce(jnp.add,sums),0,keepdims=True)
        lse=top+jnp.log(total)
        row=u*32+k
        feats_ref[0,pl.ds(row,1),:]=tok_ref[j%2,0:1,:]-lse
        feats_ref[1,pl.ds(row,1),:]=tok_ref[j%2,pl.ds(labels_ref[u,k],1),:]-lse
        real=lax.broadcasted_iota(jnp.int32,dl.shape,0)<durs
        dtop=jnp.max(jnp.where(real,dl,-1e30),0,keepdims=True)
        dlse=dtop+jnp.log(jnp.sum(jnp.where(real,jnp.exp(dl-dtop),0.0),0,keepdims=True))
        dlp=dl-dlse
        for e in range(durs):
            feats_ref[2+e,pl.ds(row,1),:]=dlp[e:e+1]
        feats_ref[2+durs,pl.ds(row,1),:]=1.0/total

def joint_forward(enc_t, pred_t, labels, w_t, vocab, durs, frames):
    joint, rows=enc_t.shape
    utts,slots=labels.shape
    groups=slots//GROUP
    return pl.pallas_call(
        partial(joint_fwd_kernel,groups,durs),
        grid=(utts*groups,),
        in_specs=[pl.BlockSpec(memory_space=pltpu.SMEM),
            pl.BlockSpec((joint,frames),lambda s:(0,s//groups)),
            pl.BlockSpec((1,joint,8),lambda s:(s,0,0)),
            pl.BlockSpec(w_t.shape,lambda s:(0,0))],
        out_specs=[pl.BlockSpec((3+durs,utts*32,frames),lambda s:(0,0,0)),
            pl.BlockSpec((1,GROUP,vocab,frames),lambda s:(s,0,0,0))],
        out_shape=[jax.ShapeDtypeStruct((3+durs,utts*32,frames),jnp.float32),
            jax.ShapeDtypeStruct((utts*groups,GROUP,vocab,frames),jnp.bfloat16)],
        scratch_shapes=[pltpu.VMEM((2,vocab,frames),jnp.float32)],
        compiler_params=pltpu.CompilerParams(vmem_limit_bytes=50<<20),
        name="joint_forward",
    )(labels,enc_t,pred_t,w_t)

def joint_bwd_kernel(groups, durs, labels_ref, enc_ref, pred_ref, w_ref, feats_ref, grads_ref, p_ref, genc_ref, gpred_ref, gtok_ref, gdur_ref, h_ref, d_ref, acc_ref):
    step=pl.program_id(0)
    vocab=p_ref.shape[2]
    frames=p_ref.shape[3]
    u=step//groups
    g=step%groups

    @pl.when(step==0)
    def _():
        acc_ref[...]=jnp.zeros_like(acc_ref)
    @pl.when(g==0)
    def _():
        genc_ref[...]=jnp.zeros_like(genc_ref)
    for j in range(GROUP):
        k=g*GROUP+j
        row=u*32+k
        cols=slice(j*frames,(j+1)*frames)
        th=jnp.tanh(enc_ref[...]+pred_ref[0,:,j:j+1])
        h_ref[:,cols]=th.astype(jnp.bfloat16)
        gb=grads_ref[0,pl.ds(row,1),:]
        gl=grads_ref[1,pl.ds(row,1),:]
        scale=-(gb+gl)*feats_ref[2+durs,pl.ds(row,1),:]
        for c in range(0,vocab,CHUNK):
            d_ref[c:c+CHUNK,cols]=(p_ref[0,j,c:c+CHUNK,:].astype(jnp.float32)*scale).astype(jnp.bfloat16)
        label=labels_ref[u,k]
        def fix(base):
            v=p_ref[0,j,pl.ds(base,16),:].astype(jnp.float32)*scale
            at=lax.broadcasted_iota(jnp.int32,v.shape,0)+base
            v=v+jnp.where(at==0,gb,0.0)+jnp.where(at==label,gl,0.0)
            d_ref[pl.ds(base,16),cols]=v.astype(jnp.bfloat16)
        fix(0)
        fix(pl.multiple_of((label//16)*16,16))
        gd=[grads_ref[2+e,pl.ds(row,1),:] for e in range(durs)]
        gsum=reduce(jnp.add,gd)
        at=lax.broadcasted_iota(jnp.int32,(16,frames),0)
        dd=jnp.zeros((16,frames),jnp.float32)
        for e in range(durs):
            dd=jnp.where(at==e,gd[e]-gsum*jnp.exp(feats_ref[2+e,pl.ds(row,1),:]),dd)
        d_ref[vocab:vocab+16,cols]=dd.astype(jnp.bfloat16)
        d_ref[vocab+16:,cols]=jnp.zeros((d_ref.shape[0]-vocab-16,frames),jnp.bfloat16)
        dh=nn(w_ref[...],d_ref[:,cols])
        th=jnp.tanh(enc_ref[...]+pred_ref[0,:,j:j+1])
        dp=dh*(1.0-th*th)
        genc_ref[...]+=dp
        gpred_ref[0,:,j:j+1]=jnp.sum(dp,1,keepdims=True)
    for c in range(0,d_ref.shape[0],384):
        acc_ref[:,c:c+384]+=nt(h_ref[...],d_ref[c:c+384,:])
    @pl.when(step==pl.num_programs(0)-1)
    def _():
        gtok_ref[...]=acc_ref[:,:vocab].astype(jnp.bfloat16)
        gdur_ref[...]=acc_ref[:,vocab:].astype(jnp.bfloat16)

def joint_backward(enc_t, pred_t, labels, w, feats, grads, p, vocab, durs, frames):
    joint, rows=enc_t.shape
    utts,slots=labels.shape
    groups=slots//GROUP
    full=lambda a: pl.BlockSpec(a.shape,lambda s:(0,)*a.ndim)
    return pl.pallas_call(
        partial(joint_bwd_kernel,groups,durs),
        grid=(utts*groups,),
        in_specs=[pl.BlockSpec(memory_space=pltpu.SMEM),
            pl.BlockSpec((joint,frames),lambda s:(0,s//groups)),
            pl.BlockSpec((1,joint,8),lambda s:(s,0,0)),
            full(w),full(feats),full(grads),
            pl.BlockSpec((1,GROUP,vocab,frames),lambda s:(s,0,0,0))],
        out_specs=[pl.BlockSpec((joint,frames),lambda s:(0,s//groups)),
            pl.BlockSpec((1,joint,8),lambda s:(s,0,0)),
            pl.BlockSpec((joint,vocab),lambda s:(0,0)),
            pl.BlockSpec((joint,128),lambda s:(0,0))],
        out_shape=[jax.ShapeDtypeStruct((joint,rows),jnp.float32),
            jax.ShapeDtypeStruct((utts*groups,joint,8),jnp.float32),
            jax.ShapeDtypeStruct((joint,vocab),jnp.bfloat16),
            jax.ShapeDtypeStruct((joint,128),jnp.bfloat16)],
        scratch_shapes=[pltpu.VMEM((joint,GROUP*frames),jnp.bfloat16),
            pltpu.VMEM((vocab+128,GROUP*frames),jnp.bfloat16),
            pltpu.VMEM((joint,vocab+128),jnp.float32)],
        compiler_params=pltpu.CompilerParams(vmem_limit_bytes=56<<20),
        name="joint_backward",
    )(labels,enc_t,pred_t,w,feats,grads,p)


MESH=pl.DeviceIdType.MESH
QA=64
QB=64
HALF=2*QA+QB
TILE=2*HALF

def place():
    dp=lax.axis_index("dp"); fs=lax.axis_index("fsdp")
    return dp, fs, dp//2, dp%2, fs//2, fs%2

def greet(n1, dp, fs, a, c, i1, i2):
    barrier=pltpu.get_barrier_semaphore()
    for d in range(1,n1):
        pl.semaphore_signal(barrier,inc=1,device_id=(dp,lax.rem(i1+d,n1)*2+i2),device_id_type=MESH)
    pl.semaphore_signal(barrier,inc=1,device_id=(dp,i1*2+1-i2),device_id_type=MESH)
    pl.semaphore_signal(barrier,inc=1,device_id=((1-a)*2+c,fs),device_id_type=MESH)
    pl.semaphore_signal(barrier,inc=1,device_id=(a*2+1-c,fs),device_id_type=MESH)
    pl.semaphore_wait(barrier,n1+2)

def remote(s, d, ss, rs, dev):
    return pltpu.make_async_remote_copy(src_ref=s,dst_ref=d,send_sem=ss,recv_sem=rs,device_id=dev,device_id_type=MESH)

def rows(base, size):
    return pl.ds(pl.multiple_of(base,16),size)

def gather_kernel(n1, tiles, lag, src, out, own_sem, sz, rz, sy, ry, sx, rx, sc, rc):
    dp,fs,a,c,i1,i2=place()
    greet(n1,dp,fs,a,c,i1,i2)
    ypeer=(dp,i1*2+1-i2); xpeer=((1-a)*2+c,fs); cpeer=(a*2+1-c,fs)
    items=n1*tiles
    def main(t): return rows(t*TILE+c*HALF+a*QA,QA+QB)
    def quarter(t,aa): return rows(t*TILE+c*HALF+aa*(QA+QB),QA)
    def half(t,cc): return rows(t*TILE+cc*HALF,HALF)
    def of(m): return m//n1, m%n1, lax.rem(i1+n1-m%n1,n1)
    def zcopy(t,d):
        j=lax.rem(i1+d,n1)
        return remote(src.at[main(t),:],out.at[fs,main(t),:],sz.at[t,d],rz.at[t,i1],(dp,j*2+i2))
    def zin(t,j):
        return remote(src.at[main(t),:],out.at[j*2+i2,main(t),:],sz.at[t,0],rz.at[t,j],ypeer)
    def ycopy(t,j):
        s=j*2+i2
        return remote(out.at[s,main(t),:],out.at[s,main(t),:],sy.at[t,j],ry.at[t,j],ypeer)
    def ycopy_own(t):
        return remote(src.at[main(t),:],out.at[fs,main(t),:],sy.at[t,i1],ry.at[t,i1],ypeer)
    def yin(t,j):
        s=j*2+1-i2
        return remote(src.at[main(t),:],out.at[s,main(t),:],sy.at[t,j],ry.at[t,j],ypeer)
    def xcopy(t,s):
        return remote(out.at[s,quarter(t,a),:],out.at[s,quarter(t,a),:],sx.at[t,s],rx.at[t,s],xpeer)
    def xin(t,s):
        return remote(src.at[quarter(t,a),:],out.at[s,quarter(t,1-a),:],sx.at[t,s],rx.at[t,s],xpeer)
    def ccopy(t,s):
        return remote(out.at[s,half(t,c),:],out.at[s,half(t,c),:],sc.at[t,s],rc.at[t,s],cpeer)
    def cin(t,s):
        return remote(src.at[half(t,c),:],out.at[s,half(t,1-c),:],sc.at[t,s],rc.at[t,s],cpeer)
    local=pltpu.make_async_copy(src,out.at[fs],own_sem)
    local.start()

    def tick(tau,carry):
        @pl.when(tau<items)
        def _():
            t,d,j=of(tau)
            @pl.when(d>0)
            def _(): zcopy(t,d).start()
            @pl.when(d==0)
            def _(): ycopy_own(t).start()
        m1=tau-lag
        @pl.when((m1>=0)&(m1<items))
        def _():
            t,d,j=of(m1)
            @pl.when(d>0)
            def _():
                zin(t,j).wait_recv()
                ycopy(t,j).start()
                xcopy(t,j*2+i2).start()
        m2=tau-2*lag
        @pl.when((m2>=0)&(m2<items))
        def _():
            t,d,j=of(m2)
            yin(t,j).wait_recv()
            xcopy(t,j*2+1-i2).start()
        m3=tau-3*lag
        @pl.when((m3>=0)&(m3<items))
        def _():
            t,d,j=of(m3)
            @pl.when(d>0)
            def _():
                xin(t,j*2+i2).wait_recv()
                ccopy(t,j*2+i2).start()
            xin(t,j*2+1-i2).wait_recv()
            ccopy(t,j*2+1-i2).start()
        return carry
    lax.fori_loop(0,items+3*lag,tick,0)
    local.wait()
    def finish(m,carry):
        t,d,j=of(m)
        @pl.when(d>0)
        def _():
            cin(t,j*2+i2).wait_recv()
            zcopy(t,d).wait_send()
            xcopy(t,j*2+i2).wait_send()
            ccopy(t,j*2+i2).wait_send()
        cin(t,j*2+1-i2).wait_recv()
        ycopy(t,j).wait_send()
        xcopy(t,j*2+1-i2).wait_send()
        ccopy(t,j*2+1-i2).wait_send()
        return carry
    lax.fori_loop(0,items,finish,0)

def gather(packed, collective_id, lag=1):
    n=lax.axis_size("fsdp"); n1=n//2
    tiles=packed.shape[0]//TILE
    dma=pltpu.SemaphoreType.DMA
    return pl.pallas_call(
        partial(gather_kernel,n1,tiles,lag),
        out_shape=jax.ShapeDtypeStruct((n,)+packed.shape,packed.dtype),
        in_specs=[pl.BlockSpec(memory_space=pl.ANY)],
        out_specs=pl.BlockSpec(memory_space=pl.ANY),
        scratch_shapes=[dma]+[dma((tiles,n1))]*4+[dma((tiles,n))]*4,
        compiler_params=pltpu.CompilerParams(collective_id=collective_id,has_side_effects=True),
        name="gather_weights",
    )(packed)

def scatter_kernel(n1, tiles, lag, src, out, own, gc, gx, gy, gz, gf, fin,
                   lo, sc, rc, sx, rx, sy, ry, sz, rz, sf, rf, se, re, wo):
    dp,fs,a,c,i1,i2=place()
    greet(n1,dp,fs,a,c,i1,i2)
    ypeer=(dp,i1*2+1-i2); xpeer=((1-a)*2+c,fs); cpeer=(a*2+1-c,fs)
    items=n1*tiles
    main=rows(a*QA,QA+QB)
    def quarter(aa): return rows(aa*(QA+QB),QA)
    middle=pl.ds(QA,QB)
    def of(m): return m//n1, lax.rem(i1+1+m%n1,n1)
    def load(t,s): return pltpu.make_async_copy(src.at[s,rows(t*TILE+c*HALF,HALF),:],own.at[t,s],lo.at[t,s])
    def ccopy(t,s): return remote(src.at[s,rows(t*TILE+(1-c)*HALF,HALF),:],gc.at[t,s],sc.at[t,s],rc.at[t,s],cpeer)
    def xcopy(t,s): return remote(own.at[t,s,quarter(1-a),:],gx.at[t,s],sx.at[t,s],rx.at[t,s],xpeer)
    def ycopy(t,j): return remote(own.at[t,j*2+1-i2,main,:],gy.at[t,j],sy.at[t,j],ry.at[t,j],ypeer)
    def zcopy(t,j): return remote(own.at[t,j*2+i2,main,:],gz.at[t,i1],sz.at[t,j],rz.at[t,i1],(dp,j*2+i2))
    def zin(t,j): return remote(own.at[t,fs,main,:],gz.at[t,j],sz.at[t,j],rz.at[t,j],ypeer)
    def fcopy(t): return remote(own.at[t,fs,main,:],gf.at[t],sf.at[t],rf.at[t],xpeer)
    def ecopy(t): return remote(fin.at[t,c],fin.at[t,c],se.at[t],re.at[t],cpeer)
    def ein(t): return remote(fin.at[t,1-c],fin.at[t,1-c],se.at[t],re.at[t],cpeer)
    def store(t): return pltpu.make_async_copy(fin.at[t],out.at[t],wo.at[t])

    def tick(tau,carry):
        def at(shift,body):
            m=tau-shift
            @pl.when((m>=0)&(m<items))
            def _(): body(*of(m))
        def at_tile(shift,body):
            m=tau-shift
            @pl.when((m>=0)&(m<items)&(lax.rem(m+n1,n1)==n1-1))
            def _(): body(m//n1)
        def stage_c(t,j):
            for i in range(2):
                load(t,j*2+i).start(); ccopy(t,j*2+i).start()
        def stage_x(t,j):
            for i in range(2):
                s=j*2+i
                load(t,s).wait(); ccopy(t,s).wait_recv()
                own[t,s]=own[t,s]+gc[t,s]
                xcopy(t,s).start()
        def stage_y(t,j):
            for i in range(2):
                s=j*2+(1-i2 if i==0 else i2)
                xcopy(t,s).wait_recv()
                own[t,s,quarter(a),:]=own[t,s,quarter(a),:]+gx[t,s]
                if i==0: ycopy(t,j).start()
        def stage_z(t,j):
            s=j*2+i2
            ycopy(t,j).wait_recv()
            own[t,s,main,:]=own[t,s,main,:]+gy[t,j]
            @pl.when(j!=i1)
            def _(): zcopy(t,j).start()
        def stage_f(t):
            total=own[t,fs,main,:].astype(jnp.float32)
            for d in range(1,n1):
                j=lax.rem(i1+n1-d,n1)
                zin(t,j).wait_recv()
                total=total+gz[t,j].astype(jnp.float32)
            own[t,fs,main,:]=total.astype(jnp.bfloat16)
            fcopy(t).start()
        def stage_e(t):
            fcopy(t).wait_recv()
            fin[t,c,quarter(a),:]=own[t,fs,quarter(a),:]
            fin[t,c,quarter(1-a),:]=gf[t,rows((1-a)*QB,QA),:]
            fin[t,c,middle,:]=own[t,fs,middle,:]+gf[t,rows(a*QA,QB),:]
            ecopy(t).start()
        def stage_o(t):
            ein(t).wait_recv()
            ecopy(t).wait_send()
            store(t).start()
        at(0,stage_c); at(lag,stage_x); at(2*lag,stage_y); at(3*lag,stage_z)
        at_tile(3*lag+1,stage_f); at_tile(4*lag+1,stage_e); at_tile(5*lag+1,stage_o)
        return carry
    lax.fori_loop(0,items+5*lag+1,tick,0)
    def finish(m,carry):
        t,j=of(m)
        for i in range(2):
            ccopy(t,j*2+i).wait_send(); xcopy(t,j*2+i).wait_send()
        ycopy(t,j).wait_send()
        @pl.when(j!=i1)
        def _(): zcopy(t,j).wait_send()
        return carry
    lax.fori_loop(0,items,finish,0)
    def finish_tile(t,carry):
        fcopy(t).wait_send(); store(t).wait()
        return carry
    lax.fori_loop(0,tiles,finish_tile,0)

def scatter(grads, collective_id, lag=2):
    n=lax.axis_size("fsdp"); n1=n//2
    tiles=grads.shape[1]//TILE; w=grads.shape[2]
    dma=pltpu.SemaphoreType.DMA
    bf=jnp.bfloat16
    out=pl.pallas_call(
        partial(scatter_kernel,n1,tiles,lag),
        out_shape=jax.ShapeDtypeStruct((tiles,2,HALF,w),bf),
        in_specs=[pl.BlockSpec(memory_space=pl.ANY)],
        out_specs=pl.BlockSpec(memory_space=pl.ANY),
        scratch_shapes=[pltpu.VMEM((tiles,n,HALF,w),bf),pltpu.VMEM((tiles,n,HALF,w),bf),pltpu.VMEM((tiles,n,QA,w),bf),
            pltpu.VMEM((tiles,n1,QA+QB,w),bf),pltpu.VMEM((tiles,n1,QA+QB,w),bf),pltpu.VMEM((tiles,QA+QB,w),bf),pltpu.VMEM((tiles,2,HALF,w),bf)]
            +[dma((tiles,n))]*5+[dma((tiles,n1))]*4+[dma((tiles,))]*5,
        compiler_params=pltpu.CompilerParams(collective_id=collective_id,has_side_effects=True,vmem_limit_bytes=56<<20),
        name="scatter_grads",
    )(grads)
    return out.reshape(tiles*TILE,w)


def pooled(parts):
    counts = [x[8:9] for x in parts]
    count = sum(counts[1:], counts[0])
    mean = sum((x[0:4] * n for x, n in zip(parts[1:], counts[1:])), parts[0][0:4] * counts[0]) / count
    dev = jnp.zeros_like(mean)
    for x, n in zip(parts, counts):
        gap = x[0:4] - mean
        dev = dev + (x[4:8] + gap * gap * n)
    return mean, dev, count


def exchange_kernel(kind, groups, n, x_ref, out_ref, near, far, s1, r1, s2, r2):
    dp = lax.axis_index("dp")
    fs = lax.axis_index("fsdp")
    barrier = pltpu.get_barrier_semaphore()
    for d in range(1, groups):
        pl.semaphore_signal(barrier, inc=1, device_id=(lax.rem(dp + d, groups), fs), device_id_type=MESH)
    for d in range(1, n):
        pl.semaphore_signal(barrier, inc=1, device_id=(dp, lax.rem(fs + d, n)), device_id_type=MESH)
    pl.semaphore_wait(barrier, groups + n - 2)

    def merge(ref, members):
        if kind == "sum":
            total = ref[0]
            for i in range(1, members):
                total = total + ref[i]
            return total
        mean, dev, count = pooled([ref[i] for i in range(members)])
        return jnp.concatenate([mean, dev, jnp.broadcast_to(count, (8, 128))], 0)

    near[dp] = x_ref[...]
    first = []
    for d in range(1, groups):
        cp = remote(near.at[dp], near.at[dp], s1.at[d], r1.at[dp], (lax.rem(dp + d, groups), fs))
        cp.start()
        first.append(cp)
    for d in range(1, groups):
        other = lax.rem(dp + d, groups)
        remote(near.at[dp], near.at[other], s1.at[d], r1.at[other], (other, fs)).wait_recv()
    far[fs] = merge(near, groups)
    for d in range(1, n):
        cp = remote(far.at[fs], far.at[fs], s2.at[d], r2.at[fs], (dp, lax.rem(fs + d, n)))
        cp.start()
        first.append(cp)
    for d in range(1, n):
        other = lax.rem(fs + d, n)
        remote(far.at[fs], far.at[other], s2.at[d], r2.at[other], (dp, other)).wait_recv()
    out_ref[...] = merge(far, n)
    for cp in first:
        cp.wait_send()


def exchange(x, kind, collective_id):
    n = lax.axis_size("fsdp")
    groups = lax.axis_size("dp")
    dma = pltpu.SemaphoreType.DMA
    return pl.pallas_call(
        partial(exchange_kernel, kind, groups, n),
        out_shape=jax.ShapeDtypeStruct(x.shape, x.dtype),
        in_specs=[pl.BlockSpec(memory_space=pltpu.VMEM)],
        out_specs=pl.BlockSpec(memory_space=pltpu.VMEM),
        scratch_shapes=[
            pltpu.VMEM((groups,) + x.shape, x.dtype),
            pltpu.VMEM((n,) + x.shape, x.dtype),
            dma((groups,)), dma((groups,)), dma((n,)), dma((n,)),
        ],
        compiler_params=pltpu.CompilerParams(collective_id=collective_id, has_side_effects=True),
        name="exchange_" + kind,
    )(x)


def global_stats(depthwise, valid_rows, collective_id):
    width = depthwise.shape[1]
    count = jnp.sum(valid_rows)
    mean = jnp.sum(depthwise * valid_rows, 0) / count
    gap = (depthwise - mean) * valid_rows
    dev = jnp.sum(gap * gap, 0)
    x = jnp.concatenate([mean.reshape(-1, 128), dev.reshape(-1, 128), jnp.full((8, 128), count)], 0)
    x = exchange(x, "pool", collective_id)
    count = x[8, 0]
    return x[0:4].reshape(width), lax.rsqrt(x[4:8].reshape(width) / count + EPS), count


def global_sums(one, two, collective_id):
    width = one.shape[0]
    x = jnp.concatenate([one.reshape(-1, 128), two.reshape(-1, 128), jnp.zeros((8, 128))], 0)
    x = exchange(x, "sum", collective_id)
    return x[0:4].reshape(width), x[4:8].reshape(width)


WIDE = 512


def to_blocks(w):
    rows, cols = w.shape
    return jnp.swapaxes(w.reshape(rows, cols // WIDE, WIDE), 0, 1).reshape(-1, WIDE)


def from_blocks(part, cols):
    n, height, _ = part.shape
    blocks = cols // WIDE
    return jnp.swapaxes(part.reshape(n, blocks, height // blocks, WIDE), 1, 2).reshape(-1, cols)


def padded(parts):
    rows = sum(p.shape[-2] for p in parts)
    short = -rows % TILE
    shape = parts[0].shape[:-2] + (short, WIDE)
    return jnp.concatenate(parts + [jnp.zeros(shape, jnp.bfloat16)], -2)


def pack_layer(mats, smalls):
    f_in, f_out, w_joint, w_proj, p_in, p_out, s_in, s_out = mats
    small = jnp.concatenate(smalls, 0)
    small = jnp.pad(small, ((0, 16 - small.shape[0]), (0, WIDE - small.shape[1])))
    return [to_blocks(f_in), f_out, to_blocks(w_joint), w_proj, to_blocks(p_in), p_out, to_blocks(s_in), s_out, small]


def pack_joint(w_enc, w_pred, w_tok, w_dur):
    tall = w_pred.shape[0]
    rest = jnp.concatenate(
        [
            jnp.pad(w_enc[:, WIDE:], ((0, tall - w_enc.shape[0]), (0, 0))),
            w_pred[:, WIDE:],
            jnp.pad(w_dur, ((0, 0), (0, 256 - w_dur.shape[1]))),
        ],
        1,
    )
    return [w_enc[:, :WIDE], w_pred[:, :WIDE], to_blocks(w_tok), rest]


def cut(whole, sizes, offset=0):
    parts = []
    for size in sizes:
        parts.append(whole[..., offset : offset + size, :])
        offset += size
    return parts


def layer_sizes(n, mats):
    return [m.shape[1] * m.shape[2] // WIDE for m in mats] + [16]


def unpack_layer(whole, sizes, mats, width):
    parts = cut(whole, sizes)
    full = [
        from_blocks(p, m.shape[2]) if m.shape[2] != WIDE else p.reshape(-1, WIDE)
        for p, m in zip(parts, mats)
    ]
    shard = width // whole.shape[0]
    small = jnp.swapaxes(parts[-1][:, :, :shard], 0, 1).reshape(16, width)
    return full, small


def unpack_joint(whole, sizes, w_enc, w_dur):
    enc, pred, tok, rest = cut(whole, sizes[1:], sizes[0])
    joint = w_enc.shape[1]
    low = w_enc.shape[0]
    w_enc = jnp.concatenate([enc, rest[:, :low, : joint - WIDE]], 2).reshape(-1, joint)
    w_pred = jnp.concatenate([pred, rest[:, :, 128 : 128 + joint - WIDE]], 2).reshape(-1, joint)
    return w_enc, w_pred, from_blocks(tok, 1024), rest[:, :, 256:384].reshape(-1, 128)


def split_rows(grad, n):
    rows, cols = grad.shape
    blocks = cols // WIDE
    grad = grad.astype(jnp.bfloat16).reshape(n, rows // n, blocks, WIDE)
    return jnp.swapaxes(grad, 1, 2).reshape(n, -1, WIDE)


def pack_layer_grads(mats, gains, depth, n):
    width = gains.shape[1]
    small = jnp.concatenate([gains, depth], 0).astype(jnp.bfloat16)
    small = jnp.swapaxes(small.reshape(-1, n, width // n), 0, 1)
    small = jnp.pad(small, ((0, 0), (0, 16 - small.shape[1]), (0, WIDE - small.shape[2])))
    return [split_rows(m, n) for m in mats] + [small]


def pack_joint_grads(g_enc, g_pred, g_tok, g_dur, n):
    def shards(grad):
        return grad.astype(jnp.bfloat16).reshape(n, -1, grad.shape[1])
    g_enc, g_pred, g_dur = shards(g_enc), shards(g_pred), shards(g_dur)
    tall = g_pred.shape[1]
    rest = jnp.concatenate(
        [
            jnp.pad(g_enc[:, :, WIDE:], ((0, 0), (0, tall - g_enc.shape[1]), (0, 0))),
            g_pred[:, :, WIDE:],
            g_dur,
            jnp.zeros((n, tall, 128), jnp.bfloat16),
        ],
        2,
    )
    return [g_enc[:, :, :WIDE], g_pred[:, :, :WIDE], split_rows(g_tok, n), rest]


def shard_from_blocks(part, cols):
    blocks = cols // WIDE
    height = part.shape[0] // blocks
    return jnp.swapaxes(part.reshape(blocks, height, WIDE), 0, 1).reshape(height, cols).astype(jnp.float32)


def norm_rows(value, gain):
    centre = jnp.mean(value, -1, keepdims=True)
    centred = value - centre
    spread = jnp.mean(centred * centred, -1, keepdims=True)
    return centred * lax.rsqrt(spread + EPS) * gain


def norm_back(value, gain, grad):
    result, pullback = jax.vjp(norm_rows, value, gain)
    return pullback(grad)


def matmul(left, right):
    return jnp.dot(left, right, preferred_element_type=jnp.float32)


def contract_rows(left, right):
    return lax.dot_general(
        left, right, (((0,), (0,)), ((), ())), preferred_element_type=jnp.float32
    )


def contract_cols(left, right):
    return lax.dot_general(
        left, right, (((1,), (1,)), ((), ())), preferred_element_type=jnp.float32
    )


def swish_slope(value):
    sigmoid_value = jax.nn.sigmoid(value)
    return sigmoid_value * (1.0 + value * (1.0 - sigmoid_value))


def ffn_forward(resid, gain, w_in, w_out):
    normed_low = norm_rows(resid, gain).astype(jnp.bfloat16)
    hidden = matmul(normed_low, w_in)
    active_low = jax.nn.silu(hidden).astype(jnp.bfloat16)
    return (resid + 0.5 * matmul(active_low, w_out), (normed_low, hidden, active_low))


def ffn_backward(resid, gain, w_in, w_out, saved, grad_out):
    normed_low, hidden, active_low = saved
    grad_branch = (0.5 * grad_out).astype(jnp.bfloat16)
    grad_w_out = contract_rows(active_low, grad_branch)
    grad_hidden = (contract_cols(grad_branch, w_out) * swish_slope(hidden)).astype(jnp.bfloat16)
    grad_w_in = contract_rows(normed_low, grad_hidden)
    grad_normed = contract_cols(grad_hidden, w_in)
    grad_resid, grad_gain = norm_back(resid, gain, grad_normed)
    return (grad_out + grad_resid, grad_gain, grad_w_in, grad_w_out)


def attend_forward(resid, gain, w_joint, w_proj, key_bias):
    rows, width = resid.shape
    utts = key_bias.shape[0]
    head_dim = width // HEADS
    normed_low = norm_rows(resid, gain).astype(jnp.bfloat16)
    joint_low = (
        matmul(normed_low, w_joint)
        .astype(jnp.bfloat16)
        .reshape(utts, rows // utts, 3, HEADS, head_dim)
    )
    scores = (
        jnp.einsum(
            "uqhe,ukhe->uhqk",
            joint_low[:, :, 0],
            joint_low[:, :, 1],
            preferred_element_type=jnp.float32,
        )
        * head_dim ** (-0.5)
        + key_bias
    )
    weights = jax.nn.softmax(scores, axis=-1)
    weights_low = weights.astype(jnp.bfloat16)
    context = jnp.einsum(
        "uhqk,ukhe->uqhe", weights_low, joint_low[:, :, 2], preferred_element_type=jnp.float32
    )
    context_low = context.reshape(rows, width).astype(jnp.bfloat16)
    return (
        resid + matmul(context_low, w_proj),
        (normed_low, joint_low, weights, weights_low, context_low),
    )


def attend_backward(resid, gain, w_joint, w_proj, saved, grad_out):
    normed_low, joint_low, weights, weights_low, context_low = saved
    rows, width = resid.shape
    utts, frames, three, heads, head_dim = joint_low.shape
    scale = head_dim ** (-0.5)
    query, key, value = (joint_low[:, :, 0], joint_low[:, :, 1], joint_low[:, :, 2])
    grad_branch = grad_out.astype(jnp.bfloat16)
    grad_proj = contract_rows(context_low, grad_branch)
    grad_context = (
        contract_cols(grad_branch, w_proj)
        .astype(jnp.bfloat16)
        .reshape(utts, frames, heads, head_dim)
    )
    grad_weights = jnp.einsum(
        "uqhe,ukhe->uhqk", grad_context, value, preferred_element_type=jnp.float32
    )
    grad_value = jnp.einsum(
        "uhqk,uqhe->ukhe", weights_low, grad_context, preferred_element_type=jnp.float32
    )
    grad_scores = (
        weights * (grad_weights - jnp.sum(grad_weights * weights, -1, keepdims=True))
    ).astype(jnp.bfloat16)
    grad_query = (
        jnp.einsum("uhqk,ukhe->uqhe", grad_scores, key, preferred_element_type=jnp.float32) * scale
    )
    grad_key = (
        jnp.einsum("uhqk,uqhe->ukhe", grad_scores, query, preferred_element_type=jnp.float32)
        * scale
    )
    grad_joint = (
        jnp.stack([grad_query, grad_key, grad_value], 2)
        .reshape(rows, 3 * width)
        .astype(jnp.bfloat16)
    )
    grad_w_joint = contract_rows(normed_low, grad_joint)
    grad_normed = contract_cols(grad_joint, w_joint)
    grad_resid, grad_gain = norm_back(resid, gain, grad_normed)
    return (grad_out + grad_resid, grad_gain, grad_w_joint, grad_proj)


def conv_inner(projected, depth, valid_rows, utts):
    rows, double = projected.shape
    width = double // 2
    frames = rows // utts
    taps = depth.shape[0]
    gated = projected[:, :width] * jax.nn.sigmoid(projected[:, width:]) * valid_rows
    padded = jnp.pad(gated.reshape(utts, frames, width), ((0, 0), (taps // 2, taps // 2), (0, 0)))
    total = padded[:, 0:frames] * depth[0]
    for tap in range(1, taps):
        total = total + padded[:, tap : tap + frames] * depth[tap]
    return total.reshape(rows, width)


def run_layer(resid, weights, valid_rows, key_bias, layer):
    gains, f_in, f_out, w_joint, w_proj, p_in, depth, bn_gain, bn_bias, p_out, s_in, s_out = weights
    gains = gains.astype(jnp.float32)
    utts = key_bias.shape[0]
    first, saved_first = ffn_forward(resid, gains[0], f_in, f_out)
    second, saved_attend = attend_forward(first, gains[1], w_joint, w_proj, key_bias)
    normed_low = norm_rows(second, gains[2]).astype(jnp.bfloat16)
    projected = matmul(normed_low, p_in)
    depthwise = conv_inner(projected, depth.astype(jnp.float32), valid_rows, utts)
    centre, inv_std, count = global_stats(depthwise, valid_rows, 8 + layer)
    normalized = (depthwise - centre) * inv_std
    shifted = normalized * bn_gain.astype(jnp.float32) + bn_bias.astype(jnp.float32)
    active_low = jax.nn.silu(shifted).astype(jnp.bfloat16)
    third = second + matmul(active_low, p_out)
    fourth, saved_fourth = ffn_forward(third, gains[3], s_in, s_out)
    output = norm_rows(fourth, gains[4])
    record = (
        resid,
        first,
        second,
        third,
        fourth,
        saved_first,
        saved_attend,
        saved_fourth,
        normed_low,
        projected,
        normalized,
        shifted,
        active_low,
        inv_std,
        count,
    )
    return (output, record)


def layer_backward(weights, record, grad_out, valid_rows, key_bias, layer):
    gains, f_in, f_out, w_joint, w_proj, p_in, depth, bn_gain, bn_bias, p_out, s_in, s_out = weights
    gains = gains.astype(jnp.float32)
    utts = key_bias.shape[0]
    (
        resid,
        first,
        second,
        third,
        fourth,
        saved_first,
        saved_attend,
        saved_fourth,
        normed_low,
        projected,
        normalized,
        shifted,
        active_low,
        inv_std,
        count,
    ) = record
    grad_fourth, grad_gain_four = norm_back(fourth, gains[4], grad_out)
    grad_third, grad_gain_three, grad_s_in, grad_s_out = ffn_backward(
        third, gains[3], s_in, s_out, saved_fourth, grad_fourth
    )
    grad_branch = grad_third.astype(jnp.bfloat16)
    grad_p_out = contract_rows(active_low, grad_branch)
    grad_shifted = contract_cols(grad_branch, p_out) * swish_slope(shifted)
    bias_sum, gain_sum = global_sums(
        jnp.sum(grad_shifted, 0), jnp.sum(grad_shifted * normalized, 0), 12 + layer
    )
    grad_depthwise = (
        bn_gain.astype(jnp.float32)
        * inv_std
        * (grad_shifted - valid_rows * (bias_sum + normalized * gain_sum) / count)
    )
    conv_local = partial(conv_inner, valid_rows=valid_rows, utts=utts)
    result, pullback = jax.vjp(conv_local, projected, depth.astype(jnp.float32))
    grad_projected, grad_depth = pullback(grad_depthwise)
    grad_projected_low = grad_projected.astype(jnp.bfloat16)
    grad_p_in = contract_rows(normed_low, grad_projected_low)
    grad_normed = contract_cols(grad_projected_low, p_in)
    grad_conv_resid, grad_gain_two = norm_back(second, gains[2], grad_normed)
    grad_second = grad_third + grad_conv_resid
    grad_first, grad_gain_one, grad_joint, grad_proj = attend_backward(
        first, gains[1], w_joint, w_proj, saved_attend, grad_second
    )
    grad_resid, grad_gain_zero, grad_f_in, grad_f_out = ffn_backward(
        resid, gains[0], f_in, f_out, saved_first, grad_first
    )
    grad_gains = jnp.stack(
        [grad_gain_zero, grad_gain_one, grad_gain_two, grad_gain_three, grad_gain_four]
    )
    return (
        grad_resid,
        (
            grad_gains,
            grad_f_in,
            grad_f_out,
            grad_joint,
            grad_proj,
            grad_p_in,
            grad_depth,
            gain_sum,
            bias_sum,
            grad_p_out,
            grad_s_in,
            grad_s_out,
        ),
    )


def local(
    frames_in,
    frame_lengths,
    label_ids,
    label_lengths,
    pred_states,
    norm_gains,
    first_in,
    first_out,
    attend_joint,
    attend_out,
    point_in,
    depth_taps,
    batch_gain,
    batch_bias,
    point_out,
    second_in,
    second_out,
    enc_weight,
    pred_weight,
    token_weight,
    duration_weight,
):
    utts, frames, width = frames_in.shape
    slots = pred_states.shape[1]
    rows = utts * frames
    positions = lax.broadcasted_iota(jnp.int32, (utts, frames), 1)
    valid = (positions < frame_lengths[:, None]).astype(jnp.float32)
    valid_rows = valid.reshape(rows, 1)
    key_bias = ((1.0 - valid) * MASKED)[:, None, None, :]
    layers = norm_gains.shape[0]
    n = lax.axis_size("fsdp")
    mats = (first_in, first_out, attend_joint, attend_out, point_in, point_out, second_in, second_out)
    sizes = layer_sizes(n, mats)
    joint_pack = pack_joint(enc_weight, pred_weight, token_weight, duration_weight)
    tail = [sum(sizes)] + [p.shape[0] for p in joint_pack]
    wholes = []
    for layer in range(layers):
        parts = pack_layer(
            [m[layer] for m in mats],
            [norm_gains[layer], depth_taps[layer], batch_gain[layer : layer + 1], batch_bias[layer : layer + 1]],
        )
        if layer == layers - 1:
            parts = parts + joint_pack
        wholes.append(gather(padded(parts), 1 + layer))
    weights_of = []
    for layer in range(layers):
        full, small = unpack_layer(wholes[layer], sizes, mats, width)
        f_in, f_out, w_joint, w_proj, p_in, p_out, s_in, s_out = full
        weights_of.append(
            (small[:5], f_in, f_out, w_joint, w_proj, p_in, small[5:14], small[14], small[15], p_out, s_in, s_out)
        )
    resid = frames_in.reshape(rows, width).astype(jnp.float32)
    records = []
    for layer in range(layers):
        resid, record = run_layer(resid, weights_of[layer], valid_rows, key_bias, layer)
        records.append((None, record))
    w_enc, w_pred, w_tok, w_dur = unpack_joint(wholes[-1], tail, enc_weight, duration_weight)
    joint = w_enc.shape[1]
    vocab = w_tok.shape[1]
    out_low = resid.astype(jnp.bfloat16)
    enc = matmul(out_low, w_enc)
    pred_low = pred_states.reshape(utts * slots, joint)
    pred = matmul(pred_low, w_pred).reshape(utts, slots, joint)
    groups = slots // GROUP
    durs = duration_weight.shape[1]
    pred_t = jnp.pad(
        jnp.swapaxes(pred.reshape(utts * groups, GROUP, joint), 1, 2),
        ((0, 0), (0, 0), (0, 8 - GROUP)),
    )
    w_cat = jnp.concatenate([w_tok, w_dur], 1)
    enc_t = enc.T
    labels_ext = jnp.concatenate([label_ids, jnp.zeros((utts, 1), jnp.int32)], 1)
    feats, expd = joint_forward(enc_t, pred_t, labels_ext, w_cat.T, vocab, durs, frames)
    lat_grads, scores = lattice(feats[: 2 + durs], frame_lengths, label_lengths, slots)
    log_prob = scores[:utts, 0]
    utt_loss = -log_prob / frame_lengths.astype(jnp.float32)
    grad_enc_t, grad_pred_t, grad_tok, grad_dur_w = joint_backward(
        enc_t, pred_t, labels_ext, w_cat, feats, lat_grads, expd, vocab, durs, frames
    )
    grad_pred_rows = jnp.swapaxes(grad_pred_t[:, :, :GROUP], 1, 2)
    grad_enc_low = grad_enc_t.T.astype(jnp.bfloat16)
    grad_w_enc = contract_rows(out_low, grad_enc_low)
    grad = contract_cols(grad_enc_low, w_enc)
    grad_w_pred = contract_rows(
        pred_low, grad_pred_rows.reshape(utts * slots, joint).astype(jnp.bfloat16)
    )
    shard = width // lax.axis_size("fsdp")
    offset = lax.axis_index("fsdp") * shard
    collected = [None] * layers
    for layer in reversed(range(layers)):
        kept, record = records[layer]
        weights = weights_of[layer]
        grad, grads = layer_backward(weights, record, grad, valid_rows, key_bias, layer)
        collected[layer] = grads

    shares = []
    for layer in range(layers):
        g = collected[layer]
        parts = pack_layer_grads([g[1], g[2], g[3], g[4], g[5], g[9], g[10], g[11]], g[0], g[6], n)
        if layer == layers - 1:
            parts = parts + pack_joint_grads(grad_w_enc, grad_w_pred, grad_tok, grad_dur_w, n)
        shares.append(scatter(padded(parts), 4 + layer))

    def stack(values):
        return jnp.stack(values)

    pieces = [cut(share, sizes) for share in shares]
    out = []
    for i, m in enumerate(mats):
        out.append(stack([shard_from_blocks(p[i], m.shape[2]) for p in pieces]))
    small = stack([p[-1][:, : norm_gains.shape[2]].astype(jnp.float32) for p in pieces])
    g_enc, g_pred, g_tok, rest = cut(shares[-1], tail[1:], tail[0])
    low = enc_weight.shape[0]
    g_enc = jnp.concatenate([g_enc, rest[:low, : joint - WIDE]], 1).astype(jnp.float32)
    g_pred = jnp.concatenate([g_pred, rest[:, 128 : 128 + joint - WIDE]], 1).astype(jnp.float32)
    g_dur = rest[:, 256 : 256 + durs].astype(jnp.float32)
    gain_piece = lax.dynamic_slice_in_dim(stack([c[7] for c in collected]), offset, shard, 1)
    bias_piece = lax.dynamic_slice_in_dim(stack([c[8] for c in collected]), offset, shard, 1)
    grad_frames = grad.reshape(utts, frames, width)
    return (
        utt_loss,
        grad_frames,
        small[:, :5],
        out[0],
        out[1],
        out[2],
        out[3],
        out[4],
        small[:, 5:14],
        gain_piece,
        bias_piece,
        out[5],
        out[6],
        out[7],
        g_enc,
        g_pred,
        shard_from_blocks(g_tok, vocab),
        g_dur,
    )


def solution(mesh):
    placed = (
        P(("dp", "fsdp"), None, None),
        P(("dp", "fsdp")),
        P(("dp", "fsdp"), None),
        P(("dp", "fsdp")),
        P(("dp", "fsdp"), None, None),
        P(None, None, "fsdp"),
        P(None, "fsdp", None),
        P(None, "fsdp", None),
        P(None, "fsdp", None),
        P(None, "fsdp", None),
        P(None, "fsdp", None),
        P(None, None, "fsdp"),
        P(None, "fsdp"),
        P(None, "fsdp"),
        P(None, "fsdp", None),
        P(None, "fsdp", None),
        P(None, "fsdp", None),
        P("fsdp", None),
        P("fsdp", None),
        P("fsdp", None),
        P("fsdp", None),
    )
    return jax.shard_map(
        local,
        mesh=mesh,
        in_specs=placed,
        out_specs=(
            P(("dp", "fsdp")),
            P(("dp", "fsdp"), None, None),
            P(None, None, "fsdp"),
            P(None, "fsdp", None),
            P(None, "fsdp", None),
            P(None, "fsdp", None),
            P(None, "fsdp", None),
            P(None, "fsdp", None),
            P(None, None, "fsdp"),
            P(None, "fsdp"),
            P(None, "fsdp"),
            P(None, "fsdp", None),
            P(None, "fsdp", None),
            P(None, "fsdp", None),
            P("fsdp", None),
            P("fsdp", None),
            P("fsdp", None),
            P("fsdp", None),
        ),
        check_vma=False,
    )
```

```python
from functools import partial, reduce

import jax
import jax.numpy as jnp
from jax import lax
from jax.experimental import pallas as pl
from jax.experimental.pallas import tpu as pltpu
from jax.sharding import PartitionSpec as P

HEADS = 8


EPS = 1e-05
MASKED = -1000000000.0
NEG = -1e30


def lattice_kernel(slots, feats_ref, tlen_ref, ulen_ref, grads_ref, prob_ref, s_ref, l_ref, ls_ref, a_ref, b_ref, init_ref):
    utts = tlen_ref.shape[0]
    frames = feats_ref.shape[2]
    rows = feats_ref.shape[1]
    wide = frames + 128
    reach = feats_ref.shape[0] - 3
    diags = frames + slots
    pad = 8
    total = a_ref.shape[0]
    body = wide

    def skew(x, sign):
        k = lax.broadcasted_iota(jnp.int32, x.shape, 0) % 32
        for bit in range(5):
            step = 1 << bit
            x = jnp.where((k // step) % 2 == 1, pltpu.roll(x, step if sign > 0 else wide - step, 1), x)
        return x

    def to_diag(x):
        x = jnp.concatenate([x, jnp.zeros((rows, 128), jnp.float32)], 1)
        x = skew(x, 1)
        x = jnp.concatenate([x, jnp.zeros((128 - rows, wide), jnp.float32)], 0)
        return x.T

    lane = lax.broadcasted_iota(jnp.int32, (wide, 128), 1)
    diag = lax.broadcasted_iota(jnp.int32, (wide, 128), 0)
    k_of = lane % 32
    t_of = diag - k_of
    t_len = jnp.full((wide, 128), -1, jnp.int32)
    u_len = jnp.full((wide, 128), -1, jnp.int32)
    for u in range(utts):
        mine = (lane // 32) == u
        t_len = jnp.where(mine, tlen_ref[u], t_len)
        u_len = jnp.where(mine, ulen_ref[u], u_len)
    blank = to_diag(feats_ref[0])
    label = to_diag(feats_ref[1])
    edge = jnp.full((pad, 128), NEG, jnp.float32)
    real = (t_of >= 0)
    for ref in (s_ref, l_ref, ls_ref):
        for e in range(ref.shape[0]):
            ref[e, 0:pad, :] = edge
            ref[e, pad + wide:, :] = jnp.full((ref.shape[1] - pad - wide, 128), NEG, jnp.float32)
    for e in range(reach + 1):
        dur = to_diag(feats_ref[2 + e])
        if e > 0:
            keep = real & (k_of <= u_len) & ((t_of + e < t_len) | ((t_of + e == t_len) & (k_of == u_len)))
            s_ref[e - 1, pad:pad + wide, :] = jnp.where(keep, blank + dur, NEG)
        keep = real & (k_of < u_len) & (t_of + e < t_len)
        lab = jnp.where(keep, label + dur, NEG)
        l_ref[e, pad:pad + wide, :] = lab
        ls_ref[e, pad:pad + wide, :] = pltpu.roll(lab, 1, 1)
    init_ref[pad:pad + wide, :] = jnp.where((t_of == t_len) & (k_of == u_len), 0.0, NEG)
    a_ref[...] = jnp.full(a_ref.shape, NEG, jnp.float32)
    b_ref[...] = jnp.full(b_ref.shape, NEG, jnp.float32)

    first = jnp.where((lax.broadcasted_iota(jnp.int32, (1, 128), 1) % 32 == 0)
                      & (lax.broadcasted_iota(jnp.int32, (1, 128), 1) < 32 * utts), 0.0, NEG)

    def lse(terms):
        tops = list(terms)
        while len(tops) > 1:
            tops = [jnp.maximum(tops[i], tops[i + 1]) if i + 1 < len(tops) else tops[i] for i in range(0, len(tops), 2)]
        top = tops[0]
        parts = [jnp.exp(x - top) for x in terms]
        while len(parts) > 1:
            parts = [parts[i] + parts[i + 1] if i + 1 < len(parts) else parts[i] for i in range(0, len(parts), 2)]
        return jnp.maximum(top + jnp.log(parts[0]), NEG)

    a_ref[pl.ds(pad, 1), :] = first
    last = diags

    def step(i, carry):
        ha, hra, hb, hrb = carry
        row = pad + i
        terms = [ha[e - 1] + s_ref[e - 1, pl.ds(row - e, 1), :] for e in range(1, reach + 1)]
        terms += [hra[e] + ls_ref[e, pl.ds(row - e - 1, 1), :] for e in range(reach + 1)]
        a = lse(terms[::-1])
        a_ref[pl.ds(row, 1), :] = a
        ra = pltpu.roll(a, 1, 1)
        rowb = pad + last - i
        terms = [hb[e - 1] + s_ref[e - 1, pl.ds(rowb, 1), :] for e in range(1, reach + 1)]
        terms += [hrb[e] + l_ref[e, pl.ds(rowb, 1), :] for e in range(reach + 1)]
        b = jnp.maximum(lse(terms[::-1]), init_ref[pl.ds(rowb, 1), :])
        b_ref[pl.ds(rowb, 1), :] = b
        rb = pltpu.roll(b, 127, 1)
        return ((a,) + ha[:-1], (ra,) + hra[:-1], (b,) + hb[:-1], (rb,) + hrb[:-1])

    b0 = init_ref[pl.ds(pad + last, 1), :]
    b_ref[pl.ds(pad + last, 1), :] = b0
    none = a_ref[pl.ds(0, 1), :]
    first = a_ref[pl.ds(pad, 1), :]
    ha = (first,) + (none,) * (reach - 1)
    hra = (pltpu.roll(first, 1, 1),) + (none,) * reach
    hb = (b0,) + (none,) * (reach - 1)
    hrb = (pltpu.roll(b0, 127, 1),) + (none,) * reach
    lax.fori_loop(1, last + 1, step, (ha, hra, hb, hrb))

    zrow = b_ref[pl.ds(pad, 1), :]
    lane1 = lax.broadcasted_iota(jnp.int32, (1, 128), 1)
    z = jnp.zeros((1, 128), jnp.float32)
    for u in range(utts):
        zu = jnp.max(jnp.where(lane1 == 32 * u, zrow, 2 * NEG), axis=1, keepdims=True)
        z = jnp.where(lane1 // 32 == u, zu, z)
        prob_ref[pl.ds(u, 1), :] = jnp.broadcast_to(zu, (1, 128))

    def from_diag(x):
        x = x.T[:rows]
        return skew(x, -1)[:, :frames]

    a = a_ref[pad:pad + wide, :] - z
    g_blank = jnp.zeros((wide, 128), jnp.float32)
    g_label = jnp.zeros((wide, 128), jnp.float32)
    for e in range(reach + 1):
        bb = b_ref[pad + e + 1: pad + e + 1 + wide, :]
        pl_ = jnp.exp(a + l_ref[e, pad:pad + wide, :] + pltpu.roll(bb, 127, 1))
        g_label = g_label - pl_
        g = -pl_
        if e > 0:
            ps = jnp.exp(a + s_ref[e - 1, pad:pad + wide, :] + b_ref[pad + e: pad + e + wide, :])
            g_blank = g_blank - ps
            g = g - ps
        grads_ref[2 + e] = from_diag(g)
    grads_ref[0] = from_diag(g_blank)
    grads_ref[1] = from_diag(g_label)


def lattice(feats, t_len, u_len, slots):
    _, rows, frames = feats.shape
    wide = frames + 128
    total = wide + 16
    reach = feats.shape[0] - 3
    return pl.pallas_call(
        partial(lattice_kernel, slots),
        out_shape=(jax.ShapeDtypeStruct(feats.shape, jnp.float32), jax.ShapeDtypeStruct((8, 128), jnp.float32)),
        in_specs=[pl.BlockSpec(memory_space=pltpu.VMEM), pl.BlockSpec(memory_space=pltpu.SMEM), pl.BlockSpec(memory_space=pltpu.SMEM)],
        out_specs=(pl.BlockSpec(memory_space=pltpu.VMEM),) * 2,
        scratch_shapes=[pltpu.VMEM((reach, total, 128), jnp.float32), pltpu.VMEM((reach + 1, total, 128), jnp.float32),
                        pltpu.VMEM((reach + 1, total, 128), jnp.float32), pltpu.VMEM((total, 128), jnp.float32),
                        pltpu.VMEM((total, 128), jnp.float32), pltpu.VMEM((total, 128), jnp.float32)],
        compiler_params=pltpu.CompilerParams(vmem_limit_bytes=48 << 20),
        name="lattice",
    )(feats, t_len, u_len)


GROUP=5
CHUNK=256

def nn(a,b): return jnp.dot(a,b,preferred_element_type=jnp.float32)
def nt(a,b): return lax.dot_general(a,b,(((1,),(1,)),((),())),preferred_element_type=jnp.float32)

def fold8(x, op):
    parts=[x[i:i+8] for i in range(0,x.shape[0],8)]
    while len(parts)>1:
        parts=[op(parts[i],parts[i+1]) if i+1<len(parts) else parts[i] for i in range(0,len(parts),2)]
    return parts[0]

def joint_fwd_kernel(groups, durs, labels_ref, enc_ref, pred_ref, wt_ref, feats_ref, p_ref, tok_ref):
    step=pl.program_id(0)
    vocab=p_ref.shape[2]
    u=step//groups
    g=step%groups
    for j in range(GROUP):
        k=g*GROUP+j
        hid=jnp.tanh(enc_ref[...]+pred_ref[0,:,j:j+1]).astype(jnp.bfloat16)
        tops=[]
        for c in range(0,vocab,CHUNK):
            t=nn(wt_ref[c:c+CHUNK,:],hid)
            tok_ref[j%2,c:c+CHUNK,:]=t
            tops.append(fold8(t,jnp.maximum))
        dl=nn(wt_ref[vocab:,:],hid)[:8]
        top=jnp.max(reduce(jnp.maximum,tops),0,keepdims=True)
        sums=[]
        for c in range(0,vocab,CHUNK):
            e=jnp.exp(tok_ref[j%2,c:c+CHUNK,:]-top)
            p_ref[0,j,c:c+CHUNK,:]=e.astype(jnp.bfloat16)
            sums.append(fold8(e,jnp.add))
        total=jnp.sum(reduce(jnp.add,sums),0,keepdims=True)
        lse=top+jnp.log(total)
        row=u*32+k
        feats_ref[0,pl.ds(row,1),:]=tok_ref[j%2,0:1,:]-lse
        feats_ref[1,pl.ds(row,1),:]=tok_ref[j%2,pl.ds(labels_ref[u,k],1),:]-lse
        real=lax.broadcasted_iota(jnp.int32,dl.shape,0)<durs
        dtop=jnp.max(jnp.where(real,dl,-1e30),0,keepdims=True)
        dlse=dtop+jnp.log(jnp.sum(jnp.where(real,jnp.exp(dl-dtop),0.0),0,keepdims=True))
        dlp=dl-dlse
        for e in range(durs):
            feats_ref[2+e,pl.ds(row,1),:]=dlp[e:e+1]
        feats_ref[2+durs,pl.ds(row,1),:]=1.0/total

def joint_forward(enc_t, pred_t, labels, w_t, vocab, durs, frames):
    joint, rows=enc_t.shape
    utts,slots=labels.shape
    groups=slots//GROUP
    return pl.pallas_call(
        partial(joint_fwd_kernel,groups,durs),
        grid=(utts*groups,),
        in_specs=[pl.BlockSpec(memory_space=pltpu.SMEM),
            pl.BlockSpec((joint,frames),lambda s:(0,s//groups)),
            pl.BlockSpec((1,joint,8),lambda s:(s,0,0)),
            pl.BlockSpec(w_t.shape,lambda s:(0,0))],
        out_specs=[pl.BlockSpec((3+durs,utts*32,frames),lambda s:(0,0,0)),
            pl.BlockSpec((1,GROUP,vocab,frames),lambda s:(s,0,0,0))],
        out_shape=[jax.ShapeDtypeStruct((3+durs,utts*32,frames),jnp.float32),
            jax.ShapeDtypeStruct((utts*groups,GROUP,vocab,frames),jnp.bfloat16)],
        scratch_shapes=[pltpu.VMEM((2,vocab,frames),jnp.float32)],
        compiler_params=pltpu.CompilerParams(vmem_limit_bytes=50<<20),
        name="joint_forward",
    )(labels,enc_t,pred_t,w_t)

def joint_bwd_kernel(groups, durs, labels_ref, enc_ref, pred_ref, w_ref, feats_ref, grads_ref, p_ref, genc_ref, gpred_ref, gtok_ref, gdur_ref, h_ref, d_ref, acc_ref):
    step=pl.program_id(0)
    vocab=p_ref.shape[2]
    frames=p_ref.shape[3]
    u=step//groups
    g=step%groups

    @pl.when(step==0)
    def _():
        acc_ref[...]=jnp.zeros_like(acc_ref)
    @pl.when(g==0)
    def _():
        genc_ref[...]=jnp.zeros_like(genc_ref)
    for j in range(GROUP):
        k=g*GROUP+j
        row=u*32+k
        cols=slice(j*frames,(j+1)*frames)
        th=jnp.tanh(enc_ref[...]+pred_ref[0,:,j:j+1])
        h_ref[:,cols]=th.astype(jnp.bfloat16)
        gb=grads_ref[0,pl.ds(row,1),:]
        gl=grads_ref[1,pl.ds(row,1),:]
        scale=-(gb+gl)*feats_ref[2+durs,pl.ds(row,1),:]
        for c in range(0,vocab,CHUNK):
            d_ref[c:c+CHUNK,cols]=(p_ref[0,j,c:c+CHUNK,:].astype(jnp.float32)*scale).astype(jnp.bfloat16)
        label=labels_ref[u,k]
        def fix(base):
            v=p_ref[0,j,pl.ds(base,16),:].astype(jnp.float32)*scale
            at=lax.broadcasted_iota(jnp.int32,v.shape,0)+base
            v=v+jnp.where(at==0,gb,0.0)+jnp.where(at==label,gl,0.0)
            d_ref[pl.ds(base,16),cols]=v.astype(jnp.bfloat16)
        fix(0)
        fix(pl.multiple_of((label//16)*16,16))
        gd=[grads_ref[2+e,pl.ds(row,1),:] for e in range(durs)]
        gsum=reduce(jnp.add,gd)
        at=lax.broadcasted_iota(jnp.int32,(16,frames),0)
        dd=jnp.zeros((16,frames),jnp.float32)
        for e in range(durs):
            dd=jnp.where(at==e,gd[e]-gsum*jnp.exp(feats_ref[2+e,pl.ds(row,1),:]),dd)
        d_ref[vocab:vocab+16,cols]=dd.astype(jnp.bfloat16)
        d_ref[vocab+16:,cols]=jnp.zeros((d_ref.shape[0]-vocab-16,frames),jnp.bfloat16)
        dh=nn(w_ref[...],d_ref[:,cols])
        th=jnp.tanh(enc_ref[...]+pred_ref[0,:,j:j+1])
        dp=dh*(1.0-th*th)
        genc_ref[...]+=dp
        gpred_ref[0,:,j:j+1]=jnp.sum(dp,1,keepdims=True)
    for c in range(0,d_ref.shape[0],384):
        acc_ref[:,c:c+384]+=nt(h_ref[...],d_ref[c:c+384,:])
    @pl.when(step==pl.num_programs(0)-1)
    def _():
        gtok_ref[...]=acc_ref[:,:vocab].astype(jnp.bfloat16)
        gdur_ref[...]=acc_ref[:,vocab:].astype(jnp.bfloat16)

def joint_backward(enc_t, pred_t, labels, w, feats, grads, p, vocab, durs, frames):
    joint, rows=enc_t.shape
    utts,slots=labels.shape
    groups=slots//GROUP
    full=lambda a: pl.BlockSpec(a.shape,lambda s:(0,)*a.ndim)
    return pl.pallas_call(
        partial(joint_bwd_kernel,groups,durs),
        grid=(utts*groups,),
        in_specs=[pl.BlockSpec(memory_space=pltpu.SMEM),
            pl.BlockSpec((joint,frames),lambda s:(0,s//groups)),
            pl.BlockSpec((1,joint,8),lambda s:(s,0,0)),
            full(w),full(feats),full(grads),
            pl.BlockSpec((1,GROUP,vocab,frames),lambda s:(s,0,0,0))],
        out_specs=[pl.BlockSpec((joint,frames),lambda s:(0,s//groups)),
            pl.BlockSpec((1,joint,8),lambda s:(s,0,0)),
            pl.BlockSpec((joint,vocab),lambda s:(0,0)),
            pl.BlockSpec((joint,128),lambda s:(0,0))],
        out_shape=[jax.ShapeDtypeStruct((joint,rows),jnp.float32),
            jax.ShapeDtypeStruct((utts*groups,joint,8),jnp.float32),
            jax.ShapeDtypeStruct((joint,vocab),jnp.bfloat16),
            jax.ShapeDtypeStruct((joint,128),jnp.bfloat16)],
        scratch_shapes=[pltpu.VMEM((joint,GROUP*frames),jnp.bfloat16),
            pltpu.VMEM((vocab+128,GROUP*frames),jnp.bfloat16),
            pltpu.VMEM((joint,vocab+128),jnp.float32)],
        compiler_params=pltpu.CompilerParams(vmem_limit_bytes=56<<20),
        name="joint_backward",
    )(labels,enc_t,pred_t,w,feats,grads,p)


MESH=pl.DeviceIdType.MESH
QA = QB = HALF = TILE = 0


def set_tile(shards):
    global QA, QB, HALF, TILE
    QA = QB = max(16, 256 // shards)
    HALF = 2 * QA + QB
    TILE = 2 * HALF


def place():
    dp=lax.axis_index("dp"); fs=lax.axis_index("fsdp")
    return dp, fs, dp//2, dp%2, fs//2, fs%2

def greet(n1, dp, fs, a, c, i1, i2):
    barrier=pltpu.get_barrier_semaphore()
    for d in range(1,n1):
        pl.semaphore_signal(barrier,inc=1,device_id=(dp,lax.rem(i1+d,n1)*2+i2),device_id_type=MESH)
    pl.semaphore_signal(barrier,inc=1,device_id=(dp,i1*2+1-i2),device_id_type=MESH)
    pl.semaphore_signal(barrier,inc=1,device_id=((1-a)*2+c,fs),device_id_type=MESH)
    pl.semaphore_signal(barrier,inc=1,device_id=(a*2+1-c,fs),device_id_type=MESH)
    pl.semaphore_wait(barrier,n1+2)

def remote(s, d, ss, rs, dev):
    return pltpu.make_async_remote_copy(src_ref=s,dst_ref=d,send_sem=ss,recv_sem=rs,device_id=dev,device_id_type=MESH)

def rows(base, size):
    return pl.ds(pl.multiple_of(base,16),size)

def gather_kernel(n1, tiles, lag, src, out, own_sem, sz, rz, sy, ry, sx, rx, sc, rc):
    dp,fs,a,c,i1,i2=place()
    greet(n1,dp,fs,a,c,i1,i2)
    ypeer=(dp,i1*2+1-i2); xpeer=((1-a)*2+c,fs); cpeer=(a*2+1-c,fs)
    items=n1*tiles
    def main(t): return rows(t*TILE+c*HALF+a*QA,QA+QB)
    def quarter(t,aa): return rows(t*TILE+c*HALF+aa*(QA+QB),QA)
    def half(t,cc): return rows(t*TILE+cc*HALF,HALF)
    def of(m): return m//n1, m%n1, lax.rem(i1+n1-m%n1,n1)
    def zcopy(t,d):
        j=lax.rem(i1+d,n1)
        return remote(src.at[main(t),:],out.at[fs,main(t),:],sz.at[t,d],rz.at[t,i1],(dp,j*2+i2))
    def zin(t,j):
        return remote(src.at[main(t),:],out.at[j*2+i2,main(t),:],sz.at[t,0],rz.at[t,j],ypeer)
    def ycopy(t,j):
        s=j*2+i2
        return remote(out.at[s,main(t),:],out.at[s,main(t),:],sy.at[t,j],ry.at[t,j],ypeer)
    def ycopy_own(t):
        return remote(src.at[main(t),:],out.at[fs,main(t),:],sy.at[t,i1],ry.at[t,i1],ypeer)
    def yin(t,j):
        s=j*2+1-i2
        return remote(src.at[main(t),:],out.at[s,main(t),:],sy.at[t,j],ry.at[t,j],ypeer)
    def xcopy(t,s):
        return remote(out.at[s,quarter(t,a),:],out.at[s,quarter(t,a),:],sx.at[t,s],rx.at[t,s],xpeer)
    def xin(t,s):
        return remote(src.at[quarter(t,a),:],out.at[s,quarter(t,1-a),:],sx.at[t,s],rx.at[t,s],xpeer)
    def ccopy(t,s):
        return remote(out.at[s,half(t,c),:],out.at[s,half(t,c),:],sc.at[t,s],rc.at[t,s],cpeer)
    def cin(t,s):
        return remote(src.at[half(t,c),:],out.at[s,half(t,1-c),:],sc.at[t,s],rc.at[t,s],cpeer)
    local=pltpu.make_async_copy(src,out.at[fs],own_sem)
    local.start()

    def tick(tau,carry):
        @pl.when(tau<items)
        def _():
            t,d,j=of(tau)
            @pl.when(d>0)
            def _(): zcopy(t,d).start()
            @pl.when(d==0)
            def _(): ycopy_own(t).start()
        m1=tau-lag
        @pl.when((m1>=0)&(m1<items))
        def _():
            t,d,j=of(m1)
            @pl.when(d>0)
            def _():
                zin(t,j).wait_recv()
                ycopy(t,j).start()
                xcopy(t,j*2+i2).start()
        m2=tau-2*lag
        @pl.when((m2>=0)&(m2<items))
        def _():
            t,d,j=of(m2)
            yin(t,j).wait_recv()
            xcopy(t,j*2+1-i2).start()
        m3=tau-3*lag
        @pl.when((m3>=0)&(m3<items))
        def _():
            t,d,j=of(m3)
            @pl.when(d>0)
            def _():
                xin(t,j*2+i2).wait_recv()
                ccopy(t,j*2+i2).start()
            xin(t,j*2+1-i2).wait_recv()
            ccopy(t,j*2+1-i2).start()
        return carry
    lax.fori_loop(0,items+3*lag,tick,0)
    local.wait()
    def finish(m,carry):
        t,d,j=of(m)
        @pl.when(d>0)
        def _():
            cin(t,j*2+i2).wait_recv()
            zcopy(t,d).wait_send()
            xcopy(t,j*2+i2).wait_send()
            ccopy(t,j*2+i2).wait_send()
        cin(t,j*2+1-i2).wait_recv()
        ycopy(t,j).wait_send()
        xcopy(t,j*2+1-i2).wait_send()
        ccopy(t,j*2+1-i2).wait_send()
        return carry
    lax.fori_loop(0,items,finish,0)

def gather(packed, collective_id, lag=4):
    n=lax.axis_size("fsdp"); n1=n//2
    tiles=packed.shape[0]//TILE
    dma=pltpu.SemaphoreType.DMA
    return pl.pallas_call(
        partial(gather_kernel,n1,tiles,lag),
        out_shape=jax.ShapeDtypeStruct((n,)+packed.shape,packed.dtype),
        in_specs=[pl.BlockSpec(memory_space=pl.ANY)],
        out_specs=pl.BlockSpec(memory_space=pl.ANY),
        scratch_shapes=[dma]+[dma((tiles,n1))]*4+[dma((tiles,n))]*4,
        compiler_params=pltpu.CompilerParams(collective_id=collective_id,has_side_effects=True),
        name="gather_weights",
    )(packed)

def scatter_kernel(n1, counts, lag, *refs):
    srcs = refs[:len(counts)]
    scatter_body(n1, counts, lag, srcs, *refs[len(counts):])

def scatter_body(n1, counts, lag, srcs, out, own, gc, gx, gy, gz, gf, fin,
                   lo, sc, rc, sx, rx, sy, ry, sz, rz, sf, rf, se, re, wo):
    dp,fs,a,c,i1,i2=place()
    greet(n1,dp,fs,a,c,i1,i2)
    ypeer=(dp,i1*2+1-i2); xpeer=((1-a)*2+c,fs); cpeer=(a*2+1-c,fs)
    tiles=sum(counts)
    items=n1*tiles
    main=rows(a*QA,QA+QB)
    def quarter(aa): return rows(aa*(QA+QB),QA)
    middle=pl.ds(QA,QB)
    def of(m): return m//n1, lax.rem(i1+1+m%n1,n1)
    def load(t,s,src=srcs[0],f=0): return pltpu.make_async_copy(src.at[s,rows((t-f)*TILE+c*HALF,HALF),:],own.at[t,s],lo.at[t,s])
    def ccopy(t,s,src=srcs[0],f=0): return remote(src.at[s,rows((t-f)*TILE+(1-c)*HALF,HALF),:],gc.at[t,s],sc.at[t,s],rc.at[t,s],cpeer)
    def xcopy(t,s): return remote(own.at[t,s,quarter(1-a),:],gx.at[t,s],sx.at[t,s],rx.at[t,s],xpeer)
    def ycopy(t,j): return remote(own.at[t,j*2+1-i2,main,:],gy.at[t,j],sy.at[t,j],ry.at[t,j],ypeer)
    def zcopy(t,j): return remote(own.at[t,j*2+i2,main,:],gz.at[t,i1],sz.at[t,j],rz.at[t,i1],(dp,j*2+i2))
    def zin(t,j): return remote(own.at[t,fs,main,:],gz.at[t,j],sz.at[t,j],rz.at[t,j],ypeer)
    def fcopy(t): return remote(own.at[t,fs,main,:],gf.at[t],sf.at[t],rf.at[t],xpeer)
    def ecopy(t): return remote(fin.at[t,c],fin.at[t,c],se.at[t],re.at[t],cpeer)
    def ein(t): return remote(fin.at[t,1-c],fin.at[t,1-c],se.at[t],re.at[t],cpeer)
    def store(t): return pltpu.make_async_copy(fin.at[t],out.at[t],wo.at[t])

    def tick(tau,carry):
        def at(shift,body):
            m=tau-shift
            @pl.when((m>=0)&(m<items))
            def _(): body(*of(m))
        def at_tile(shift,body):
            m=tau-shift
            @pl.when((m>=0)&(m<items)&(lax.rem(m+n1,n1)==n1-1))
            def _(): body(m//n1)
        def stage_c(t,j):
            first=0
            for src,count in zip(srcs,counts):
                @pl.when((t>=first)&(t<first+count))
                def _(src=src,first=first):
                    for i in range(2):
                        load(t,j*2+i,src,first).start(); ccopy(t,j*2+i,src,first).start()
                first+=count
        def stage_x(t,j):
            for i in range(2):
                s=j*2+i
                pltpu.make_async_copy(own.at[t,s],own.at[t,s],lo.at[t,s]).wait(); remote(own.at[t,s],gc.at[t,s],sc.at[t,s],rc.at[t,s],cpeer).wait_recv()
                own[t,s]=own[t,s]+gc[t,s]
                xcopy(t,s).start()
        def stage_y(t,j):
            for i in range(2):
                s=j*2+(1-i2 if i==0 else i2)
                xcopy(t,s).wait_recv()
                own[t,s,quarter(a),:]=own[t,s,quarter(a),:]+gx[t,s]
                if i==0: ycopy(t,j).start()
        def stage_z(t,j):
            s=j*2+i2
            ycopy(t,j).wait_recv()
            own[t,s,main,:]=own[t,s,main,:]+gy[t,j]
            @pl.when(j!=i1)
            def _(): zcopy(t,j).start()
        def stage_f(t):
            total=own[t,fs,main,:].astype(jnp.float32)
            for d in range(1,n1):
                j=lax.rem(i1+n1-d,n1)
                zin(t,j).wait_recv()
                total=total+gz[t,j].astype(jnp.float32)
            own[t,fs,main,:]=total.astype(jnp.bfloat16)
            fcopy(t).start()
        def stage_e(t):
            fcopy(t).wait_recv()
            fin[t,c,quarter(a),:]=own[t,fs,quarter(a),:]
            fin[t,c,quarter(1-a),:]=gf[t,rows((1-a)*QB,QA),:]
            fin[t,c,middle,:]=own[t,fs,middle,:]+gf[t,rows(a*QA,QB),:]
            ecopy(t).start()
        def stage_o(t):
            ein(t).wait_recv()
            ecopy(t).wait_send()
            store(t).start()
        at(0,stage_c); at(lag,stage_x); at(2*lag,stage_y); at(3*lag,stage_z)
        at_tile(3*lag+1,stage_f); at_tile(4*lag+1,stage_e); at_tile(5*lag+1,stage_o)
        return carry
    lax.fori_loop(0,items+5*lag+1,tick,0)
    def finish(m,carry):
        t,j=of(m)
        for i in range(2):
            remote(own.at[t,j*2+i],gc.at[t,j*2+i],sc.at[t,j*2+i],rc.at[t,j*2+i],cpeer).wait_send(); xcopy(t,j*2+i).wait_send()
        ycopy(t,j).wait_send()
        @pl.when(j!=i1)
        def _(): zcopy(t,j).wait_send()
        return carry
    lax.fori_loop(0,items,finish,0)
    def finish_tile(t,carry):
        fcopy(t).wait_send(); store(t).wait()
        return carry
    lax.fori_loop(0,tiles,finish_tile,0)

def scatter(sources, collective_id, lag=3):
    n=lax.axis_size("fsdp"); n1=n//2
    counts=tuple(x.shape[1]//TILE for x in sources)
    tiles=sum(counts); w=sources[0].shape[2]
    dma=pltpu.SemaphoreType.DMA
    bf=jnp.bfloat16
    out=pl.pallas_call(
        partial(scatter_kernel,n1,counts,lag),
        out_shape=jax.ShapeDtypeStruct((tiles,2,HALF,w),bf),
        in_specs=[pl.BlockSpec(memory_space=pl.ANY)]*len(sources),
        out_specs=pl.BlockSpec(memory_space=pl.ANY),
        scratch_shapes=[pltpu.VMEM((tiles,n,HALF,w),bf),pltpu.VMEM((tiles,n,HALF,w),bf),pltpu.VMEM((tiles,n,QA,w),bf),
            pltpu.VMEM((tiles,n1,QA+QB,w),bf),pltpu.VMEM((tiles,n1,QA+QB,w),bf),pltpu.VMEM((tiles,QA+QB,w),bf),pltpu.VMEM((tiles,2,HALF,w),bf)]
            +[dma((tiles,n))]*5+[dma((tiles,n1))]*4+[dma((tiles,))]*5,
        compiler_params=pltpu.CompilerParams(collective_id=collective_id,has_side_effects=True,vmem_limit_bytes=60<<20),
        name="scatter_grads",
    )(*sources)
    out=out.reshape(tiles*TILE,w)
    return out


def pooled(parts):
    counts = [x[8:9] for x in parts]
    count = sum(counts[1:], counts[0])
    mean = sum((x[0:4] * n for x, n in zip(parts[1:], counts[1:])), parts[0][0:4] * counts[0]) / count
    dev = jnp.zeros_like(mean)
    for x, n in zip(parts, counts):
        gap = x[0:4] - mean
        dev = dev + (x[4:8] + gap * gap * n)
    return mean, dev, count


def exchange_kernel(kind, groups, n, x_ref, out_ref, near, far, s1, r1, s2, r2):
    dp = lax.axis_index("dp")
    fs = lax.axis_index("fsdp")
    barrier = pltpu.get_barrier_semaphore()
    for d in range(1, groups):
        pl.semaphore_signal(barrier, inc=1, device_id=(lax.rem(dp + d, groups), fs), device_id_type=MESH)
    for d in range(1, n):
        pl.semaphore_signal(barrier, inc=1, device_id=(dp, lax.rem(fs + d, n)), device_id_type=MESH)
    pl.semaphore_wait(barrier, groups + n - 2)

    def merge(ref, members):
        if kind == "sum":
            total = ref[0]
            for i in range(1, members):
                total = total + ref[i]
            return total
        mean, dev, count = pooled([ref[i] for i in range(members)])
        return jnp.concatenate([mean, dev, jnp.broadcast_to(count, (8, 128))], 0)

    near[dp] = x_ref[...]
    first = []
    for d in range(1, groups):
        cp = remote(near.at[dp], near.at[dp], s1.at[d], r1.at[dp], (lax.rem(dp + d, groups), fs))
        cp.start()
        first.append(cp)
    for d in range(1, groups):
        other = lax.rem(dp + d, groups)
        remote(near.at[dp], near.at[other], s1.at[d], r1.at[other], (other, fs)).wait_recv()
    far[fs] = merge(near, groups)
    for d in range(1, n):
        cp = remote(far.at[fs], far.at[fs], s2.at[d], r2.at[fs], (dp, lax.rem(fs + d, n)))
        cp.start()
        first.append(cp)
    for d in range(1, n):
        other = lax.rem(fs + d, n)
        remote(far.at[fs], far.at[other], s2.at[d], r2.at[other], (dp, other)).wait_recv()
    out_ref[...] = merge(far, n)
    for cp in first:
        cp.wait_send()


def exchange(x, kind, collective_id):
    n = lax.axis_size("fsdp")
    groups = lax.axis_size("dp")
    dma = pltpu.SemaphoreType.DMA
    return pl.pallas_call(
        partial(exchange_kernel, kind, groups, n),
        out_shape=jax.ShapeDtypeStruct(x.shape, x.dtype),
        in_specs=[pl.BlockSpec(memory_space=pltpu.VMEM)],
        out_specs=pl.BlockSpec(memory_space=pltpu.VMEM),
        scratch_shapes=[
            pltpu.VMEM((groups,) + x.shape, x.dtype),
            pltpu.VMEM((n,) + x.shape, x.dtype),
            dma((groups,)), dma((groups,)), dma((n,)), dma((n,)),
        ],
        compiler_params=pltpu.CompilerParams(collective_id=collective_id, has_side_effects=True),
        name="exchange_" + kind,
    )(x)


CHUNK_ROWS = 64
WIDE = 512
PLACE = ("p_out", "s_in", "s_out", "p_in", "w_proj", "w_joint", "f_in", "f_out")


def tn(a, b):
    return lax.dot_general(a, b, (((0,), (0,)), ((), ())), preferred_element_type=jnp.float32)


def row_loop(count, body, init=0):
    def step(i, carry):
        return body(pl.ds(pl.multiple_of(i * CHUNK_ROWS, CHUNK_ROWS), CHUNK_ROWS), i, carry)

    return lax.fori_loop(0, count // CHUNK_ROWS, step, init)


def ln_parts(v):
    centred = v - jnp.mean(v, -1, keepdims=True)
    rstd = lax.rsqrt(jnp.mean(centred * centred, -1, keepdims=True) + EPS)
    return centred * rstd, rstd


def ln_back(v, gain, grad):
    hat, rstd = ln_parts(v)
    dy = grad * gain
    dv = rstd * (dy - jnp.mean(dy, -1, keepdims=True) - hat * jnp.mean(dy * hat, -1, keepdims=True))
    return dv, fold8(grad * hat, jnp.add)


def offsets(n, width, ff):
    low = width // n
    tall = ff // n
    sizes = {
        "p_out": low, "s_in": low * (ff // WIDE), "s_out": tall, "p_in": 2 * low,
        "w_proj": low, "w_joint": 3 * low, "f_in": low * (ff // WIDE), "f_out": tall,
    }
    table = {}
    at = 0
    for name in PLACE:
        table[name] = at
        at += sizes[name]
    return table, at


class Mover:
    def __init__(self, sems):
        self.sems = sems
        self.used = 0
        self.pending = []

    def take(self):
        self.used += 1
        return self.sems.at[self.used - 1]

    def load(self, src, dst):
        cp = pltpu.make_async_copy(src, dst, self.take())
        cp.start()
        return cp

    def put(self, src, dst):
        cp = pltpu.make_async_copy(src, dst, self.take())
        cp.start()
        self.pending.append(cp)

    def load_weight(self, whole, at, dst, tall):
        n = whole.shape[0]
        height = dst.shape[0] // n
        sem = self.take()

        def one(s, carry):
            for b in range(dst.shape[1] // WIDE):
                pltpu.make_async_copy(
                    whole.at[s, pl.ds(at + b * height, height), :],
                    dst.at[pl.ds(pl.multiple_of(s * height, 16), height), pl.ds(b * WIDE, WIDE)],
                    sem,
                ).start()
            return carry

        lax.fori_loop(0, n, one, 0)
        return pltpu.make_async_copy(dst, dst, sem)

    def put_weight(self, src, grads, at):
        n = grads.shape[0]
        height = src.shape[0] // n
        sem = self.take()

        def one(s, carry):
            for b in range(src.shape[1] // WIDE):
                pltpu.make_async_copy(
                    src.at[pl.ds(pl.multiple_of(s * height, 16), height), pl.ds(b * WIDE, WIDE)],
                    grads.at[s, pl.ds(at + b * height, height), :],
                    sem,
                ).start()
            return carry

        lax.fori_loop(0, n, one, 0)
        self.pending.append(pltpu.make_async_copy(src, src, sem))

    def finish(self):
        for cp in self.pending:
            cp.wait()


def valid_rows_of(t_ref, frames, i):
    per = frames // CHUNK_ROWS
    t_len = t_ref[i // per]
    at = lax.broadcasted_iota(jnp.int32, (CHUNK_ROWS, 1), 0) + lax.rem(i, per) * CHUNK_ROWS
    return jnp.where(at < t_len, 1.0, 0.0)


def write_rows(out, base, vec):
    for i in range(vec.shape[1] // 128):
        out[base + i : base + i + 1, :] = vec[:, i * 128 : (i + 1) * 128]


def read_rows(ref, base, width):
    return jnp.concatenate([ref[base + i : base + i + 1, :] for i in range(width // 128)], 1)


def ffn_fwd(rows, x_ref, gain, w_in, w_out, normed, h, act, y, mover, h_out):
    def prepare(r, i, c):
        normed[r, :] = (ln_parts(x_ref[r, :].astype(jnp.float32))[0] * gain).astype(jnp.bfloat16)
        return c

    row_loop(rows, prepare)
    w_in[1].wait()
    for b in range(h.shape[0]):
        h[b] = nn(normed[...], w_in[0][:, b * WIDE : (b + 1) * WIDE])
        mover.put(h.at[b], h_out.at[b])

        def swish(r, i, c):
            v = h[b, r, :]
            act[r, b * WIDE : (b + 1) * WIDE] = (v * jax.nn.sigmoid(v)).astype(jnp.bfloat16)
            return c

        row_loop(rows, swish)
    w_out[1].wait()
    y[...] = x_ref[...].astype(jnp.float32) + 0.5 * nn(act[...], w_out[0][...])


def part_one_kernel(utts, table, t_ref, x_ref, small, whole, y1_out, h_out, y2_out, t_out, c_out, r_out, d_out, stats,
                    w_fin, w_fout, w_joint, w_proj, w_pin, y1, y2, normed, h, act, tq, ctx, r, gp, d, sems):
    rows, width = y1.shape
    frames = rows // utts
    mover = Mover(sems)
    gains = small[...]
    fin = mover.load_weight(whole, table["f_in"], w_fin, False)
    fout = mover.load_weight(whole, table["f_out"], w_fout, True)
    wj = mover.load_weight(whole, table["w_joint"], w_joint, False)
    wp = mover.load_weight(whole, table["w_proj"], w_proj, False)
    wi = mover.load_weight(whole, table["p_in"], w_pin, False)
    ffn_fwd(rows, x_ref, gains[0:1], (w_fin, fin), (w_fout, fout), normed, h, act, y1, mover, h_out)
    mover.put(y1, y1_out)

    def prepare(rr, i, c):
        normed[rr, :] = (ln_parts(y1[rr, :])[0] * gains[1:2]).astype(jnp.bfloat16)
        return c

    row_loop(rows, prepare)
    wj.wait()
    for b in range(3):
        tq[:, b * width : (b + 1) * width] = nn(normed[...], w_joint[:, b * width : (b + 1) * width]).astype(jnp.bfloat16)
    mover.put(tq, t_out)
    pairs = width // 128
    side = lax.broadcasted_iota(jnp.int32, (frames, 128), 1) < 64
    key_at = lax.broadcasted_iota(jnp.int32, (1, frames), 1)

    def pair_step(m, carry):
        u = m // pairs
        base = lax.rem(m, pairs) * 128
        rr = pl.ds(pl.multiple_of(u * frames, frames), frames)
        bias = jnp.where(key_at < t_ref[u], 0.0, MASKED)
        q = tq[rr, pl.ds(pl.multiple_of(base, 128), 128)]
        k = tq[rr, pl.ds(pl.multiple_of(base + width, 128), 128)]
        v = tq[rr, pl.ds(pl.multiple_of(base + 2 * width, 128), 128)]
        got = []
        for half in range(2):
            mine = side if half == 0 else ~side
            s = nt(jnp.where(mine, q, jnp.zeros_like(q)), k) * 0.125 + bias
            p = jnp.exp(s - jnp.max(s, -1, keepdims=True))
            p = p * (1.0 / jnp.sum(p, -1, keepdims=True))
            got.append(nn(p.astype(jnp.bfloat16), v))
        ctx[rr, pl.ds(pl.multiple_of(base, 128), 128)] = jnp.where(side, got[0], got[1]).astype(jnp.bfloat16)
        return carry

    lax.fori_loop(0, utts * pairs, pair_step, 0)
    mover.put(ctx, c_out)
    wp.wait()
    y2[...] = y1[...] + nn(ctx[...], w_proj[...])
    mover.put(y2, y2_out)

    def prepare_conv(rr, i, c):
        normed[rr, :] = (ln_parts(y2[rr, :])[0] * gains[2:3]).astype(jnp.bfloat16)
        return c

    row_loop(rows, prepare_conv)
    wi.wait()
    for b in range(2):
        r[:, b * width : (b + 1) * width] = nn(normed[...], w_pin[:, b * width : (b + 1) * width])
    mover.put(r, r_out)
    fill_gated(utts, frames, t_ref, r, gp)
    taps = gains[5:14]

    def conv(rr, i, total):
        d_chunk = spread(gp, utts, frames, i, taps)
        d[rr, :] = d_chunk
        return total + fold8(d_chunk * valid_rows_of(t_ref, frames, i), jnp.add)

    total = row_loop(rows, conv, jnp.zeros((8, width), jnp.float32))
    mover.put(d, d_out)
    count = t_ref[0]
    for u in range(1, utts):
        count = count + t_ref[u]
    count = count.astype(jnp.float32)
    mean = jnp.sum(total, 0, keepdims=True) / count

    def deviate(rr, i, total):
        gap = (d[rr, :] - mean) * valid_rows_of(t_ref, frames, i)
        return total + fold8(gap * gap, jnp.add)

    dev = jnp.sum(row_loop(rows, deviate, jnp.zeros((8, width), jnp.float32)), 0, keepdims=True)
    write_rows(stats, 0, mean)
    write_rows(stats, 4, dev)
    stats[8:16, :] = jnp.full((8, 128), count, jnp.float32)
    mover.finish()


def fill_gated(utts, frames, t_ref, r, gp):
    width = gp.shape[1]
    span = frames + 16
    per = frames // CHUNK_ROWS
    for u in range(utts):
        gp[u * span : u * span + 8, :] = jnp.zeros((8, width), jnp.float32)
        gp[u * span + 8 + frames : (u + 1) * span, :] = jnp.zeros((8, width), jnp.float32)

    def gate(rr, i, c):
        g = r[rr, :width] * jax.nn.sigmoid(r[rr, width:]) * valid_rows_of(t_ref, frames, i)
        at = (i // per) * span + 8 + lax.rem(i, per) * CHUNK_ROWS
        gp[pl.ds(pl.multiple_of(at, 8), CHUNK_ROWS), :] = g
        return c

    row_loop(utts * frames, gate)


def window(gp, frames, i):
    per = frames // CHUNK_ROWS
    at = (i // per) * (frames + 16) + lax.rem(i, per) * CHUNK_ROWS
    return gp[pl.ds(pl.multiple_of(at, 8), CHUNK_ROWS + 16), :]


def spread(gp, utts, frames, i, taps, flip=False):
    win = window(gp, frames, i)
    count = taps.shape[0]
    total = None
    for j in range(count):
        shift = 8 - count // 2 + (count - 1 - j if flip else j)
        term = win[shift : shift + CHUNK_ROWS] * taps[j : j + 1]
        total = term if total is None else total + term
    return total


def part_two_kernel(table, d_ref, y2_ref, pooled_ref, small, whole, y3_out, h_out, y4_out, x_out,
                    w_pout, w_sin, w_sout, act_b, y3, normed, h, act, y4, x, sems):
    rows, width = y3.shape
    mover = Mover(sems)
    gains = small[...]
    wo = mover.load_weight(whole, table["p_out"], w_pout, False)
    sin = mover.load_weight(whole, table["s_in"], w_sin, False)
    sout = mover.load_weight(whole, table["s_out"], w_sout, True)
    mean = read_rows(pooled_ref, 0, width)
    count = pooled_ref[8:9, 0:1]
    istd = lax.rsqrt(read_rows(pooled_ref, 4, width) / count + EPS)

    def bn(rr, i, c):
        b = (d_ref[rr, :] - mean) * istd * gains[14:15] + gains[15:16]
        act_b[rr, :] = (b * jax.nn.sigmoid(b)).astype(jnp.bfloat16)
        return c

    row_loop(rows, bn)
    wo.wait()
    y3[...] = y2_ref[...] + nn(act_b[...], w_pout[...])
    mover.put(y3, y3_out)
    ffn_fwd(rows, y3, gains[3:4], (w_sin, sin), (w_sout, sout), normed, h, act, y4, mover, h_out)
    mover.put(y4, y4_out)

    def last(rr, i, c):
        x[rr, :] = ln_parts(y4[rr, :])[0] * gains[4:5]
        return c

    row_loop(rows, last)
    mover.put(x, x_out)
    mover.finish()


def ffn_bwd(rows, v_ref, gain, w_in, w_out, h, loads, g_ref, gb, normed, dact, act, dh, dn, dw_in, dw_out, mover, grads, at_in, at_out):
    def prepare(rr, i, c):
        normed[rr, :] = (ln_parts(v_ref[rr, :].astype(jnp.float32))[0] * gain).astype(jnp.bfloat16)
        gb[rr, :] = (0.5 * g_ref[rr, :]).astype(jnp.bfloat16)
        return c

    row_loop(rows, prepare)
    w_out[1].wait()
    for b in range(h.shape[0]):
        cols = slice(b * WIDE, (b + 1) * WIDE)
        dact[...] = nt(gb[...], w_out[0][cols, :])
        loads[b].wait()

        def slope(rr, i, c):
            v = h[b, rr, :]
            sg = jax.nn.sigmoid(v)
            act[rr, :] = (v * sg).astype(jnp.bfloat16)
            dh[rr, cols] = (dact[rr, :] * (sg * (1.0 + v * (1.0 - sg)))).astype(jnp.bfloat16)
            return c

        row_loop(rows, slope)
        dw_out[cols, :] = tn(act[...], gb[...]).astype(jnp.bfloat16)
        dw_in[:, cols] = tn(normed[...], dh[:, cols]).astype(jnp.bfloat16)
    mover.put_weight(dw_out, grads, at_out)
    mover.put_weight(dw_in, grads, at_in)
    w_in[1].wait()
    dn[...] = nt(dh[...], w_in[0][...])

    def back(rr, i, total):
        dv, dg = ln_back(v_ref[rr, :].astype(jnp.float32), gain, dn[rr, :])
        g_ref[rr, :] = g_ref[rr, :] + dv
        return total + dg

    return row_loop(rows, back, jnp.zeros((8, g_ref.shape[1]), jnp.float32))


def down(folded):
    return jnp.sum(folded, 0, keepdims=True)


def back_one_kernel(table, grad_ref, y4_ref, y3_ref, d_ref, pooled_ref, small, whole, h_hbm, g_out, db_out, grads, sums, gain_out,
                    w_pout, w_sin, w_sout, g, gb, normed, dact, act, dh, dn, dw_in, dw_out, dw_pout, h, db, sems):
    rows, width = g.shape
    mover = Mover(sems)
    gains = small[...]
    sout = mover.load_weight(whole, table["s_out"], w_sout, True)
    loads = [mover.load(h_hbm.at[b], h.at[b]) for b in range(h.shape[0])]
    sin = mover.load_weight(whole, table["s_in"], w_sin, False)
    wo = mover.load_weight(whole, table["p_out"], w_pout, False)

    def first(rr, i, total):
        dv, dg = ln_back(y4_ref[rr, :], gains[4:5], grad_ref[rr, :])
        g[rr, :] = dv
        return total + dg

    gain4 = down(row_loop(rows, first, jnp.zeros((8, width), jnp.float32)))
    gain3 = down(ffn_bwd(rows, y3_ref, gains[3:4], (w_sin, sin), (w_sout, sout), h, loads, g, gb, normed, dact, act, dh, dn,
                         dw_in, dw_out, mover, grads, table["s_in"], table["s_out"]))
    mover.put(g, g_out)
    gain_out[...] = jnp.concatenate([gain3, gain4, jnp.zeros((6, width), jnp.float32)], 0)
    mean = read_rows(pooled_ref, 0, width)
    istd = lax.rsqrt(read_rows(pooled_ref, 4, width) / pooled_ref[8:9, 0:1] + EPS)

    def cast(rr, i, c):
        gb[rr, :] = g[rr, :].astype(jnp.bfloat16)
        return c

    row_loop(rows, cast)
    wo.wait()
    dact[...] = nt(gb[...], w_pout[...])

    def bn(rr, i, totals):
        z = (d_ref[rr, :] - mean) * istd
        b = z * gains[14:15] + gains[15:16]
        sg = jax.nn.sigmoid(b)
        act[rr, :] = (b * sg).astype(jnp.bfloat16)
        db_chunk = dact[rr, :] * (sg * (1.0 + b * (1.0 - sg)))
        db[rr, :] = db_chunk
        return totals[0] + fold8(db_chunk, jnp.add), totals[1] + fold8(db_chunk * z, jnp.add)

    zero = jnp.zeros((8, width), jnp.float32)
    one, two = row_loop(rows, bn, (zero, zero))
    mover.put(db, db_out)
    write_rows(sums, 0, down(one))
    write_rows(sums, 4, down(two))
    sums[8:16, :] = jnp.zeros((8, 128), jnp.float32)
    dw_pout[...] = tn(act[...], gb[...]).astype(jnp.bfloat16)
    mover.put_weight(dw_pout, grads, table["p_out"])
    mover.finish()


def back_two_kernel(utts, table, start, end, t_ref, x_ref, y1_ref, y2_ref, r_ref, t_in, c_ref, d_ref, db_ref, g_in, pooled_ref, sums_ref, late_ref, small, whole, h_hbm,
                    g_out, grads,
                    w_pin, w_proj, w_joint, w_fin, w_fout, g, gb, normed, dact, act, dh, dn, dw_pin, dw_proj, dw_joint, dw_in, dw_out, h, gp, dd, dr, dt, sm, sems):
    rows, width = g.shape
    frames = rows // utts
    mover = Mover(sems)
    gains = small[...]
    wi = mover.load_weight(whole, table["p_in"], w_pin, False)
    wp = mover.load_weight(whole, table["w_proj"], w_proj, False)
    wj = mover.load_weight(whole, table["w_joint"], w_joint, False)
    fout = mover.load_weight(whole, table["f_out"], w_fout, True)
    loads = [mover.load(h_hbm.at[b], h.at[b]) for b in range(h.shape[0])]
    fin = mover.load_weight(whole, table["f_in"], w_fin, False)
    mean = read_rows(pooled_ref, 0, width)
    count = pooled_ref[8:9, 0:1]
    istd = lax.rsqrt(read_rows(pooled_ref, 4, width) / count + EPS)
    bias_sum = read_rows(sums_ref, 0, width)
    gain_sum = read_rows(sums_ref, 4, width)
    taps = gains[5:14]
    ntaps = taps.shape[0]
    span = frames + 16
    per = frames // CHUNK_ROWS
    fill_gated(utts, frames, t_ref, r_ref, gp)
    for u in range(utts):
        dd[u * span : u * span + 8, :] = jnp.zeros((8, width), jnp.float32)
        dd[u * span + 8 + frames : (u + 1) * span, :] = jnp.zeros((8, width), jnp.float32)

    def bn(rr, i, c):
        z = (d_ref[rr, :] - mean) * istd
        v = gains[14:15] * istd * (db_ref[rr, :] - valid_rows_of(t_ref, frames, i) * (bias_sum + z * gain_sum) / count)
        at = (i // per) * span + 8 + lax.rem(i, per) * CHUNK_ROWS
        dd[pl.ds(pl.multiple_of(at, 8), CHUNK_ROWS), :] = v
        return c

    row_loop(rows, bn)

    def conv(rr, i, totals):
        dg = spread(dd, utts, frames, i, taps, True) * valid_rows_of(t_ref, frames, i)
        sg = jax.nn.sigmoid(r_ref[rr, width:])
        dr[rr, :width] = (dg * sg).astype(jnp.bfloat16)
        dr[rr, width:] = (dg * r_ref[rr, :width] * sg * (1.0 - sg)).astype(jnp.bfloat16)
        win = window(gp, frames, i)
        mine = window(dd, frames, i)[8 : 8 + CHUNK_ROWS]
        normed[rr, :] = (ln_parts(y2_ref[rr, :])[0] * gains[2:3]).astype(jnp.bfloat16)
        return tuple(
            totals[j] + fold8(win[8 - ntaps // 2 + j : 8 - ntaps // 2 + j + CHUNK_ROWS] * mine, jnp.add) for j in range(ntaps)
        )

    zero = jnp.zeros((8, width), jnp.float32)
    tap_grads = [down(x) for x in row_loop(rows, conv, (zero,) * ntaps)]
    for b in range(2):
        cols = slice(b * width, (b + 1) * width)
        dw_pin[:, cols] = tn(normed[...], dr[:, cols]).astype(jnp.bfloat16)
    mover.put_weight(dw_pin, grads, table["p_in"] - start)
    wi.wait()
    dn[...] = nt(dr[...], w_pin[...])

    def back_conv(rr, i, total):
        dv, dg = ln_back(y2_ref[rr, :], gains[2:3], dn[rr, :])
        v = g_in[rr, :] + dv
        g[rr, :] = v
        gb[rr, :] = v.astype(jnp.bfloat16)
        normed[rr, :] = (ln_parts(y1_ref[rr, :])[0] * gains[1:2]).astype(jnp.bfloat16)
        return total + dg

    gain2 = down(row_loop(rows, back_conv, zero))
    dw_proj[...] = tn(c_ref[...], gb[...]).astype(jnp.bfloat16)
    mover.put_weight(dw_proj, grads, table["w_proj"] - start)
    wp.wait()
    act[...] = nt(gb[...], w_proj[...]).astype(jnp.bfloat16)
    pairs = width // 128
    side = lax.broadcasted_iota(jnp.int32, (frames, 128), 1) < 64
    key_at = lax.broadcasted_iota(jnp.int32, (frames, 1), 0)

    def pair_step(m, carry):
        u = m // pairs
        base = lax.rem(m, pairs) * 128
        rr = pl.ds(pl.multiple_of(u * frames, frames), frames)
        at = [pl.ds(pl.multiple_of(base + b * width, 128), 128) for b in range(3)]
        bias = jnp.where(key_at < t_ref[u], 0.0, MASKED)
        q = t_in[rr, at[0]]
        k = t_in[rr, at[1]]
        v = t_in[rr, at[2]]
        dc = act[rr, at[0]]
        got = []
        for half in range(2):
            mine = side if half == 0 else ~side
            nothing = jnp.zeros_like(k)
            s = nt(jnp.where(mine, k, nothing), q) * 0.125 + bias
            p = jnp.exp(s - jnp.max(s, 0, keepdims=True))
            p = p * (1.0 / jnp.sum(p, 0, keepdims=True))
            dp = nt(jnp.where(mine, v, nothing), dc)
            ds = (p * (dp - jnp.sum(dp * p, 0, keepdims=True))).astype(jnp.bfloat16)
            got.append((tn(ds, k) * 0.125, nn(ds, q) * 0.125, nn(p.astype(jnp.bfloat16), dc)))
        for b in range(3):
            dt[rr, at[b]] = jnp.where(side, got[0][b], got[1][b]).astype(jnp.bfloat16)
        return carry

    lax.fori_loop(0, utts * pairs, pair_step, 0)
    for b in range(3):
        cols = slice(b * width, (b + 1) * width)
        dw_joint[:, cols] = tn(normed[...], dt[:, cols]).astype(jnp.bfloat16)
    mover.put_weight(dw_joint, grads, table["w_joint"] - start)
    wj.wait()
    dn[...] = nt(dt[...], w_joint[...])

    def back_attend(rr, i, total):
        dv, dg = ln_back(y1_ref[rr, :], gains[1:2], dn[rr, :])
        g[rr, :] = g[rr, :] + dv
        return total + dg

    gain1 = down(row_loop(rows, back_attend, zero))
    gain0 = down(ffn_bwd(rows, x_ref, gains[0:1], (w_fin, fin), (w_fout, fout), h, loads, g, gb, normed, dact, act, dh, dn,
                         dw_in, dw_out, mover, grads, table["f_in"] - start, table["f_out"] - start))
    mover.put(g, g_out)
    packed = jnp.concatenate([gain0, gain1, gain2, late_ref[0:2, :]] + tap_grads + [jnp.zeros((2, width), jnp.float32)], 0)
    n = grads.shape[0]
    low = width // n
    for s in range(n):
        sm[s] = jnp.concatenate([packed[:, s * low : (s + 1) * low], jnp.zeros((16, WIDE - low), jnp.float32)], 1).astype(jnp.bfloat16)
    mover.put(sm, grads.at[:, pl.ds(end - start, 16), :])
    mover.finish()


VMEM_SPEC = pl.BlockSpec(memory_space=pltpu.VMEM)
SMEM_SPEC = pl.BlockSpec(memory_space=pltpu.SMEM)
ANY_SPEC = pl.BlockSpec(memory_space=pl.ANY)
F32 = jnp.float32
BF16 = jnp.bfloat16


def sds(shape, dtype=jnp.float32):
    return jax.ShapeDtypeStruct(shape, dtype)


def part_one(t_len, x, small, whole, ff):
    rows, width = x.shape
    utts = t_len.shape[0]
    table, _ = offsets(whole.shape[0], width, ff)
    nb = ff // WIDE
    v = pltpu.VMEM
    return pl.pallas_call(
        partial(part_one_kernel, utts, table),
        in_specs=[SMEM_SPEC, VMEM_SPEC, VMEM_SPEC, ANY_SPEC],
        out_specs=[ANY_SPEC] * 7 + [VMEM_SPEC],
        out_shape=[sds((rows, width)), sds((nb, rows, WIDE)), sds((rows, width)), sds((rows, 3 * width), BF16),
                   sds((rows, width), BF16), sds((rows, 2 * width)), sds((rows, width)), sds((16, 128))],
        scratch_shapes=[v((width, ff), BF16), v((ff, width), BF16), v((width, 3 * width), BF16), v((width, width), BF16),
                        v((width, 2 * width), BF16), v((rows, width), F32), v((rows, width), F32), v((rows, width), BF16),
                        v((nb, rows, WIDE), F32), v((rows, ff), BF16), v((rows, 3 * width), BF16), v((rows, width), BF16),
                        v((rows, 2 * width), F32), v((utts * (rows // utts + 16), width), F32), v((rows, width), F32),
                        pltpu.SemaphoreType.DMA((24,))],
        compiler_params=pltpu.CompilerParams(vmem_limit_bytes=56 << 20),
        name="layer_part_one",
    )(t_len, x, small, whole)


def part_two(d, y2, pooled, small, whole, ff):
    rows, width = d.shape
    table, _ = offsets(whole.shape[0], width, ff)
    nb = ff // WIDE
    v = pltpu.VMEM
    return pl.pallas_call(
        partial(part_two_kernel, table),
        in_specs=[VMEM_SPEC] * 4 + [ANY_SPEC],
        out_specs=[ANY_SPEC] * 4,
        out_shape=[sds((rows, width)), sds((nb, rows, WIDE)), sds((rows, width)), sds((rows, width))],
        scratch_shapes=[v((width, width), BF16), v((width, ff), BF16), v((ff, width), BF16), v((rows, width), BF16),
                        v((rows, width), F32), v((rows, width), BF16), v((nb, rows, WIDE), F32), v((rows, ff), BF16),
                        v((rows, width), F32), v((rows, width), F32), pltpu.SemaphoreType.DMA((16,))],
        compiler_params=pltpu.CompilerParams(vmem_limit_bytes=56 << 20),
        name="layer_part_two",
    )(d, y2, pooled, small, whole)


def tiled(count):
    return -(-count // TILE) * TILE


def back_one(grad, y4, y3, d, pooled, small, whole, h, ff):
    rows, width = grad.shape
    n = whole.shape[0]
    table, _ = offsets(n, width, ff)
    nb = ff // WIDE
    v = pltpu.VMEM
    return pl.pallas_call(
        partial(back_one_kernel, table),
        in_specs=[VMEM_SPEC] * 6 + [ANY_SPEC] * 2,
        out_specs=[ANY_SPEC] * 3 + [VMEM_SPEC] * 2,
        out_shape=[sds((rows, width)), sds((rows, width)), sds((n, tiled(table["p_in"]), WIDE), BF16), sds((16, 128)), sds((8, width))],
        scratch_shapes=[v((width, width), BF16), v((width, ff), BF16), v((ff, width), BF16), v((rows, width), F32),
                        v((rows, width), BF16), v((rows, width), BF16), v((rows, width), F32), v((rows, width), BF16),
                        v((rows, ff), BF16), v((rows, width), F32), v((width, ff), BF16), v((ff, width), BF16),
                        v((width, width), BF16), v((nb, rows, WIDE), F32), v((rows, width), F32), pltpu.SemaphoreType.DMA((16,))],
        compiler_params=pltpu.CompilerParams(vmem_limit_bytes=56 << 20),
        name="back_part_one",
    )(grad, y4, y3, d, pooled, small, whole, h)


def back_two(t_len, x, y1, y2, r, t, c, d, db, g, pooled, sums, late, small, whole, h, ff):
    rows, width = d.shape
    utts = t_len.shape[0]
    n = whole.shape[0]
    table, end = offsets(n, width, ff)
    start = table["p_in"]
    nb = ff // WIDE
    v = pltpu.VMEM
    pad_rows = utts * (rows // utts + 16)
    return pl.pallas_call(
        partial(back_two_kernel, utts, table, start, end),
        in_specs=[SMEM_SPEC] + [VMEM_SPEC] * 13 + [ANY_SPEC] * 2,
        out_specs=[ANY_SPEC] * 2,
        out_shape=[sds((rows, width)), sds((n, tiled(end - start + 16), WIDE), BF16)],
        scratch_shapes=[v((width, 2 * width), BF16), v((width, width), BF16), v((width, 3 * width), BF16), v((width, ff), BF16),
                        v((ff, width), BF16), v((rows, width), F32), v((rows, width), BF16), v((rows, width), BF16),
                        v((rows, width), F32), v((rows, width), BF16), v((rows, ff), BF16), v((rows, width), F32),
                        v((width, 2 * width), BF16), v((width, width), BF16), v((width, 3 * width), BF16), v((width, ff), BF16),
                        v((ff, width), BF16), v((nb, rows, WIDE), F32), v((pad_rows, width), F32), v((pad_rows, width), F32),
                        v((rows, 2 * width), BF16), v((rows, 3 * width), BF16), v((n, 16, WIDE), BF16), pltpu.SemaphoreType.DMA((20,))],
        compiler_params=pltpu.CompilerParams(vmem_limit_bytes=60 << 20),
        name="back_part_two",
    )(t_len, x, y1, y2, r, t, c, d, db, g, pooled, sums, late, small, whole, h)


def lift(rows):
    return -(-rows // 16) * 16


def joint_sizes(w_enc, w_pred, w_tok):
    low, tall = lift(w_enc.shape[0]), lift(w_pred.shape[0])
    return [low, tall, tall * (w_tok.shape[1] // WIDE), tall]


def pack_kernel(layers, table, end, *refs):
    names = PLACE + ("gains", "taps", "bn_gain", "bn_bias", "enc", "pred", "tok", "dur")
    src = dict(zip(names, refs))
    outs = refs[len(names) :]
    for layer in range(layers):
        out = outs[layer]
        for name in PLACE:
            ref = src[name]
            height = ref.shape[1]
            for b in range(ref.shape[2] // WIDE):
                at = table[name] + b * height
                out[at : at + height, :] = ref[layer, :, b * WIDE : (b + 1) * WIDE]
        small = [src["gains"][layer], src["taps"][layer], src["bn_gain"][layer : layer + 1, :], src["bn_bias"][layer : layer + 1, :]]
        small = jnp.concatenate([x.astype(jnp.float32) for x in small], 0)
        small = jnp.concatenate([small, jnp.zeros((16, WIDE - small.shape[1]), jnp.float32)], 1)
        out[end : end + 16, :] = small.astype(jnp.bfloat16)
        if out.shape[0] > end + 16:
            out[end + 16 :, :] = jnp.zeros((out.shape[0] - end - 16, WIDE), jnp.bfloat16)
    out = outs[layers - 1]
    enc, pred, tok, dur = src["enc"], src["pred"], src["tok"], src["dur"]
    low, tall = enc.shape[0], pred.shape[0]
    at = end + 16
    out[at : at + low, :] = enc[:, :WIDE]
    at += lift(low)
    out[at : at + tall, :] = pred[:, :WIDE]
    at += lift(tall)
    for b in range(tok.shape[1] // WIDE):
        out[at : at + tall, :] = tok[:, b * WIDE : (b + 1) * WIDE]
        at += lift(tall)
    out[at : at + low, 0:128] = enc[:, WIDE:]
    out[at : at + tall, 128:256] = pred[:, WIDE:]
    dur = dur[...].astype(jnp.float32)
    out[at : at + tall, 256:384] = jnp.concatenate([dur, jnp.zeros((tall, 128 - dur.shape[1]), jnp.float32)], 1).astype(jnp.bfloat16)


def pack(layers, table, end, extra, arrays):
    shapes = []
    for layer in range(layers):
        count = end + 16 + (extra if layer == layers - 1 else 0)
        shapes.append(sds((tiled(count), WIDE), BF16))
    return pl.pallas_call(
        partial(pack_kernel, layers, table, end),
        in_specs=[VMEM_SPEC] * len(arrays),
        out_specs=[VMEM_SPEC] * layers,
        out_shape=shapes,
        compiler_params=pltpu.CompilerParams(vmem_limit_bytes=48 << 20),
        name="pack_weights",
    )(*arrays)


def unpack_kernel(layers, table, end, dims, share, gains, f_in, f_out, w_joint, w_proj, p_in, taps, p_out, s_in, s_out, enc, pred, tok, dur):
    outs = {"f_in": f_in, "f_out": f_out, "w_joint": w_joint, "w_proj": w_proj, "p_in": p_in, "p_out": p_out, "s_in": s_in, "s_out": s_out}
    starts, width, joint = dims
    shard = gains.shape[2]
    for layer in range(layers):
        for name in PLACE:
            out = outs[name]
            height = out.shape[1]
            early = table[name] < table["p_in"]
            base = starts[layer][0] + table[name] if early else starts[layer][1] + table[name] - table["p_in"]
            for b in range(out.shape[2] // WIDE):
                out[layer, :, b * WIDE : (b + 1) * WIDE] = share[base + b * height : base + (b + 1) * height, :].astype(jnp.float32)
        base = starts[layer][1] + end - table["p_in"]
        small = share[base : base + 16, 0:128].astype(jnp.float32)
        gains[layer] = small[0:5, :shard]
        taps[layer] = small[5 : 5 + taps.shape[1], :shard]
    at = starts[layers]
    low, tall = enc.shape[0], pred.shape[0]
    enc[:, :WIDE] = share[at : at + low, :].astype(jnp.float32)
    at += lift(low)
    pred[:, :WIDE] = share[at : at + tall, :].astype(jnp.float32)
    at += lift(tall)
    for b in range(tok.shape[1] // WIDE):
        tok[:, b * WIDE : (b + 1) * WIDE] = share[at : at + tall, :].astype(jnp.float32)
        at += lift(tall)
    enc[:, WIDE:] = share[at : at + low, 0:128].astype(jnp.float32)
    pred[:, WIDE:] = share[at : at + tall, 128:256].astype(jnp.float32)
    dur[...] = share[at : at + tall, 256:384].astype(jnp.float32)[:, : dur.shape[1]]


def unpack(layers, table, end, dims, share, like):
    return pl.pallas_call(
        partial(unpack_kernel, layers, table, end, dims),
        in_specs=[VMEM_SPEC],
        out_specs=[VMEM_SPEC] * len(like),
        out_shape=[sds(x.shape) for x in like],
        compiler_params=pltpu.CompilerParams(vmem_limit_bytes=48 << 20),
        name="unpack_grads",
    )(share)


def cut(whole, sizes, offset=0):
    parts = []
    for size in sizes:
        parts.append(whole[..., offset : offset + size, :])
        offset += size
    return parts


def from_blocks(part, cols, rows):
    n, height, _ = part.shape
    blocks = cols // WIDE
    return jnp.swapaxes(part.reshape(n, blocks, height // blocks, WIDE)[:, :, :rows], 1, 2).reshape(-1, cols)


def unpack_joint(whole, first, sizes, w_enc, w_pred, vocab):
    enc, pred, tok, rest = cut(whole, sizes, first)
    joint = w_enc.shape[1]
    low = w_enc.shape[0]
    tall = w_pred.shape[0]
    w_enc = jnp.concatenate([enc[:, :low], rest[:, :low, : joint - WIDE]], 2).reshape(-1, joint)
    w_pred = jnp.concatenate([pred[:, :tall], rest[:, :tall, 128 : 128 + joint - WIDE]], 2).reshape(-1, joint)
    return w_enc, w_pred, from_blocks(tok, vocab, tall), rest[:, :tall, 256:384].reshape(-1, 128)


def grow(part):
    short = lift(part.shape[1]) - part.shape[1]
    return jnp.pad(part, ((0, 0), (0, short), (0, 0))) if short else part


def pack_joint_grads(g_enc, g_pred, g_tok, g_dur, n):
    def shards(grad):
        return grow(grad.astype(jnp.bfloat16).reshape(n, -1, grad.shape[1]))
    g_enc, g_pred, g_tok, g_dur = shards(g_enc), shards(g_pred), shards(g_tok), shards(g_dur)
    tall = g_pred.shape[1]
    rest = jnp.concatenate(
        [
            jnp.pad(g_enc[:, :, WIDE:], ((0, 0), (0, tall - g_enc.shape[1]), (0, 0))),
            g_pred[:, :, WIDE:],
            g_dur,
            jnp.zeros((n, tall, 128), jnp.bfloat16),
        ],
        2,
    )
    parts = [g_enc[:, :, :WIDE], g_pred[:, :, :WIDE]]
    parts += [g_tok[:, :, b : b + WIDE] for b in range(0, g_tok.shape[2], WIDE)] + [rest]
    rows = sum(p.shape[1] for p in parts)
    return jnp.concatenate(parts + [jnp.zeros((n, tiled(rows) - rows, WIDE), jnp.bfloat16)], 1)


def matmul(left, right):
    return jnp.dot(left, right, preferred_element_type=jnp.float32)


def contract_rows(left, right):
    return lax.dot_general(
        left, right, (((0,), (0,)), ((), ())), preferred_element_type=jnp.float32
    )


def contract_cols(left, right):
    return lax.dot_general(
        left, right, (((1,), (1,)), ((), ())), preferred_element_type=jnp.float32
    )


def local(
    frames_in,
    frame_lengths,
    label_ids,
    label_lengths,
    pred_states,
    norm_gains,
    first_in,
    first_out,
    attend_joint,
    attend_out,
    point_in,
    depth_taps,
    batch_gain,
    batch_bias,
    point_out,
    second_in,
    second_out,
    enc_weight,
    pred_weight,
    token_weight,
    duration_weight,
):
    utts, frames, width = frames_in.shape
    slots = pred_states.shape[1]
    rows = utts * frames
    layers = norm_gains.shape[0]
    n = lax.axis_size("fsdp")
    ff = first_in.shape[2]
    mats = {
        "f_in": first_in, "f_out": first_out, "w_joint": attend_joint, "w_proj": attend_out,
        "p_in": point_in, "p_out": point_out, "s_in": second_in, "s_out": second_out,
    }
    table, end = offsets(n, width, ff)
    shard = width // n
    sizes = joint_sizes(enc_weight, pred_weight, token_weight)
    vocab = token_weight.shape[1]
    packs = pack(
        layers,
        table,
        end,
        sum(sizes),
        [mats[name] for name in PLACE]
        + [norm_gains, depth_taps, batch_gain, batch_bias, enc_weight, pred_weight, token_weight, duration_weight],
    )
    wholes = []
    smalls = []
    for layer in range(layers):
        whole = gather(packs[layer], 1 + layer)
        small = whole[:, end : end + 16, :shard].astype(jnp.float32)
        wholes.append(whole)
        smalls.append(jnp.swapaxes(small, 0, 1).reshape(16, width))
    resid = frames_in.reshape(rows, width)
    records = []
    for layer in range(layers):
        y1, h1, y2, qkv, ctx, gates, depthwise, stats = part_one(frame_lengths, resid, smalls[layer], wholes[layer], ff)
        pooled = exchange(stats, "pool", 8 + layer)
        y3, h2, y4, result = part_two(depthwise, y2, pooled, smalls[layer], wholes[layer], ff)
        records.append((resid, y1, h1, y2, qkv, ctx, gates, depthwise, pooled, y3, h2, y4))
        resid = result
    w_enc, w_pred, w_tok, w_dur = unpack_joint(wholes[-1], end + 16, sizes, enc_weight, pred_weight, vocab)
    joint = w_enc.shape[1]
    vocab = w_tok.shape[1]
    out_low = resid.astype(jnp.bfloat16)
    enc = matmul(out_low, w_enc)
    pred_low = pred_states.reshape(utts * slots, joint)
    pred = matmul(pred_low, w_pred).reshape(utts, slots, joint)
    groups = slots // GROUP
    durs = duration_weight.shape[1]
    pred_t = jnp.pad(
        jnp.swapaxes(pred.reshape(utts * groups, GROUP, joint), 1, 2),
        ((0, 0), (0, 0), (0, 8 - GROUP)),
    )
    w_cat = jnp.concatenate([w_tok, w_dur], 1)
    enc_t = enc.T
    labels_ext = jnp.concatenate([label_ids, jnp.zeros((utts, 1), jnp.int32)], 1)
    feats, expd = joint_forward(enc_t, pred_t, labels_ext, w_cat.T, vocab, durs, frames)
    lat_grads, scores = lattice(feats[: 2 + durs], frame_lengths, label_lengths, slots)
    log_prob = scores[:utts, 0]
    utt_loss = -log_prob / frame_lengths.astype(jnp.float32)
    grad_enc_t, grad_pred_t, grad_tok, grad_dur_w = joint_backward(
        enc_t, pred_t, labels_ext, w_cat, feats, lat_grads, expd, vocab, durs, frames
    )
    grad_pred_rows = jnp.swapaxes(grad_pred_t[:, :, :GROUP], 1, 2)
    grad_enc_low = grad_enc_t.T.astype(jnp.bfloat16)
    grad_w_enc = contract_rows(out_low, grad_enc_low)
    grad = contract_cols(grad_enc_low, w_enc)
    grad_w_pred = contract_rows(
        pred_low, grad_pred_rows.reshape(utts * slots, joint).astype(jnp.bfloat16)
    )
    sources = [pack_joint_grads(grad_w_enc, grad_w_pred, grad_tok, grad_dur_w, n)]
    bn_grads = [None] * layers
    for layer in reversed(range(layers)):
        x0, y1, h1, y2, qkv, ctx, gates, depthwise, pooled, y3, h2, y4 = records[layer]
        g3, db, grads_one, sums, late_gains = back_one(grad, y4, y3, depthwise, pooled, smalls[layer], wholes[layer], h2, ff)
        sums = exchange(sums, "sum", 12 + layer)
        grad, grads_two = back_two(
            frame_lengths, x0, y1, y2, gates, qkv, ctx, depthwise, db, g3, pooled, sums, late_gains, smalls[layer], wholes[layer], h1, ff
        )
        sources += [grads_one, grads_two]
        bn_grads[layer] = (sums[4:8].reshape(width), sums[0:4].reshape(width))
    share = scatter(sources, 4)
    starts = [None] * layers + [0]
    at = sources[0].shape[1]
    for place, layer in enumerate(reversed(range(layers))):
        one, two = sources[1 + 2 * place], sources[2 + 2 * place]
        starts[layer] = (at, at + one.shape[1])
        at += one.shape[1] + two.shape[1]
    grads = unpack(
        layers,
        table,
        end,
        (starts, width, joint),
        share,
        [norm_gains, first_in, first_out, attend_joint, attend_out, point_in, depth_taps, point_out, second_in, second_out,
         enc_weight, pred_weight, token_weight, duration_weight],
    )
    offset = lax.axis_index("fsdp") * shard
    gain_piece = lax.dynamic_slice_in_dim(jnp.stack([g[0] for g in bn_grads]), offset, shard, 1)
    bias_piece = lax.dynamic_slice_in_dim(jnp.stack([g[1] for g in bn_grads]), offset, shard, 1)
    return (
        utt_loss,
        grad.reshape(utts, frames, width),
        *grads[:7],
        gain_piece,
        bias_piece,
        *grads[7:],
    )


def solution(mesh):
    set_tile(mesh.shape["fsdp"])
    placed = (
        P(("dp", "fsdp"), None, None),
        P(("dp", "fsdp")),
        P(("dp", "fsdp"), None),
        P(("dp", "fsdp")),
        P(("dp", "fsdp"), None, None),
        P(None, None, "fsdp"),
        P(None, "fsdp", None),
        P(None, "fsdp", None),
        P(None, "fsdp", None),
        P(None, "fsdp", None),
        P(None, "fsdp", None),
        P(None, None, "fsdp"),
        P(None, "fsdp"),
        P(None, "fsdp"),
        P(None, "fsdp", None),
        P(None, "fsdp", None),
        P(None, "fsdp", None),
        P("fsdp", None),
        P("fsdp", None),
        P("fsdp", None),
        P("fsdp", None),
    )
    return jax.shard_map(
        local,
        mesh=mesh,
        in_specs=placed,
        out_specs=(
            P(("dp", "fsdp")),
            P(("dp", "fsdp"), None, None),
            P(None, None, "fsdp"),
            P(None, "fsdp", None),
            P(None, "fsdp", None),
            P(None, "fsdp", None),
            P(None, "fsdp", None),
            P(None, "fsdp", None),
            P(None, None, "fsdp"),
            P(None, "fsdp"),
            P(None, "fsdp"),
            P(None, "fsdp", None),
            P(None, "fsdp", None),
            P(None, "fsdp", None),
            P("fsdp", None),
            P("fsdp", None),
            P("fsdp", None),
            P("fsdp", None),
        ),
        check_vma=False,
    )
```

```python
from functools import partial, reduce

import jax
import jax.numpy as jnp
from jax import lax
from jax.experimental import pallas as pl
from jax.experimental.pallas import tpu as pltpu
from jax.sharding import PartitionSpec as P

HEADS = 8


EPS = 1e-05
MASKED = -1000000000.0
NEG = -1e30


def lattice_kernel(slots, feats_ref, tlen_ref, ulen_ref, grads_ref, prob_ref, s_ref, l_ref, ls_ref, a_ref, b_ref, init_ref):
    utts = tlen_ref.shape[0]
    frames = feats_ref.shape[2]
    rows = feats_ref.shape[1]
    wide = frames + 128
    reach = feats_ref.shape[0] - 3
    diags = frames + slots
    pad = 8
    total = a_ref.shape[0]
    body = wide

    def skew(x, sign):
        k = lax.broadcasted_iota(jnp.int32, x.shape, 0) % 32
        for bit in range(5):
            step = 1 << bit
            x = jnp.where((k // step) % 2 == 1, pltpu.roll(x, step if sign > 0 else wide - step, 1), x)
        return x

    def to_diag(x):
        x = jnp.concatenate([x, jnp.zeros((rows, 128), jnp.float32)], 1)
        x = skew(x, 1)
        x = jnp.concatenate([x, jnp.zeros((128 - rows, wide), jnp.float32)], 0)
        return x.T

    lane = lax.broadcasted_iota(jnp.int32, (wide, 128), 1)
    diag = lax.broadcasted_iota(jnp.int32, (wide, 128), 0)
    k_of = lane % 32
    t_of = diag - k_of
    t_len = jnp.full((wide, 128), -1, jnp.int32)
    u_len = jnp.full((wide, 128), -1, jnp.int32)
    for u in range(utts):
        mine = (lane // 32) == u
        t_len = jnp.where(mine, tlen_ref[u], t_len)
        u_len = jnp.where(mine, ulen_ref[u], u_len)
    blank = to_diag(feats_ref[0])
    label = to_diag(feats_ref[1])
    edge = jnp.full((pad, 128), NEG, jnp.float32)
    real = (t_of >= 0)
    for ref in (s_ref, l_ref, ls_ref):
        for e in range(ref.shape[0]):
            ref[e, 0:pad, :] = edge
            ref[e, pad + wide:, :] = jnp.full((ref.shape[1] - pad - wide, 128), NEG, jnp.float32)
    for e in range(reach + 1):
        dur = to_diag(feats_ref[2 + e])
        if e > 0:
            keep = real & (k_of <= u_len) & ((t_of + e < t_len) | ((t_of + e == t_len) & (k_of == u_len)))
            s_ref[e - 1, pad:pad + wide, :] = jnp.where(keep, blank + dur, NEG)
        keep = real & (k_of < u_len) & (t_of + e < t_len)
        lab = jnp.where(keep, label + dur, NEG)
        l_ref[e, pad:pad + wide, :] = lab
        ls_ref[e, pad:pad + wide, :] = pltpu.roll(lab, 1, 1)
    init_ref[pad:pad + wide, :] = jnp.where((t_of == t_len) & (k_of == u_len), 0.0, NEG)
    a_ref[...] = jnp.full(a_ref.shape, NEG, jnp.float32)
    b_ref[...] = jnp.full(b_ref.shape, NEG, jnp.float32)

    first = jnp.where((lax.broadcasted_iota(jnp.int32, (1, 128), 1) % 32 == 0)
                      & (lax.broadcasted_iota(jnp.int32, (1, 128), 1) < 32 * utts), 0.0, NEG)

    def lse(terms):
        tops = list(terms)
        while len(tops) > 1:
            tops = [jnp.maximum(tops[i], tops[i + 1]) if i + 1 < len(tops) else tops[i] for i in range(0, len(tops), 2)]
        top = tops[0]
        parts = [jnp.exp(x - top) for x in terms]
        while len(parts) > 1:
            parts = [parts[i] + parts[i + 1] if i + 1 < len(parts) else parts[i] for i in range(0, len(parts), 2)]
        return jnp.maximum(top + jnp.log(parts[0]), NEG)

    a_ref[pl.ds(pad, 1), :] = first
    last = diags

    def step(i, carry):
        ha, hra, hb, hrb = carry
        row = pad + i
        terms = [ha[e - 1] + s_ref[e - 1, pl.ds(row - e, 1), :] for e in range(1, reach + 1)]
        terms += [hra[e] + ls_ref[e, pl.ds(row - e - 1, 1), :] for e in range(reach + 1)]
        a = lse(terms[::-1])
        a_ref[pl.ds(row, 1), :] = a
        ra = pltpu.roll(a, 1, 1)
        rowb = pad + last - i
        terms = [hb[e - 1] + s_ref[e - 1, pl.ds(rowb, 1), :] for e in range(1, reach + 1)]
        terms += [hrb[e] + l_ref[e, pl.ds(rowb, 1), :] for e in range(reach + 1)]
        b = jnp.maximum(lse(terms[::-1]), init_ref[pl.ds(rowb, 1), :])
        b_ref[pl.ds(rowb, 1), :] = b
        rb = pltpu.roll(b, 127, 1)
        return ((a,) + ha[:-1], (ra,) + hra[:-1], (b,) + hb[:-1], (rb,) + hrb[:-1])

    b0 = init_ref[pl.ds(pad + last, 1), :]
    b_ref[pl.ds(pad + last, 1), :] = b0
    none = a_ref[pl.ds(0, 1), :]
    first = a_ref[pl.ds(pad, 1), :]
    ha = (first,) + (none,) * (reach - 1)
    hra = (pltpu.roll(first, 1, 1),) + (none,) * reach
    hb = (b0,) + (none,) * (reach - 1)
    hrb = (pltpu.roll(b0, 127, 1),) + (none,) * reach
    lax.fori_loop(1, last + 1, step, (ha, hra, hb, hrb))

    zrow = b_ref[pl.ds(pad, 1), :]
    lane1 = lax.broadcasted_iota(jnp.int32, (1, 128), 1)
    z = jnp.zeros((1, 128), jnp.float32)
    for u in range(utts):
        zu = jnp.max(jnp.where(lane1 == 32 * u, zrow, 2 * NEG), axis=1, keepdims=True)
        z = jnp.where(lane1 // 32 == u, zu, z)
        prob_ref[pl.ds(u, 1), :] = jnp.broadcast_to(zu, (1, 128))

    def from_diag(x):
        x = x.T[:rows]
        return skew(x, -1)[:, :frames]

    a = a_ref[pad:pad + wide, :] - z
    g_blank = jnp.zeros((wide, 128), jnp.float32)
    g_label = jnp.zeros((wide, 128), jnp.float32)
    for e in range(reach + 1):
        bb = b_ref[pad + e + 1: pad + e + 1 + wide, :]
        pl_ = jnp.exp(a + l_ref[e, pad:pad + wide, :] + pltpu.roll(bb, 127, 1))
        g_label = g_label - pl_
        g = -pl_
        if e > 0:
            ps = jnp.exp(a + s_ref[e - 1, pad:pad + wide, :] + b_ref[pad + e: pad + e + wide, :])
            g_blank = g_blank - ps
            g = g - ps
        grads_ref[2 + e] = from_diag(g)
    grads_ref[0] = from_diag(g_blank)
    grads_ref[1] = from_diag(g_label)


def lattice(feats, t_len, u_len, slots):
    _, rows, frames = feats.shape
    wide = frames + 128
    total = wide + 16
    reach = feats.shape[0] - 3
    return pl.pallas_call(
        partial(lattice_kernel, slots),
        out_shape=(jax.ShapeDtypeStruct(feats.shape, jnp.float32), jax.ShapeDtypeStruct((8, 128), jnp.float32)),
        in_specs=[pl.BlockSpec(memory_space=pltpu.VMEM), pl.BlockSpec(memory_space=pltpu.SMEM), pl.BlockSpec(memory_space=pltpu.SMEM)],
        out_specs=(pl.BlockSpec(memory_space=pltpu.VMEM),) * 2,
        scratch_shapes=[pltpu.VMEM((reach, total, 128), jnp.float32), pltpu.VMEM((reach + 1, total, 128), jnp.float32),
                        pltpu.VMEM((reach + 1, total, 128), jnp.float32), pltpu.VMEM((total, 128), jnp.float32),
                        pltpu.VMEM((total, 128), jnp.float32), pltpu.VMEM((total, 128), jnp.float32)],
        compiler_params=pltpu.CompilerParams(vmem_limit_bytes=48 << 20),
        name="lattice",
    )(feats, t_len, u_len)


GROUP=5
CHUNK=256

def nn(a,b): return jnp.dot(a,b,preferred_element_type=jnp.float32)
def nt(a,b): return lax.dot_general(a,b,(((1,),(1,)),((),())),preferred_element_type=jnp.float32)

def fold8(x, op):
    parts=[x[i:i+8] for i in range(0,x.shape[0],8)]
    while len(parts)>1:
        parts=[op(parts[i],parts[i+1]) if i+1<len(parts) else parts[i] for i in range(0,len(parts),2)]
    return parts[0]

def joint_fwd_kernel(groups, durs, labels_ref, enc_ref, pred_ref, wt_ref, feats_ref, p_ref, tok_ref):
    step=pl.program_id(0)
    vocab=p_ref.shape[2]
    u=step//groups
    g=step%groups
    for j in range(GROUP):
        k=g*GROUP+j
        hid=jnp.tanh(enc_ref[...]+pred_ref[0,:,j:j+1]).astype(jnp.bfloat16)
        tops=[]
        for c in range(0,vocab,CHUNK):
            t=nn(wt_ref[c:c+CHUNK,:],hid)
            tok_ref[j%2,c:c+CHUNK,:]=t
            tops.append(fold8(t,jnp.maximum))
        dl=nn(wt_ref[vocab:,:],hid)[:8]
        top=jnp.max(reduce(jnp.maximum,tops),0,keepdims=True)
        sums=[]
        for c in range(0,vocab,CHUNK):
            e=jnp.exp(tok_ref[j%2,c:c+CHUNK,:]-top)
            p_ref[0,j,c:c+CHUNK,:]=e.astype(jnp.bfloat16)
            sums.append(fold8(e,jnp.add))
        total=jnp.sum(reduce(jnp.add,sums),0,keepdims=True)
        lse=top+jnp.log(total)
        row=u*32+k
        feats_ref[0,pl.ds(row,1),:]=tok_ref[j%2,0:1,:]-lse
        feats_ref[1,pl.ds(row,1),:]=tok_ref[j%2,pl.ds(labels_ref[u,k],1),:]-lse
        real=lax.broadcasted_iota(jnp.int32,dl.shape,0)<durs
        dtop=jnp.max(jnp.where(real,dl,-1e30),0,keepdims=True)
        dlse=dtop+jnp.log(jnp.sum(jnp.where(real,jnp.exp(dl-dtop),0.0),0,keepdims=True))
        dlp=dl-dlse
        for e in range(durs):
            feats_ref[2+e,pl.ds(row,1),:]=dlp[e:e+1]
        feats_ref[2+durs,pl.ds(row,1),:]=1.0/total

def joint_forward(enc_t, pred_t, labels, w_t, vocab, durs, frames):
    joint, rows=enc_t.shape
    utts,slots=labels.shape
    groups=slots//GROUP
    return pl.pallas_call(
        partial(joint_fwd_kernel,groups,durs),
        grid=(utts*groups,),
        in_specs=[pl.BlockSpec(memory_space=pltpu.SMEM),
            pl.BlockSpec((joint,frames),lambda s:(0,s//groups)),
            pl.BlockSpec((1,joint,8),lambda s:(s,0,0)),
            pl.BlockSpec(w_t.shape,lambda s:(0,0))],
        out_specs=[pl.BlockSpec((3+durs,utts*32,frames),lambda s:(0,0,0)),
            pl.BlockSpec((1,GROUP,vocab,frames),lambda s:(s,0,0,0))],
        out_shape=[jax.ShapeDtypeStruct((3+durs,utts*32,frames),jnp.float32),
            jax.ShapeDtypeStruct((utts*groups,GROUP,vocab,frames),jnp.bfloat16)],
        scratch_shapes=[pltpu.VMEM((2,vocab,frames),jnp.float32)],
        compiler_params=pltpu.CompilerParams(vmem_limit_bytes=50<<20),
        name="joint_forward",
    )(labels,enc_t,pred_t,w_t)

def joint_bwd_kernel(groups, durs, labels_ref, enc_ref, pred_ref, w_ref, feats_ref, grads_ref, p_ref, genc_ref, gpred_ref, gtok_ref, gdur_ref, h_ref, d_ref, acc_ref):
    step=pl.program_id(0)
    vocab=p_ref.shape[2]
    frames=p_ref.shape[3]
    u=step//groups
    g=step%groups

    @pl.when(step==0)
    def _():
        acc_ref[...]=jnp.zeros_like(acc_ref)
    @pl.when(g==0)
    def _():
        genc_ref[...]=jnp.zeros_like(genc_ref)
    for j in range(GROUP):
        k=g*GROUP+j
        row=u*32+k
        cols=slice(j*frames,(j+1)*frames)
        th=jnp.tanh(enc_ref[...]+pred_ref[0,:,j:j+1])
        h_ref[:,cols]=th.astype(jnp.bfloat16)
        gb=grads_ref[0,pl.ds(row,1),:]
        gl=grads_ref[1,pl.ds(row,1),:]
        scale=-(gb+gl)*feats_ref[2+durs,pl.ds(row,1),:]
        for c in range(0,vocab,CHUNK):
            d_ref[c:c+CHUNK,cols]=(p_ref[0,j,c:c+CHUNK,:].astype(jnp.float32)*scale).astype(jnp.bfloat16)
        label=labels_ref[u,k]
        def fix(base):
            v=p_ref[0,j,pl.ds(base,16),:].astype(jnp.float32)*scale
            at=lax.broadcasted_iota(jnp.int32,v.shape,0)+base
            v=v+jnp.where(at==0,gb,0.0)+jnp.where(at==label,gl,0.0)
            d_ref[pl.ds(base,16),cols]=v.astype(jnp.bfloat16)
        fix(0)
        fix(pl.multiple_of((label//16)*16,16))
        gd=[grads_ref[2+e,pl.ds(row,1),:] for e in range(durs)]
        gsum=reduce(jnp.add,gd)
        at=lax.broadcasted_iota(jnp.int32,(16,frames),0)
        dd=jnp.zeros((16,frames),jnp.float32)
        for e in range(durs):
            dd=jnp.where(at==e,gd[e]-gsum*jnp.exp(feats_ref[2+e,pl.ds(row,1),:]),dd)
        d_ref[vocab:vocab+16,cols]=dd.astype(jnp.bfloat16)
        d_ref[vocab+16:,cols]=jnp.zeros((d_ref.shape[0]-vocab-16,frames),jnp.bfloat16)
        dh=nn(w_ref[...],d_ref[:,cols])
        th=jnp.tanh(enc_ref[...]+pred_ref[0,:,j:j+1])
        dp=dh*(1.0-th*th)
        genc_ref[...]+=dp
        gpred_ref[0,:,j:j+1]=jnp.sum(dp,1,keepdims=True)
    for c in range(0,d_ref.shape[0],384):
        acc_ref[:,c:c+384]+=nt(h_ref[...],d_ref[c:c+384,:])
    @pl.when(step==pl.num_programs(0)-1)
    def _():
        gtok_ref[...]=acc_ref[:,:vocab].astype(jnp.bfloat16)
        gdur_ref[...]=acc_ref[:,vocab:].astype(jnp.bfloat16)

def joint_backward(enc_t, pred_t, labels, w, feats, grads, p, vocab, durs, frames):
    joint, rows=enc_t.shape
    utts,slots=labels.shape
    groups=slots//GROUP
    full=lambda a: pl.BlockSpec(a.shape,lambda s:(0,)*a.ndim)
    return pl.pallas_call(
        partial(joint_bwd_kernel,groups,durs),
        grid=(utts*groups,),
        in_specs=[pl.BlockSpec(memory_space=pltpu.SMEM),
            pl.BlockSpec((joint,frames),lambda s:(0,s//groups)),
            pl.BlockSpec((1,joint,8),lambda s:(s,0,0)),
            full(w),full(feats),full(grads),
            pl.BlockSpec((1,GROUP,vocab,frames),lambda s:(s,0,0,0))],
        out_specs=[pl.BlockSpec((joint,frames),lambda s:(0,s//groups)),
            pl.BlockSpec((1,joint,8),lambda s:(s,0,0)),
            pl.BlockSpec((joint,vocab),lambda s:(0,0)),
            pl.BlockSpec((joint,128),lambda s:(0,0))],
        out_shape=[jax.ShapeDtypeStruct((joint,rows),jnp.float32),
            jax.ShapeDtypeStruct((utts*groups,joint,8),jnp.float32),
            jax.ShapeDtypeStruct((joint,vocab),jnp.bfloat16),
            jax.ShapeDtypeStruct((joint,128),jnp.bfloat16)],
        scratch_shapes=[pltpu.VMEM((joint,GROUP*frames),jnp.bfloat16),
            pltpu.VMEM((vocab+128,GROUP*frames),jnp.bfloat16),
            pltpu.VMEM((joint,vocab+128),jnp.float32)],
        compiler_params=pltpu.CompilerParams(vmem_limit_bytes=56<<20),
        name="joint_backward",
    )(labels,enc_t,pred_t,w,feats,grads,p)


MESH=pl.DeviceIdType.MESH
QA = QB = 16
HALF = 2 * QA + QB
TILE = 2 * HALF


def place():
    dp=lax.axis_index("dp"); fs=lax.axis_index("fsdp")
    return dp, fs, dp//2, dp%2, fs//2, fs%2

def greet(n1, dp, fs, a, c, i1, i2):
    barrier=pltpu.get_barrier_semaphore()
    for d in range(1,n1):
        pl.semaphore_signal(barrier,inc=1,device_id=(dp,lax.rem(i1+d,n1)*2+i2),device_id_type=MESH)
    pl.semaphore_signal(barrier,inc=1,device_id=(dp,i1*2+1-i2),device_id_type=MESH)
    pl.semaphore_signal(barrier,inc=1,device_id=((1-a)*2+c,fs),device_id_type=MESH)
    pl.semaphore_signal(barrier,inc=1,device_id=(a*2+1-c,fs),device_id_type=MESH)
    pl.semaphore_wait(barrier,n1+2)

def remote(s, d, ss, rs, dev):
    return pltpu.make_async_remote_copy(src_ref=s,dst_ref=d,send_sem=ss,recv_sem=rs,device_id=dev,device_id_type=MESH)

def rows(base, size):
    return pl.ds(pl.multiple_of(base,16),size)

def gather_kernel(n1, tiles, lag, part, src, out, own_sem, sz, rz, sy, ry, sx, rx, sc, rc):
    dp,fs,a,c,i1,i2=place()
    greet(n1,dp,fs,a,c,i1,i2)
    ypeer=(dp,i1*2+1-i2); xpeer=((1-a)*2+c,fs); cpeer=(a*2+1-c,fs)
    items=n1*tiles
    half_rows=3*part
    def main(t): return rows((2*t+c)*half_rows+a*part,2*part)
    def quarter(t,aa): return rows((2*t+c)*half_rows+aa*2*part,part)
    def half(t,cc): return rows((2*t+cc)*half_rows,half_rows)
    def of(m): return m//n1, m%n1, lax.rem(i1+n1-m%n1,n1)
    def zcopy(t,d):
        j=lax.rem(i1+d,n1)
        return remote(src.at[main(t),:],out.at[fs,main(t),:],sz.at[t,d],rz.at[t,i1],(dp,j*2+i2))
    def zin(t,j):
        return remote(src.at[main(t),:],out.at[j*2+i2,main(t),:],sz.at[t,0],rz.at[t,j],ypeer)
    def ycopy(t,j):
        s=j*2+i2
        return remote(out.at[s,main(t),:],out.at[s,main(t),:],sy.at[t,j],ry.at[t,j],ypeer)
    def ycopy_own(t):
        return remote(src.at[main(t),:],out.at[fs,main(t),:],sy.at[t,i1],ry.at[t,i1],ypeer)
    def yin(t,j):
        s=j*2+1-i2
        return remote(src.at[main(t),:],out.at[s,main(t),:],sy.at[t,j],ry.at[t,j],ypeer)
    def xcopy(t,s):
        return remote(out.at[s,quarter(t,a),:],out.at[s,quarter(t,a),:],sx.at[t,s],rx.at[t,s],xpeer)
    def xin(t,s):
        return remote(src.at[quarter(t,a),:],out.at[s,quarter(t,1-a),:],sx.at[t,s],rx.at[t,s],xpeer)
    def ccopy(t,s):
        return remote(out.at[s,half(t,c),:],out.at[s,half(t,c),:],sc.at[t,s],rc.at[t,s],cpeer)
    def cin(t,s):
        return remote(src.at[half(t,c),:],out.at[s,half(t,1-c),:],sc.at[t,s],rc.at[t,s],cpeer)
    local=pltpu.make_async_copy(src,out.at[fs],own_sem)
    local.start()

    def tick(tau,carry):
        @pl.when(tau<items)
        def _():
            t,d,j=of(tau)
            @pl.when(d>0)
            def _(): zcopy(t,d).start()
            @pl.when(d==0)
            def _(): ycopy_own(t).start()
        m1=tau-lag
        @pl.when((m1>=0)&(m1<items))
        def _():
            t,d,j=of(m1)
            @pl.when(d>0)
            def _():
                zin(t,j).wait_recv()
                ycopy(t,j).start()
                xcopy(t,j*2+i2).start()
        m2=tau-2*lag
        @pl.when((m2>=0)&(m2<items))
        def _():
            t,d,j=of(m2)
            yin(t,j).wait_recv()
            xcopy(t,j*2+1-i2).start()
        m3=tau-3*lag
        @pl.when((m3>=0)&(m3<items))
        def _():
            t,d,j=of(m3)
            @pl.when(d>0)
            def _():
                xin(t,j*2+i2).wait_recv()
                ccopy(t,j*2+i2).start()
            xin(t,j*2+1-i2).wait_recv()
            ccopy(t,j*2+1-i2).start()
        return carry
    lax.fori_loop(0,items+3*lag,tick,0)
    local.wait()
    def finish(m,carry):
        t,d,j=of(m)
        @pl.when(d>0)
        def _():
            cin(t,j*2+i2).wait_recv()
            zcopy(t,d).wait_send()
            xcopy(t,j*2+i2).wait_send()
            ccopy(t,j*2+i2).wait_send()
        cin(t,j*2+1-i2).wait_recv()
        ycopy(t,j).wait_send()
        xcopy(t,j*2+1-i2).wait_send()
        ccopy(t,j*2+1-i2).wait_send()
        return carry
    lax.fori_loop(0,items,finish,0)

def gather(packed, collective_id, lag=4):
    n=lax.axis_size("fsdp"); n1=n//2
    part=32 if packed.shape[0]%192==0 else 16
    tiles=packed.shape[0]//(6*part)
    dma=pltpu.SemaphoreType.DMA
    return pl.pallas_call(
        partial(gather_kernel,n1,tiles,lag,part),
        out_shape=jax.ShapeDtypeStruct((n,)+packed.shape,packed.dtype),
        in_specs=[pl.BlockSpec(memory_space=pl.ANY)],
        out_specs=pl.BlockSpec(memory_space=pl.ANY),
        scratch_shapes=[dma]+[dma((tiles,n1))]*4+[dma((tiles,n))]*4,
        compiler_params=pltpu.CompilerParams(collective_id=collective_id,has_side_effects=True),
        name="gather_weights",
    )(packed)

class Beats:
    def __init__(self, tick=None, total=0, sites=1):
        self.tick = tick
        self.total = total
        self.at = 0
        self.credit = 0.0
        self.scale = total / sites

    def grant(self, count):
        self.credit += count * self.scale
        steps = min(int(self.credit), self.total - self.at)
        self.credit -= int(self.credit)
        first = self.at
        self.at += steps
        return first, steps

    def span(self, low, high):
        def step(i, carry):
            self.tick(i)
            return carry

        lax.fori_loop(low, high, step, 0)

    def loop(self, count):
        if self.tick is None:
            return lambda i: None
        first, steps = self.grant(count)
        return lambda i: self.span(first + i * steps // count, first + (i + 1) * steps // count)

    def run(self, count):
        if self.tick is None:
            return
        first, steps = self.grant(count)
        if steps:
            self.span(first, first + steps)

    def rest(self):
        if self.at < self.total:
            self.span(self.at, self.total)
            self.at = self.total


class ScatterEngine:
    def __init__(self, n1, plan, lag, srcs, out, own, gc, gx, gy, gz, gf, fin, lo, sc, rc, sx, rx, sy, ry, sz, rz, sf, rf, se, re, wo):
        dp, fs, a, c, i1, i2 = place()
        greet(n1, dp, fs, a, c, i1, i2)
        ypeer = (dp, i1 * 2 + 1 - i2)
        xpeer = ((1 - a) * 2 + c, fs)
        cpeer = (a * 2 + 1 - c, fs)
        tiles = sum(count for _, count in plan)
        main = rows(a * QA, QA + QB)
        middle = pl.ds(QA, QB)

        def quarter(aa):
            return rows(aa * (QA + QB), QA)

        def cwait(t):
            return remote(own.at[t], gc.at[t], sc.at[t], rc.at[t], cpeer)

        def xcopy(t):
            return remote(own.at[t, :, :, quarter(1 - a), :], gx.at[t], sx.at[t], rx.at[t], xpeer)

        def ycopy(t):
            return remote(own.at[t, :, 1 - i2, main, :], gy.at[t], sy.at[t], ry.at[t], ypeer)

        def zcopy(t, j):
            return remote(own.at[t, j, i2, main, :], gz.at[t, i1], sz.at[t, j], rz.at[t, i1], (dp, j * 2 + i2))

        def zin(t, j):
            return remote(own.at[t, i1, i2, main, :], gz.at[t, j], sz.at[t, j], rz.at[t, j], ypeer)

        def fcopy(t):
            return remote(own.at[t, i1, i2, main, :], gf.at[t], sf.at[t], rf.at[t], xpeer)

        def ecopy(t):
            return remote(fin.at[t, c], fin.at[t, c], se.at[t], re.at[t], cpeer)

        def ein(t):
            return remote(fin.at[t, 1 - c], fin.at[t, 1 - c], se.at[t], re.at[t], cpeer)

        def store(t):
            return pltpu.make_async_copy(fin.at[t], out.at[t], wo.at[t])

        def stage_c(t):
            first = 0
            for src, (base, count) in zip(srcs, plan):

                @pl.when((t >= first) & (t < first + count))
                def _(src=src, skip=base - first):
                    at = (t + skip) * TILE
                    pltpu.make_async_copy(src.at[:, :, rows(at + c * HALF, HALF), :], own.at[t], lo.at[t]).start()
                    remote(src.at[:, :, rows(at + (1 - c) * HALF, HALF), :], gc.at[t], sc.at[t], rc.at[t], cpeer).start()

                first += count

        def stage_x(t):
            pltpu.make_async_copy(own.at[t], own.at[t], lo.at[t]).wait()
            cwait(t).wait_recv()
            own[t] = own[t] + gc[t]
            xcopy(t).start()

        def stage_y(t):
            xcopy(t).wait_recv()
            own[t, :, :, quarter(a), :] = own[t, :, :, quarter(a), :] + gx[t]
            ycopy(t).start()

        def stage_z(t):
            ycopy(t).wait_recv()
            own[t, :, i2, main, :] = own[t, :, i2, main, :] + gy[t]
            for d in range(1, n1):
                zcopy(t, lax.rem(i1 + d, n1)).start()

        def stage_f(t):
            total = own[t, i1, i2, main, :].astype(jnp.float32)
            for d in range(1, n1):
                j = lax.rem(i1 + n1 - d, n1)
                zin(t, j).wait_recv()
                total = total + gz[t, j].astype(jnp.float32)
            own[t, i1, i2, main, :] = total.astype(jnp.bfloat16)
            fcopy(t).start()

        def stage_e(t):
            fcopy(t).wait_recv()
            fin[t, c, quarter(a), :] = own[t, i1, i2, quarter(a), :]
            fin[t, c, quarter(1 - a), :] = gf[t, rows((1 - a) * QB, QA), :]
            fin[t, c, middle, :] = own[t, i1, i2, middle, :] + gf[t, rows(a * QA, QB), :]
            ecopy(t).start()

        def stage_o(t):
            ein(t).wait_recv()
            ecopy(t).wait_send()
            store(t).start()

        stages = (stage_c, stage_x, stage_y, stage_z, stage_f, stage_e, stage_o)

        def tick(tau):
            for place_of, stage in enumerate(stages):
                t = tau - place_of * lag

                @pl.when((t >= 0) & (t < tiles))
                def _(stage=stage, t=t):
                    stage(t)

        def finish():
            def tile(t, carry):
                cwait(t).wait_send()
                xcopy(t).wait_send()
                ycopy(t).wait_send()
                for d in range(1, n1):
                    zcopy(t, lax.rem(i1 + d, n1)).wait_send()
                fcopy(t).wait_send()
                store(t).wait()
                return carry

            lax.fori_loop(0, tiles, tile, 0)

        self.tick = tick
        self.total = tiles + (len(stages) - 1) * lag
        self.finish = finish


def scatter_plan(sources):
    return tuple((first, count) for _, first, count in sources)


def scatter_scratch(n, tiles):
    n1 = n // 2
    dma = pltpu.SemaphoreType.DMA
    v = lambda *shape: pltpu.VMEM((tiles,) + shape + (WIDE,), jnp.bfloat16)
    one = dma((tiles,))
    return [
        v(n1, 2, HALF), v(n1, 2, HALF), v(n1, 2, QA), v(n1, QA + QB), v(n1, QA + QB), v(QA + QB), v(2, HALF),
        one, one, one, one, one, one, one, dma((tiles, n1)), dma((tiles, n1)), one, one, one, one, one,
    ]


def riding_kernel(kernel, counts, plan, lag, n1, sites, *refs):
    n_in, n_out, n_scratch = counts
    k = len(plan)
    ins, refs = refs[:n_in], refs[n_in:]
    srcs, refs = refs[:k], refs[k:]
    outs, refs = refs[:n_out], refs[n_out:]
    share, refs = refs[0], refs[1:]
    scratch, refs = refs[:n_scratch], refs[n_scratch:]
    engine = ScatterEngine(n1, plan, lag, srcs, share, *refs)
    beats = Beats(engine.tick, engine.total, sites)
    kernel(beats, *ins, *outs, *scratch)
    beats.rest()
    engine.finish()


def call(kernel, args, in_specs, out_specs, out_shape, scratch, name, ride=None, collective_id=None, sites=1, lag=2):
    if not ride:
        return pl.pallas_call(
            partial(kernel, Beats()),
            in_specs=in_specs,
            out_specs=out_specs,
            out_shape=out_shape,
            scratch_shapes=scratch,
            compiler_params=pltpu.CompilerParams(vmem_limit_bytes=60 << 20),
            name=name,
        )(*args)
    n = lax.axis_size("fsdp")
    tiles = sum(count for _, _, count in ride)
    counts = (len(args), len(out_shape), len(scratch))
    *outs, share = pl.pallas_call(
        partial(riding_kernel, kernel, counts, scatter_plan(ride), lag, n // 2, sites),
        in_specs=in_specs + [ANY_SPEC] * len(ride),
        out_specs=out_specs + [ANY_SPEC],
        out_shape=out_shape + [sds((tiles, 2, HALF, WIDE), BF16)],
        scratch_shapes=scratch + scatter_scratch(n, tiles),
        compiler_params=pltpu.CompilerParams(collective_id=collective_id, has_side_effects=True, vmem_limit_bytes=61 << 20),
        name=name + "_and_scatter",
    )(*args, *[grads.reshape(n // 2, 2, -1, WIDE) for grads, _, _ in ride])
    return outs, share.reshape(tiles * TILE, WIDE)


def idle_kernel(beats):
    pass


def scatter(ride, collective_id):
    return call(idle_kernel, [], [], [], [], [], "idle", ride, collective_id)[1]


def pooled(parts):
    counts = [x[8:9] for x in parts]
    count = sum(counts[1:], counts[0])
    mean = sum((x[0:4] * n for x, n in zip(parts[1:], counts[1:])), parts[0][0:4] * counts[0]) / count
    dev = jnp.zeros_like(mean)
    for x, n in zip(parts, counts):
        gap = x[0:4] - mean
        dev = dev + (x[4:8] + gap * gap * n)
    return mean, dev, count


def exchange_kernel(kind, groups, n, x_ref, out_ref, near, far, s1, r1, s2, r2):
    dp = lax.axis_index("dp")
    fs = lax.axis_index("fsdp")
    barrier = pltpu.get_barrier_semaphore()
    for d in range(1, groups):
        pl.semaphore_signal(barrier, inc=1, device_id=(lax.rem(dp + d, groups), fs), device_id_type=MESH)
    for d in range(1, n):
        pl.semaphore_signal(barrier, inc=1, device_id=(dp, lax.rem(fs + d, n)), device_id_type=MESH)
    pl.semaphore_wait(barrier, groups + n - 2)

    def merge(ref, members):
        if kind == "sum":
            total = ref[0]
            for i in range(1, members):
                total = total + ref[i]
            return total
        mean, dev, count = pooled([ref[i] for i in range(members)])
        return jnp.concatenate([mean, dev, jnp.broadcast_to(count, (8, 128))], 0)

    near[dp] = x_ref[...]
    first = []
    for d in range(1, groups):
        cp = remote(near.at[dp], near.at[dp], s1.at[d], r1.at[dp], (lax.rem(dp + d, groups), fs))
        cp.start()
        first.append(cp)
    for d in range(1, groups):
        other = lax.rem(dp + d, groups)
        remote(near.at[dp], near.at[other], s1.at[d], r1.at[other], (other, fs)).wait_recv()
    far[fs] = merge(near, groups)
    for d in range(1, n):
        cp = remote(far.at[fs], far.at[fs], s2.at[d], r2.at[fs], (dp, lax.rem(fs + d, n)))
        cp.start()
        first.append(cp)
    for d in range(1, n):
        other = lax.rem(fs + d, n)
        remote(far.at[fs], far.at[other], s2.at[d], r2.at[other], (dp, other)).wait_recv()
    out_ref[...] = merge(far, n)
    for cp in first:
        cp.wait_send()


def exchange(x, kind, collective_id):
    n = lax.axis_size("fsdp")
    groups = lax.axis_size("dp")
    dma = pltpu.SemaphoreType.DMA
    return pl.pallas_call(
        partial(exchange_kernel, kind, groups, n),
        out_shape=jax.ShapeDtypeStruct(x.shape, x.dtype),
        in_specs=[pl.BlockSpec(memory_space=pltpu.VMEM)],
        out_specs=pl.BlockSpec(memory_space=pltpu.VMEM),
        scratch_shapes=[
            pltpu.VMEM((groups,) + x.shape, x.dtype),
            pltpu.VMEM((n,) + x.shape, x.dtype),
            dma((groups,)), dma((groups,)), dma((n,)), dma((n,)),
        ],
        compiler_params=pltpu.CompilerParams(collective_id=collective_id, has_side_effects=True),
        name="exchange_" + kind,
    )(x)


CHUNK_ROWS = 64
WIDE = 512
PLACE = ("p_out", "s_in", "s_out", "p_in", "w_proj", "w_joint", "f_in", "f_out")


def tn(a, b):
    return lax.dot_general(a, b, (((0,), (0,)), ((), ())), preferred_element_type=jnp.float32)


def row_loop(count, body, init=0):
    def step(i, carry):
        return body(pl.ds(pl.multiple_of(i * CHUNK_ROWS, CHUNK_ROWS), CHUNK_ROWS), i, carry)

    return lax.fori_loop(0, count // CHUNK_ROWS, step, init)


def ln_parts(v):
    centred = v - jnp.mean(v, -1, keepdims=True)
    rstd = lax.rsqrt(jnp.mean(centred * centred, -1, keepdims=True) + EPS)
    return centred * rstd, rstd


def ln_back(v, gain, grad):
    hat, rstd = ln_parts(v)
    dy = grad * gain
    dv = rstd * (dy - jnp.mean(dy, -1, keepdims=True) - hat * jnp.mean(dy * hat, -1, keepdims=True))
    return dv, fold8(grad * hat, jnp.add)


def offsets(n, width, ff):
    low = width // n
    tall = ff // n
    sizes = {
        "p_out": low, "s_in": low * (ff // WIDE), "s_out": tall, "p_in": 2 * low,
        "w_proj": low, "w_joint": 3 * low, "f_in": low * (ff // WIDE), "f_out": tall,
    }
    table = {}
    at = 0
    for name in PLACE:
        table[name] = at
        at += sizes[name]
    return table, at


class Mover:
    def __init__(self, sems):
        self.sems = sems
        self.used = 0
        self.pending = []

    def take(self):
        self.used += 1
        return self.sems.at[self.used - 1]

    def load(self, src, dst):
        cp = pltpu.make_async_copy(src, dst, self.take())
        cp.start()
        return cp

    def put(self, src, dst):
        cp = pltpu.make_async_copy(src, dst, self.take())
        cp.start()
        self.pending.append(cp)

    def load_weight(self, whole, at, dst, tall):
        n = whole.shape[0]
        height = dst.shape[0] // n
        sem = self.take()

        def one(s, carry):
            for b in range(dst.shape[1] // WIDE):
                pltpu.make_async_copy(
                    whole.at[s, pl.ds(at + b * height, height), :],
                    dst.at[pl.ds(pl.multiple_of(s * height, 16), height), pl.ds(b * WIDE, WIDE)],
                    sem,
                ).start()
            return carry

        lax.fori_loop(0, n, one, 0)
        return pltpu.make_async_copy(dst, dst, sem)

    def put_weight(self, src, grads, at):
        n = grads.shape[0]
        height = src.shape[0] // n
        sem = self.take()

        def one(s, carry):
            for b in range(src.shape[1] // WIDE):
                pltpu.make_async_copy(
                    src.at[pl.ds(pl.multiple_of(s * height, 16), height), pl.ds(b * WIDE, WIDE)],
                    grads.at[s, pl.ds(at + b * height, height), :],
                    sem,
                ).start()
            return carry

        lax.fori_loop(0, n, one, 0)
        self.pending.append(pltpu.make_async_copy(src, src, sem))

    def finish(self):
        for cp in self.pending:
            cp.wait()


def valid_rows_of(t_ref, frames, i):
    per = frames // CHUNK_ROWS
    t_len = t_ref[i // per]
    at = lax.broadcasted_iota(jnp.int32, (CHUNK_ROWS, 1), 0) + lax.rem(i, per) * CHUNK_ROWS
    return jnp.where(at < t_len, 1.0, 0.0)


def write_rows(out, base, vec):
    for i in range(vec.shape[1] // 128):
        out[base + i : base + i + 1, :] = vec[:, i * 128 : (i + 1) * 128]


def read_rows(ref, base, width):
    return jnp.concatenate([ref[base + i : base + i + 1, :] for i in range(width // 128)], 1)


def ffn_fwd(rows, x_ref, gain, w_in, w_out, normed, h, act, y, mover, h_out):
    def prepare(r, i, c):
        normed[r, :] = (ln_parts(x_ref[r, :].astype(jnp.float32))[0] * gain).astype(jnp.bfloat16)
        return c

    row_loop(rows, prepare)
    w_in[1].wait()
    for b in range(h.shape[0]):
        h[b] = nn(normed[...], w_in[0][:, b * WIDE : (b + 1) * WIDE])
        mover.put(h.at[b], h_out.at[b])

        def swish(r, i, c):
            v = h[b, r, :]
            act[r, b * WIDE : (b + 1) * WIDE] = (v * jax.nn.sigmoid(v)).astype(jnp.bfloat16)
            return c

        row_loop(rows, swish)
    w_out[1].wait()
    y[...] = x_ref[...].astype(jnp.float32) + 0.5 * nn(act[...], w_out[0][...])


def part_one_kernel(utts, table, t_ref, x_ref, small, whole, y1_out, h_out, y2_out, t_out, c_out, r_out, d_out, stats,
                    w_fin, w_fout, w_joint, w_proj, w_pin, y1, y2, normed, h, act, tq, ctx, r, gp, d, sems):
    rows, width = y1.shape
    frames = rows // utts
    mover = Mover(sems)
    gains = small[...]
    fin = mover.load_weight(whole, table["f_in"], w_fin, False)
    fout = mover.load_weight(whole, table["f_out"], w_fout, True)
    wj = mover.load_weight(whole, table["w_joint"], w_joint, False)
    wp = mover.load_weight(whole, table["w_proj"], w_proj, False)
    wi = mover.load_weight(whole, table["p_in"], w_pin, False)
    ffn_fwd(rows, x_ref, gains[0:1], (w_fin, fin), (w_fout, fout), normed, h, act, y1, mover, h_out)
    mover.put(y1, y1_out)

    def prepare(rr, i, c):
        normed[rr, :] = (ln_parts(y1[rr, :])[0] * gains[1:2]).astype(jnp.bfloat16)
        return c

    row_loop(rows, prepare)
    wj.wait()
    for b in range(3):
        tq[:, b * width : (b + 1) * width] = nn(normed[...], w_joint[:, b * width : (b + 1) * width]).astype(jnp.bfloat16)
    mover.put(tq, t_out)
    pairs = width // 128
    side = lax.broadcasted_iota(jnp.int32, (frames, 128), 1) < 64
    key_at = lax.broadcasted_iota(jnp.int32, (1, frames), 1)

    def pair_step(m, carry):
        u = m // pairs
        base = lax.rem(m, pairs) * 128
        rr = pl.ds(pl.multiple_of(u * frames, frames), frames)
        bias = jnp.where(key_at < t_ref[u], 0.0, MASKED)
        q = tq[rr, pl.ds(pl.multiple_of(base, 128), 128)]
        k = tq[rr, pl.ds(pl.multiple_of(base + width, 128), 128)]
        v = tq[rr, pl.ds(pl.multiple_of(base + 2 * width, 128), 128)]
        got = []
        for half in range(2):
            mine = side if half == 0 else ~side
            s = nt(jnp.where(mine, q, jnp.zeros_like(q)), k) * 0.125 + bias
            p = jnp.exp(s - jnp.max(s, -1, keepdims=True))
            p = p * (1.0 / jnp.sum(p, -1, keepdims=True))
            got.append(nn(p.astype(jnp.bfloat16), v))
        ctx[rr, pl.ds(pl.multiple_of(base, 128), 128)] = jnp.where(side, got[0], got[1]).astype(jnp.bfloat16)
        return carry

    lax.fori_loop(0, utts * pairs, pair_step, 0)
    mover.put(ctx, c_out)
    wp.wait()
    y2[...] = y1[...] + nn(ctx[...], w_proj[...])
    mover.put(y2, y2_out)

    def prepare_conv(rr, i, c):
        normed[rr, :] = (ln_parts(y2[rr, :])[0] * gains[2:3]).astype(jnp.bfloat16)
        return c

    row_loop(rows, prepare_conv)
    wi.wait()
    for b in range(2):
        r[:, b * width : (b + 1) * width] = nn(normed[...], w_pin[:, b * width : (b + 1) * width])
    mover.put(r, r_out)
    fill_gated(utts, frames, t_ref, r, gp)
    taps = gains[5:14]

    def conv(rr, i, total):
        d_chunk = spread(gp, utts, frames, i, taps)
        d[rr, :] = d_chunk
        return total + fold8(d_chunk * valid_rows_of(t_ref, frames, i), jnp.add)

    total = row_loop(rows, conv, jnp.zeros((8, width), jnp.float32))
    mover.put(d, d_out)
    count = t_ref[0]
    for u in range(1, utts):
        count = count + t_ref[u]
    count = count.astype(jnp.float32)
    mean = jnp.sum(total, 0, keepdims=True) / count

    def deviate(rr, i, total):
        gap = (d[rr, :] - mean) * valid_rows_of(t_ref, frames, i)
        return total + fold8(gap * gap, jnp.add)

    dev = jnp.sum(row_loop(rows, deviate, jnp.zeros((8, width), jnp.float32)), 0, keepdims=True)
    write_rows(stats, 0, mean)
    write_rows(stats, 4, dev)
    stats[8:16, :] = jnp.full((8, 128), count, jnp.float32)
    mover.finish()


def fill_gated(utts, frames, t_ref, r, gp):
    width = gp.shape[1]
    span = frames + 16
    per = frames // CHUNK_ROWS
    for u in range(utts):
        gp[u * span : u * span + 8, :] = jnp.zeros((8, width), jnp.float32)
        gp[u * span + 8 + frames : (u + 1) * span, :] = jnp.zeros((8, width), jnp.float32)

    def gate(rr, i, c):
        g = r[rr, :width] * jax.nn.sigmoid(r[rr, width:]) * valid_rows_of(t_ref, frames, i)
        at = (i // per) * span + 8 + lax.rem(i, per) * CHUNK_ROWS
        gp[pl.ds(pl.multiple_of(at, 8), CHUNK_ROWS), :] = g
        return c

    row_loop(utts * frames, gate)


def window(gp, frames, i):
    per = frames // CHUNK_ROWS
    at = (i // per) * (frames + 16) + lax.rem(i, per) * CHUNK_ROWS
    return gp[pl.ds(pl.multiple_of(at, 8), CHUNK_ROWS + 16), :]


def spread(gp, utts, frames, i, taps, flip=False):
    win = window(gp, frames, i)
    count = taps.shape[0]
    total = None
    for j in range(count):
        shift = 8 - count // 2 + (count - 1 - j if flip else j)
        term = win[shift : shift + CHUNK_ROWS] * taps[j : j + 1]
        total = term if total is None else total + term
    return total


def part_two_kernel(table, d_ref, y2_ref, pooled_ref, small, whole, y3_out, h_out, y4_out, x_out,
                    w_pout, w_sin, w_sout, act_b, y3, normed, h, act, y4, x, sems):
    rows, width = y3.shape
    mover = Mover(sems)
    gains = small[...]
    wo = mover.load_weight(whole, table["p_out"], w_pout, False)
    sin = mover.load_weight(whole, table["s_in"], w_sin, False)
    sout = mover.load_weight(whole, table["s_out"], w_sout, True)
    mean = read_rows(pooled_ref, 0, width)
    count = pooled_ref[8:9, 0:1]
    istd = lax.rsqrt(read_rows(pooled_ref, 4, width) / count + EPS)

    def bn(rr, i, c):
        b = (d_ref[rr, :] - mean) * istd * gains[14:15] + gains[15:16]
        act_b[rr, :] = (b * jax.nn.sigmoid(b)).astype(jnp.bfloat16)
        return c

    row_loop(rows, bn)
    wo.wait()
    y3[...] = y2_ref[...] + nn(act_b[...], w_pout[...])
    mover.put(y3, y3_out)
    ffn_fwd(rows, y3, gains[3:4], (w_sin, sin), (w_sout, sout), normed, h, act, y4, mover, h_out)
    mover.put(y4, y4_out)

    def last(rr, i, c):
        x[rr, :] = ln_parts(y4[rr, :])[0] * gains[4:5]
        return c

    row_loop(rows, last)
    mover.put(x, x_out)
    mover.finish()


def ffn_bwd(rows, v_ref, gain, w_in, w_out, h, loads, g_ref, gb, normed, dact, act, dh, dn, dw_in, dw_out, mover, grads, at_in, at_out, beats):
    def prepare(rr, i, c):
        normed[rr, :] = (ln_parts(v_ref[rr, :].astype(jnp.float32))[0] * gain).astype(jnp.bfloat16)
        gb[rr, :] = (0.5 * g_ref[rr, :]).astype(jnp.bfloat16)
        return c

    row_loop(rows, prepare)
    w_out[1].wait()
    for b in range(h.shape[0]):
        cols = slice(b * WIDE, (b + 1) * WIDE)
        dact[...] = nt(gb[...], w_out[0][cols, :])
        beats.run(1)
        loads[b].wait()

        def slope(rr, i, c):
            v = h[b, rr, :]
            sg = jax.nn.sigmoid(v)
            act[rr, :] = (v * sg).astype(jnp.bfloat16)
            dh[rr, cols] = (dact[rr, :] * (sg * (1.0 + v * (1.0 - sg)))).astype(jnp.bfloat16)
            return c

        row_loop(rows, slope)
        beats.run(1)
        dw_out[cols, :] = tn(act[...], gb[...]).astype(jnp.bfloat16)
        beats.run(1)
        dw_in[:, cols] = tn(normed[...], dh[:, cols]).astype(jnp.bfloat16)
        beats.run(1)
    mover.put_weight(dw_out, grads, at_out)
    mover.put_weight(dw_in, grads, at_in)
    w_in[1].wait()
    dn[...] = nt(dh[...], w_in[0][...])
    beats.run(2)

    def back(rr, i, total):
        dv, dg = ln_back(v_ref[rr, :].astype(jnp.float32), gain, dn[rr, :])
        g_ref[rr, :] = g_ref[rr, :] + dv
        return total + dg

    return row_loop(rows, back, jnp.zeros((8, g_ref.shape[1]), jnp.float32))


def down(folded):
    return jnp.sum(folded, 0, keepdims=True)


def back_one_kernel(table, beats, grad_ref, y4_ref, y3_ref, d_ref, pooled_ref, small, whole, h_hbm, g_out, db_out, grads, sums, gain_out,
                    w_pout, w_sin, w_sout, g, gb, normed, dact, act, dh, dn, dw_in, dw_out, dw_pout, h, db, sems):
    rows, width = g.shape
    mover = Mover(sems)
    gains = small[...]
    sout = mover.load_weight(whole, table["s_out"], w_sout, True)
    loads = [mover.load(h_hbm.at[b], h.at[b]) for b in range(h.shape[0])]
    sin = mover.load_weight(whole, table["s_in"], w_sin, False)
    wo = mover.load_weight(whole, table["p_out"], w_pout, False)
    beats.run(5)

    def first(rr, i, total):
        dv, dg = ln_back(y4_ref[rr, :], gains[4:5], grad_ref[rr, :])
        g[rr, :] = dv
        return total + dg

    gain4 = down(row_loop(rows, first, jnp.zeros((8, width), jnp.float32)))
    gain3 = down(ffn_bwd(rows, y3_ref, gains[3:4], (w_sin, sin), (w_sout, sout), h, loads, g, gb, normed, dact, act, dh, dn,
                         dw_in, dw_out, mover, grads, table["s_in"], table["s_out"], beats))
    mover.put(g, g_out)
    gain_out[...] = jnp.concatenate([gain3, gain4, jnp.zeros((6, width), jnp.float32)], 0)
    mean = read_rows(pooled_ref, 0, width)
    istd = lax.rsqrt(read_rows(pooled_ref, 4, width) / pooled_ref[8:9, 0:1] + EPS)

    def cast(rr, i, c):
        gb[rr, :] = g[rr, :].astype(jnp.bfloat16)
        return c

    row_loop(rows, cast)
    wo.wait()
    dact[...] = nt(gb[...], w_pout[...])
    beats.run(1)

    def bn(rr, i, totals):
        z = (d_ref[rr, :] - mean) * istd
        b = z * gains[14:15] + gains[15:16]
        sg = jax.nn.sigmoid(b)
        act[rr, :] = (b * sg).astype(jnp.bfloat16)
        db_chunk = dact[rr, :] * (sg * (1.0 + b * (1.0 - sg)))
        db[rr, :] = db_chunk
        return totals[0] + fold8(db_chunk, jnp.add), totals[1] + fold8(db_chunk * z, jnp.add)

    zero = jnp.zeros((8, width), jnp.float32)
    one, two = row_loop(rows, bn, (zero, zero))
    beats.run(2)
    mover.put(db, db_out)
    write_rows(sums, 0, down(one))
    write_rows(sums, 4, down(two))
    sums[8:16, :] = jnp.zeros((8, 128), jnp.float32)
    dw_pout[...] = tn(act[...], gb[...]).astype(jnp.bfloat16)
    mover.put_weight(dw_pout, grads, table["p_out"])
    mover.finish()


def back_two_kernel(utts, table, start, end, beats, t_ref, x_ref, y1_ref, y2_ref, r_ref, t_in, c_ref, d_ref, db_ref, g_in, pooled_ref, sums_ref, late_ref, small, whole, h_hbm,
                    g_out, grads,
                    w_pin, w_proj, w_joint, w_fin, w_fout, g, gb, normed, dact, act, dh, dn, dw_pin, dw_proj, dw_joint, dw_in, dw_out, h, gp, dd, dr, dt, sm, sems):
    rows, width = g.shape
    frames = rows // utts
    mover = Mover(sems)
    gains = small[...]
    wi = mover.load_weight(whole, table["p_in"], w_pin, False)
    wp = mover.load_weight(whole, table["w_proj"], w_proj, False)
    wj = mover.load_weight(whole, table["w_joint"], w_joint, False)
    fout = mover.load_weight(whole, table["f_out"], w_fout, True)
    loads = [mover.load(h_hbm.at[b], h.at[b]) for b in range(h.shape[0])]
    fin = mover.load_weight(whole, table["f_in"], w_fin, False)
    mean = read_rows(pooled_ref, 0, width)
    count = pooled_ref[8:9, 0:1]
    istd = lax.rsqrt(read_rows(pooled_ref, 4, width) / count + EPS)
    bias_sum = read_rows(sums_ref, 0, width)
    gain_sum = read_rows(sums_ref, 4, width)
    taps = gains[5:14]
    ntaps = taps.shape[0]
    span = frames + 16
    per = frames // CHUNK_ROWS
    beats.run(5)
    fill_gated(utts, frames, t_ref, r_ref, gp)
    beats.run(1)
    for u in range(utts):
        dd[u * span : u * span + 8, :] = jnp.zeros((8, width), jnp.float32)
        dd[u * span + 8 + frames : (u + 1) * span, :] = jnp.zeros((8, width), jnp.float32)

    def bn(rr, i, c):
        z = (d_ref[rr, :] - mean) * istd
        v = gains[14:15] * istd * (db_ref[rr, :] - valid_rows_of(t_ref, frames, i) * (bias_sum + z * gain_sum) / count)
        at = (i // per) * span + 8 + lax.rem(i, per) * CHUNK_ROWS
        dd[pl.ds(pl.multiple_of(at, 8), CHUNK_ROWS), :] = v
        return c

    row_loop(rows, bn)

    def conv(rr, i, totals):
        dg = spread(dd, utts, frames, i, taps, True) * valid_rows_of(t_ref, frames, i)
        sg = jax.nn.sigmoid(r_ref[rr, width:])
        dr[rr, :width] = (dg * sg).astype(jnp.bfloat16)
        dr[rr, width:] = (dg * r_ref[rr, :width] * sg * (1.0 - sg)).astype(jnp.bfloat16)
        win = window(gp, frames, i)
        mine = window(dd, frames, i)[8 : 8 + CHUNK_ROWS]
        normed[rr, :] = (ln_parts(y2_ref[rr, :])[0] * gains[2:3]).astype(jnp.bfloat16)
        return tuple(
            totals[j] + fold8(win[8 - ntaps // 2 + j : 8 - ntaps // 2 + j + CHUNK_ROWS] * mine, jnp.add) for j in range(ntaps)
        )

    zero = jnp.zeros((8, width), jnp.float32)
    tap_grads = [down(x) for x in row_loop(rows, conv, (zero,) * ntaps)]
    beats.run(2)
    for b in range(2):
        cols = slice(b * width, (b + 1) * width)
        dw_pin[:, cols] = tn(normed[...], dr[:, cols]).astype(jnp.bfloat16)
    mover.put_weight(dw_pin, grads, table["p_in"] - start)
    beats.run(2)
    wi.wait()
    dn[...] = nt(dr[...], w_pin[...])
    beats.run(1)

    def back_conv(rr, i, total):
        dv, dg = ln_back(y2_ref[rr, :], gains[2:3], dn[rr, :])
        v = g_in[rr, :] + dv
        g[rr, :] = v
        gb[rr, :] = v.astype(jnp.bfloat16)
        normed[rr, :] = (ln_parts(y1_ref[rr, :])[0] * gains[1:2]).astype(jnp.bfloat16)
        return total + dg

    gain2 = down(row_loop(rows, back_conv, zero))
    dw_proj[...] = tn(c_ref[...], gb[...]).astype(jnp.bfloat16)
    mover.put_weight(dw_proj, grads, table["w_proj"] - start)
    beats.run(1)
    wp.wait()
    act[...] = nt(gb[...], w_proj[...]).astype(jnp.bfloat16)
    pairs = width // 128
    side = lax.broadcasted_iota(jnp.int32, (frames, 128), 1) < 64
    key_at = lax.broadcasted_iota(jnp.int32, (frames, 1), 0)
    hook = beats.loop(utts * pairs)

    def pair_step(m, carry):
        hook(m)
        u = m // pairs
        base = lax.rem(m, pairs) * 128
        rr = pl.ds(pl.multiple_of(u * frames, frames), frames)
        at = [pl.ds(pl.multiple_of(base + b * width, 128), 128) for b in range(3)]
        bias = jnp.where(key_at < t_ref[u], 0.0, MASKED)
        q = t_in[rr, at[0]]
        k = t_in[rr, at[1]]
        v = t_in[rr, at[2]]
        dc = act[rr, at[0]]
        got = []
        for half in range(2):
            mine = side if half == 0 else ~side
            nothing = jnp.zeros_like(k)
            s = nt(jnp.where(mine, k, nothing), q) * 0.125 + bias
            p = jnp.exp(s - jnp.max(s, 0, keepdims=True))
            p = p * (1.0 / jnp.sum(p, 0, keepdims=True))
            dp = nt(jnp.where(mine, v, nothing), dc)
            ds = (p * (dp - jnp.sum(dp * p, 0, keepdims=True))).astype(jnp.bfloat16)
            got.append((tn(ds, k) * 0.125, nn(ds, q) * 0.125, nn(p.astype(jnp.bfloat16), dc)))
        for b in range(3):
            dt[rr, at[b]] = jnp.where(side, got[0][b], got[1][b]).astype(jnp.bfloat16)
        return carry

    lax.fori_loop(0, utts * pairs, pair_step, 0)
    for b in range(3):
        cols = slice(b * width, (b + 1) * width)
        dw_joint[:, cols] = tn(normed[...], dt[:, cols]).astype(jnp.bfloat16)
    mover.put_weight(dw_joint, grads, table["w_joint"] - start)
    beats.run(2)
    wj.wait()
    dn[...] = nt(dt[...], w_joint[...])
    beats.run(1)

    def back_attend(rr, i, total):
        dv, dg = ln_back(y1_ref[rr, :], gains[1:2], dn[rr, :])
        g[rr, :] = g[rr, :] + dv
        return total + dg

    gain1 = down(row_loop(rows, back_attend, zero))
    gain0 = down(ffn_bwd(rows, x_ref, gains[0:1], (w_fin, fin), (w_fout, fout), h, loads, g, gb, normed, dact, act, dh, dn,
                         dw_in, dw_out, mover, grads, table["f_in"] - start, table["f_out"] - start, beats))
    mover.put(g, g_out)
    packed = jnp.concatenate([gain0, gain1, gain2, late_ref[0:2, :]] + tap_grads + [jnp.zeros((2, width), jnp.float32)], 0)
    n = grads.shape[0]
    low = width // n
    for s in range(n):
        sm[s] = jnp.concatenate([packed[:, s * low : (s + 1) * low], jnp.zeros((16, WIDE - low), jnp.float32)], 1).astype(jnp.bfloat16)
    mover.put(sm, grads.at[:, pl.ds(end - start, 16), :])
    mover.finish()


VMEM_SPEC = pl.BlockSpec(memory_space=pltpu.VMEM)
SMEM_SPEC = pl.BlockSpec(memory_space=pltpu.SMEM)
ANY_SPEC = pl.BlockSpec(memory_space=pl.ANY)
F32 = jnp.float32
BF16 = jnp.bfloat16


def sds(shape, dtype=jnp.float32):
    return jax.ShapeDtypeStruct(shape, dtype)


def part_one(t_len, x, small, whole, ff):
    rows, width = x.shape
    utts = t_len.shape[0]
    table, _ = offsets(whole.shape[0], width, ff)
    nb = ff // WIDE
    v = pltpu.VMEM
    return pl.pallas_call(
        partial(part_one_kernel, utts, table),
        in_specs=[SMEM_SPEC, VMEM_SPEC, VMEM_SPEC, ANY_SPEC],
        out_specs=[ANY_SPEC] * 7 + [VMEM_SPEC],
        out_shape=[sds((rows, width)), sds((nb, rows, WIDE)), sds((rows, width)), sds((rows, 3 * width), BF16),
                   sds((rows, width), BF16), sds((rows, 2 * width)), sds((rows, width)), sds((16, 128))],
        scratch_shapes=[v((width, ff), BF16), v((ff, width), BF16), v((width, 3 * width), BF16), v((width, width), BF16),
                        v((width, 2 * width), BF16), v((rows, width), F32), v((rows, width), F32), v((rows, width), BF16),
                        v((nb, rows, WIDE), F32), v((rows, ff), BF16), v((rows, 3 * width), BF16), v((rows, width), BF16),
                        v((rows, 2 * width), F32), v((utts * (rows // utts + 16), width), F32), v((rows, width), F32),
                        pltpu.SemaphoreType.DMA((24,))],
        compiler_params=pltpu.CompilerParams(vmem_limit_bytes=56 << 20),
        name="layer_part_one",
    )(t_len, x, small, whole)


def part_two(d, y2, pooled, small, whole, ff):
    rows, width = d.shape
    table, _ = offsets(whole.shape[0], width, ff)
    nb = ff // WIDE
    v = pltpu.VMEM
    return pl.pallas_call(
        partial(part_two_kernel, table),
        in_specs=[VMEM_SPEC] * 4 + [ANY_SPEC],
        out_specs=[ANY_SPEC] * 4,
        out_shape=[sds((rows, width)), sds((nb, rows, WIDE)), sds((rows, width)), sds((rows, width))],
        scratch_shapes=[v((width, width), BF16), v((width, ff), BF16), v((ff, width), BF16), v((rows, width), BF16),
                        v((rows, width), F32), v((rows, width), BF16), v((nb, rows, WIDE), F32), v((rows, ff), BF16),
                        v((rows, width), F32), v((rows, width), F32), pltpu.SemaphoreType.DMA((16,))],
        compiler_params=pltpu.CompilerParams(vmem_limit_bytes=56 << 20),
        name="layer_part_two",
    )(d, y2, pooled, small, whole)


def tiled(count):
    return -(-count // TILE) * TILE


def back_one(grad, y4, y3, d, pooled, small, whole, h, ff, ride=None, collective_id=None):
    rows, width = grad.shape
    n = whole.shape[0]
    table, _ = offsets(n, width, ff)
    nb = ff // WIDE
    v = pltpu.VMEM
    return call(
        partial(back_one_kernel, table),
        (grad, y4, y3, d, pooled, small, whole, h),
        [VMEM_SPEC] * 6 + [ANY_SPEC] * 2,
        [ANY_SPEC] * 3 + [VMEM_SPEC] * 2,
        [sds((rows, width)), sds((rows, width)), sds((n, tiled(table["p_in"]), WIDE), BF16), sds((16, 128)), sds((8, width))],
        [v((width, width), BF16), v((width, ff), BF16), v((ff, width), BF16), v((rows, width), F32),
         v((rows, width), BF16), v((rows, width), BF16), v((rows, width), F32), v((rows, width), BF16),
         v((rows, ff), BF16), v((rows, width), F32), v((width, ff), BF16), v((ff, width), BF16),
         v((width, width), BF16), v((nb, rows, WIDE), F32), v((rows, width), F32), pltpu.SemaphoreType.DMA((16,))],
        "back_part_one",
        ride,
        collective_id,
        28,
    )


def back_two(t_len, x, y1, y2, r, t, c, d, db, g, pooled, sums, late, small, whole, h, ff, ride=None, collective_id=None):
    rows, width = d.shape
    utts = t_len.shape[0]
    n = whole.shape[0]
    table, end = offsets(n, width, ff)
    start = table["p_in"]
    nb = ff // WIDE
    v = pltpu.VMEM
    pad_rows = utts * (rows // utts + 16)
    return call(
        partial(back_two_kernel, utts, table, start, end),
        (t_len, x, y1, y2, r, t, c, d, db, g, pooled, sums, late, small, whole, h),
        [SMEM_SPEC] + [VMEM_SPEC] * 13 + [ANY_SPEC] * 2,
        [ANY_SPEC] * 2,
        [sds((rows, width)), sds((n, tiled(end - start + 16), WIDE), BF16)],
        [v((width, 2 * width), BF16), v((width, width), BF16), v((width, 3 * width), BF16), v((width, ff), BF16),
         v((ff, width), BF16), v((rows, width), F32), v((rows, width), BF16), v((rows, width), BF16),
         v((rows, width), F32), v((rows, width), BF16), v((rows, ff), BF16), v((rows, width), F32),
         v((width, 2 * width), BF16), v((width, width), BF16), v((width, 3 * width), BF16), v((width, ff), BF16),
         v((ff, width), BF16), v((nb, rows, WIDE), F32), v((pad_rows, width), F32), v((pad_rows, width), F32),
         v((rows, 2 * width), BF16), v((rows, 3 * width), BF16), v((n, 16, WIDE), BF16), pltpu.SemaphoreType.DMA((20,))],
        "back_part_two",
        ride,
        collective_id,
        44,
    )


def lift(rows):
    return -(-rows // 16) * 16


def joint_sizes(w_enc, w_pred, w_tok):
    low, tall = lift(w_enc.shape[0]), lift(w_pred.shape[0])
    return [low, tall, tall * (w_tok.shape[1] // WIDE), tall]


def pack_kernel(layers, table, end, *refs):
    names = PLACE + ("gains", "taps", "bn_gain", "bn_bias", "enc", "pred", "tok", "dur")
    src = dict(zip(names, refs))
    outs = refs[len(names) :]
    for layer in range(layers):
        out = outs[layer]
        for name in PLACE:
            ref = src[name]
            height = ref.shape[1]
            for b in range(ref.shape[2] // WIDE):
                at = table[name] + b * height
                out[at : at + height, :] = ref[layer, :, b * WIDE : (b + 1) * WIDE]
        small = [src["gains"][layer], src["taps"][layer], src["bn_gain"][layer : layer + 1, :], src["bn_bias"][layer : layer + 1, :]]
        small = jnp.concatenate([x.astype(jnp.float32) for x in small], 0)
        small = jnp.concatenate([small, jnp.zeros((16, WIDE - small.shape[1]), jnp.float32)], 1)
        out[end : end + 16, :] = small.astype(jnp.bfloat16)
        if out.shape[0] > end + 16:
            out[end + 16 :, :] = jnp.zeros((out.shape[0] - end - 16, WIDE), jnp.bfloat16)
    out = outs[layers - 1]
    enc, pred, tok, dur = src["enc"], src["pred"], src["tok"], src["dur"]
    low, tall = enc.shape[0], pred.shape[0]
    at = end + 16
    out[at : at + low, :] = enc[:, :WIDE]
    at += lift(low)
    out[at : at + tall, :] = pred[:, :WIDE]
    at += lift(tall)
    for b in range(tok.shape[1] // WIDE):
        out[at : at + tall, :] = tok[:, b * WIDE : (b + 1) * WIDE]
        at += lift(tall)
    out[at : at + low, 0:128] = enc[:, WIDE:]
    out[at : at + tall, 128:256] = pred[:, WIDE:]
    dur = dur[...].astype(jnp.float32)
    out[at : at + tall, 256:384] = jnp.concatenate([dur, jnp.zeros((tall, 128 - dur.shape[1]), jnp.float32)], 1).astype(jnp.bfloat16)


def pack(layers, table, end, extra, arrays):
    shapes = []
    for layer in range(layers):
        count = end + 16 + (extra if layer == layers - 1 else 0)
        shapes.append(sds((tiled(count), WIDE), BF16))
    return pl.pallas_call(
        partial(pack_kernel, layers, table, end),
        in_specs=[VMEM_SPEC] * len(arrays),
        out_specs=[VMEM_SPEC] * layers,
        out_shape=shapes,
        compiler_params=pltpu.CompilerParams(vmem_limit_bytes=48 << 20),
        name="pack_weights",
    )(*arrays)


class Joined:
    def __init__(self, parts, ends):
        self.parts = parts
        self.ends = ends

    def __getitem__(self, key):
        rows_of, cols = key
        got = []
        first = 0
        for part, last in zip(self.parts, self.ends):
            lo, hi = max(rows_of.start, first), min(rows_of.stop, last)
            if lo < hi:
                got.append(part[lo - first : hi - first, cols])
            first = last
        return got[0] if len(got) == 1 else jnp.concatenate(got, 0)


def unpack_kernel(layers, table, end, dims, ends, *refs):
    parts, refs = refs[: len(ends)], refs[len(ends) :]
    gains, f_in, f_out, w_joint, w_proj, p_in, taps, p_out, s_in, s_out, enc, pred, tok, dur = refs
    share = Joined(parts, ends)
    outs = {"f_in": f_in, "f_out": f_out, "w_joint": w_joint, "w_proj": w_proj, "p_in": p_in, "p_out": p_out, "s_in": s_in, "s_out": s_out}
    starts, width, joint = dims
    shard = gains.shape[2]
    for layer in range(layers):
        for name in PLACE:
            out = outs[name]
            height = out.shape[1]
            early = table[name] < table["p_in"]
            base = starts[layer][0] + table[name] if early else starts[layer][1] + table[name] - table["p_in"]
            for b in range(out.shape[2] // WIDE):
                out[layer, :, b * WIDE : (b + 1) * WIDE] = share[base + b * height : base + (b + 1) * height, :].astype(jnp.float32)
        base = starts[layer][1] + end - table["p_in"]
        small = share[base : base + 16, 0:128].astype(jnp.float32)
        gains[layer] = small[0:5, :shard]
        taps[layer] = small[5 : 5 + taps.shape[1], :shard]
    at = starts[layers]
    low, tall = enc.shape[0], pred.shape[0]
    enc[:, :WIDE] = share[at : at + low, :].astype(jnp.float32)
    at += lift(low)
    pred[:, :WIDE] = share[at : at + tall, :].astype(jnp.float32)
    at += lift(tall)
    for b in range(tok.shape[1] // WIDE):
        tok[:, b * WIDE : (b + 1) * WIDE] = share[at : at + tall, :].astype(jnp.float32)
        at += lift(tall)
    enc[:, WIDE:] = share[at : at + low, 0:128].astype(jnp.float32)
    pred[:, WIDE:] = share[at : at + tall, 128:256].astype(jnp.float32)
    dur[...] = share[at : at + tall, 256:384].astype(jnp.float32)[:, : dur.shape[1]]


def unpack(layers, table, end, dims, shares, like):
    ends = []
    for share in shares:
        ends.append(share.shape[0] + (ends[-1] if ends else 0))
    return pl.pallas_call(
        partial(unpack_kernel, layers, table, end, dims, tuple(ends)),
        in_specs=[VMEM_SPEC] * len(shares),
        out_specs=[VMEM_SPEC] * len(like),
        out_shape=[sds(x.shape) for x in like],
        compiler_params=pltpu.CompilerParams(vmem_limit_bytes=48 << 20),
        name="unpack_grads",
    )(*shares)


def cut(whole, sizes, offset=0):
    parts = []
    for size in sizes:
        parts.append(whole[..., offset : offset + size, :])
        offset += size
    return parts


def from_blocks(part, cols, rows):
    n, height, _ = part.shape
    blocks = cols // WIDE
    return jnp.swapaxes(part.reshape(n, blocks, height // blocks, WIDE)[:, :, :rows], 1, 2).reshape(-1, cols)


def unpack_joint(whole, first, sizes, w_enc, w_pred, vocab):
    enc, pred, tok, rest = cut(whole, sizes, first)
    joint = w_enc.shape[1]
    low = w_enc.shape[0]
    tall = w_pred.shape[0]
    w_enc = jnp.concatenate([enc[:, :low], rest[:, :low, : joint - WIDE]], 2).reshape(-1, joint)
    w_pred = jnp.concatenate([pred[:, :tall], rest[:, :tall, 128 : 128 + joint - WIDE]], 2).reshape(-1, joint)
    return w_enc, w_pred, from_blocks(tok, vocab, tall), rest[:, :tall, 256:384].reshape(-1, 128)


def grow(part):
    short = lift(part.shape[1]) - part.shape[1]
    return jnp.pad(part, ((0, 0), (0, short), (0, 0))) if short else part


def pack_joint_grads(g_enc, g_pred, g_tok, g_dur, n):
    def shards(grad):
        return grow(grad.astype(jnp.bfloat16).reshape(n, -1, grad.shape[1]))
    g_enc, g_pred, g_tok, g_dur = shards(g_enc), shards(g_pred), shards(g_tok), shards(g_dur)
    tall = g_pred.shape[1]
    rest = jnp.concatenate(
        [
            jnp.pad(g_enc[:, :, WIDE:], ((0, 0), (0, tall - g_enc.shape[1]), (0, 0))),
            g_pred[:, :, WIDE:],
            g_dur,
            jnp.zeros((n, tall, 128), jnp.bfloat16),
        ],
        2,
    )
    parts = [g_enc[:, :, :WIDE], g_pred[:, :, :WIDE]]
    parts += [g_tok[:, :, b : b + WIDE] for b in range(0, g_tok.shape[2], WIDE)] + [rest]
    rows = sum(p.shape[1] for p in parts)
    return jnp.concatenate(parts + [jnp.zeros((n, tiled(rows) - rows, WIDE), jnp.bfloat16)], 1)


def matmul(left, right):
    return jnp.dot(left, right, preferred_element_type=jnp.float32)


def contract_rows(left, right):
    return lax.dot_general(
        left, right, (((0,), (0,)), ((), ())), preferred_element_type=jnp.float32
    )


def contract_cols(left, right):
    return lax.dot_general(
        left, right, (((1,), (1,)), ((), ())), preferred_element_type=jnp.float32
    )


def local(
    frames_in,
    frame_lengths,
    label_ids,
    label_lengths,
    pred_states,
    norm_gains,
    first_in,
    first_out,
    attend_joint,
    attend_out,
    point_in,
    depth_taps,
    batch_gain,
    batch_bias,
    point_out,
    second_in,
    second_out,
    enc_weight,
    pred_weight,
    token_weight,
    duration_weight,
):
    utts, frames, width = frames_in.shape
    slots = pred_states.shape[1]
    rows = utts * frames
    layers = norm_gains.shape[0]
    n = lax.axis_size("fsdp")
    ff = first_in.shape[2]
    mats = {
        "f_in": first_in, "f_out": first_out, "w_joint": attend_joint, "w_proj": attend_out,
        "p_in": point_in, "p_out": point_out, "s_in": second_in, "s_out": second_out,
    }
    table, end = offsets(n, width, ff)
    shard = width // n
    sizes = joint_sizes(enc_weight, pred_weight, token_weight)
    vocab = token_weight.shape[1]
    packs = pack(
        layers,
        table,
        end,
        sum(sizes),
        [mats[name] for name in PLACE]
        + [norm_gains, depth_taps, batch_gain, batch_bias, enc_weight, pred_weight, token_weight, duration_weight],
    )
    wholes = []
    smalls = []
    for layer in range(layers):
        whole = gather(packs[layer], 1 + layer)
        small = whole[:, end : end + 16, :shard].astype(jnp.float32)
        wholes.append(whole)
        smalls.append(jnp.swapaxes(small, 0, 1).reshape(16, width))
    resid = frames_in.reshape(rows, width)
    records = []
    for layer in range(layers):
        y1, h1, y2, qkv, ctx, gates, depthwise, stats = part_one(frame_lengths, resid, smalls[layer], wholes[layer], ff)
        pooled = exchange(stats, "pool", 8 + layer)
        y3, h2, y4, result = part_two(depthwise, y2, pooled, smalls[layer], wholes[layer], ff)
        records.append((resid, y1, h1, y2, qkv, ctx, gates, depthwise, pooled, y3, h2, y4))
        resid = result
    w_enc, w_pred, w_tok, w_dur = unpack_joint(wholes[-1], end + 16, sizes, enc_weight, pred_weight, vocab)
    joint = w_enc.shape[1]
    vocab = w_tok.shape[1]
    out_low = resid.astype(jnp.bfloat16)
    enc = matmul(out_low, w_enc)
    pred_low = pred_states.reshape(utts * slots, joint)
    pred = matmul(pred_low, w_pred).reshape(utts, slots, joint)
    groups = slots // GROUP
    durs = duration_weight.shape[1]
    pred_t = jnp.pad(
        jnp.swapaxes(pred.reshape(utts * groups, GROUP, joint), 1, 2),
        ((0, 0), (0, 0), (0, 8 - GROUP)),
    )
    w_cat = jnp.concatenate([w_tok, w_dur], 1)
    enc_t = enc.T
    labels_ext = jnp.concatenate([label_ids, jnp.zeros((utts, 1), jnp.int32)], 1)
    feats, expd = joint_forward(enc_t, pred_t, labels_ext, w_cat.T, vocab, durs, frames)
    lat_grads, scores = lattice(feats[: 2 + durs], frame_lengths, label_lengths, slots)
    log_prob = scores[:utts, 0]
    utt_loss = -log_prob / frame_lengths.astype(jnp.float32)
    grad_enc_t, grad_pred_t, grad_tok, grad_dur_w = joint_backward(
        enc_t, pred_t, labels_ext, w_cat, feats, lat_grads, expd, vocab, durs, frames
    )
    grad_pred_rows = jnp.swapaxes(grad_pred_t[:, :, :GROUP], 1, 2)
    grad_enc_low = grad_enc_t.T.astype(jnp.bfloat16)
    grad_w_enc = contract_rows(out_low, grad_enc_low)
    grad = contract_cols(grad_enc_low, w_enc)
    grad_w_pred = contract_rows(
        pred_low, grad_pred_rows.reshape(utts * slots, joint).astype(jnp.bfloat16)
    )
    def whole_of(source):
        return (source, 0, source.shape[1] // TILE)

    joint_grads = pack_joint_grads(grad_w_enc, grad_w_pred, grad_tok, grad_dur_w, n)
    waiting = [whole_of(joint_grads)]
    shares = []
    starts = [None] * layers + [0]
    at = joint_grads.shape[1]
    bn_grads = [None] * layers
    for layer in reversed(range(layers)):
        x0, y1, h1, y2, qkv, ctx, gates, depthwise, pooled, y3, h2, y4 = records[layer]
        args = (grad, y4, y3, depthwise, pooled, smalls[layer], wholes[layer], h2, ff)
        if layer == layers - 1:
            outs = back_one(*args)
        else:
            source, first, count = waiting.pop()
            early = min(count, -(-count * 3 // 5))
            outs, share = back_one(*args, [(source, first, early)], 16 + layer)
            shares.append(share)
            if early < count:
                waiting.append((source, first + early, count - early))
        g3, db, grads_one, sums, late_gains = outs
        sums = exchange(sums, "sum", 12 + layer)
        waiting.append(whole_of(grads_one))
        args = (frame_lengths, x0, y1, y2, gates, qkv, ctx, depthwise, db, g3, pooled, sums, late_gains)
        (grad, grads_two), share = back_two(*args, smalls[layer], wholes[layer], h1, ff, waiting, 20 + layer)
        shares.append(share)
        waiting = [whole_of(grads_two)]
        starts[layer] = (at, at + grads_one.shape[1])
        at += grads_one.shape[1] + grads_two.shape[1]
        bn_grads[layer] = (sums[4:8].reshape(width), sums[0:4].reshape(width))
    shares.append(scatter(waiting, 4))
    grads = unpack(
        layers,
        table,
        end,
        (starts, width, joint),
        shares,
        [norm_gains, first_in, first_out, attend_joint, attend_out, point_in, depth_taps, point_out, second_in, second_out,
         enc_weight, pred_weight, token_weight, duration_weight],
    )
    offset = lax.axis_index("fsdp") * shard
    gain_piece = lax.dynamic_slice_in_dim(jnp.stack([g[0] for g in bn_grads]), offset, shard, 1)
    bias_piece = lax.dynamic_slice_in_dim(jnp.stack([g[1] for g in bn_grads]), offset, shard, 1)
    return (
        utt_loss,
        grad.reshape(utts, frames, width),
        *grads[:7],
        gain_piece,
        bias_piece,
        *grads[7:],
    )


def solution(mesh):
    placed = (
        P(("dp", "fsdp"), None, None),
        P(("dp", "fsdp")),
        P(("dp", "fsdp"), None),
        P(("dp", "fsdp")),
        P(("dp", "fsdp"), None, None),
        P(None, None, "fsdp"),
        P(None, "fsdp", None),
        P(None, "fsdp", None),
        P(None, "fsdp", None),
        P(None, "fsdp", None),
        P(None, "fsdp", None),
        P(None, None, "fsdp"),
        P(None, "fsdp"),
        P(None, "fsdp"),
        P(None, "fsdp", None),
        P(None, "fsdp", None),
        P(None, "fsdp", None),
        P("fsdp", None),
        P("fsdp", None),
        P("fsdp", None),
        P("fsdp", None),
    )
    return jax.shard_map(
        local,
        mesh=mesh,
        in_specs=placed,
        out_specs=(
            P(("dp", "fsdp")),
            P(("dp", "fsdp"), None, None),
            P(None, None, "fsdp"),
            P(None, "fsdp", None),
            P(None, "fsdp", None),
            P(None, "fsdp", None),
            P(None, "fsdp", None),
            P(None, "fsdp", None),
            P(None, None, "fsdp"),
            P(None, "fsdp"),
            P(None, "fsdp"),
            P(None, "fsdp", None),
            P(None, "fsdp", None),
            P(None, "fsdp", None),
            P("fsdp", None),
            P("fsdp", None),
            P("fsdp", None),
            P("fsdp", None),
        ),
        check_vma=False,
    )
```

```python
from functools import partial, reduce

import jax
import jax.numpy as jnp
from jax import lax
from jax.experimental import pallas as pl
from jax.experimental.pallas import tpu as pltpu
from jax.sharding import PartitionSpec as P

HEADS = 8


EPS = 1e-05
MASKED = -1000000000.0
NEG = -1e30


def lattice_kernel(slots, feats_ref, tlen_ref, ulen_ref, grads_ref, prob_ref, s_ref, l_ref, ls_ref, a_ref, b_ref, init_ref):
    utts = tlen_ref.shape[0]
    frames = feats_ref.shape[2]
    rows = feats_ref.shape[1]
    wide = frames + 128
    reach = feats_ref.shape[0] - 3
    diags = frames + slots
    pad = 8
    total = a_ref.shape[0]
    body = wide

    def skew(x, sign):
        k = lax.broadcasted_iota(jnp.int32, x.shape, 0) % 32
        for bit in range(5):
            step = 1 << bit
            x = jnp.where((k // step) % 2 == 1, pltpu.roll(x, step if sign > 0 else wide - step, 1), x)
        return x

    def to_diag(x):
        x = jnp.concatenate([x, jnp.zeros((rows, 128), jnp.float32)], 1)
        x = skew(x, 1)
        x = jnp.concatenate([x, jnp.zeros((128 - rows, wide), jnp.float32)], 0)
        return x.T

    lane = lax.broadcasted_iota(jnp.int32, (wide, 128), 1)
    diag = lax.broadcasted_iota(jnp.int32, (wide, 128), 0)
    k_of = lane % 32
    t_of = diag - k_of
    t_len = jnp.full((wide, 128), -1, jnp.int32)
    u_len = jnp.full((wide, 128), -1, jnp.int32)
    for u in range(utts):
        mine = (lane // 32) == u
        t_len = jnp.where(mine, tlen_ref[u], t_len)
        u_len = jnp.where(mine, ulen_ref[u], u_len)
    blank = to_diag(feats_ref[0])
    label = to_diag(feats_ref[1])
    edge = jnp.full((pad, 128), NEG, jnp.float32)
    real = (t_of >= 0)
    for ref in (s_ref, l_ref, ls_ref):
        for e in range(ref.shape[0]):
            ref[e, 0:pad, :] = edge
            ref[e, pad + wide:, :] = jnp.full((ref.shape[1] - pad - wide, 128), NEG, jnp.float32)
    for e in range(reach + 1):
        dur = to_diag(feats_ref[2 + e])
        if e > 0:
            keep = real & (k_of <= u_len) & ((t_of + e < t_len) | ((t_of + e == t_len) & (k_of == u_len)))
            s_ref[e - 1, pad:pad + wide, :] = jnp.where(keep, blank + dur, NEG)
        keep = real & (k_of < u_len) & (t_of + e < t_len)
        lab = jnp.where(keep, label + dur, NEG)
        l_ref[e, pad:pad + wide, :] = lab
        ls_ref[e, pad:pad + wide, :] = pltpu.roll(lab, 1, 1)
    init_ref[pad:pad + wide, :] = jnp.where((t_of == t_len) & (k_of == u_len), 0.0, NEG)
    a_ref[...] = jnp.full(a_ref.shape, NEG, jnp.float32)
    b_ref[...] = jnp.full(b_ref.shape, NEG, jnp.float32)

    first = jnp.where((lax.broadcasted_iota(jnp.int32, (1, 128), 1) % 32 == 0)
                      & (lax.broadcasted_iota(jnp.int32, (1, 128), 1) < 32 * utts), 0.0, NEG)

    a_ref[pl.ds(pad, 1), :] = first
    last = diags

    def tree(parts, op):
        while len(parts) > 1:
            parts = [op(parts[i], parts[i + 1]) if i + 1 < len(parts) else parts[i] for i in range(0, len(parts), 2)]
        return parts[0]

    def older(hist, rolled, edge_s, edge_l):
        terms = [hist[e - 2] + edge_s(e) for e in range(2, reach + 1)]
        terms += [rolled[e - 1] + edge_l(e) for e in range(1, reach + 1)]
        top = tree(terms, jnp.maximum)
        return top, tree([jnp.exp(x - top) for x in terms], jnp.add)

    def newest(old, one, two):
        top = jnp.maximum(jnp.maximum(one, two), old[0])
        total = (jnp.exp(one - top) + jnp.exp(two - top)) + old[1] * jnp.exp(old[0] - top)
        return jnp.maximum(top + jnp.log(total), NEG)

    def step(i, carry):
        ha, hra, olda, hb, hrb, oldb = carry
        row = pad + i
        rowb = pad + last - i
        nexta = older(ha, hra, lambda e: s_ref[e - 1, pl.ds(row + 1 - e, 1), :], lambda e: ls_ref[e, pl.ds(row - e, 1), :])
        nextb = older(hb, hrb, lambda e: s_ref[e - 1, pl.ds(rowb - 1, 1), :], lambda e: l_ref[e, pl.ds(rowb - 1, 1), :])
        a = newest(olda, ha[0] + s_ref[0, pl.ds(row - 1, 1), :], hra[0] + ls_ref[0, pl.ds(row - 1, 1), :])
        b = newest(oldb, hb[0] + s_ref[0, pl.ds(rowb, 1), :], hrb[0] + l_ref[0, pl.ds(rowb, 1), :])
        b = jnp.maximum(b, init_ref[pl.ds(rowb, 1), :])
        a_ref[pl.ds(row, 1), :] = a
        b_ref[pl.ds(rowb, 1), :] = b
        ra = pltpu.roll(a, 1, 1)
        rb = pltpu.roll(b, 127, 1)
        return ((a,) + ha[:-1], (ra,) + hra[:-1], nexta, (b,) + hb[:-1], (rb,) + hrb[:-1], nextb)

    b0 = init_ref[pl.ds(pad + last, 1), :]
    b_ref[pl.ds(pad + last, 1), :] = b0
    none = a_ref[pl.ds(0, 1), :]
    first = a_ref[pl.ds(pad, 1), :]
    ha = (first,) + (none,) * (reach - 2)
    hra = (pltpu.roll(first, 1, 1),) + (none,) * (reach - 1)
    hb = (b0,) + (none,) * (reach - 2)
    hrb = (pltpu.roll(b0, 127, 1),) + (none,) * (reach - 1)
    empty = (none, none - none)
    lax.fori_loop(1, last + 1, step, (ha, hra, empty, hb, hrb, empty), unroll=4)

    zrow = b_ref[pl.ds(pad, 1), :]
    lane1 = lax.broadcasted_iota(jnp.int32, (1, 128), 1)
    z = jnp.zeros((1, 128), jnp.float32)
    for u in range(utts):
        zu = jnp.max(jnp.where(lane1 == 32 * u, zrow, 2 * NEG), axis=1, keepdims=True)
        z = jnp.where(lane1 // 32 == u, zu, z)
        prob_ref[pl.ds(u, 1), :] = jnp.broadcast_to(zu, (1, 128))

    def from_diag(x):
        x = x.T[:rows]
        return skew(x, -1)[:, :frames]

    a = a_ref[pad:pad + wide, :] - z
    g_blank = jnp.zeros((wide, 128), jnp.float32)
    g_label = jnp.zeros((wide, 128), jnp.float32)
    for e in range(reach + 1):
        bb = b_ref[pad + e + 1: pad + e + 1 + wide, :]
        pl_ = jnp.exp(a + l_ref[e, pad:pad + wide, :] + pltpu.roll(bb, 127, 1))
        g_label = g_label - pl_
        g = -pl_
        if e > 0:
            ps = jnp.exp(a + s_ref[e - 1, pad:pad + wide, :] + b_ref[pad + e: pad + e + wide, :])
            g_blank = g_blank - ps
            g = g - ps
        grads_ref[2 + e] = from_diag(g)
    grads_ref[0] = from_diag(g_blank)
    grads_ref[1] = from_diag(g_label)


def lattice(feats, t_len, u_len, slots):
    _, rows, frames = feats.shape
    wide = frames + 128
    total = wide + 16
    reach = feats.shape[0] - 3
    return pl.pallas_call(
        partial(lattice_kernel, slots),
        out_shape=(jax.ShapeDtypeStruct(feats.shape, jnp.float32), jax.ShapeDtypeStruct((8, 128), jnp.float32)),
        in_specs=[pl.BlockSpec(memory_space=pltpu.VMEM), pl.BlockSpec(memory_space=pltpu.SMEM), pl.BlockSpec(memory_space=pltpu.SMEM)],
        out_specs=(pl.BlockSpec(memory_space=pltpu.VMEM),) * 2,
        scratch_shapes=[pltpu.VMEM((reach, total, 128), jnp.float32), pltpu.VMEM((reach + 1, total, 128), jnp.float32),
                        pltpu.VMEM((reach + 1, total, 128), jnp.float32), pltpu.VMEM((total, 128), jnp.float32),
                        pltpu.VMEM((total, 128), jnp.float32), pltpu.VMEM((total, 128), jnp.float32)],
        compiler_params=pltpu.CompilerParams(vmem_limit_bytes=48 << 20),
        name="lattice",
    )(feats, t_len, u_len)


GROUP=5
CHUNK=256

def nn(a,b): return jnp.dot(a,b,preferred_element_type=jnp.float32)
def nt(a,b): return lax.dot_general(a,b,(((1,),(1,)),((),())),preferred_element_type=jnp.float32)

def fold8(x, op):
    parts=[x[i:i+8] for i in range(0,x.shape[0],8)]
    while len(parts)>1:
        parts=[op(parts[i],parts[i+1]) if i+1<len(parts) else parts[i] for i in range(0,len(parts),2)]
    return parts[0]

def joint_fwd_kernel(groups, durs, labels_ref, enc_ref, pred_ref, wt_ref, feats_ref, p_ref, tok_ref):
    step=pl.program_id(0)
    vocab=p_ref.shape[2]
    u=step//groups
    g=step%groups
    for j in range(GROUP):
        k=g*GROUP+j
        hid=jnp.tanh(enc_ref[...]+pred_ref[0,:,j:j+1]).astype(jnp.bfloat16)
        tops=[]
        for c in range(0,vocab,CHUNK):
            t=nn(wt_ref[c:c+CHUNK,:],hid)
            tok_ref[j%2,c:c+CHUNK,:]=t
            tops.append(fold8(t,jnp.maximum))
        dl=nn(wt_ref[vocab:,:],hid)[:8]
        top=jnp.max(reduce(jnp.maximum,tops),0,keepdims=True)
        sums=[]
        for c in range(0,vocab,CHUNK):
            e=jnp.exp(tok_ref[j%2,c:c+CHUNK,:]-top)
            p_ref[0,j,c:c+CHUNK,:]=e.astype(jnp.bfloat16)
            sums.append(fold8(e,jnp.add))
        total=jnp.sum(reduce(jnp.add,sums),0,keepdims=True)
        lse=top+jnp.log(total)
        row=u*32+k
        feats_ref[0,pl.ds(row,1),:]=tok_ref[j%2,0:1,:]-lse
        feats_ref[1,pl.ds(row,1),:]=tok_ref[j%2,pl.ds(labels_ref[u,k],1),:]-lse
        real=lax.broadcasted_iota(jnp.int32,dl.shape,0)<durs
        dtop=jnp.max(jnp.where(real,dl,-1e30),0,keepdims=True)
        dlse=dtop+jnp.log(jnp.sum(jnp.where(real,jnp.exp(dl-dtop),0.0),0,keepdims=True))
        dlp=dl-dlse
        for e in range(durs):
            feats_ref[2+e,pl.ds(row,1),:]=dlp[e:e+1]
        feats_ref[2+durs,pl.ds(row,1),:]=1.0/total

def joint_forward(enc_t, pred_t, labels, w_t, vocab, durs, frames):
    joint, rows=enc_t.shape
    utts,slots=labels.shape
    groups=slots//GROUP
    return pl.pallas_call(
        partial(joint_fwd_kernel,groups,durs),
        grid=(utts*groups,),
        in_specs=[pl.BlockSpec(memory_space=pltpu.SMEM),
            pl.BlockSpec((joint,frames),lambda s:(0,s//groups)),
            pl.BlockSpec((1,joint,8),lambda s:(s,0,0)),
            pl.BlockSpec(w_t.shape,lambda s:(0,0))],
        out_specs=[pl.BlockSpec((3+durs,utts*32,frames),lambda s:(0,0,0)),
            pl.BlockSpec((1,GROUP,vocab,frames),lambda s:(s,0,0,0))],
        out_shape=[jax.ShapeDtypeStruct((3+durs,utts*32,frames),jnp.float32),
            jax.ShapeDtypeStruct((utts*groups,GROUP,vocab,frames),jnp.bfloat16)],
        scratch_shapes=[pltpu.VMEM((2,vocab,frames),jnp.float32)],
        compiler_params=pltpu.CompilerParams(vmem_limit_bytes=50<<20),
        name="joint_forward",
    )(labels,enc_t,pred_t,w_t)

def joint_bwd_kernel(groups, durs, labels_ref, enc_ref, pred_ref, w_ref, feats_ref, grads_ref, p_ref, genc_ref, gpred_ref, gtok_ref, gdur_ref, h_ref, d_ref, acc_ref):
    step=pl.program_id(0)
    vocab=p_ref.shape[2]
    frames=p_ref.shape[3]
    u=step//groups
    g=step%groups

    @pl.when(step==0)
    def _():
        acc_ref[...]=jnp.zeros_like(acc_ref)
    @pl.when(g==0)
    def _():
        genc_ref[...]=jnp.zeros_like(genc_ref)
    for j in range(GROUP):
        k=g*GROUP+j
        row=u*32+k
        cols=slice(j*frames,(j+1)*frames)
        th=jnp.tanh(enc_ref[...]+pred_ref[0,:,j:j+1])
        h_ref[:,cols]=th.astype(jnp.bfloat16)
        gb=grads_ref[0,pl.ds(row,1),:]
        gl=grads_ref[1,pl.ds(row,1),:]
        scale=-(gb+gl)*feats_ref[2+durs,pl.ds(row,1),:]
        for c in range(0,vocab,CHUNK):
            d_ref[c:c+CHUNK,cols]=(p_ref[0,j,c:c+CHUNK,:].astype(jnp.float32)*scale).astype(jnp.bfloat16)
        label=labels_ref[u,k]
        def fix(base):
            v=p_ref[0,j,pl.ds(base,16),:].astype(jnp.float32)*scale
            at=lax.broadcasted_iota(jnp.int32,v.shape,0)+base
            v=v+jnp.where(at==0,gb,0.0)+jnp.where(at==label,gl,0.0)
            d_ref[pl.ds(base,16),cols]=v.astype(jnp.bfloat16)
        fix(0)
        fix(pl.multiple_of((label//16)*16,16))
        gd=[grads_ref[2+e,pl.ds(row,1),:] for e in range(durs)]
        gsum=reduce(jnp.add,gd)
        at=lax.broadcasted_iota(jnp.int32,(16,frames),0)
        dd=jnp.zeros((16,frames),jnp.float32)
        for e in range(durs):
            dd=jnp.where(at==e,gd[e]-gsum*jnp.exp(feats_ref[2+e,pl.ds(row,1),:]),dd)
        d_ref[vocab:vocab+16,cols]=dd.astype(jnp.bfloat16)
        d_ref[vocab+16:,cols]=jnp.zeros((d_ref.shape[0]-vocab-16,frames),jnp.bfloat16)
        dh=nn(w_ref[...],d_ref[:,cols])
        th=jnp.tanh(enc_ref[...]+pred_ref[0,:,j:j+1])
        dp=dh*(1.0-th*th)
        genc_ref[...]+=dp
        gpred_ref[0,:,j:j+1]=jnp.sum(dp,1,keepdims=True)
    for c in range(0,d_ref.shape[0],384):
        acc_ref[:,c:c+384]+=nt(h_ref[...],d_ref[c:c+384,:])
    @pl.when(step==pl.num_programs(0)-1)
    def _():
        gtok_ref[...]=acc_ref[:,:vocab].astype(jnp.bfloat16)
        gdur_ref[...]=acc_ref[:,vocab:].astype(jnp.bfloat16)

def joint_backward(enc_t, pred_t, labels, w, feats, grads, p, vocab, durs, frames):
    joint, rows=enc_t.shape
    utts,slots=labels.shape
    groups=slots//GROUP
    full=lambda a: pl.BlockSpec(a.shape,lambda s:(0,)*a.ndim)
    return pl.pallas_call(
        partial(joint_bwd_kernel,groups,durs),
        grid=(utts*groups,),
        in_specs=[pl.BlockSpec(memory_space=pltpu.SMEM),
            pl.BlockSpec((joint,frames),lambda s:(0,s//groups)),
            pl.BlockSpec((1,joint,8),lambda s:(s,0,0)),
            full(w),full(feats),full(grads),
            pl.BlockSpec((1,GROUP,vocab,frames),lambda s:(s,0,0,0))],
        out_specs=[pl.BlockSpec((joint,frames),lambda s:(0,s//groups)),
            pl.BlockSpec((1,joint,8),lambda s:(s,0,0)),
            pl.BlockSpec((joint,vocab),lambda s:(0,0)),
            pl.BlockSpec((joint,128),lambda s:(0,0))],
        out_shape=[jax.ShapeDtypeStruct((joint,rows),jnp.float32),
            jax.ShapeDtypeStruct((utts*groups,joint,8),jnp.float32),
            jax.ShapeDtypeStruct((joint,vocab),jnp.bfloat16),
            jax.ShapeDtypeStruct((joint,128),jnp.bfloat16)],
        scratch_shapes=[pltpu.VMEM((joint,GROUP*frames),jnp.bfloat16),
            pltpu.VMEM((vocab+128,GROUP*frames),jnp.bfloat16),
            pltpu.VMEM((joint,vocab+128),jnp.float32)],
        compiler_params=pltpu.CompilerParams(vmem_limit_bytes=56<<20),
        name="joint_backward",
    )(labels,enc_t,pred_t,w,feats,grads,p)


MESH=pl.DeviceIdType.MESH
QA = QB = 16
HALF = 2 * QA + QB
TILE = 2 * HALF


def place():
    dp=lax.axis_index("dp"); fs=lax.axis_index("fsdp")
    return dp, fs, dp//2, dp%2, fs//2, fs%2

def greet(n1, dp, fs, a, c, i1, i2):
    barrier=pltpu.get_barrier_semaphore()
    for d in range(1,n1):
        pl.semaphore_signal(barrier,inc=1,device_id=(dp,lax.rem(i1+d,n1)*2+i2),device_id_type=MESH)
    pl.semaphore_signal(barrier,inc=1,device_id=(dp,i1*2+1-i2),device_id_type=MESH)
    pl.semaphore_signal(barrier,inc=1,device_id=((1-a)*2+c,fs),device_id_type=MESH)
    pl.semaphore_signal(barrier,inc=1,device_id=(a*2+1-c,fs),device_id_type=MESH)
    pl.semaphore_wait(barrier,n1+2)

def remote(s, d, ss, rs, dev):
    return pltpu.make_async_remote_copy(src_ref=s,dst_ref=d,send_sem=ss,recv_sem=rs,device_id=dev,device_id_type=MESH)

def rows(base, size):
    return pl.ds(pl.multiple_of(base,16),size)

class Beats:
    def __init__(self, tick=None, total=0, sites=None):
        self.tick = tick
        self.total = total
        self.at = 0
        self.credit = 0.0
        self.scale = total / sites if sites else 1.0

    def grant(self, count):
        self.credit += count * self.scale
        steps = min(int(self.credit), self.total - self.at)
        self.credit -= int(self.credit)
        first = self.at
        self.at += steps
        return first, steps

    def span(self, low, high):
        def step(i, carry):
            self.tick(i)
            return carry

        lax.fori_loop(low, high, step, 0)

    def loop(self, sites, count=None):
        if self.tick is None:
            return lambda i: None
        first, steps = self.grant(sites)
        count = count or sites
        return lambda i: self.span(first + i * steps // count, first + (i + 1) * steps // count)

    def run(self, count):
        if self.tick is None:
            return
        first, steps = self.grant(count)
        if steps:
            self.span(first, first + steps)

    def until(self, step):
        if self.at < step:
            self.span(self.at, step)
            self.at = step

    def rest(self):
        self.until(self.total)


class ScatterEngine:
    def __init__(self, n1, plan, lag, srcs, out, own, gc, gx, gy, gz, gf, fin, lo, sc, rc, sx, rx, sy, ry, sz, rz, sf, rf, se, re, wo):
        dp, fs, a, c, i1, i2 = place()
        greet(n1, dp, fs, a, c, i1, i2)
        ypeer = (dp, i1 * 2 + 1 - i2)
        xpeer = ((1 - a) * 2 + c, fs)
        cpeer = (a * 2 + 1 - c, fs)
        tiles = sum(count for _, count in plan)
        main = rows(a * QA, QA + QB)
        middle = pl.ds(QA, QB)

        def quarter(aa):
            return rows(aa * (QA + QB), QA)

        def cwait(t):
            return remote(own.at[t], gc.at[t], sc.at[t], rc.at[t], cpeer)

        def xcopy(t):
            return remote(own.at[t, :, :, quarter(1 - a), :], gx.at[t], sx.at[t], rx.at[t], xpeer)

        def ycopy(t):
            return remote(own.at[t, :, 1 - i2, main, :], gy.at[t], sy.at[t], ry.at[t], ypeer)

        def zcopy(t, j):
            return remote(own.at[t, j, i2, main, :], gz.at[t, i1], sz.at[t, j], rz.at[t, i1], (dp, j * 2 + i2))

        def zin(t, j):
            return remote(own.at[t, i1, i2, main, :], gz.at[t, j], sz.at[t, j], rz.at[t, j], ypeer)

        def fcopy(t):
            return remote(own.at[t, i1, i2, main, :], gf.at[t], sf.at[t], rf.at[t], xpeer)

        def ecopy(t):
            return remote(fin.at[t, c], fin.at[t, c], se.at[t], re.at[t], cpeer)

        def ein(t):
            return remote(fin.at[t, 1 - c], fin.at[t, 1 - c], se.at[t], re.at[t], cpeer)

        def store(t):
            return pltpu.make_async_copy(fin.at[t], out.at[t], wo.at[t])

        def stage_c(t):
            first = 0
            for src, (base, count) in zip(srcs, plan):

                @pl.when((t >= first) & (t < first + count))
                def _(src=src, skip=base - first):
                    at = (t + skip) * TILE
                    pltpu.make_async_copy(src.at[:, :, rows(at + c * HALF, HALF), :], own.at[t], lo.at[t]).start()
                    remote(src.at[:, :, rows(at + (1 - c) * HALF, HALF), :], gc.at[t], sc.at[t], rc.at[t], cpeer).start()

                first += count

        def stage_x(t):
            pltpu.make_async_copy(own.at[t], own.at[t], lo.at[t]).wait()
            cwait(t).wait_recv()
            own[t] = own[t] + gc[t]
            xcopy(t).start()

        def stage_y(t):
            xcopy(t).wait_recv()
            own[t, :, :, quarter(a), :] = own[t, :, :, quarter(a), :] + gx[t]
            ycopy(t).start()

        def stage_z(t):
            ycopy(t).wait_recv()
            own[t, :, i2, main, :] = own[t, :, i2, main, :] + gy[t]
            for d in range(1, n1):
                zcopy(t, lax.rem(i1 + d, n1)).start()

        def stage_f(t):
            total = own[t, i1, i2, main, :].astype(jnp.float32)
            for d in range(1, n1):
                j = lax.rem(i1 + n1 - d, n1)
                zin(t, j).wait_recv()
                total = total + gz[t, j].astype(jnp.float32)
            own[t, i1, i2, main, :] = total.astype(jnp.bfloat16)
            fcopy(t).start()

        def stage_e(t):
            fcopy(t).wait_recv()
            fin[t, c, quarter(a), :] = own[t, i1, i2, quarter(a), :]
            fin[t, c, quarter(1 - a), :] = gf[t, rows((1 - a) * QB, QA), :]
            fin[t, c, middle, :] = own[t, i1, i2, middle, :] + gf[t, rows(a * QA, QB), :]
            ecopy(t).start()

        def stage_o(t):
            ein(t).wait_recv()
            ecopy(t).wait_send()
            store(t).start()

        stages = (stage_c, stage_x, stage_y, stage_z, stage_f, stage_e, stage_o)

        def tick(tau):
            for place_of, stage in enumerate(stages):
                t = tau - place_of * lag

                @pl.when((t >= 0) & (t < tiles))
                def _(stage=stage, t=t):
                    stage(t)

        def finish():
            def tile(t, carry):
                cwait(t).wait_send()
                xcopy(t).wait_send()
                ycopy(t).wait_send()
                for d in range(1, n1):
                    zcopy(t, lax.rem(i1 + d, n1)).wait_send()
                fcopy(t).wait_send()
                store(t).wait()
                return carry

            lax.fori_loop(0, tiles, tile, 0)

        self.tick = tick
        self.total = tiles + (len(stages) - 1) * lag
        self.finish = finish


def scatter_plan(sources):
    return tuple((first, count) for _, first, count in sources)


def scatter_scratch(n, tiles):
    n1 = n // 2
    dma = pltpu.SemaphoreType.DMA
    v = lambda *shape: pltpu.VMEM((tiles,) + shape + (WIDE,), jnp.bfloat16)
    one = dma((tiles,))
    return [
        v(n1, 2, HALF), v(n1, 2, HALF), v(n1, 2, QA), v(n1, QA + QB), v(n1, QA + QB), v(QA + QB), v(2, HALF),
        one, one, one, one, one, one, one, dma((tiles, n1)), dma((tiles, n1)), one, one, one, one, one,
    ]


def riding_kernel(kernel, counts, plan, lag, n1, sites, *refs):
    n_in, n_out, n_scratch = counts
    k = len(plan)
    ins, refs = refs[:n_in], refs[n_in:]
    srcs, refs = refs[:k], refs[k:]
    outs, refs = refs[:n_out], refs[n_out:]
    share, refs = refs[0], refs[1:]
    scratch, refs = refs[:n_scratch], refs[n_scratch:]
    engine = ScatterEngine(n1, plan, lag, srcs, share, *refs)
    beats = Beats(engine.tick, engine.total, sites)
    kernel(beats, *ins, *outs, *scratch)
    beats.rest()
    engine.finish()


def call(kernel, args, in_specs, out_specs, out_shape, scratch, name, ride=None, collective_id=None, sites=None, lag=2):
    if not ride:
        return pl.pallas_call(
            partial(kernel, Beats()),
            in_specs=in_specs,
            out_specs=out_specs,
            out_shape=out_shape,
            scratch_shapes=scratch,
            compiler_params=pltpu.CompilerParams(vmem_limit_bytes=60 << 20),
            name=name,
        )(*args)
    n = lax.axis_size("fsdp")
    tiles = sum(count for _, _, count in ride)
    counts = (len(args), len(out_shape), len(scratch))
    *outs, share = pl.pallas_call(
        partial(riding_kernel, kernel, counts, scatter_plan(ride), lag, n // 2, sites),
        in_specs=in_specs + [ANY_SPEC] * len(ride),
        out_specs=out_specs + [ANY_SPEC],
        out_shape=out_shape + [sds((tiles, 2, HALF, WIDE), BF16)],
        scratch_shapes=scratch + scatter_scratch(n, tiles),
        compiler_params=pltpu.CompilerParams(collective_id=collective_id, has_side_effects=True, vmem_limit_bytes=61 << 20),
        name=name + "_and_scatter",
    )(*args, *[grads.reshape(n // 2, 2, -1, WIDE) for grads, _, _ in ride])
    return outs, share.reshape(tiles * TILE, WIDE)


def idle_kernel(beats):
    pass


def scatter(ride, collective_id):
    return call(idle_kernel, [], [], [], [], [], "idle", ride, collective_id)[1]


def pooled(parts):
    counts = [x[8:9] for x in parts]
    count = sum(counts[1:], counts[0])
    mean = sum((x[0:4] * n for x, n in zip(parts[1:], counts[1:])), parts[0][0:4] * counts[0]) / count
    dev = jnp.zeros_like(mean)
    for x, n in zip(parts, counts):
        gap = x[0:4] - mean
        dev = dev + (x[4:8] + gap * gap * n)
    return mean, dev, count


def exchange_kernel(kind, groups, n, x_ref, out_ref, near, far, s1, r1, s2, r2):
    dp = lax.axis_index("dp")
    fs = lax.axis_index("fsdp")
    barrier = pltpu.get_barrier_semaphore()
    for d in range(1, groups):
        pl.semaphore_signal(barrier, inc=1, device_id=(lax.rem(dp + d, groups), fs), device_id_type=MESH)
    for d in range(1, n):
        pl.semaphore_signal(barrier, inc=1, device_id=(dp, lax.rem(fs + d, n)), device_id_type=MESH)
    pl.semaphore_wait(barrier, groups + n - 2)

    def merge(ref, members):
        if kind == "sum":
            total = ref[0]
            for i in range(1, members):
                total = total + ref[i]
            return total
        mean, dev, count = pooled([ref[i] for i in range(members)])
        return jnp.concatenate([mean, dev, jnp.broadcast_to(count, (8, 128))], 0)

    near[dp] = x_ref[...]
    first = []
    for d in range(1, groups):
        cp = remote(near.at[dp], near.at[dp], s1.at[d], r1.at[dp], (lax.rem(dp + d, groups), fs))
        cp.start()
        first.append(cp)
    for d in range(1, groups):
        other = lax.rem(dp + d, groups)
        remote(near.at[dp], near.at[other], s1.at[d], r1.at[other], (other, fs)).wait_recv()
    far[fs] = merge(near, groups)
    for d in range(1, n):
        cp = remote(far.at[fs], far.at[fs], s2.at[d], r2.at[fs], (dp, lax.rem(fs + d, n)))
        cp.start()
        first.append(cp)
    for d in range(1, n):
        other = lax.rem(fs + d, n)
        remote(far.at[fs], far.at[other], s2.at[d], r2.at[other], (dp, other)).wait_recv()
    out_ref[...] = merge(far, n)
    for cp in first:
        cp.wait_send()


def exchange(x, kind, collective_id):
    n = lax.axis_size("fsdp")
    groups = lax.axis_size("dp")
    dma = pltpu.SemaphoreType.DMA
    return pl.pallas_call(
        partial(exchange_kernel, kind, groups, n),
        out_shape=jax.ShapeDtypeStruct(x.shape, x.dtype),
        in_specs=[pl.BlockSpec(memory_space=pltpu.VMEM)],
        out_specs=pl.BlockSpec(memory_space=pltpu.VMEM),
        scratch_shapes=[
            pltpu.VMEM((groups,) + x.shape, x.dtype),
            pltpu.VMEM((n,) + x.shape, x.dtype),
            dma((groups,)), dma((groups,)), dma((n,)), dma((n,)),
        ],
        compiler_params=pltpu.CompilerParams(collective_id=collective_id, has_side_effects=True),
        name="exchange_" + kind,
    )(x)


CHUNK_ROWS = 64
WIDE = 512
PLACE = ("p_out", "s_in", "s_out", "p_in", "w_proj", "w_joint", "f_in", "f_out")


def tn(a, b):
    return lax.dot_general(a, b, (((0,), (0,)), ((), ())), preferred_element_type=jnp.float32)


def row_loop(count, body, init=0):
    def step(i, carry):
        return body(pl.ds(pl.multiple_of(i * CHUNK_ROWS, CHUNK_ROWS), CHUNK_ROWS), i, carry)

    return lax.fori_loop(0, count // CHUNK_ROWS, step, init)


def ln_parts(v):
    centred = v - jnp.mean(v, -1, keepdims=True)
    rstd = lax.rsqrt(jnp.mean(centred * centred, -1, keepdims=True) + EPS)
    return centred * rstd, rstd


def ln_back(v, gain, grad):
    hat, rstd = ln_parts(v)
    dy = grad * gain
    dv = rstd * (dy - jnp.mean(dy, -1, keepdims=True) - hat * jnp.mean(dy * hat, -1, keepdims=True))
    return dv, fold8(grad * hat, jnp.add)


def offsets(n, width, ff):
    low = width // n
    tall = ff // n
    sizes = {
        "p_out": low, "s_in": low * (ff // WIDE), "s_out": tall, "p_in": 2 * low,
        "w_proj": low, "w_joint": 3 * low, "f_in": low * (ff // WIDE), "f_out": tall,
    }
    table = {}
    at = 0
    for name in PLACE:
        table[name] = at
        at += sizes[name]
    return table, at


class Mover:
    def __init__(self, sems, used=0):
        self.sems = sems
        self.used = used
        self.pending = []

    def take(self):
        self.used += 1
        return self.sems.at[self.used - 1]

    def load(self, src, dst):
        cp = pltpu.make_async_copy(src, dst, self.take())
        cp.start()
        return cp

    def put(self, src, dst):
        cp = pltpu.make_async_copy(src, dst, self.take())
        cp.start()
        self.pending.append(cp)

    def load_weight(self, whole, at, dst):
        flat = len(whole.shape) == 3
        n = whole.shape[0] if flat else 2 * whole.shape[0]
        height = dst.shape[0] // n
        sem = self.take()

        def one(s, carry):
            for b in range(dst.shape[1] // WIDE):
                pltpu.make_async_copy(
                    (whole.at[s] if flat else whole.at[s // 2, s % 2]).at[pl.ds(at + b * height, height), :],
                    dst.at[pl.ds(pl.multiple_of(s * height, 16), height), pl.ds(b * WIDE, WIDE)],
                    sem,
                ).start()
            return carry

        lax.fori_loop(0, n, one, 0)
        return pltpu.make_async_copy(dst, dst, sem)

    def put_weight(self, src, grads, at):
        n = grads.shape[0]
        height = src.shape[0] // n
        sem = self.take()

        def one(s, carry):
            for b in range(src.shape[1] // WIDE):
                pltpu.make_async_copy(
                    src.at[pl.ds(pl.multiple_of(s * height, 16), height), pl.ds(b * WIDE, WIDE)],
                    grads.at[s, pl.ds(at + b * height, height), :],
                    sem,
                ).start()
            return carry

        lax.fori_loop(0, n, one, 0)
        self.pending.append(pltpu.make_async_copy(src, src, sem))

    def finish(self):
        for cp in self.pending:
            cp.wait()
        self.pending = []


def valid_rows_of(t_ref, frames, i):
    per = frames // CHUNK_ROWS
    t_len = t_ref[i // per]
    at = lax.broadcasted_iota(jnp.int32, (CHUNK_ROWS, 1), 0) + lax.rem(i, per) * CHUNK_ROWS
    return jnp.where(at < t_len, 1.0, 0.0)


def write_rows(out, base, vec):
    for i in range(vec.shape[1] // 128):
        out[base + i : base + i + 1, :] = vec[:, i * 128 : (i + 1) * 128]


def read_rows(ref, base, width):
    return jnp.concatenate([ref[base + i : base + i + 1, :] for i in range(width // 128)], 1)


def fill_gated(utts, frames, t_ref, r, gp):
    width = gp.shape[1]
    span = frames + 16
    per = frames // CHUNK_ROWS
    for u in range(utts):
        gp[u * span : u * span + 8, :] = jnp.zeros((8, width), jnp.float32)
        gp[u * span + 8 + frames : (u + 1) * span, :] = jnp.zeros((8, width), jnp.float32)

    def gate(rr, i, c):
        g = r[rr, :width] * jax.nn.sigmoid(r[rr, width:]) * valid_rows_of(t_ref, frames, i)
        at = (i // per) * span + 8 + lax.rem(i, per) * CHUNK_ROWS
        gp[pl.ds(pl.multiple_of(at, 8), CHUNK_ROWS), :] = g
        return c

    row_loop(utts * frames, gate)


def window(gp, frames, i):
    per = frames // CHUNK_ROWS
    at = (i // per) * (frames + 16) + lax.rem(i, per) * CHUNK_ROWS
    return gp[pl.ds(pl.multiple_of(at, 8), CHUNK_ROWS + 16), :]


def spread(gp, utts, frames, i, taps, flip=False):
    win = window(gp, frames, i)
    count = taps.shape[0]
    total = None
    for j in range(count):
        shift = 8 - count // 2 + (count - 1 - j if flip else j)
        term = win[shift : shift + CHUNK_ROWS] * taps[j : j + 1]
        total = term if total is None else total + term
    return total


def ffn_bwd(rows, v_ref, gain, w_in, w_out, h, loads, g_ref, gb, normed, dact, act, dh, dn, dw_in, dw_out, mover, grads, at_in, at_out, beats):
    def prepare(rr, i, c):
        normed[rr, :] = (ln_parts(v_ref[rr, :].astype(jnp.float32))[0] * gain).astype(jnp.bfloat16)
        gb[rr, :] = (0.5 * g_ref[rr, :]).astype(jnp.bfloat16)
        return c

    row_loop(rows, prepare)
    w_out[1].wait()
    for b in range(h.shape[0]):
        cols = slice(b * WIDE, (b + 1) * WIDE)
        dact[...] = nt(gb[...], w_out[0][cols, :])
        beats.run(1)
        loads[b].wait()

        def slope(rr, i, c):
            v = h[b, rr, :]
            sg = jax.nn.sigmoid(v)
            act[rr, :] = (v * sg).astype(jnp.bfloat16)
            dh[rr, cols] = (dact[rr, :] * (sg * (1.0 + v * (1.0 - sg)))).astype(jnp.bfloat16)
            return c

        row_loop(rows, slope)
        beats.run(1)
        dw_out[cols, :] = tn(act[...], gb[...]).astype(jnp.bfloat16)
        beats.run(1)
        dw_in[:, cols] = tn(normed[...], dh[:, cols]).astype(jnp.bfloat16)
        beats.run(1)
    mover.put_weight(dw_out, grads, at_out)
    mover.put_weight(dw_in, grads, at_in)
    w_in[1].wait()
    dn[...] = nt(dh[...], w_in[0][...])
    beats.run(2)

    def back(rr, i, total):
        dv, dg = ln_back(v_ref[rr, :].astype(jnp.float32), gain, dn[rr, :])
        g_ref[rr, :] = g_ref[rr, :] + dv
        return total + dg

    return row_loop(rows, back, jnp.zeros((8, g_ref.shape[1]), jnp.float32))


def down(folded):
    return jnp.sum(folded, 0, keepdims=True)


def back_one_kernel(table, held, beats, grad_ref, y4_ref, y3_ref, d_ref, pooled_ref, small, whole, h_hbm, g_out, db_out, grads, sums, gain_out,
                    w_pout, w_sin, w_sout, g, gb, normed, dact, act, dh, dn, dw_in, dw_out, dw_pout, h, db, sems):
    rows, width = g.shape
    mover = Mover(sems)
    gains = small[...]
    sout = mover.load_weight(whole, held["s_out"], w_sout)
    loads = [mover.load(h_hbm.at[b], h.at[b]) for b in range(h.shape[0])]
    sin = mover.load_weight(whole, held["s_in"], w_sin)
    wo = mover.load_weight(whole, held["p_out"], w_pout)
    beats.run(5)

    def first(rr, i, total):
        dv, dg = ln_back(y4_ref[rr, :], gains[4:5], grad_ref[rr, :])
        g[rr, :] = dv
        return total + dg

    gain4 = down(row_loop(rows, first, jnp.zeros((8, width), jnp.float32)))
    gain3 = down(ffn_bwd(rows, y3_ref, gains[3:4], (w_sin, sin), (w_sout, sout), h, loads, g, gb, normed, dact, act, dh, dn,
                         dw_in, dw_out, mover, grads, table["s_in"], table["s_out"], beats))
    mover.put(g, g_out)
    gain_out[...] = jnp.concatenate([gain3, gain4, jnp.zeros((6, width), jnp.float32)], 0)
    mean = read_rows(pooled_ref, 0, width)
    istd = lax.rsqrt(read_rows(pooled_ref, 4, width) / pooled_ref[8:9, 0:1] + EPS)

    def cast(rr, i, c):
        gb[rr, :] = g[rr, :].astype(jnp.bfloat16)
        return c

    row_loop(rows, cast)
    wo.wait()
    dact[...] = nt(gb[...], w_pout[...])
    beats.run(1)

    def bn(rr, i, totals):
        z = (d_ref[rr, :] - mean) * istd
        b = z * gains[14:15] + gains[15:16]
        sg = jax.nn.sigmoid(b)
        act[rr, :] = (b * sg).astype(jnp.bfloat16)
        db_chunk = dact[rr, :] * (sg * (1.0 + b * (1.0 - sg)))
        db[rr, :] = db_chunk
        return totals[0] + fold8(db_chunk, jnp.add), totals[1] + fold8(db_chunk * z, jnp.add)

    zero = jnp.zeros((8, width), jnp.float32)
    one, two = row_loop(rows, bn, (zero, zero))
    beats.run(2)
    mover.put(db, db_out)
    write_rows(sums, 0, down(one))
    write_rows(sums, 4, down(two))
    sums[8:16, :] = jnp.zeros((8, 128), jnp.float32)
    dw_pout[...] = tn(act[...], gb[...]).astype(jnp.bfloat16)
    mover.put_weight(dw_pout, grads, table["p_out"])
    mover.finish()


def back_two_kernel(utts, table, held, start, end, beats, t_ref, x_ref, y1_ref, y2_ref, r_ref, t_in, c_ref, d_ref, db_ref, g_in, pooled_ref, sums_ref, late_ref, small, whole, h_hbm,
                    g_out, grads,
                    w_pin, w_proj, w_joint, w_fin, w_fout, g, gb, normed, dact, act, dh, dn, dw_pin, dw_proj, dw_joint, dw_in, dw_out, h, gp, dd, dr, dt, sm, sems):
    rows, width = g.shape
    frames = rows // utts
    mover = Mover(sems)
    gains = small[...]
    wi = mover.load_weight(whole, held["p_in"], w_pin)
    wp = mover.load_weight(whole, held["w_proj"], w_proj)
    wj = mover.load_weight(whole, held["w_joint"], w_joint)
    fout = mover.load_weight(whole, held["f_out"], w_fout)
    loads = [mover.load(h_hbm.at[b], h.at[b]) for b in range(h.shape[0])]
    fin = mover.load_weight(whole, held["f_in"], w_fin)
    mean = read_rows(pooled_ref, 0, width)
    count = pooled_ref[8:9, 0:1]
    istd = lax.rsqrt(read_rows(pooled_ref, 4, width) / count + EPS)
    bias_sum = read_rows(sums_ref, 0, width)
    gain_sum = read_rows(sums_ref, 4, width)
    taps = gains[5:14]
    ntaps = taps.shape[0]
    span = frames + 16
    per = frames // CHUNK_ROWS
    beats.run(5)
    fill_gated(utts, frames, t_ref, r_ref, gp)
    beats.run(1)
    for u in range(utts):
        dd[u * span : u * span + 8, :] = jnp.zeros((8, width), jnp.float32)
        dd[u * span + 8 + frames : (u + 1) * span, :] = jnp.zeros((8, width), jnp.float32)

    def bn(rr, i, c):
        z = (d_ref[rr, :] - mean) * istd
        v = gains[14:15] * istd * (db_ref[rr, :] - valid_rows_of(t_ref, frames, i) * (bias_sum + z * gain_sum) / count)
        at = (i // per) * span + 8 + lax.rem(i, per) * CHUNK_ROWS
        dd[pl.ds(pl.multiple_of(at, 8), CHUNK_ROWS), :] = v
        return c

    row_loop(rows, bn)

    def conv(rr, i, totals):
        dg = spread(dd, utts, frames, i, taps, True) * valid_rows_of(t_ref, frames, i)
        sg = jax.nn.sigmoid(r_ref[rr, width:])
        dr[rr, :width] = (dg * sg).astype(jnp.bfloat16)
        dr[rr, width:] = (dg * r_ref[rr, :width] * sg * (1.0 - sg)).astype(jnp.bfloat16)
        win = window(gp, frames, i)
        mine = window(dd, frames, i)[8 : 8 + CHUNK_ROWS]
        normed[rr, :] = (ln_parts(y2_ref[rr, :])[0] * gains[2:3]).astype(jnp.bfloat16)
        return tuple(
            totals[j] + fold8(win[8 - ntaps // 2 + j : 8 - ntaps // 2 + j + CHUNK_ROWS] * mine, jnp.add) for j in range(ntaps)
        )

    zero = jnp.zeros((8, width), jnp.float32)
    tap_grads = [down(x) for x in row_loop(rows, conv, (zero,) * ntaps)]
    beats.run(2)
    for b in range(2):
        cols = slice(b * width, (b + 1) * width)
        dw_pin[:, cols] = tn(normed[...], dr[:, cols]).astype(jnp.bfloat16)
    mover.put_weight(dw_pin, grads, table["p_in"] - start)
    beats.run(2)
    wi.wait()
    dn[...] = nt(dr[...], w_pin[...])
    beats.run(1)

    def back_conv(rr, i, total):
        dv, dg = ln_back(y2_ref[rr, :], gains[2:3], dn[rr, :])
        v = g_in[rr, :] + dv
        g[rr, :] = v
        gb[rr, :] = v.astype(jnp.bfloat16)
        normed[rr, :] = (ln_parts(y1_ref[rr, :])[0] * gains[1:2]).astype(jnp.bfloat16)
        return total + dg

    gain2 = down(row_loop(rows, back_conv, zero))
    dw_proj[...] = tn(c_ref[...], gb[...]).astype(jnp.bfloat16)
    mover.put_weight(dw_proj, grads, table["w_proj"] - start)
    beats.run(1)
    wp.wait()
    act[...] = nt(gb[...], w_proj[...]).astype(jnp.bfloat16)
    pairs = width // 128
    side = lax.broadcasted_iota(jnp.int32, (frames, 128), 1) < 64
    key_at = lax.broadcasted_iota(jnp.int32, (frames, 1), 0)
    hook = beats.loop(utts * pairs)

    def pair_step(m, carry):
        hook(m)
        u = m // pairs
        base = lax.rem(m, pairs) * 128
        rr = pl.ds(pl.multiple_of(u * frames, frames), frames)
        at = [pl.ds(pl.multiple_of(base + b * width, 128), 128) for b in range(3)]
        bias = jnp.where(key_at < t_ref[u], 0.0, MASKED)
        q = t_in[rr, at[0]]
        k = t_in[rr, at[1]]
        v = t_in[rr, at[2]]
        dc = act[rr, at[0]]
        got = []
        for half in range(2):
            mine = side if half == 0 else ~side
            nothing = jnp.zeros_like(k)
            s = nt(jnp.where(mine, k, nothing), q) * 0.125 + bias
            p = jnp.exp(s - jnp.max(s, 0, keepdims=True))
            p = p * (1.0 / jnp.sum(p, 0, keepdims=True))
            dp = nt(jnp.where(mine, v, nothing), dc)
            ds = (p * (dp - jnp.sum(dp * p, 0, keepdims=True))).astype(jnp.bfloat16)
            got.append((tn(ds, k) * 0.125, nn(ds, q) * 0.125, nn(p.astype(jnp.bfloat16), dc)))
        for b in range(3):
            dt[rr, at[b]] = jnp.where(side, got[0][b], got[1][b]).astype(jnp.bfloat16)
        return carry

    lax.fori_loop(0, utts * pairs, pair_step, 0)
    for b in range(3):
        cols = slice(b * width, (b + 1) * width)
        dw_joint[:, cols] = tn(normed[...], dt[:, cols]).astype(jnp.bfloat16)
    mover.put_weight(dw_joint, grads, table["w_joint"] - start)
    beats.run(2)
    wj.wait()
    dn[...] = nt(dt[...], w_joint[...])
    beats.run(1)

    def back_attend(rr, i, total):
        dv, dg = ln_back(y1_ref[rr, :], gains[1:2], dn[rr, :])
        g[rr, :] = g[rr, :] + dv
        return total + dg

    gain1 = down(row_loop(rows, back_attend, zero))
    gain0 = down(ffn_bwd(rows, x_ref, gains[0:1], (w_fin, fin), (w_fout, fout), h, loads, g, gb, normed, dact, act, dh, dn,
                         dw_in, dw_out, mover, grads, table["f_in"] - start, table["f_out"] - start, beats))
    mover.put(g, g_out)
    packed = jnp.concatenate([gain0, gain1, gain2, late_ref[0:2, :]] + tap_grads + [jnp.zeros((2, width), jnp.float32)], 0)
    n = grads.shape[0]
    low = width // n
    for s in range(n):
        sm[s] = jnp.concatenate([packed[:, s * low : (s + 1) * low], jnp.zeros((16, WIDE - low), jnp.float32)], 1).astype(jnp.bfloat16)
    mover.put(sm, grads.at[:, pl.ds(end - start, 16), :])
    mover.finish()


VMEM_SPEC = pl.BlockSpec(memory_space=pltpu.VMEM)
SMEM_SPEC = pl.BlockSpec(memory_space=pltpu.SMEM)
ANY_SPEC = pl.BlockSpec(memory_space=pl.ANY)
F32 = jnp.float32
BF16 = jnp.bfloat16


def sds(shape, dtype=jnp.float32):
    return jax.ShapeDtypeStruct(shape, dtype)


def tiled(count):
    return -(-count // TILE) * TILE


def back_one(grad, y4, y3, d, pooled, small, whole, h, ff, held, ride=None, collective_id=None):
    rows, width = grad.shape
    n = whole.shape[0]
    table, _ = offsets(n, width, ff)
    nb = ff // WIDE
    v = pltpu.VMEM
    return call(
        partial(back_one_kernel, table, held),
        (grad, y4, y3, d, pooled, small, whole, h),
        [VMEM_SPEC] * 6 + [ANY_SPEC] * 2,
        [ANY_SPEC] * 3 + [VMEM_SPEC] * 2,
        [sds((rows, width)), sds((rows, width)), sds((n, tiled(table["p_in"]), WIDE), BF16), sds((16, 128)), sds((8, width))],
        [v((width, width), BF16), v((width, ff), BF16), v((ff, width), BF16), v((rows, width), F32),
         v((rows, width), BF16), v((rows, width), BF16), v((rows, width), F32), v((rows, width), BF16),
         v((rows, ff), BF16), v((rows, width), F32), v((width, ff), BF16), v((ff, width), BF16),
         v((width, width), BF16), v((nb, rows, WIDE), F32), v((rows, width), F32), pltpu.SemaphoreType.DMA((16,))],
        "back_part_one",
        ride,
        collective_id,
        28,
    )


def back_two(t_len, x, y1, y2, r, t, c, d, db, g, pooled, sums, late, small, whole, h, ff, held, ride=None, collective_id=None):
    rows, width = d.shape
    utts = t_len.shape[0]
    n = whole.shape[0]
    table, end = offsets(n, width, ff)
    start = table["p_in"]
    nb = ff // WIDE
    v = pltpu.VMEM
    pad_rows = utts * (rows // utts + 16)
    return call(
        partial(back_two_kernel, utts, table, held, start, end),
        (t_len, x, y1, y2, r, t, c, d, db, g, pooled, sums, late, small, whole, h),
        [SMEM_SPEC] + [VMEM_SPEC] * 13 + [ANY_SPEC] * 2,
        [ANY_SPEC] * 2,
        [sds((rows, width)), sds((n, tiled(end - start + 16), WIDE), BF16)],
        [v((width, 2 * width), BF16), v((width, width), BF16), v((width, 3 * width), BF16), v((width, ff), BF16),
         v((ff, width), BF16), v((rows, width), F32), v((rows, width), BF16), v((rows, width), BF16),
         v((rows, width), F32), v((rows, width), BF16), v((rows, ff), BF16), v((rows, width), F32),
         v((width, 2 * width), BF16), v((width, width), BF16), v((width, 3 * width), BF16), v((width, ff), BF16),
         v((ff, width), BF16), v((nb, rows, WIDE), F32), v((pad_rows, width), F32), v((pad_rows, width), F32),
         v((rows, 2 * width), BF16), v((rows, 3 * width), BF16), v((n, 16, WIDE), BF16), pltpu.SemaphoreType.DMA((20,))],
        "back_part_two",
        ride,
        collective_id,
        44,
    )


FIRST = ("small", "f_in", "f_out", "w_joint", "w_proj", "p_in", "p_out", "s_in", "s_out")


def gathered_rows(n, width, ff, layers):
    low = width // n
    tall = ff // n
    sizes = {
        "f_in": low * (ff // WIDE), "f_out": tall, "small": 16, "w_joint": 3 * low, "w_proj": low,
        "p_in": 2 * low, "p_out": low, "s_in": low * (ff // WIDE), "s_out": tall,
    }
    tables = []
    at = 0
    for layer in range(layers):
        table = {}
        for name in FIRST:
            table[name] = (at, at + sizes[name])
            at += sizes[name]
        tables.append(table)
    return tables, at


class GatherEngine:
    def __init__(self, n1, tiles, lag, packed, out, so, sz, rz, sy, ry, sx, rx, sc, rc):
        dp, fs, a, c, i1, i2 = place()
        ypeer = (dp, i1 * 2 + 1 - i2)
        xpeer = ((1 - a) * 2 + c, fs)
        cpeer = (a * 2 + 1 - c, fs)

        def main(t):
            return rows(t * TILE + c * HALF + a * QA, QA + QB)

        def quarter(t, aa):
            return rows(t * TILE + c * HALF + aa * (QA + QB), QA)

        def half(t, cc):
            return rows(t * TILE + cc * HALF, HALF)

        def local(t):
            return pltpu.make_async_copy(packed.at[main(t), :], out.at[i1, i2, main(t), :], so.at[t])

        def zcopy(t, j):
            return remote(packed.at[main(t), :], out.at[i1, i2, main(t), :], sz.at[t, j], rz.at[t, i1], (dp, j * 2 + i2))

        def zin(t, j):
            return remote(packed.at[main(t), :], out.at[j, i2, main(t), :], sz.at[t, j], rz.at[t, j], ypeer)

        def ycopy(t):
            return remote(out.at[:, i2, main(t), :], out.at[:, i2, main(t), :], sy.at[t], ry.at[t], ypeer)

        def yin(t):
            return remote(out.at[:, i2, main(t), :], out.at[:, 1 - i2, main(t), :], sy.at[t], ry.at[t], ypeer)

        def xcopy(t):
            return remote(out.at[:, :, quarter(t, a), :], out.at[:, :, quarter(t, a), :], sx.at[t], rx.at[t], xpeer)

        def xin(t):
            return remote(out.at[:, :, quarter(t, a), :], out.at[:, :, quarter(t, 1 - a), :], sx.at[t], rx.at[t], xpeer)

        def ccopy(t):
            return remote(out.at[:, :, half(t, c), :], out.at[:, :, half(t, c), :], sc.at[t], rc.at[t], cpeer)

        def cin(t):
            return remote(out.at[:, :, half(t, c), :], out.at[:, :, half(t, 1 - c), :], sc.at[t], rc.at[t], cpeer)

        def stage_z(t):
            for d in range(1, n1):
                zcopy(t, lax.rem(i1 + d, n1)).start()
            local(t).start()

        def stage_y(t):
            local(t).wait()
            for d in range(1, n1):
                zin(t, lax.rem(i1 + n1 - d, n1)).wait_recv()
            ycopy(t).start()

        def stage_x(t):
            yin(t).wait_recv()
            xcopy(t).start()

        def stage_c(t):
            xin(t).wait_recv()
            ccopy(t).start()

        def stage_o(t):
            cin(t).wait_recv()

        stages = (stage_z, stage_y, stage_x, stage_c, stage_o)

        def tick(tau):
            for place_of, stage in enumerate(stages):
                t = tau - place_of * lag

                @pl.when((t >= 0) & (t < tiles))
                def _(stage=stage, t=t):
                    stage(t)

        def finish():
            def tile(t, carry):
                for d in range(1, n1):
                    zcopy(t, lax.rem(i1 + d, n1)).wait_send()
                ycopy(t).wait_send()
                xcopy(t).wait_send()
                ccopy(t).wait_send()
                return carry

            lax.fori_loop(0, tiles, tile, 0)

        self.tick = tick
        self.total = tiles + (len(stages) - 1) * lag
        self.after = lambda end: -(-end // TILE) + (len(stages) - 1) * lag
        self.finish = finish


class Exchange:
    def __init__(self, groups, n, near, far, s1, r1, s2, r2):
        self.groups, self.n = groups, n
        self.near, self.far = near, far
        self.sems = (s1, r1, s2, r2)

    def merge(self, ref, members):
        mean, dev, count = pooled([ref[i] for i in range(members)])
        return jnp.concatenate([mean, dev, jnp.broadcast_to(count, (8, 128))], 0)

    def run(self, x, beats):
        dp = lax.axis_index("dp")
        fs = lax.axis_index("fsdp")
        near, far, groups, n = self.near, self.far, self.groups, self.n
        s1, r1, s2, r2 = self.sems
        near[dp] = x
        sent = []
        for d in range(1, groups):
            cp = remote(near.at[dp], near.at[dp], s1.at[d], r1.at[dp], (lax.rem(dp + d, groups), fs))
            cp.start()
            sent.append(cp)
        beats.run(1)
        for d in range(1, groups):
            other = lax.rem(dp + d, groups)
            remote(near.at[dp], near.at[other], s1.at[d], r1.at[other], (other, fs)).wait_recv()
        far[fs] = self.merge(near, groups)
        for d in range(1, n):
            cp = remote(far.at[fs], far.at[fs], s2.at[d], r2.at[fs], (dp, lax.rem(fs + d, n)))
            cp.start()
            sent.append(cp)
        beats.run(1)
        for d in range(1, n):
            other = lax.rem(fs + d, n)
            remote(far.at[fs], far.at[other], s2.at[d], r2.at[other], (dp, other)).wait_recv()
        for cp in sent:
            cp.wait_send()
        return self.merge(far, n)


def meet(groups, n):
    dp = lax.axis_index("dp")
    fs = lax.axis_index("fsdp")
    barrier = pltpu.get_barrier_semaphore()
    for d in range(1, groups):
        pl.semaphore_signal(barrier, inc=1, device_id=(lax.rem(dp + d, groups), fs), device_id_type=MESH)
    for d in range(1, n):
        pl.semaphore_signal(barrier, inc=1, device_id=(dp, lax.rem(fs + d, n)), device_id_type=MESH)
    return lambda: pl.semaphore_wait(barrier, groups + n - 2)


def pack_into(out, src, tables, joint_at, layers):
    for layer in range(layers):
        for name in FIRST:
            base, stop = tables[layer][name]
            if name == "small":
                small = [src["gains"][layer], src["taps"][layer], src["bn_gain"][layer : layer + 1, :], src["bn_bias"][layer : layer + 1, :]]
                small = jnp.concatenate([x.astype(jnp.float32) for x in small], 0)
                small = jnp.concatenate([small, jnp.zeros((16, WIDE - small.shape[1]), jnp.float32)], 1)
                out[base:stop, :] = small.astype(jnp.bfloat16)
                continue
            ref = src[name]
            height = ref.shape[1]
            for b in range(ref.shape[2] // WIDE):
                out[base + b * height : base + (b + 1) * height, :] = ref[layer, :, b * WIDE : (b + 1) * WIDE]
    enc, pred, tok, dur = src["enc"], src["pred"], src["tok"], src["dur"]
    low, tall = enc.shape[0], pred.shape[0]
    at = joint_at
    out[at : at + low, :] = enc[:, :WIDE]
    at += lift(low)
    out[at : at + tall, :] = pred[:, :WIDE]
    at += lift(tall)
    for b in range(tok.shape[1] // WIDE):
        out[at : at + tall, :] = tok[:, b * WIDE : (b + 1) * WIDE]
        at += lift(tall)
    out[at : at + low, 0:128] = enc[:, WIDE:]
    out[at : at + tall, 128:256] = pred[:, WIDE:]
    dur = dur[...].astype(jnp.float32)
    out[at : at + tall, 256:384] = jnp.concatenate([dur, jnp.zeros((tall, 128 - dur.shape[1]), jnp.float32)], 1).astype(jnp.bfloat16)


def ffn_fwd(rows, x_ref, gain, weights, names, normed, h, act, y, mover, h_out, beats):
    w_in = weights[names[0]]

    def prepare(r, i, c):
        normed[r, :] = (ln_parts(x_ref[r, :].astype(jnp.float32))[0] * gain).astype(jnp.bfloat16)
        return c

    row_loop(rows, prepare)
    w_in[1].wait()
    for b in range(h.shape[0]):
        h[b] = nn(normed[...], w_in[0][:, b * WIDE : (b + 1) * WIDE])
        mover.put(h.at[b], h_out.at[b])

        def swish(r, i, c):
            v = h[b, r, :]
            act[r, b * WIDE : (b + 1) * WIDE] = (v * jax.nn.sigmoid(v)).astype(jnp.bfloat16)
            return c

        row_loop(rows, swish)
        beats.run(1)
    w_out = weights[names[1]]
    w_out[1].wait()
    y[...] = x_ref[...].astype(jnp.float32) + 0.5 * nn(act[...], w_out[0][...])
    beats.run(1)


def part_one(utts, beats, mover, t_ref, x_ref, gains, weights, outs, scratch):
    y1_out, h_out, y2_out, t_out, c_out, r_out, d_out = outs
    y1, y2, normed, h, act, tq, ctx, r, gp, d = scratch
    rows, width = y1.shape
    frames = rows // utts
    ffn_fwd(rows, x_ref, gains[0:1], weights, ("f_in", "f_out"), normed, h, act, y1, mover, h_out, beats)
    mover.put(y1, y1_out)

    def prepare(rr, i, c):
        normed[rr, :] = (ln_parts(y1[rr, :])[0] * gains[1:2]).astype(jnp.bfloat16)
        return c

    row_loop(rows, prepare)
    w_joint = weights["w_joint"][0]
    weights["w_joint"][1].wait()
    for b in range(3):
        tq[:, b * width : (b + 1) * width] = nn(normed[...], w_joint[:, b * width : (b + 1) * width]).astype(jnp.bfloat16)
    mover.put(tq, t_out)
    beats.run(1)
    pairs = width // 128
    side = lax.broadcasted_iota(jnp.int32, (frames, 128), 1) < 64
    key_at = lax.broadcasted_iota(jnp.int32, (1, frames), 1)
    hook = beats.loop(3, utts * pairs)

    def pair_step(m, carry):
        hook(m)
        u = m // pairs
        base = lax.rem(m, pairs) * 128
        rr = pl.ds(pl.multiple_of(u * frames, frames), frames)
        bias = jnp.where(key_at < t_ref[u], 0.0, MASKED)
        q = tq[rr, pl.ds(pl.multiple_of(base, 128), 128)]
        k = tq[rr, pl.ds(pl.multiple_of(base + width, 128), 128)]
        v = tq[rr, pl.ds(pl.multiple_of(base + 2 * width, 128), 128)]
        got = []
        for half in range(2):
            mine = side if half == 0 else ~side
            s = nt(jnp.where(mine, q, jnp.zeros_like(q)), k) * 0.125 + bias
            p = jnp.exp(s - jnp.max(s, -1, keepdims=True))
            p = p * (1.0 / jnp.sum(p, -1, keepdims=True))
            got.append(nn(p.astype(jnp.bfloat16), v))
        ctx[rr, pl.ds(pl.multiple_of(base, 128), 128)] = jnp.where(side, got[0], got[1]).astype(jnp.bfloat16)
        return carry

    lax.fori_loop(0, utts * pairs, pair_step, 0)
    mover.put(ctx, c_out)
    weights["w_proj"][1].wait()
    y2[...] = y1[...] + nn(ctx[...], weights["w_proj"][0][...])
    mover.put(y2, y2_out)

    def prepare_conv(rr, i, c):
        normed[rr, :] = (ln_parts(y2[rr, :])[0] * gains[2:3]).astype(jnp.bfloat16)
        return c

    row_loop(rows, prepare_conv)
    w_pin = weights["p_in"][0]
    weights["p_in"][1].wait()
    for b in range(2):
        r[:, b * width : (b + 1) * width] = nn(normed[...], w_pin[:, b * width : (b + 1) * width])
    mover.put(r, r_out)
    beats.run(1)
    fill_gated(utts, frames, t_ref, r, gp)
    taps = gains[5:14]

    def conv(rr, i, total):
        d_chunk = spread(gp, utts, frames, i, taps)
        d[rr, :] = d_chunk
        return total + fold8(d_chunk * valid_rows_of(t_ref, frames, i), jnp.add)

    total = row_loop(rows, conv, jnp.zeros((8, width), jnp.float32))
    mover.put(d, d_out)
    beats.run(1)
    count = t_ref[0]
    for u in range(1, utts):
        count = count + t_ref[u]
    count = count.astype(jnp.float32)
    mean = jnp.sum(total, 0, keepdims=True) / count

    def deviate(rr, i, total):
        gap = (d[rr, :] - mean) * valid_rows_of(t_ref, frames, i)
        return total + fold8(gap * gap, jnp.add)

    dev = jnp.sum(row_loop(rows, deviate, jnp.zeros((8, width), jnp.float32)), 0, keepdims=True)
    cut4 = lambda v: [v[:, i * 128 : (i + 1) * 128] for i in range(width // 128)]
    return jnp.concatenate(cut4(mean) + cut4(dev) + [jnp.full((8, 128), count, jnp.float32)], 0)


def part_two(beats, mover, pooled_ref, gains, weights, outs, scratch):
    y3_out, h_out, y4_out, x_out = outs
    d, y2, y3, normed, h, act, y4, x = scratch
    rows, width = y3.shape
    mean = read_rows(pooled_ref, 0, width)
    count = pooled_ref[8:9, 0:1]
    istd = lax.rsqrt(read_rows(pooled_ref, 4, width) / count + EPS)

    def bn(rr, i, c):
        b = (d[rr, :] - mean) * istd * gains[14:15] + gains[15:16]
        normed[rr, :] = (b * jax.nn.sigmoid(b)).astype(jnp.bfloat16)
        return c

    row_loop(rows, bn)
    weights["p_out"][1].wait()
    y3[...] = y2[...] + nn(normed[...], weights["p_out"][0][...])
    mover.put(y3, y3_out)
    ffn_fwd(rows, y3, gains[3:4], weights, ("s_in", "s_out"), normed, h, act, y4, mover, h_out, beats)
    mover.put(y4, y4_out)

    def last(rr, i, c):
        x[rr, :] = ln_parts(y4[rr, :])[0] * gains[4:5]
        return c

    row_loop(rows, last)
    mover.put(x, x_out)


def forward_kernel(utts, layers, n1, groups, tables, joint_at, tiles, lag, t_ref, frames_ref, *refs):
    n = 2 * n1
    names = PLACE + ("gains", "taps", "bn_gain", "bn_bias", "enc", "pred", "tok", "dur")
    src = dict(zip(names, refs))
    refs = refs[len(names) :]
    whole, refs = refs[0], refs[1:]
    layer_outs = []
    for layer in range(layers):
        layer_outs.append((refs[0:7], refs[7:11], refs[11], refs[12]))
        refs = refs[13:]
    buffers, refs = refs[:8], refs[8:]
    packed, smalls, y1, y2, normed, h, act, tq, ctx, r, gp, d, y3, y4, x, sems = refs[:16]
    refs = refs[16:]
    entered = meet(groups, n)
    pack_into(packed, src, tables, joint_at, layers)
    entered()
    engine = GatherEngine(n1, tiles, lag, packed, whole, *refs[:9])
    refs = refs[9:]
    beats = Beats(engine.tick, engine.total)
    held = dict(zip(("f_in", "f_out", "w_joint", "w_proj", "p_in", "p_out", "s_in", "s_out"), buffers))
    used = 0
    for layer in range(layers):
        table = tables[layer]
        mover = Mover(sems, used)

        def load(name):
            beats.until(engine.after(table[name][1]))
            return held[name], mover.load_weight(whole, table[name][0], held[name])

        weights = {"f_in": load("f_in")}
        small = mover.load(whole.at[:, :, pl.ds(table["small"][0], 16), :], smalls)
        small.wait()
        gains = None
        for s in range(n):
            part = smalls[s // 2, s % 2].astype(jnp.float32)
            part = part if s == 0 else pltpu.roll(part, s * (WIDE // n), 1)
            gains = part if gains is None else gains + part
        layer_outs[layer][3][...] = gains
        weights = Late(weights, load)
        first, second, pooled_out, _ = layer_outs[layer]
        source = frames_ref if layer == 0 else x
        stats = part_one(utts, beats, mover, t_ref, source, gains, weights, first, (y1, y2, normed, h, act, tq, ctx, r, gp, d))
        exchange = Exchange(groups, n, *refs[:6])
        refs = refs[6:]
        for name in ("p_out", "s_in", "s_out"):
            weights.fetch(name)
        pooled_out[...] = exchange.run(stats, beats)
        mover.finish()
        part_two(beats, mover, pooled_out, gains, weights, second, (d, y2, y3, normed, h, act, y4, x))
        mover.finish()
        used = mover.used
    beats.rest()
    engine.finish()


class Late:
    def __init__(self, got, load):
        self.got = got
        self.load = load

    def fetch(self, name):
        if name not in self.got:
            self.got[name] = self.load(name)

    def __getitem__(self, name):
        self.fetch(name)
        return self.got[name]


def forward(t_len, frames_in, arrays, layers, ff, sizes, collective_id, lag=2):
    rows, width = frames_in.shape
    utts = t_len.shape[0]
    n = lax.axis_size("fsdp")
    groups = lax.axis_size("dp")
    n1 = n // 2
    tables, joint_at = gathered_rows(n, width, ff, layers)
    total = tiled(joint_at + sum(sizes))
    tiles = total // TILE
    nb = ff // WIDE
    v = pltpu.VMEM
    dma = pltpu.SemaphoreType.DMA
    big = sds((rows, width))
    one = [big, sds((nb, rows, WIDE)), big, sds((rows, 3 * width), BF16), sds((rows, width), BF16), sds((rows, 2 * width)), big]
    two = [big, sds((nb, rows, WIDE)), big, big]
    pad_rows = utts * (rows // utts + 16)
    outs = pl.pallas_call(
        partial(forward_kernel, utts, layers, n1, groups, tables, joint_at, tiles, lag),
        in_specs=[SMEM_SPEC] + [VMEM_SPEC] * (1 + len(arrays)),
        out_specs=[ANY_SPEC] + ([ANY_SPEC] * 11 + [VMEM_SPEC] * 2) * layers,
        out_shape=[sds((n1, 2, total, WIDE), BF16)] + (one + two + [sds((16, 128)), sds((16, width))]) * layers,
        scratch_shapes=[
            v((width, ff), BF16), v((ff, width), BF16), v((width, 3 * width), BF16), v((width, width), BF16), v((width, 2 * width), BF16),
            v((width, width), BF16), v((width, ff), BF16), v((ff, width), BF16),
            v((total, WIDE), BF16), v((n1, 2, 16, WIDE), BF16), v((rows, width), F32), v((rows, width), F32), v((rows, width), BF16),
            v((nb, rows, WIDE), F32), v((rows, ff), BF16), v((rows, 3 * width), BF16), v((rows, width), BF16), v((rows, 2 * width), F32),
            v((pad_rows, width), F32), v((rows, width), F32), v((rows, width), F32), v((rows, width), F32), v((rows, width), F32), dma((80,)),
            dma((tiles,)), dma((tiles, n1)), dma((tiles, n1)), dma((tiles,)), dma((tiles,)), dma((tiles,)), dma((tiles,)), dma((tiles,)), dma((tiles,)),
        ]
        + [v((groups, 16, 128), F32), v((n, 16, 128), F32), dma((groups,)), dma((groups,)), dma((n,)), dma((n,))] * layers,
        compiler_params=pltpu.CompilerParams(collective_id=collective_id, has_side_effects=True, vmem_limit_bytes=61 << 20),
        name="gather_and_forward",
    )(t_len, frames_in, *arrays)
    whole = outs[0].reshape(n, total, WIDE)
    return whole, [outs[1 + 13 * layer : 14 + 13 * layer] for layer in range(layers)], tables, joint_at


def lift(rows):
    return -(-rows // 16) * 16


def joint_sizes(w_enc, w_pred, w_tok):
    low, tall = lift(w_enc.shape[0]), lift(w_pred.shape[0])
    return [low, tall, tall * (w_tok.shape[1] // WIDE), tall]


class Joined:
    def __init__(self, parts, ends):
        self.parts = parts
        self.ends = ends

    def __getitem__(self, key):
        rows_of, cols = key
        got = []
        first = 0
        for part, last in zip(self.parts, self.ends):
            lo, hi = max(rows_of.start, first), min(rows_of.stop, last)
            if lo < hi:
                got.append(part[lo - first : hi - first, cols])
            first = last
        return got[0] if len(got) == 1 else jnp.concatenate(got, 0)


def unpack_kernel(layers, table, end, dims, ends, *refs):
    parts, refs = refs[: len(ends)], refs[len(ends) :]
    gains, f_in, f_out, w_joint, w_proj, p_in, taps, p_out, s_in, s_out, enc, pred, tok, dur = refs
    share = Joined(parts, ends)
    outs = {"f_in": f_in, "f_out": f_out, "w_joint": w_joint, "w_proj": w_proj, "p_in": p_in, "p_out": p_out, "s_in": s_in, "s_out": s_out}
    starts, width, joint = dims
    shard = gains.shape[2]
    for layer in range(layers):
        for name in PLACE:
            out = outs[name]
            height = out.shape[1]
            early = table[name] < table["p_in"]
            base = starts[layer][0] + table[name] if early else starts[layer][1] + table[name] - table["p_in"]
            for b in range(out.shape[2] // WIDE):
                out[layer, :, b * WIDE : (b + 1) * WIDE] = share[base + b * height : base + (b + 1) * height, :].astype(jnp.float32)
        base = starts[layer][1] + end - table["p_in"]
        small = share[base : base + 16, 0:128].astype(jnp.float32)
        gains[layer] = small[0:5, :shard]
        taps[layer] = small[5 : 5 + taps.shape[1], :shard]
    at = starts[layers]
    low, tall = enc.shape[0], pred.shape[0]
    enc[:, :WIDE] = share[at : at + low, :].astype(jnp.float32)
    at += lift(low)
    pred[:, :WIDE] = share[at : at + tall, :].astype(jnp.float32)
    at += lift(tall)
    for b in range(tok.shape[1] // WIDE):
        tok[:, b * WIDE : (b + 1) * WIDE] = share[at : at + tall, :].astype(jnp.float32)
        at += lift(tall)
    enc[:, WIDE:] = share[at : at + low, 0:128].astype(jnp.float32)
    pred[:, WIDE:] = share[at : at + tall, 128:256].astype(jnp.float32)
    dur[...] = share[at : at + tall, 256:384].astype(jnp.float32)[:, : dur.shape[1]]


def unpack(layers, table, end, dims, shares, like):
    ends = []
    for share in shares:
        ends.append(share.shape[0] + (ends[-1] if ends else 0))
    return pl.pallas_call(
        partial(unpack_kernel, layers, table, end, dims, tuple(ends)),
        in_specs=[VMEM_SPEC] * len(shares),
        out_specs=[VMEM_SPEC] * len(like),
        out_shape=[sds(x.shape) for x in like],
        compiler_params=pltpu.CompilerParams(vmem_limit_bytes=48 << 20),
        name="unpack_grads",
    )(*shares)


def cut(whole, sizes, offset=0):
    parts = []
    for size in sizes:
        parts.append(whole[..., offset : offset + size, :])
        offset += size
    return parts


def from_blocks(part, cols, rows):
    n, height, _ = part.shape
    blocks = cols // WIDE
    return jnp.swapaxes(part.reshape(n, blocks, height // blocks, WIDE)[:, :, :rows], 1, 2).reshape(-1, cols)


def joint_inputs_kernel(base, x_ref, pred_ref, whole, low_ref, enc_t, pred_t, w_t, w_enc, w_pred, w_cat, sems):
    n = whole.shape[0]
    joint = w_enc.shape[1]
    low, tall = w_enc.shape[0] // n, w_pred.shape[0] // n
    vocab = w_cat.shape[1] - 128
    first = base + low + tall
    rest = first + tall * (vocab // WIDE)

    def spread(at, height, dst, cols, lanes, sem):
        def one(s, carry):
            pltpu.make_async_copy(
                whole.at[s, pl.ds(at, height), lanes], dst.at[pl.ds(pl.multiple_of(s * height, 16), height), cols], sem
            ).start()
            return carry

        lax.fori_loop(0, n, one, 0)

    every = pl.ds(0, WIDE)
    spread(base, low, w_enc, every, every, sems.at[0])
    spread(rest, low, w_enc, pl.ds(WIDE, 128), pl.ds(0, 128), sems.at[0])
    spread(base + low, tall, w_pred, every, every, sems.at[1])
    spread(rest, tall, w_pred, pl.ds(WIDE, 128), pl.ds(128, 128), sems.at[1])
    for b in range(vocab // WIDE):
        spread(first + b * tall, tall, w_cat, pl.ds(b * WIDE, WIDE), every, sems.at[2])
    spread(rest, tall, w_cat, pl.ds(vocab, 128), pl.ds(256, 128), sems.at[2])
    low_ref[...] = x_ref[...].astype(jnp.bfloat16)
    pltpu.make_async_copy(w_enc, w_enc, sems.at[0]).wait()
    enc_t[...] = nn(low_ref[...], w_enc[...]).T
    pltpu.make_async_copy(w_pred, w_pred, sems.at[1]).wait()
    pred = nn(pred_ref[...], w_pred[...])
    for g in range(pred_t.shape[0]):
        pred_t[g] = pred[g * 8 : (g + 1) * 8, :].T
    pltpu.make_async_copy(w_cat, w_cat, sems.at[2]).wait()
    w_t[...] = w_cat[...].T


def joint_inputs(x, pred_low, whole, base, joint, vocab):
    rows, width = x.shape
    groups = pred_low.shape[0] // 8
    return pl.pallas_call(
        partial(joint_inputs_kernel, base),
        in_specs=[VMEM_SPEC, VMEM_SPEC, ANY_SPEC],
        out_specs=[VMEM_SPEC] * 7,
        out_shape=[sds((rows, width), BF16), sds((joint, rows)), sds((groups, joint, 8)), sds((vocab + 128, joint), BF16),
                   sds((width, joint), BF16), sds((joint, joint), BF16), sds((joint, vocab + 128), BF16)],
        scratch_shapes=[pltpu.SemaphoreType.DMA((3,))],
        compiler_params=pltpu.CompilerParams(vmem_limit_bytes=48 << 20),
        name="joint_inputs",
    )(x, pred_low, whole)


def joint_outputs_kernel(genc_t, gpred_t, gtok, gdur, low_ref, pred_ref, w_enc, gx, pack, g_low, gp):
    n = pack.shape[0]
    joint = w_enc.shape[1]
    low, tall = w_enc.shape[0] // n, joint // n
    g_low[...] = genc_t[...].T.astype(jnp.bfloat16)
    gx[...] = nt(g_low[...], w_enc[...])
    g_enc = tn(low_ref[...], g_low[...]).astype(jnp.bfloat16)
    real = lax.broadcasted_iota(jnp.int32, (8, joint), 0) < GROUP
    for g in range(gpred_t.shape[0]):
        gp[g * 8 : (g + 1) * 8, :] = jnp.where(real, gpred_t[g].T, 0.0)
    g_pred = tn(pred_ref[...], gp[...].astype(jnp.bfloat16)).astype(jnp.bfloat16)
    blocks = gtok.shape[1] // WIDE
    rest = low + tall * (1 + blocks)
    for s in range(n):
        mine = slice(s * tall, (s + 1) * tall)
        pack[s, 0:low, :] = g_enc[s * low : (s + 1) * low, :WIDE]
        pack[s, low : low + tall, :] = g_pred[mine, :WIDE]
        for b in range(blocks):
            at = low + tall * (1 + b)
            pack[s, at : at + tall, :] = gtok[mine, b * WIDE : (b + 1) * WIDE]
        pack[s, rest : rest + low, 0:128] = g_enc[s * low : (s + 1) * low, WIDE:]
        if tall > low:
            pack[s, rest + low : rest + tall, 0:128] = jnp.zeros((tall - low, 128), jnp.bfloat16)
        pack[s, rest : rest + tall, 128:256] = g_pred[mine, WIDE:]
        pack[s, rest : rest + tall, 256:384] = gdur[mine, :]
        pack[s, rest : rest + tall, 384:] = jnp.zeros((tall, WIDE - 384), jnp.bfloat16)
        if pack.shape[1] > rest + tall:
            pack[s, rest + tall :, :] = jnp.zeros((pack.shape[1] - rest - tall, WIDE), jnp.bfloat16)


def joint_outputs(genc_t, gpred_t, gtok, gdur, low, pred_low, w_enc, n):
    rows, width = low.shape
    joint = w_enc.shape[1]
    count = width // n + (joint // n) * (2 + gtok.shape[1] // WIDE)
    return pl.pallas_call(
        joint_outputs_kernel,
        in_specs=[VMEM_SPEC] * 7,
        out_specs=[VMEM_SPEC] * 2,
        out_shape=[sds((rows, width)), sds((n, tiled(count), WIDE), BF16)],
        scratch_shapes=[pltpu.VMEM((rows, joint), BF16), pltpu.VMEM((pred_low.shape[0], joint), F32)],
        compiler_params=pltpu.CompilerParams(vmem_limit_bytes=48 << 20),
        name="joint_outputs",
    )(genc_t, gpred_t, gtok, gdur, low, pred_low, w_enc)


def unpack_joint(whole, first, sizes, w_enc, w_pred, vocab):
    enc, pred, tok, rest = cut(whole, sizes, first)
    joint = w_enc.shape[1]
    low = w_enc.shape[0]
    tall = w_pred.shape[0]
    w_enc = jnp.concatenate([enc[:, :low], rest[:, :low, : joint - WIDE]], 2).reshape(-1, joint)
    w_pred = jnp.concatenate([pred[:, :tall], rest[:, :tall, 128 : 128 + joint - WIDE]], 2).reshape(-1, joint)
    return w_enc, w_pred, from_blocks(tok, vocab, tall), rest[:, :tall, 256:384].reshape(-1, 128)


def grow(part):
    short = lift(part.shape[1]) - part.shape[1]
    return jnp.pad(part, ((0, 0), (0, short), (0, 0))) if short else part


def pack_joint_grads(g_enc, g_pred, g_tok, g_dur, n):
    def shards(grad):
        return grow(grad.astype(jnp.bfloat16).reshape(n, -1, grad.shape[1]))
    g_enc, g_pred, g_tok, g_dur = shards(g_enc), shards(g_pred), shards(g_tok), shards(g_dur)
    tall = g_pred.shape[1]
    rest = jnp.concatenate(
        [
            jnp.pad(g_enc[:, :, WIDE:], ((0, 0), (0, tall - g_enc.shape[1]), (0, 0))),
            g_pred[:, :, WIDE:],
            g_dur,
            jnp.zeros((n, tall, 128), jnp.bfloat16),
        ],
        2,
    )
    parts = [g_enc[:, :, :WIDE], g_pred[:, :, :WIDE]]
    parts += [g_tok[:, :, b : b + WIDE] for b in range(0, g_tok.shape[2], WIDE)] + [rest]
    rows = sum(p.shape[1] for p in parts)
    return jnp.concatenate(parts + [jnp.zeros((n, tiled(rows) - rows, WIDE), jnp.bfloat16)], 1)


def matmul(left, right):
    return jnp.dot(left, right, preferred_element_type=jnp.float32)


def contract_rows(left, right):
    return lax.dot_general(
        left, right, (((0,), (0,)), ((), ())), preferred_element_type=jnp.float32
    )


def contract_cols(left, right):
    return lax.dot_general(
        left, right, (((1,), (1,)), ((), ())), preferred_element_type=jnp.float32
    )


def local(
    frames_in,
    frame_lengths,
    label_ids,
    label_lengths,
    pred_states,
    norm_gains,
    first_in,
    first_out,
    attend_joint,
    attend_out,
    point_in,
    depth_taps,
    batch_gain,
    batch_bias,
    point_out,
    second_in,
    second_out,
    enc_weight,
    pred_weight,
    token_weight,
    duration_weight,
):
    utts, frames, width = frames_in.shape
    slots = pred_states.shape[1]
    rows = utts * frames
    layers = norm_gains.shape[0]
    n = lax.axis_size("fsdp")
    ff = first_in.shape[2]
    mats = {
        "f_in": first_in, "f_out": first_out, "w_joint": attend_joint, "w_proj": attend_out,
        "p_in": point_in, "p_out": point_out, "s_in": second_in, "s_out": second_out,
    }
    table, end = offsets(n, width, ff)
    shard = width // n
    sizes = joint_sizes(enc_weight, pred_weight, token_weight)
    vocab = token_weight.shape[1]
    arrays = [mats[name] for name in PLACE]
    arrays += [norm_gains, depth_taps, batch_gain, batch_bias, enc_weight, pred_weight, token_weight, duration_weight]
    resid = frames_in.reshape(rows, width)
    whole, records, tables, joint_at = forward(frame_lengths, resid, arrays, layers, ff, sizes, 1)
    held = [{name: spot[0] for name, spot in t.items()} for t in tables]
    starts_of = [resid] + [record[10] for record in records]
    resid = starts_of[-1]
    joint = enc_weight.shape[1]
    groups = slots // GROUP
    durs = duration_weight.shape[1]
    aligned = joint % (16 * n) == 0 and width % (16 * n) == 0
    pred_low = pred_states.reshape(utts * groups, GROUP, joint)
    pred_low = jnp.pad(pred_low, ((0, 0), (0, 8 - GROUP), (0, 0))).reshape(-1, joint)
    if aligned:
        out_low, enc_t, pred_t, w_cat_t, w_enc, _, w_cat = joint_inputs(resid, pred_low, whole, joint_at, joint, vocab)
    else:
        w_enc, w_pred, w_tok, w_dur = unpack_joint(whole, joint_at, sizes, enc_weight, pred_weight, vocab)
        out_low = resid.astype(jnp.bfloat16)
        enc_t = matmul(out_low, w_enc).T
        pred_t = jnp.swapaxes(matmul(pred_low, w_pred).reshape(utts * groups, 8, joint), 1, 2)
        w_cat = jnp.concatenate([w_tok, w_dur], 1)
        w_cat_t = w_cat.T
    labels_ext = jnp.concatenate([label_ids, jnp.zeros((utts, 1), jnp.int32)], 1)
    feats, expd = joint_forward(enc_t, pred_t, labels_ext, w_cat_t, vocab, durs, frames)
    lat_grads, scores = lattice(feats[: 2 + durs], frame_lengths, label_lengths, slots)
    log_prob = scores[:utts, 0]
    utt_loss = -log_prob / frame_lengths.astype(jnp.float32)
    grad_enc_t, grad_pred_t, grad_tok, grad_dur_w = joint_backward(
        enc_t, pred_t, labels_ext, w_cat, feats, lat_grads, expd, vocab, durs, frames
    )
    if aligned:
        grad, joint_grads = joint_outputs(grad_enc_t, grad_pred_t, grad_tok, grad_dur_w, out_low, pred_low, w_enc, n)
    else:
        grad_pred_rows = jnp.swapaxes(grad_pred_t[:, :, :GROUP], 1, 2)
        grad_pred_rows = jnp.pad(grad_pred_rows, ((0, 0), (0, 8 - GROUP), (0, 0))).reshape(-1, joint)
        grad_enc_low = grad_enc_t.T.astype(jnp.bfloat16)
        grad = contract_cols(grad_enc_low, w_enc)
        grad_w_enc = contract_rows(out_low, grad_enc_low)
        grad_w_pred = contract_rows(pred_low, grad_pred_rows.astype(jnp.bfloat16))
        joint_grads = pack_joint_grads(grad_w_enc, grad_w_pred, grad_tok, grad_dur_w, n)

    def whole_of(source):
        return (source, 0, source.shape[1] // TILE)

    waiting = [whole_of(joint_grads)]
    shares = []
    starts = [None] * layers + [0]
    at = joint_grads.shape[1]
    bn_grads = [None] * layers
    for layer in reversed(range(layers)):
        x0 = starts_of[layer]
        y1, h1, y2, qkv, ctx, gates, depthwise, y3, h2, y4, result, pooled, small = records[layer]
        args = (grad, y4, y3, depthwise, pooled, small, whole, h2, ff, held[layer])
        if layer == layers - 1:
            outs = back_one(*args)
        else:
            source, first, count = waiting.pop()
            early = min(count, -(-count * 3 // 5))
            outs, share = back_one(*args, [(source, first, early)], 16 + layer)
            shares.append(share)
            if early < count:
                waiting.append((source, first + early, count - early))
        g3, db, grads_one, sums, late_gains = outs
        sums = exchange(sums, "sum", 12 + layer)
        waiting.append(whole_of(grads_one))
        args = (frame_lengths, x0, y1, y2, gates, qkv, ctx, depthwise, db, g3, pooled, sums, late_gains)
        (grad, grads_two), share = back_two(*args, small, whole, h1, ff, held[layer], waiting, 20 + layer)
        shares.append(share)
        waiting = [whole_of(grads_two)]
        starts[layer] = (at, at + grads_one.shape[1])
        at += grads_one.shape[1] + grads_two.shape[1]
        bn_grads[layer] = (sums[4:8].reshape(width), sums[0:4].reshape(width))
    shares.append(scatter(waiting, 4))
    grads = unpack(
        layers,
        table,
        end,
        (starts, width, joint),
        shares,
        [norm_gains, first_in, first_out, attend_joint, attend_out, point_in, depth_taps, point_out, second_in, second_out,
         enc_weight, pred_weight, token_weight, duration_weight],
    )
    offset = lax.axis_index("fsdp") * shard
    gain_piece = lax.dynamic_slice_in_dim(jnp.stack([g[0] for g in bn_grads]), offset, shard, 1)
    bias_piece = lax.dynamic_slice_in_dim(jnp.stack([g[1] for g in bn_grads]), offset, shard, 1)
    return (
        utt_loss,
        grad.reshape(utts, frames, width),
        *grads[:7],
        gain_piece,
        bias_piece,
        *grads[7:],
    )


def solution(mesh):
    placed = (
        P(("dp", "fsdp"), None, None),
        P(("dp", "fsdp")),
        P(("dp", "fsdp"), None),
        P(("dp", "fsdp")),
        P(("dp", "fsdp"), None, None),
        P(None, None, "fsdp"),
        P(None, "fsdp", None),
        P(None, "fsdp", None),
        P(None, "fsdp", None),
        P(None, "fsdp", None),
        P(None, "fsdp", None),
        P(None, None, "fsdp"),
        P(None, "fsdp"),
        P(None, "fsdp"),
        P(None, "fsdp", None),
        P(None, "fsdp", None),
        P(None, "fsdp", None),
        P("fsdp", None),
        P("fsdp", None),
        P("fsdp", None),
        P("fsdp", None),
    )
    return jax.shard_map(
        local,
        mesh=mesh,
        in_specs=placed,
        out_specs=(
            P(("dp", "fsdp")),
            P(("dp", "fsdp"), None, None),
            P(None, None, "fsdp"),
            P(None, "fsdp", None),
            P(None, "fsdp", None),
            P(None, "fsdp", None),
            P(None, "fsdp", None),
            P(None, "fsdp", None),
            P(None, None, "fsdp"),
            P(None, "fsdp"),
            P(None, "fsdp"),
            P(None, "fsdp", None),
            P(None, "fsdp", None),
            P(None, "fsdp", None),
            P("fsdp", None),
            P("fsdp", None),
            P("fsdp", None),
            P("fsdp", None),
        ),
        check_vma=False,
    )
```

```python
from functools import partial, reduce

import jax
import jax.numpy as jnp
from jax import lax
from jax.experimental import pallas as pl
from jax.experimental.pallas import tpu as pltpu
from jax.sharding import PartitionSpec as P

HEADS = 8


EPS = 1e-05
MASKED = -1000000000.0
NEG = -1e30


def lattice_kernel(slots, feats_ref, tlen_ref, ulen_ref, grads_ref, prob_ref, s_ref, l_ref, ls_ref, a_ref, b_ref, init_ref):
    utts = tlen_ref.shape[0]
    frames = feats_ref.shape[2]
    rows = feats_ref.shape[1]
    wide = frames + 128
    reach = feats_ref.shape[0] - 3
    diags = frames + slots
    pad = 8
    total = a_ref.shape[0]
    body = wide

    def skew(x, sign):
        k = lax.broadcasted_iota(jnp.int32, x.shape, 0) % 32
        for bit in range(5):
            step = 1 << bit
            x = jnp.where((k // step) % 2 == 1, pltpu.roll(x, step if sign > 0 else wide - step, 1), x)
        return x

    def to_diag(x):
        x = jnp.concatenate([x, jnp.zeros((rows, 128), jnp.float32)], 1)
        x = skew(x, 1)
        x = jnp.concatenate([x, jnp.zeros((128 - rows, wide), jnp.float32)], 0)
        return x.T

    lane = lax.broadcasted_iota(jnp.int32, (wide, 128), 1)
    diag = lax.broadcasted_iota(jnp.int32, (wide, 128), 0)
    k_of = lane % 32
    t_of = diag - k_of
    t_len = jnp.full((wide, 128), -1, jnp.int32)
    u_len = jnp.full((wide, 128), -1, jnp.int32)
    for u in range(utts):
        mine = (lane // 32) == u
        t_len = jnp.where(mine, tlen_ref[u], t_len)
        u_len = jnp.where(mine, ulen_ref[u], u_len)
    blank = to_diag(feats_ref[0])
    label = to_diag(feats_ref[1])
    edge = jnp.full((pad, 128), NEG, jnp.float32)
    real = (t_of >= 0)
    for ref in (s_ref, l_ref, ls_ref):
        for e in range(ref.shape[0]):
            ref[e, 0:pad, :] = edge
            ref[e, pad + wide:, :] = jnp.full((ref.shape[1] - pad - wide, 128), NEG, jnp.float32)
    for e in range(reach + 1):
        dur = to_diag(feats_ref[2 + e])
        if e > 0:
            keep = real & (k_of <= u_len) & ((t_of + e < t_len) | ((t_of + e == t_len) & (k_of == u_len)))
            s_ref[e - 1, pad:pad + wide, :] = jnp.where(keep, blank + dur, NEG)
        keep = real & (k_of < u_len) & (t_of + e < t_len)
        lab = jnp.where(keep, label + dur, NEG)
        l_ref[e, pad:pad + wide, :] = lab
        ls_ref[e, pad:pad + wide, :] = pltpu.roll(lab, 1, 1)
    init_ref[pad:pad + wide, :] = jnp.where((t_of == t_len) & (k_of == u_len), 0.0, NEG)
    a_ref[...] = jnp.full(a_ref.shape, NEG, jnp.float32)
    b_ref[...] = jnp.full(b_ref.shape, NEG, jnp.float32)

    first = jnp.where((lax.broadcasted_iota(jnp.int32, (1, 128), 1) % 32 == 0)
                      & (lax.broadcasted_iota(jnp.int32, (1, 128), 1) < 32 * utts), 0.0, NEG)

    a_ref[pl.ds(pad, 1), :] = first
    last = diags

    def tree(parts, op):
        while len(parts) > 1:
            parts = [op(parts[i], parts[i + 1]) if i + 1 < len(parts) else parts[i] for i in range(0, len(parts), 2)]
        return parts[0]

    def older(hist, rolled, edge_s, edge_l):
        terms = [hist[e - 2] + edge_s(e) for e in range(2, reach + 1)]
        terms += [rolled[e - 1] + edge_l(e) for e in range(1, reach + 1)]
        top = tree(terms, jnp.maximum)
        return top, tree([jnp.exp(x - top) for x in terms], jnp.add)

    def newest(old, one, two):
        top = jnp.maximum(jnp.maximum(one, two), old[0])
        total = (jnp.exp(one - top) + jnp.exp(two - top)) + old[1] * jnp.exp(old[0] - top)
        return jnp.maximum(top + jnp.log(total), NEG)

    def step(i, carry):
        ha, hra, olda, hb, hrb, oldb = carry
        row = pad + i
        rowb = pad + last - i
        nexta = older(ha, hra, lambda e: s_ref[e - 1, pl.ds(row + 1 - e, 1), :], lambda e: ls_ref[e, pl.ds(row - e, 1), :])
        nextb = older(hb, hrb, lambda e: s_ref[e - 1, pl.ds(rowb - 1, 1), :], lambda e: l_ref[e, pl.ds(rowb - 1, 1), :])
        a = newest(olda, ha[0] + s_ref[0, pl.ds(row - 1, 1), :], hra[0] + ls_ref[0, pl.ds(row - 1, 1), :])
        b = newest(oldb, hb[0] + s_ref[0, pl.ds(rowb, 1), :], hrb[0] + l_ref[0, pl.ds(rowb, 1), :])
        b = jnp.maximum(b, init_ref[pl.ds(rowb, 1), :])
        a_ref[pl.ds(row, 1), :] = a
        b_ref[pl.ds(rowb, 1), :] = b
        ra = pltpu.roll(a, 1, 1)
        rb = pltpu.roll(b, 127, 1)
        return ((a,) + ha[:-1], (ra,) + hra[:-1], nexta, (b,) + hb[:-1], (rb,) + hrb[:-1], nextb)

    b0 = init_ref[pl.ds(pad + last, 1), :]
    b_ref[pl.ds(pad + last, 1), :] = b0
    none = a_ref[pl.ds(0, 1), :]
    first = a_ref[pl.ds(pad, 1), :]
    ha = (first,) + (none,) * (reach - 2)
    hra = (pltpu.roll(first, 1, 1),) + (none,) * (reach - 1)
    hb = (b0,) + (none,) * (reach - 2)
    hrb = (pltpu.roll(b0, 127, 1),) + (none,) * (reach - 1)
    empty = (none, none - none)
    lax.fori_loop(1, last + 1, step, (ha, hra, empty, hb, hrb, empty), unroll=4)

    zrow = b_ref[pl.ds(pad, 1), :]
    lane1 = lax.broadcasted_iota(jnp.int32, (1, 128), 1)
    z = jnp.zeros((1, 128), jnp.float32)
    for u in range(utts):
        zu = jnp.max(jnp.where(lane1 == 32 * u, zrow, 2 * NEG), axis=1, keepdims=True)
        z = jnp.where(lane1 // 32 == u, zu, z)
        prob_ref[pl.ds(u, 1), :] = jnp.broadcast_to(zu, (1, 128))

    def from_diag(x):
        x = x.T[:rows]
        return skew(x, -1)[:, :frames]

    a = a_ref[pad:pad + wide, :] - z
    g_blank = jnp.zeros((wide, 128), jnp.float32)
    g_label = jnp.zeros((wide, 128), jnp.float32)
    for e in range(reach + 1):
        bb = b_ref[pad + e + 1: pad + e + 1 + wide, :]
        pl_ = jnp.exp(a + l_ref[e, pad:pad + wide, :] + pltpu.roll(bb, 127, 1))
        g_label = g_label - pl_
        g = -pl_
        if e > 0:
            ps = jnp.exp(a + s_ref[e - 1, pad:pad + wide, :] + b_ref[pad + e: pad + e + wide, :])
            g_blank = g_blank - ps
            g = g - ps
        grads_ref[2 + e] = from_diag(g)
    grads_ref[0] = from_diag(g_blank)
    grads_ref[1] = from_diag(g_label)


def lattice(feats, t_len, u_len, slots):
    _, rows, frames = feats.shape
    wide = frames + 128
    total = wide + 16
    reach = feats.shape[0] - 3
    return pl.pallas_call(
        partial(lattice_kernel, slots),
        out_shape=(jax.ShapeDtypeStruct(feats.shape, jnp.float32), jax.ShapeDtypeStruct((8, 128), jnp.float32)),
        in_specs=[pl.BlockSpec(memory_space=pltpu.VMEM), pl.BlockSpec(memory_space=pltpu.SMEM), pl.BlockSpec(memory_space=pltpu.SMEM)],
        out_specs=(pl.BlockSpec(memory_space=pltpu.VMEM),) * 2,
        scratch_shapes=[pltpu.VMEM((reach, total, 128), jnp.float32), pltpu.VMEM((reach + 1, total, 128), jnp.float32),
                        pltpu.VMEM((reach + 1, total, 128), jnp.float32), pltpu.VMEM((total, 128), jnp.float32),
                        pltpu.VMEM((total, 128), jnp.float32), pltpu.VMEM((total, 128), jnp.float32)],
        compiler_params=pltpu.CompilerParams(vmem_limit_bytes=48 << 20),
        name="lattice",
    )(feats, t_len, u_len)


GROUP=5
CHUNK=256

def nn(a,b): return jnp.dot(a,b,preferred_element_type=jnp.float32)
def nt(a,b): return lax.dot_general(a,b,(((1,),(1,)),((),())),preferred_element_type=jnp.float32)

def fold8(x, op):
    parts=[x[i:i+8] for i in range(0,x.shape[0],8)]
    while len(parts)>1:
        parts=[op(parts[i],parts[i+1]) if i+1<len(parts) else parts[i] for i in range(0,len(parts),2)]
    return parts[0]

def joint_fwd_kernel(groups, durs, labels_ref, enc_ref, pred_ref, wt_ref, feats_ref, p_ref, tok_ref):
    step=pl.program_id(0)
    vocab=p_ref.shape[2]
    u=step//groups
    g=step%groups
    for j in range(GROUP):
        k=g*GROUP+j
        hid=jnp.tanh(enc_ref[...]+pred_ref[0,:,j:j+1]).astype(jnp.bfloat16)
        tops=[]
        for c in range(0,vocab,CHUNK):
            t=nn(wt_ref[c:c+CHUNK,:],hid)
            tok_ref[j%2,c:c+CHUNK,:]=t
            tops.append(fold8(t,jnp.maximum))
        dl=nn(wt_ref[vocab:,:],hid)[:8]
        top=jnp.max(reduce(jnp.maximum,tops),0,keepdims=True)
        sums=[]
        for c in range(0,vocab,CHUNK):
            e=jnp.exp(tok_ref[j%2,c:c+CHUNK,:]-top)
            p_ref[0,j,c:c+CHUNK,:]=e.astype(jnp.bfloat16)
            sums.append(fold8(e,jnp.add))
        total=jnp.sum(reduce(jnp.add,sums),0,keepdims=True)
        lse=top+jnp.log(total)
        row=u*32+k
        feats_ref[0,pl.ds(row,1),:]=tok_ref[j%2,0:1,:]-lse
        feats_ref[1,pl.ds(row,1),:]=tok_ref[j%2,pl.ds(labels_ref[u,k],1),:]-lse
        real=lax.broadcasted_iota(jnp.int32,dl.shape,0)<durs
        dtop=jnp.max(jnp.where(real,dl,-1e30),0,keepdims=True)
        dlse=dtop+jnp.log(jnp.sum(jnp.where(real,jnp.exp(dl-dtop),0.0),0,keepdims=True))
        dlp=dl-dlse
        for e in range(durs):
            feats_ref[2+e,pl.ds(row,1),:]=dlp[e:e+1]
        feats_ref[2+durs,pl.ds(row,1),:]=1.0/total

def joint_forward(enc_t, pred_t, labels, w_t, vocab, durs, frames):
    joint, rows=enc_t.shape
    utts,slots=labels.shape
    groups=slots//GROUP
    return pl.pallas_call(
        partial(joint_fwd_kernel,groups,durs),
        grid=(utts*groups,),
        in_specs=[pl.BlockSpec(memory_space=pltpu.SMEM),
            pl.BlockSpec((joint,frames),lambda s:(0,s//groups)),
            pl.BlockSpec((1,joint,8),lambda s:(s,0,0)),
            pl.BlockSpec(w_t.shape,lambda s:(0,0))],
        out_specs=[pl.BlockSpec((3+durs,utts*32,frames),lambda s:(0,0,0)),
            pl.BlockSpec((1,GROUP,vocab,frames),lambda s:(s,0,0,0))],
        out_shape=[jax.ShapeDtypeStruct((3+durs,utts*32,frames),jnp.float32),
            jax.ShapeDtypeStruct((utts*groups,GROUP,vocab,frames),jnp.bfloat16)],
        scratch_shapes=[pltpu.VMEM((2,vocab,frames),jnp.float32)],
        compiler_params=pltpu.CompilerParams(vmem_limit_bytes=50<<20),
        name="joint_forward",
    )(labels,enc_t,pred_t,w_t)

def joint_bwd_kernel(groups, durs, labels_ref, enc_ref, pred_ref, w_ref, feats_ref, grads_ref, p_ref, genc_ref, gpred_ref, gtok_ref, gdur_ref, h_ref, d_ref, acc_ref, th_ref):
    step=pl.program_id(0)
    vocab=p_ref.shape[2]
    frames=p_ref.shape[3]
    u=step//groups
    g=step%groups

    @pl.when(step==0)
    def _():
        acc_ref[...]=jnp.zeros_like(acc_ref)
    @pl.when(g==0)
    def _():
        genc_ref[...]=jnp.zeros_like(genc_ref)
    for j in range(GROUP):
        k=g*GROUP+j
        row=u*32+k
        cols=slice(j*frames,(j+1)*frames)
        th=jnp.tanh(enc_ref[...]+pred_ref[0,:,j:j+1])
        h_ref[:,cols]=th.astype(jnp.bfloat16)
        th_ref[...]=th
        gb=grads_ref[0,pl.ds(row,1),:]
        gl=grads_ref[1,pl.ds(row,1),:]
        scale=-(gb+gl)*feats_ref[2+durs,pl.ds(row,1),:]
        for c in range(0,vocab,CHUNK):
            d_ref[c:c+CHUNK,cols]=(p_ref[0,j,c:c+CHUNK,:].astype(jnp.float32)*scale).astype(jnp.bfloat16)
        label=labels_ref[u,k]
        def fix(base):
            v=p_ref[0,j,pl.ds(base,16),:].astype(jnp.float32)*scale
            at=lax.broadcasted_iota(jnp.int32,v.shape,0)+base
            v=v+jnp.where(at==0,gb,0.0)+jnp.where(at==label,gl,0.0)
            d_ref[pl.ds(base,16),cols]=v.astype(jnp.bfloat16)
        fix(0)
        fix(pl.multiple_of((label//16)*16,16))
        gd=[grads_ref[2+e,pl.ds(row,1),:] for e in range(durs)]
        gsum=reduce(jnp.add,gd)
        at=lax.broadcasted_iota(jnp.int32,(16,frames),0)
        dd=jnp.zeros((16,frames),jnp.float32)
        for e in range(durs):
            dd=jnp.where(at==e,gd[e]-gsum*jnp.exp(feats_ref[2+e,pl.ds(row,1),:]),dd)
        d_ref[vocab:vocab+16,cols]=dd.astype(jnp.bfloat16)
        d_ref[vocab+16:,cols]=jnp.zeros((d_ref.shape[0]-vocab-16,frames),jnp.bfloat16)
        dh=nn(w_ref[...],d_ref[:,cols])
        th=th_ref[...]
        dp=dh*(1.0-th*th)
        genc_ref[...]+=dp
        gpred_ref[0,:,j:j+1]=jnp.sum(dp,1,keepdims=True)
    acc_ref[...]+=nt(h_ref[...],d_ref[...])
    @pl.when(step==pl.num_programs(0)-1)
    def _():
        gtok_ref[...]=acc_ref[:,:vocab].astype(jnp.bfloat16)
        gdur_ref[...]=acc_ref[:,vocab:].astype(jnp.bfloat16)

def joint_backward(enc_t, pred_t, labels, w, feats, grads, p, vocab, durs, frames):
    joint, rows=enc_t.shape
    utts,slots=labels.shape
    groups=slots//GROUP
    full=lambda a: pl.BlockSpec(a.shape,lambda s:(0,)*a.ndim)
    return pl.pallas_call(
        partial(joint_bwd_kernel,groups,durs),
        grid=(utts*groups,),
        in_specs=[pl.BlockSpec(memory_space=pltpu.SMEM),
            pl.BlockSpec((joint,frames),lambda s:(0,s//groups)),
            pl.BlockSpec((1,joint,8),lambda s:(s,0,0)),
            full(w),full(feats),full(grads),
            pl.BlockSpec((1,GROUP,vocab,frames),lambda s:(s,0,0,0))],
        out_specs=[pl.BlockSpec((joint,frames),lambda s:(0,s//groups)),
            pl.BlockSpec((1,joint,8),lambda s:(s,0,0)),
            pl.BlockSpec((joint,vocab),lambda s:(0,0)),
            pl.BlockSpec((joint,128),lambda s:(0,0))],
        out_shape=[jax.ShapeDtypeStruct((joint,rows),jnp.float32),
            jax.ShapeDtypeStruct((utts*groups,joint,8),jnp.float32),
            jax.ShapeDtypeStruct((joint,vocab),jnp.bfloat16),
            jax.ShapeDtypeStruct((joint,128),jnp.bfloat16)],
        scratch_shapes=[pltpu.VMEM((joint,GROUP*frames),jnp.bfloat16),
            pltpu.VMEM((vocab+128,GROUP*frames),jnp.bfloat16),
            pltpu.VMEM((joint,vocab+128),jnp.float32),pltpu.VMEM((joint,frames),jnp.float32)],
        compiler_params=pltpu.CompilerParams(vmem_limit_bytes=56<<20),
        name="joint_backward",
    )(labels,enc_t,pred_t,w,feats,grads,p)


MESH=pl.DeviceIdType.MESH
QA = QB = 16
HALF = 2 * QA + QB
TILE = 2 * HALF


def place():
    dp=lax.axis_index("dp"); fs=lax.axis_index("fsdp")
    return dp, fs, dp//2, dp%2, fs//2, fs%2

def greet(n1, dp, fs, a, c, i1, i2):
    barrier=pltpu.get_barrier_semaphore()
    for d in range(1,n1):
        pl.semaphore_signal(barrier,inc=1,device_id=(dp,lax.rem(i1+d,n1)*2+i2),device_id_type=MESH)
    pl.semaphore_signal(barrier,inc=1,device_id=(dp,i1*2+1-i2),device_id_type=MESH)
    pl.semaphore_signal(barrier,inc=1,device_id=((1-a)*2+c,fs),device_id_type=MESH)
    pl.semaphore_signal(barrier,inc=1,device_id=(a*2+1-c,fs),device_id_type=MESH)
    pl.semaphore_wait(barrier,n1+2)

def remote(s, d, ss, rs, dev):
    return pltpu.make_async_remote_copy(src_ref=s,dst_ref=d,send_sem=ss,recv_sem=rs,device_id=dev,device_id_type=MESH)

def rows(base, size):
    return pl.ds(pl.multiple_of(base,16),size)

class Beats:
    def __init__(self, tick=None, total=0, sites=None):
        self.tick = tick
        self.total = total
        self.at = 0
        self.credit = 0.0
        self.scale = total / sites if sites else 1.0

    def grant(self, count):
        self.credit += count * self.scale
        steps = min(int(self.credit), self.total - self.at)
        self.credit -= int(self.credit)
        first = self.at
        self.at += steps
        return first, steps

    def span(self, low, high):
        def step(i, carry):
            self.tick(i)
            return carry

        lax.fori_loop(low, high, step, 0)

    def loop(self, sites, count=None):
        if self.tick is None:
            return lambda i: None
        first, steps = self.grant(sites)
        count = count or sites
        return lambda i: self.span(first + i * steps // count, first + (i + 1) * steps // count)

    def run(self, count):
        if self.tick is None:
            return
        first, steps = self.grant(count)
        if steps:
            self.span(first, first + steps)

    def until(self, step):
        if self.at < step:
            self.span(self.at, step)
            self.at = step

    def rest(self):
        self.until(self.total)


class ScatterEngine:
    def __init__(self, n1, plan, lag, srcs, out, own, gc, gx, gy, gz, gf, fin, lo, sc, rc, sx, rx, sy, ry, sz, rz, sf, rf, se, re, wo):
        dp, fs, a, c, i1, i2 = place()
        ypeer = (dp, i1 * 2 + 1 - i2)
        xpeer = ((1 - a) * 2 + c, fs)
        cpeer = (a * 2 + 1 - c, fs)
        tiles = sum(count for _, count in plan)
        main = rows(a * QA, QA + QB)
        middle = pl.ds(QA, QB)

        def quarter(aa):
            return rows(aa * (QA + QB), QA)

        def cwait(t):
            return remote(own.at[t], gc.at[t], sc.at[0], rc.at[t], cpeer)

        def xcopy(t):
            return remote(own.at[t, :, :, quarter(1 - a), :], gx.at[t], sx.at[0], rx.at[t], xpeer)

        def ycopy(t):
            return remote(own.at[t, :, 1 - i2, main, :], gy.at[t], sy.at[0], ry.at[t], ypeer)

        def zcopy(t, j):
            return remote(own.at[t, j, i2, main, :], gz.at[t, i1], sz.at[0], rz.at[t], (dp, j * 2 + i2))

        def zin(t):
            arrived = gz.at[t, pl.ds(0, n1 - 1)]
            return remote(arrived, arrived, sz.at[0], rz.at[t], ypeer)

        def fcopy(t):
            return remote(own.at[t, i1, i2, main, :], gf.at[t], sf.at[0], rf.at[t], xpeer)

        def ecopy(t):
            return remote(fin.at[t, c], fin.at[t, c], se.at[0], re.at[t], cpeer)

        def ein(t):
            return remote(fin.at[t, 1 - c], fin.at[t, 1 - c], se.at[0], re.at[t], cpeer)

        def store(t):
            return pltpu.make_async_copy(fin.at[t], out.at[t], wo.at[0])

        def stage_c(t):
            first = 0
            for src, (base, count) in zip(srcs, plan):

                @pl.when((t >= first) & (t < first + count))
                def _(src=src, skip=base - first):
                    at = (t + skip) * TILE
                    pltpu.make_async_copy(src.at[:, :, rows(at + c * HALF, HALF), :], own.at[t], lo.at[t]).start()
                    remote(src.at[:, :, rows(at + (1 - c) * HALF, HALF), :], gc.at[t], sc.at[0], rc.at[t], cpeer).start()

                first += count

        def stage_x(t):
            pltpu.make_async_copy(own.at[t], own.at[t], lo.at[t]).wait()
            cwait(t).wait_recv()
            own[t] = own[t] + gc[t]
            xcopy(t).start()

        def stage_y(t):
            xcopy(t).wait_recv()
            own[t, :, :, quarter(a), :] = own[t, :, :, quarter(a), :] + gx[t]
            ycopy(t).start()

        def stage_z(t):
            ycopy(t).wait_recv()
            own[t, :, i2, main, :] = own[t, :, i2, main, :] + gy[t]
            for d in range(1, n1):
                zcopy(t, lax.rem(i1 + d, n1)).start()

        def stage_f(t):
            total = own[t, i1, i2, main, :].astype(jnp.float32)
            zin(t).wait_recv()
            for d in range(1, n1):
                j = lax.rem(i1 + n1 - d, n1)
                total = total + gz[t, j].astype(jnp.float32)
            own[t, i1, i2, main, :] = total.astype(jnp.bfloat16)
            fcopy(t).start()

        def stage_e(t):
            fcopy(t).wait_recv()
            fin[t, c, quarter(a), :] = own[t, i1, i2, quarter(a), :]
            fin[t, c, quarter(1 - a), :] = gf[t, rows((1 - a) * QB, QA), :]
            fin[t, c, middle, :] = own[t, i1, i2, middle, :] + gf[t, rows(a * QA, QB), :]
            ecopy(t).start()

        def stage_o(t):
            ein(t).wait_recv()
            store(t).start()

        stages = (stage_c, stage_x, stage_y, stage_z, stage_f, stage_e, stage_o)

        def tick(tau):
            for place_of, stage in enumerate(stages):
                t = tau - place_of * lag

                @pl.when((t >= 0) & (t < tiles))
                def _(stage=stage, t=t):
                    stage(t)

        def finish():
            for sent, sem in (
                (own, sc), (gx, sx), (gy, sy), (gz.at[:, pl.ds(0, n1 - 1)], sz), (gf, sf), (fin.at[:, 0], se),
            ):
                remote(sent, sent, sem.at[0], rc.at[0], cpeer).wait_send()
            pltpu.make_async_copy(fin, fin, wo.at[0]).wait()

        self.tick = tick
        self.total = tiles + (len(stages) - 1) * lag
        self.finish = finish


def scatter_plan(sources):
    return tuple((first, count) for _, first, count in sources)


def scatter_scratch(n, tiles):
    n1 = n // 2
    dma = pltpu.SemaphoreType.DMA
    v = lambda *shape: pltpu.VMEM((tiles,) + shape + (WIDE,), jnp.bfloat16)
    one = dma((1,))
    each = dma((tiles,))
    return [
        v(n1, 2, HALF), v(n1, 2, HALF), v(n1, 2, QA), v(n1, QA + QB), v(n1, QA + QB), v(QA + QB), v(2, HALF),
        each, one, each, one, each, one, each, one, each, one, each, one, each, one,
    ]


def riding_kernel(kernel, counts, plan, lag, n1, sites, groups, *refs):
    n_in, n_out, n_scratch = counts
    k = len(plan)
    ins, refs = refs[:n_in], refs[n_in:]
    srcs, refs = refs[:k], refs[k:]
    outs, refs = refs[:n_out], refs[n_out:]
    share, refs = refs[0], refs[1:]
    scratch, refs = refs[:n_scratch], refs[n_scratch:]
    if groups:
        meet(groups, 2 * n1)()
    else:
        greet(n1, *place())
    engine = ScatterEngine(n1, plan, lag, srcs, share, *refs)
    beats = Beats(engine.tick, engine.total, sites)
    kernel(beats, *ins, *outs, *scratch)
    beats.rest()
    engine.finish()


def call(kernel, args, in_specs, out_specs, out_shape, scratch, name, ride=None, collective_id=None, sites=None, groups=0, lag=2):
    if not ride:
        return pl.pallas_call(
            partial(kernel, Beats()),
            in_specs=in_specs,
            out_specs=out_specs,
            out_shape=out_shape,
            scratch_shapes=scratch,
            compiler_params=pltpu.CompilerParams(vmem_limit_bytes=60 << 20),
            name=name,
        )(*args)
    n = lax.axis_size("fsdp")
    tiles = sum(count for _, _, count in ride)
    counts = (len(args), len(out_shape), len(scratch))
    *outs, share = pl.pallas_call(
        partial(riding_kernel, kernel, counts, scatter_plan(ride), lag, n // 2, sites, groups),
        in_specs=in_specs + [ANY_SPEC] * len(ride),
        out_specs=out_specs + [ANY_SPEC],
        out_shape=out_shape + [sds((tiles, 2, HALF, WIDE), BF16)],
        scratch_shapes=scratch + scatter_scratch(n, tiles),
        compiler_params=pltpu.CompilerParams(collective_id=collective_id, has_side_effects=True, vmem_limit_bytes=61 << 20),
        name=name + "_and_scatter",
    )(*args, *[grads.reshape(n // 2, 2, -1, WIDE) for grads, _, _ in ride])
    return outs, share.reshape(tiles * TILE, WIDE)


def idle_kernel(beats):
    pass


def scatter(ride, collective_id):
    return call(idle_kernel, [], [], [], [], [], "idle", ride, collective_id)[1]


def pooled(parts):
    counts = [x[8:9] for x in parts]
    count = sum(counts[1:], counts[0])
    mean = sum((x[0:4] * n for x, n in zip(parts[1:], counts[1:])), parts[0][0:4] * counts[0]) / count
    dev = jnp.zeros_like(mean)
    for x, n in zip(parts, counts):
        gap = x[0:4] - mean
        dev = dev + (x[4:8] + gap * gap * n)
    return mean, dev, count


CHUNK_ROWS = 64
WIDE = 512
PLACE = ("p_out", "s_in", "s_out", "p_in", "w_proj", "w_joint", "f_in", "f_out")


def tn(a, b):
    return lax.dot_general(a, b, (((0,), (0,)), ((), ())), preferred_element_type=jnp.float32)


def row_loop(count, body, init=0):
    def step(i, carry):
        return body(pl.ds(pl.multiple_of(i * CHUNK_ROWS, CHUNK_ROWS), CHUNK_ROWS), i, carry)

    return lax.fori_loop(0, count // CHUNK_ROWS, step, init)


def ln_parts(v):
    centred = v - jnp.mean(v, -1, keepdims=True)
    rstd = lax.rsqrt(jnp.mean(centred * centred, -1, keepdims=True) + EPS)
    return centred * rstd, rstd


def ln_back(v, gain, grad):
    hat, rstd = ln_parts(v)
    dy = grad * gain
    dv = rstd * (dy - jnp.mean(dy, -1, keepdims=True) - hat * jnp.mean(dy * hat, -1, keepdims=True))
    return dv, fold8(grad * hat, jnp.add)


def offsets(n, width, ff):
    low = width // n
    tall = ff // n
    sizes = {
        "p_out": low, "s_in": low * (ff // WIDE), "s_out": tall, "p_in": 2 * low,
        "w_proj": low, "w_joint": 3 * low, "f_in": low * (ff // WIDE), "f_out": tall,
    }
    table = {}
    at = 0
    for name in PLACE:
        table[name] = at
        at += sizes[name]
    return table, at


class Mover:
    def __init__(self, sems, used=0):
        self.sems = sems
        self.used = used
        self.pending = []

    def take(self):
        self.used += 1
        return self.sems.at[self.used - 1]

    def load(self, src, dst):
        cp = pltpu.make_async_copy(src, dst, self.take())
        cp.start()
        return cp

    def put(self, src, dst):
        cp = pltpu.make_async_copy(src, dst, self.take())
        cp.start()
        self.pending.append(cp)

    def load_weight(self, whole, at, dst):
        flat = len(whole.shape) == 3
        n = whole.shape[0] if flat else 2 * whole.shape[0]
        height = dst.shape[0] // n
        sem = self.take()

        def one(s, carry):
            for b in range(dst.shape[1] // WIDE):
                pltpu.make_async_copy(
                    (whole.at[s] if flat else whole.at[s // 2, s % 2]).at[pl.ds(at + b * height, height), :],
                    dst.at[pl.ds(pl.multiple_of(s * height, 16), height), pl.ds(b * WIDE, WIDE)],
                    sem,
                ).start()
            return carry

        lax.fori_loop(0, n, one, 0)
        return pltpu.make_async_copy(dst, dst, sem)

    def put_weight(self, src, grads, at):
        n = grads.shape[0]
        height = src.shape[0] // n
        sem = self.take()

        def one(s, carry):
            for b in range(src.shape[1] // WIDE):
                pltpu.make_async_copy(
                    src.at[pl.ds(pl.multiple_of(s * height, 16), height), pl.ds(b * WIDE, WIDE)],
                    grads.at[s, pl.ds(at + b * height, height), :],
                    sem,
                ).start()
            return carry

        lax.fori_loop(0, n, one, 0)
        self.pending.append(pltpu.make_async_copy(src, src, sem))

    def finish(self):
        for cp in self.pending:
            cp.wait()
        self.pending = []


def valid_rows_of(t_ref, frames, i):
    per = frames // CHUNK_ROWS
    t_len = t_ref[i // per]
    at = lax.broadcasted_iota(jnp.int32, (CHUNK_ROWS, 1), 0) + lax.rem(i, per) * CHUNK_ROWS
    return jnp.where(at < t_len, 1.0, 0.0)


def write_rows(out, base, vec):
    for i in range(vec.shape[1] // 128):
        out[base + i : base + i + 1, :] = vec[:, i * 128 : (i + 1) * 128]


def read_rows(ref, base, width):
    return jnp.concatenate([ref[base + i : base + i + 1, :] for i in range(width // 128)], 1)


def fill_gated(utts, frames, t_ref, r, gp):
    width = gp.shape[1]
    span = frames + 16
    per = frames // CHUNK_ROWS
    for u in range(utts):
        gp[u * span : u * span + 8, :] = jnp.zeros((8, width), jnp.float32)
        gp[u * span + 8 + frames : (u + 1) * span, :] = jnp.zeros((8, width), jnp.float32)

    def gate(rr, i, c):
        g = r[rr, :width] * jax.nn.sigmoid(r[rr, width:]) * valid_rows_of(t_ref, frames, i)
        at = (i // per) * span + 8 + lax.rem(i, per) * CHUNK_ROWS
        gp[pl.ds(pl.multiple_of(at, 8), CHUNK_ROWS), :] = g
        return c

    row_loop(utts * frames, gate)


def window(gp, frames, i):
    per = frames // CHUNK_ROWS
    at = (i // per) * (frames + 16) + lax.rem(i, per) * CHUNK_ROWS
    return gp[pl.ds(pl.multiple_of(at, 8), CHUNK_ROWS + 16), :]


def spread(gp, utts, frames, i, taps, flip=False):
    win = window(gp, frames, i)
    count = taps.shape[0]
    total = None
    for j in range(count):
        shift = 8 - count // 2 + (count - 1 - j if flip else j)
        term = win[shift : shift + CHUNK_ROWS] * taps[j : j + 1]
        total = term if total is None else total + term
    return total


def ffn_bwd(rows, v_ref, gain, w_in, w_out, h, loads, g_ref, gb, normed, dact, act, dh, dn, dw_in, dw_out, mover, grads, at_in, at_out, beats):
    def prepare(rr, i, c):
        normed[rr, :] = (ln_parts(v_ref[rr, :].astype(jnp.float32))[0] * gain).astype(jnp.bfloat16)
        gb[rr, :] = (0.5 * g_ref[rr, :]).astype(jnp.bfloat16)
        return c

    row_loop(rows, prepare)
    w_out[1].wait()
    for b in range(h.shape[0]):
        cols = slice(b * WIDE, (b + 1) * WIDE)
        dact[...] = nt(gb[...], w_out[0][cols, :])
        beats.run(1)
        loads[b].wait()

        def slope(rr, i, c):
            v = h[b, rr, :]
            sg = jax.nn.sigmoid(v)
            act[rr, :] = (v * sg).astype(jnp.bfloat16)
            dh[rr, cols] = (dact[rr, :] * (sg * (1.0 + v * (1.0 - sg)))).astype(jnp.bfloat16)
            return c

        row_loop(rows, slope)
        beats.run(1)
        dw_out[cols, :] = tn(act[...], gb[...]).astype(jnp.bfloat16)
        beats.run(1)
        dw_in[:, cols] = tn(normed[...], dh[:, cols]).astype(jnp.bfloat16)
        beats.run(1)
    mover.put_weight(dw_out, grads, at_out)
    mover.put_weight(dw_in, grads, at_in)
    w_in[1].wait()
    dn[...] = nt(dh[...], w_in[0][...])
    beats.run(2)

    def back(rr, i, total):
        dv, dg = ln_back(v_ref[rr, :].astype(jnp.float32), gain, dn[rr, :])
        g_ref[rr, :] = g_ref[rr, :] + dv
        return total + dg

    return row_loop(rows, back, jnp.zeros((8, g_ref.shape[1]), jnp.float32))


def down(folded):
    return jnp.sum(folded, 0, keepdims=True)


def back_one_kernel(table, held, beats, grad_ref, y4_ref, y3_ref, d_ref, pooled_ref, small, whole, h_hbm, g_out, db_out, grads, sums, gain_out,
                    w_pout, w_sin, w_sout, g, gb, normed, dact, act, dh, dn, dw_in, dw_out, dw_pout, h, db, sems):
    rows, width = g.shape
    mover = Mover(sems)
    gains = small[...]
    sout = mover.load_weight(whole, held["s_out"], w_sout)
    loads = [mover.load(h_hbm.at[b], h.at[b]) for b in range(h.shape[0])]
    sin = mover.load_weight(whole, held["s_in"], w_sin)
    wo = mover.load_weight(whole, held["p_out"], w_pout)
    beats.run(5)

    def first(rr, i, total):
        dv, dg = ln_back(y4_ref[rr, :], gains[4:5], grad_ref[rr, :])
        g[rr, :] = dv
        return total + dg

    gain4 = down(row_loop(rows, first, jnp.zeros((8, width), jnp.float32)))
    gain3 = down(ffn_bwd(rows, y3_ref, gains[3:4], (w_sin, sin), (w_sout, sout), h, loads, g, gb, normed, dact, act, dh, dn,
                         dw_in, dw_out, mover, grads, table["s_in"], table["s_out"], beats))
    mover.put(g, g_out)
    gain_out[...] = jnp.concatenate([gain3, gain4, jnp.zeros((6, width), jnp.float32)], 0)
    mean = read_rows(pooled_ref, 0, width)
    istd = lax.rsqrt(read_rows(pooled_ref, 4, width) / pooled_ref[8:9, 0:1] + EPS)

    def cast(rr, i, c):
        gb[rr, :] = g[rr, :].astype(jnp.bfloat16)
        return c

    row_loop(rows, cast)
    wo.wait()
    dact[...] = nt(gb[...], w_pout[...])
    beats.run(1)

    def bn(rr, i, totals):
        z = (d_ref[rr, :] - mean) * istd
        b = z * gains[14:15] + gains[15:16]
        sg = jax.nn.sigmoid(b)
        act[rr, :] = (b * sg).astype(jnp.bfloat16)
        db_chunk = dact[rr, :] * (sg * (1.0 + b * (1.0 - sg)))
        db[rr, :] = db_chunk
        return totals[0] + fold8(db_chunk, jnp.add), totals[1] + fold8(db_chunk * z, jnp.add)

    zero = jnp.zeros((8, width), jnp.float32)
    one, two = row_loop(rows, bn, (zero, zero))
    beats.run(2)
    mover.put(db, db_out)
    write_rows(sums, 0, down(one))
    write_rows(sums, 4, down(two))
    sums[8:16, :] = jnp.zeros((8, 128), jnp.float32)
    dw_pout[...] = tn(act[...], gb[...]).astype(jnp.bfloat16)
    mover.put_weight(dw_pout, grads, table["p_out"])
    mover.finish()


def back_two_kernel(utts, table, held, start, end, beats, t_ref, x_ref, y1_ref, y2_ref, r_ref, t_in, c_ref, d_ref, db_ref, g_in, pooled_ref, local_ref, late_ref, small, whole, h_hbm,
                    g_out, grads, sums_ref,
                    w_pin, w_proj, w_joint, w_fin, w_fout, g, gb, normed, dact, act, dh, dn, dw_pin, dw_proj, dw_joint, dw_in, dw_out, h, gp, dd, dr, dt, sm, sems, *meeting):
    rows, width = g.shape
    frames = rows // utts
    mover = Mover(sems)
    gains = small[...]
    wi = mover.load_weight(whole, held["p_in"], w_pin)
    wp = mover.load_weight(whole, held["w_proj"], w_proj)
    wj = mover.load_weight(whole, held["w_joint"], w_joint)
    fout = mover.load_weight(whole, held["f_out"], w_fout)
    loads = [mover.load(h_hbm.at[b], h.at[b]) for b in range(h.shape[0])]
    fin = mover.load_weight(whole, held["f_in"], w_fin)
    mean = read_rows(pooled_ref, 0, width)
    count = pooled_ref[8:9, 0:1]
    istd = lax.rsqrt(read_rows(pooled_ref, 4, width) / count + EPS)
    taps = gains[5:14]
    ntaps = taps.shape[0]
    span = frames + 16
    per = frames // CHUNK_ROWS
    beats.run(5)
    exchange = Exchange("sum", meeting[0].shape[0], meeting[1].shape[0], *meeting)
    exchange.begin(local_ref[...])
    fill_gated(utts, frames, t_ref, r_ref, gp)
    exchange.middle()
    beats.run(1)
    for u in range(utts):
        dd[u * span : u * span + 8, :] = jnp.zeros((8, width), jnp.float32)
        dd[u * span + 8 + frames : (u + 1) * span, :] = jnp.zeros((8, width), jnp.float32)

    sums_ref[...] = exchange.end()
    bias_sum = read_rows(sums_ref, 0, width)
    gain_sum = read_rows(sums_ref, 4, width)

    def bn(rr, i, c):
        z = (d_ref[rr, :] - mean) * istd
        v = gains[14:15] * istd * (db_ref[rr, :] - valid_rows_of(t_ref, frames, i) * (bias_sum + z * gain_sum) / count)
        at = (i // per) * span + 8 + lax.rem(i, per) * CHUNK_ROWS
        dd[pl.ds(pl.multiple_of(at, 8), CHUNK_ROWS), :] = v
        return c

    row_loop(rows, bn)

    def conv(rr, i, totals):
        dg = spread(dd, utts, frames, i, taps, True) * valid_rows_of(t_ref, frames, i)
        sg = jax.nn.sigmoid(r_ref[rr, width:])
        dr[rr, :width] = (dg * sg).astype(jnp.bfloat16)
        dr[rr, width:] = (dg * r_ref[rr, :width] * sg * (1.0 - sg)).astype(jnp.bfloat16)
        win = window(gp, frames, i)
        mine = window(dd, frames, i)[8 : 8 + CHUNK_ROWS]
        normed[rr, :] = (ln_parts(y2_ref[rr, :])[0] * gains[2:3]).astype(jnp.bfloat16)
        return tuple(
            totals[j] + fold8(win[8 - ntaps // 2 + j : 8 - ntaps // 2 + j + CHUNK_ROWS] * mine, jnp.add) for j in range(ntaps)
        )

    zero = jnp.zeros((8, width), jnp.float32)
    tap_grads = [down(x) for x in row_loop(rows, conv, (zero,) * ntaps)]
    beats.run(2)
    for b in range(2):
        cols = slice(b * width, (b + 1) * width)
        dw_pin[:, cols] = tn(normed[...], dr[:, cols]).astype(jnp.bfloat16)
    mover.put_weight(dw_pin, grads, table["p_in"] - start)
    beats.run(2)
    wi.wait()
    dn[...] = nt(dr[...], w_pin[...])
    beats.run(1)

    def back_conv(rr, i, total):
        dv, dg = ln_back(y2_ref[rr, :], gains[2:3], dn[rr, :])
        v = g_in[rr, :] + dv
        g[rr, :] = v
        gb[rr, :] = v.astype(jnp.bfloat16)
        normed[rr, :] = (ln_parts(y1_ref[rr, :])[0] * gains[1:2]).astype(jnp.bfloat16)
        return total + dg

    gain2 = down(row_loop(rows, back_conv, zero))
    dw_proj[...] = tn(c_ref[...], gb[...]).astype(jnp.bfloat16)
    mover.put_weight(dw_proj, grads, table["w_proj"] - start)
    beats.run(1)
    wp.wait()
    act[...] = nt(gb[...], w_proj[...]).astype(jnp.bfloat16)
    pairs = width // 128
    side = lax.broadcasted_iota(jnp.int32, (frames, 128), 1) < 64
    key_at = lax.broadcasted_iota(jnp.int32, (frames, 1), 0)
    hook = beats.loop(utts * pairs)

    def pair_step(m, carry):
        hook(m)
        u = m // pairs
        base = lax.rem(m, pairs) * 128
        rr = pl.ds(pl.multiple_of(u * frames, frames), frames)
        at = [pl.ds(pl.multiple_of(base + b * width, 128), 128) for b in range(3)]
        bias = jnp.where(key_at < t_ref[u], 0.0, MASKED)
        q = t_in[rr, at[0]]
        k = t_in[rr, at[1]]
        v = t_in[rr, at[2]]
        dc = act[rr, at[0]]
        got = []
        for half in range(2):
            mine = side if half == 0 else ~side
            nothing = jnp.zeros_like(k)
            s = nt(jnp.where(mine, k, nothing), q) * 0.125 + bias
            p = jnp.exp(s - jnp.max(s, 0, keepdims=True))
            p = p * (1.0 / jnp.sum(p, 0, keepdims=True))
            dp = nt(jnp.where(mine, v, nothing), dc)
            ds = (p * (dp - jnp.sum(dp * p, 0, keepdims=True))).astype(jnp.bfloat16)
            got.append((tn(ds, k) * 0.125, nn(ds, q) * 0.125, nn(p.astype(jnp.bfloat16), dc)))
        for b in range(3):
            dt[rr, at[b]] = jnp.where(side, got[0][b], got[1][b]).astype(jnp.bfloat16)
        return carry

    lax.fori_loop(0, utts * pairs, pair_step, 0)
    for b in range(3):
        cols = slice(b * width, (b + 1) * width)
        dw_joint[:, cols] = tn(normed[...], dt[:, cols]).astype(jnp.bfloat16)
    mover.put_weight(dw_joint, grads, table["w_joint"] - start)
    beats.run(2)
    wj.wait()
    dn[...] = nt(dt[...], w_joint[...])
    beats.run(1)

    def back_attend(rr, i, total):
        dv, dg = ln_back(y1_ref[rr, :], gains[1:2], dn[rr, :])
        g[rr, :] = g[rr, :] + dv
        return total + dg

    gain1 = down(row_loop(rows, back_attend, zero))
    gain0 = down(ffn_bwd(rows, x_ref, gains[0:1], (w_fin, fin), (w_fout, fout), h, loads, g, gb, normed, dact, act, dh, dn,
                         dw_in, dw_out, mover, grads, table["f_in"] - start, table["f_out"] - start, beats))
    mover.put(g, g_out)
    packed = jnp.concatenate([gain0, gain1, gain2, late_ref[0:2, :]] + tap_grads + [jnp.zeros((2, width), jnp.float32)], 0)
    n = grads.shape[0]
    low = width // n
    for s in range(n):
        sm[s] = jnp.concatenate([packed[:, s * low : (s + 1) * low], jnp.zeros((16, WIDE - low), jnp.float32)], 1).astype(jnp.bfloat16)
    mover.put(sm, grads.at[:, pl.ds(end - start, 16), :])
    mover.finish()


VMEM_SPEC = pl.BlockSpec(memory_space=pltpu.VMEM)
SMEM_SPEC = pl.BlockSpec(memory_space=pltpu.SMEM)
ANY_SPEC = pl.BlockSpec(memory_space=pl.ANY)
F32 = jnp.float32
BF16 = jnp.bfloat16


def sds(shape, dtype=jnp.float32):
    return jax.ShapeDtypeStruct(shape, dtype)


def tiled(count):
    return -(-count // TILE) * TILE


def back_one(grad, y4, y3, d, pooled, small, whole, h, ff, held, ride=None, collective_id=None):
    rows, width = grad.shape
    n = whole.shape[0]
    table, _ = offsets(n, width, ff)
    nb = ff // WIDE
    v = pltpu.VMEM
    return call(
        partial(back_one_kernel, table, held),
        (grad, y4, y3, d, pooled, small, whole, h),
        [VMEM_SPEC] * 6 + [ANY_SPEC] * 2,
        [ANY_SPEC] * 3 + [VMEM_SPEC] * 2,
        [sds((rows, width)), sds((rows, width)), sds((n, tiled(table["p_in"]), WIDE), BF16), sds((16, 128)), sds((8, width))],
        [v((width, width), BF16), v((width, ff), BF16), v((ff, width), BF16), v((rows, width), F32),
         v((rows, width), BF16), v((rows, width), BF16), v((rows, width), F32), v((rows, width), BF16),
         v((rows, ff), BF16), v((rows, width), F32), v((width, ff), BF16), v((ff, width), BF16),
         v((width, width), BF16), v((nb, rows, WIDE), F32), v((rows, width), F32), pltpu.SemaphoreType.DMA((16,))],
        "back_part_one",
        ride,
        collective_id,
        28,
    )


def back_two(t_len, x, y1, y2, r, t, c, d, db, g, pooled, sums, late, small, whole, h, ff, held, ride=None, collective_id=None):
    rows, width = d.shape
    utts = t_len.shape[0]
    n = whole.shape[0]
    table, end = offsets(n, width, ff)
    start = table["p_in"]
    nb = ff // WIDE
    v = pltpu.VMEM
    dma = pltpu.SemaphoreType.DMA
    groups = lax.axis_size("dp")
    pad_rows = utts * (rows // utts + 16)
    return call(
        partial(back_two_kernel, utts, table, held, start, end),
        (t_len, x, y1, y2, r, t, c, d, db, g, pooled, sums, late, small, whole, h),
        [SMEM_SPEC] + [VMEM_SPEC] * 13 + [ANY_SPEC] * 2,
        [ANY_SPEC] * 2 + [VMEM_SPEC],
        [sds((rows, width)), sds((n, tiled(end - start + 16), WIDE), BF16), sds((16, 128))],
        [v((width, 2 * width), BF16), v((width, width), BF16), v((width, 3 * width), BF16), v((width, ff), BF16),
         v((ff, width), BF16), v((rows, width), F32), v((rows, width), BF16), v((rows, width), BF16),
         v((rows, width), F32), v((rows, width), BF16), v((rows, ff), BF16), v((rows, width), F32),
         v((width, 2 * width), BF16), v((width, width), BF16), v((width, 3 * width), BF16), v((width, ff), BF16),
         v((ff, width), BF16), v((nb, rows, WIDE), F32), v((pad_rows, width), F32), v((pad_rows, width), F32),
         v((rows, 2 * width), BF16), v((rows, 3 * width), BF16), v((n, 16, WIDE), BF16), pltpu.SemaphoreType.DMA((20,)),
         v((groups, 16, 128), F32), v((n, 16, 128), F32), dma((groups,)), dma((groups,)), dma((n,)), dma((n,))],
        "back_part_two",
        ride,
        collective_id,
        44,
        groups,
    )


FIRST = ("small", "f_in", "f_out", "w_joint", "w_proj", "p_in", "p_out", "s_in", "s_out")


def gathered_rows(n, width, ff, layers):
    low = width // n
    tall = ff // n
    sizes = {
        "f_in": low * (ff // WIDE), "f_out": tall, "small": 16, "w_joint": 3 * low, "w_proj": low,
        "p_in": 2 * low, "p_out": low, "s_in": low * (ff // WIDE), "s_out": tall,
    }
    tables = []
    at = 0
    for layer in range(layers):
        table = {}
        for name in FIRST:
            table[name] = (at, at + sizes[name])
            at += sizes[name]
        tables.append(table)
    return tables, at


class GatherEngine:
    def __init__(self, n1, tiles, lag, packed, out, so, sz, rz, sy, ry, sx, rx, sc, rc):
        dp, fs, a, c, i1, i2 = place()
        ypeer = (dp, i1 * 2 + 1 - i2)
        xpeer = ((1 - a) * 2 + c, fs)
        cpeer = (a * 2 + 1 - c, fs)

        def main(t):
            return rows(t * TILE + c * HALF + a * QA, QA + QB)

        def quarter(t, aa):
            return rows(t * TILE + c * HALF + aa * (QA + QB), QA)

        def half(t, cc):
            return rows(t * TILE + cc * HALF, HALF)

        def local(t):
            return pltpu.make_async_copy(packed.at[main(t), :], out.at[i1, i2, main(t), :], so.at[t])

        def zcopy(t, j):
            return remote(packed.at[main(t), :], out.at[i1, i2, main(t), :], sz.at[0], rz.at[t], (dp, j * 2 + i2))

        def zin(t):
            arrived = out.at[pl.ds(0, n1 - 1), i2, main(t), :]
            return remote(arrived, arrived, sz.at[0], rz.at[t], ypeer)

        def ycopy(t):
            return remote(out.at[:, i2, main(t), :], out.at[:, i2, main(t), :], sy.at[0], ry.at[t], ypeer)

        def yin(t):
            return remote(out.at[:, i2, main(t), :], out.at[:, 1 - i2, main(t), :], sy.at[0], ry.at[t], ypeer)

        def xcopy(t):
            return remote(out.at[:, :, quarter(t, a), :], out.at[:, :, quarter(t, a), :], sx.at[0], rx.at[t], xpeer)

        def xin(t):
            return remote(out.at[:, :, quarter(t, a), :], out.at[:, :, quarter(t, 1 - a), :], sx.at[0], rx.at[t], xpeer)

        def ccopy(t):
            return remote(out.at[:, :, half(t, c), :], out.at[:, :, half(t, c), :], sc.at[0], rc.at[t], cpeer)

        def cin(t):
            return remote(out.at[:, :, half(t, c), :], out.at[:, :, half(t, 1 - c), :], sc.at[0], rc.at[t], cpeer)

        def stage_z(t):
            for d in range(1, n1):
                zcopy(t, lax.rem(i1 + d, n1)).start()
            local(t).start()

        def stage_y(t):
            local(t).wait()
            zin(t).wait_recv()
            ycopy(t).start()

        def stage_x(t):
            yin(t).wait_recv()
            xcopy(t).start()

        def stage_c(t):
            xin(t).wait_recv()
            ccopy(t).start()

        def stage_o(t):
            cin(t).wait_recv()

        stages = (stage_z, stage_y, stage_x, stage_c, stage_o)

        def tick(tau):
            for place_of, stage in enumerate(stages):
                t = tau - place_of * lag

                @pl.when((t >= 0) & (t < tiles))
                def _(stage=stage, t=t):
                    stage(t)

        def finish():
            every = pl.ds(0, n1)
            for peer, sem, far, near, height in (
                (ypeer, sz, pl.ds(0, n1 - 1), 0, QA + QB),
                (ypeer, sy, every, 0, QA + QB),
                (xpeer, sx, every, pl.ds(0, 2), QA),
                (cpeer, sc, every, pl.ds(0, 2), HALF),
            ):
                sent = out.at[far, near, pl.ds(0, tiles * height), :]
                remote(sent, sent, sem.at[0], rc.at[0], peer).wait_send()

        self.tick = tick
        self.total = tiles + (len(stages) - 1) * lag
        self.after = lambda end: -(-end // TILE) + (len(stages) - 1) * lag
        self.finish = finish


class Exchange:
    def __init__(self, kind, groups, n, near, far, s1, r1, s2, r2):
        self.kind = kind
        self.groups, self.n = groups, n
        self.near, self.far = near, far
        self.sems = (s1, r1, s2, r2)
        self.sent = []

    def merge(self, ref, members):
        if self.kind == "sum":
            total = ref[0]
            for i in range(1, members):
                total = total + ref[i]
            return total
        mean, dev, count = pooled([ref[i] for i in range(members)])
        return jnp.concatenate([mean, dev, jnp.broadcast_to(count, (8, 128))], 0)

    def begin(self, x):
        dp = lax.axis_index("dp")
        fs = lax.axis_index("fsdp")
        near, groups = self.near, self.groups
        s1, r1, s2, r2 = self.sems
        near[dp] = x
        for d in range(1, groups):
            cp = remote(near.at[dp], near.at[dp], s1.at[d], r1.at[dp], (lax.rem(dp + d, groups), fs))
            cp.start()
            self.sent.append(cp)

    def middle(self):
        dp = lax.axis_index("dp")
        fs = lax.axis_index("fsdp")
        near, far, groups, n = self.near, self.far, self.groups, self.n
        s1, r1, s2, r2 = self.sems
        for d in range(1, groups):
            other = lax.rem(dp + d, groups)
            remote(near.at[dp], near.at[other], s1.at[d], r1.at[other], (other, fs)).wait_recv()
        far[fs] = self.merge(near, groups)
        for d in range(1, n):
            cp = remote(far.at[fs], far.at[fs], s2.at[d], r2.at[fs], (dp, lax.rem(fs + d, n)))
            cp.start()
            self.sent.append(cp)

    def end(self):
        dp = lax.axis_index("dp")
        fs = lax.axis_index("fsdp")
        far, n = self.far, self.n
        s1, r1, s2, r2 = self.sems
        for d in range(1, n):
            other = lax.rem(fs + d, n)
            remote(far.at[fs], far.at[other], s2.at[d], r2.at[other], (dp, other)).wait_recv()
        for cp in self.sent:
            cp.wait_send()
        return self.merge(far, n)


def meet(groups, n):
    dp = lax.axis_index("dp")
    fs = lax.axis_index("fsdp")
    barrier = pltpu.get_barrier_semaphore()
    for d in range(1, groups):
        pl.semaphore_signal(barrier, inc=1, device_id=(lax.rem(dp + d, groups), fs), device_id_type=MESH)
    for d in range(1, n):
        pl.semaphore_signal(barrier, inc=1, device_id=(dp, lax.rem(fs + d, n)), device_id_type=MESH)
    return lambda: pl.semaphore_wait(barrier, groups + n - 2)


def pack_into(out, src, tables, joint_at, layers):
    for layer in range(layers):
        for name in FIRST:
            base, stop = tables[layer][name]
            if name == "small":
                small = [src["gains"][layer], src["taps"][layer], src["bn_gain"][layer : layer + 1, :], src["bn_bias"][layer : layer + 1, :]]
                small = jnp.concatenate([x.astype(jnp.float32) for x in small], 0)
                small = jnp.concatenate([small, jnp.zeros((16, WIDE - small.shape[1]), jnp.float32)], 1)
                out[base:stop, :] = small.astype(jnp.bfloat16)
                continue
            ref = src[name]
            height = ref.shape[1]
            for b in range(ref.shape[2] // WIDE):
                out[base + b * height : base + (b + 1) * height, :] = ref[layer, :, b * WIDE : (b + 1) * WIDE]
    enc, pred, tok, dur = src["enc"], src["pred"], src["tok"], src["dur"]
    low, tall = enc.shape[0], pred.shape[0]
    at = joint_at
    out[at : at + low, :] = enc[:, :WIDE]
    at += lift(low)
    out[at : at + tall, :] = pred[:, :WIDE]
    at += lift(tall)
    for b in range(tok.shape[1] // WIDE):
        out[at : at + tall, :] = tok[:, b * WIDE : (b + 1) * WIDE]
        at += lift(tall)
    out[at : at + low, 0:128] = enc[:, WIDE:]
    out[at : at + tall, 128:256] = pred[:, WIDE:]
    dur = dur[...].astype(jnp.float32)
    out[at : at + tall, 256:384] = jnp.concatenate([dur, jnp.zeros((tall, 128 - dur.shape[1]), jnp.float32)], 1).astype(jnp.bfloat16)


def ffn_fwd(rows, x_ref, gain, weights, names, normed, h, act, y, mover, h_out, beats):
    w_in = weights[names[0]]

    def prepare(r, i, c):
        normed[r, :] = (ln_parts(x_ref[r, :].astype(jnp.float32))[0] * gain).astype(jnp.bfloat16)
        return c

    row_loop(rows, prepare)
    w_in[1].wait()
    for b in range(h.shape[0]):
        h[b] = nn(normed[...], w_in[0][:, b * WIDE : (b + 1) * WIDE])
        mover.put(h.at[b], h_out.at[b])

        def swish(r, i, c):
            v = h[b, r, :]
            act[r, b * WIDE : (b + 1) * WIDE] = (v * jax.nn.sigmoid(v)).astype(jnp.bfloat16)
            return c

        row_loop(rows, swish)
        beats.run(1)
    w_out = weights[names[1]]
    w_out[1].wait()
    y[...] = x_ref[...].astype(jnp.float32) + 0.5 * nn(act[...], w_out[0][...])
    beats.run(1)


def part_one(utts, beats, mover, t_ref, x_ref, gains, weights, outs, scratch):
    y1_out, h_out, y2_out, t_out, c_out, r_out, d_out = outs
    y1, y2, normed, h, act, tq, ctx, r, gp, d = scratch
    rows, width = y1.shape
    frames = rows // utts
    ffn_fwd(rows, x_ref, gains[0:1], weights, ("f_in", "f_out"), normed, h, act, y1, mover, h_out, beats)
    mover.put(y1, y1_out)

    def prepare(rr, i, c):
        normed[rr, :] = (ln_parts(y1[rr, :])[0] * gains[1:2]).astype(jnp.bfloat16)
        return c

    row_loop(rows, prepare)
    w_joint = weights["w_joint"][0]
    weights["w_joint"][1].wait()
    for b in range(3):
        tq[:, b * width : (b + 1) * width] = nn(normed[...], w_joint[:, b * width : (b + 1) * width]).astype(jnp.bfloat16)
    mover.put(tq, t_out)
    beats.run(1)
    pairs = width // 128
    side = lax.broadcasted_iota(jnp.int32, (frames, 128), 1) < 64
    key_at = lax.broadcasted_iota(jnp.int32, (1, frames), 1)
    hook = beats.loop(3, utts * pairs)

    def pair_step(m, carry):
        hook(m)
        u = m // pairs
        base = lax.rem(m, pairs) * 128
        rr = pl.ds(pl.multiple_of(u * frames, frames), frames)
        bias = jnp.where(key_at < t_ref[u], 0.0, MASKED)
        q = tq[rr, pl.ds(pl.multiple_of(base, 128), 128)]
        k = tq[rr, pl.ds(pl.multiple_of(base + width, 128), 128)]
        v = tq[rr, pl.ds(pl.multiple_of(base + 2 * width, 128), 128)]
        got = []
        for half in range(2):
            mine = side if half == 0 else ~side
            s = nt(jnp.where(mine, q, jnp.zeros_like(q)), k) * 0.125 + bias
            p = jnp.exp(s - jnp.max(s, -1, keepdims=True))
            p = p * (1.0 / jnp.sum(p, -1, keepdims=True))
            got.append(nn(p.astype(jnp.bfloat16), v))
        ctx[rr, pl.ds(pl.multiple_of(base, 128), 128)] = jnp.where(side, got[0], got[1]).astype(jnp.bfloat16)
        return carry

    lax.fori_loop(0, utts * pairs, pair_step, 0)
    mover.put(ctx, c_out)
    weights["w_proj"][1].wait()
    y2[...] = y1[...] + nn(ctx[...], weights["w_proj"][0][...])
    mover.put(y2, y2_out)

    def prepare_conv(rr, i, c):
        normed[rr, :] = (ln_parts(y2[rr, :])[0] * gains[2:3]).astype(jnp.bfloat16)
        return c

    row_loop(rows, prepare_conv)
    w_pin = weights["p_in"][0]
    weights["p_in"][1].wait()
    for b in range(2):
        r[:, b * width : (b + 1) * width] = nn(normed[...], w_pin[:, b * width : (b + 1) * width])
    mover.put(r, r_out)
    beats.run(1)
    fill_gated(utts, frames, t_ref, r, gp)
    taps = gains[5:14]

    def conv(rr, i, total):
        d_chunk = spread(gp, utts, frames, i, taps)
        d[rr, :] = d_chunk
        return total + fold8(d_chunk * valid_rows_of(t_ref, frames, i), jnp.add)

    total = row_loop(rows, conv, jnp.zeros((8, width), jnp.float32))
    mover.put(d, d_out)
    beats.run(1)
    count = t_ref[0]
    for u in range(1, utts):
        count = count + t_ref[u]
    count = count.astype(jnp.float32)
    mean = jnp.sum(total, 0, keepdims=True) / count

    def deviate(rr, i, total):
        gap = (d[rr, :] - mean) * valid_rows_of(t_ref, frames, i)
        return total + fold8(gap * gap, jnp.add)

    dev = jnp.sum(row_loop(rows, deviate, jnp.zeros((8, width), jnp.float32)), 0, keepdims=True)
    cut4 = lambda v: [v[:, i * 128 : (i + 1) * 128] for i in range(width // 128)]
    return jnp.concatenate(cut4(mean) + cut4(dev) + [jnp.full((8, 128), count, jnp.float32)], 0)


def part_two(beats, mover, pooled_ref, gains, weights, outs, scratch):
    y3_out, h_out, y4_out, x_out = outs
    d, y2, y3, normed, h, act, y4, x = scratch
    rows, width = y3.shape
    mean = read_rows(pooled_ref, 0, width)
    count = pooled_ref[8:9, 0:1]
    istd = lax.rsqrt(read_rows(pooled_ref, 4, width) / count + EPS)

    def bn(rr, i, c):
        b = (d[rr, :] - mean) * istd * gains[14:15] + gains[15:16]
        normed[rr, :] = (b * jax.nn.sigmoid(b)).astype(jnp.bfloat16)
        return c

    row_loop(rows, bn)
    weights["p_out"][1].wait()
    y3[...] = y2[...] + nn(normed[...], weights["p_out"][0][...])
    mover.put(y3, y3_out)
    ffn_fwd(rows, y3, gains[3:4], weights, ("s_in", "s_out"), normed, h, act, y4, mover, h_out, beats)
    mover.put(y4, y4_out)

    def last(rr, i, c):
        x[rr, :] = ln_parts(y4[rr, :])[0] * gains[4:5]
        return c

    row_loop(rows, last)
    mover.put(x, x_out)


def forward_kernel(utts, layers, n1, groups, tables, joint_at, tiles, lag, t_ref, frames_ref, *refs):
    n = 2 * n1
    names = PLACE + ("gains", "taps", "bn_gain", "bn_bias", "enc", "pred", "tok", "dur")
    src = dict(zip(names, refs))
    refs = refs[len(names) :]
    whole, refs = refs[0], refs[1:]
    layer_outs = []
    for layer in range(layers):
        layer_outs.append((refs[0:7], refs[7:11], refs[11], refs[12]))
        refs = refs[13:]
    buffers, refs = refs[:8], refs[8:]
    packed, smalls, y1, y2, normed, h, act, tq, ctx, r, gp, d, y3, y4, x, sems = refs[:16]
    refs = refs[16:]
    entered = meet(groups, n)
    pack_into(packed, src, tables, joint_at, layers)
    entered()
    engine = GatherEngine(n1, tiles, lag, packed, whole, *refs[:9])
    refs = refs[9:]
    beats = Beats(engine.tick, engine.total)
    held = dict(zip(("f_in", "f_out", "w_joint", "w_proj", "p_in", "p_out", "s_in", "s_out"), buffers))
    used = 0
    for layer in range(layers):
        table = tables[layer]
        mover = Mover(sems, used)

        def load(name):
            beats.until(engine.after(table[name][1]))
            return held[name], mover.load_weight(whole, table[name][0], held[name])

        weights = {"f_in": load("f_in")}
        small = mover.load(whole.at[:, :, pl.ds(table["small"][0], 16), :], smalls)
        small.wait()
        gains = None
        for s in range(n):
            part = smalls[s // 2, s % 2].astype(jnp.float32)
            part = part if s == 0 else pltpu.roll(part, s * (WIDE // n), 1)
            gains = part if gains is None else gains + part
        layer_outs[layer][3][...] = gains
        weights = Late(weights, load)
        first, second, pooled_out, _ = layer_outs[layer]
        source = frames_ref if layer == 0 else x
        stats = part_one(utts, beats, mover, t_ref, source, gains, weights, first, (y1, y2, normed, h, act, tq, ctx, r, gp, d))
        exchange = Exchange("pool", groups, n, *refs[:6])
        exchange.begin(stats)
        refs = refs[6:]
        for name in ("p_out", "s_in", "s_out"):
            weights.fetch(name)
        exchange.middle()
        beats.run(1)
        mover.finish()
        pooled_out[...] = exchange.end()
        part_two(beats, mover, pooled_out, gains, weights, second, (d, y2, y3, normed, h, act, y4, x))
        mover.finish()
        used = mover.used
    beats.rest()
    engine.finish()


class Late:
    def __init__(self, got, load):
        self.got = got
        self.load = load

    def fetch(self, name):
        if name not in self.got:
            self.got[name] = self.load(name)

    def __getitem__(self, name):
        self.fetch(name)
        return self.got[name]


def forward(t_len, frames_in, arrays, layers, ff, sizes, collective_id, lag=2):
    rows, width = frames_in.shape
    utts = t_len.shape[0]
    n = lax.axis_size("fsdp")
    groups = lax.axis_size("dp")
    n1 = n // 2
    tables, joint_at = gathered_rows(n, width, ff, layers)
    total = tiled(joint_at + sum(sizes))
    tiles = total // TILE
    nb = ff // WIDE
    v = pltpu.VMEM
    dma = pltpu.SemaphoreType.DMA
    big = sds((rows, width))
    one = [big, sds((nb, rows, WIDE)), big, sds((rows, 3 * width), BF16), sds((rows, width), BF16), sds((rows, 2 * width)), big]
    two = [big, sds((nb, rows, WIDE)), big, big]
    pad_rows = utts * (rows // utts + 16)
    outs = pl.pallas_call(
        partial(forward_kernel, utts, layers, n1, groups, tables, joint_at, tiles, lag),
        in_specs=[SMEM_SPEC] + [VMEM_SPEC] * (1 + len(arrays)),
        out_specs=[ANY_SPEC] + ([ANY_SPEC] * 11 + [VMEM_SPEC] * 2) * layers,
        out_shape=[sds((n1, 2, total, WIDE), BF16)] + (one + two + [sds((16, 128)), sds((16, width))]) * layers,
        scratch_shapes=[
            v((width, ff), BF16), v((ff, width), BF16), v((width, 3 * width), BF16), v((width, width), BF16), v((width, 2 * width), BF16),
            v((width, width), BF16), v((width, ff), BF16), v((ff, width), BF16),
            v((total, WIDE), BF16), v((n1, 2, 16, WIDE), BF16), v((rows, width), F32), v((rows, width), F32), v((rows, width), BF16),
            v((nb, rows, WIDE), F32), v((rows, ff), BF16), v((rows, 3 * width), BF16), v((rows, width), BF16), v((rows, 2 * width), F32),
            v((pad_rows, width), F32), v((rows, width), F32), v((rows, width), F32), v((rows, width), F32), v((rows, width), F32), dma((80,)),
            dma((tiles,)), dma((1,)), dma((tiles,)), dma((1,)), dma((tiles,)), dma((1,)), dma((tiles,)), dma((1,)), dma((tiles,)),
        ]
        + [v((groups, 16, 128), F32), v((n, 16, 128), F32), dma((groups,)), dma((groups,)), dma((n,)), dma((n,))] * layers,
        compiler_params=pltpu.CompilerParams(collective_id=collective_id, has_side_effects=True, vmem_limit_bytes=61 << 20),
        name="gather_and_forward",
    )(t_len, frames_in, *arrays)
    whole = outs[0].reshape(n, total, WIDE)
    return whole, [outs[1 + 13 * layer : 14 + 13 * layer] for layer in range(layers)], tables, joint_at


def lift(rows):
    return -(-rows // 16) * 16


def joint_sizes(w_enc, w_pred, w_tok):
    low, tall = lift(w_enc.shape[0]), lift(w_pred.shape[0])
    return [low, tall, tall * (w_tok.shape[1] // WIDE), tall]


class Joined:
    def __init__(self, parts, ends):
        self.parts = parts
        self.ends = ends

    def __getitem__(self, key):
        rows_of, cols = key
        got = []
        first = 0
        for part, last in zip(self.parts, self.ends):
            lo, hi = max(rows_of.start, first), min(rows_of.stop, last)
            if lo < hi:
                got.append(part[lo - first : hi - first, cols])
            first = last
        return got[0] if len(got) == 1 else jnp.concatenate(got, 0)


def unpack_kernel(layers, table, end, dims, ends, *refs):
    parts, refs = refs[: len(ends)], refs[len(ends) :]
    gains, f_in, f_out, w_joint, w_proj, p_in, taps, p_out, s_in, s_out, enc, pred, tok, dur = refs
    share = Joined(parts, ends)
    outs = {"f_in": f_in, "f_out": f_out, "w_joint": w_joint, "w_proj": w_proj, "p_in": p_in, "p_out": p_out, "s_in": s_in, "s_out": s_out}
    starts, width, joint = dims
    shard = gains.shape[2]
    for layer in range(layers):
        for name in PLACE:
            out = outs[name]
            height = out.shape[1]
            early = table[name] < table["p_in"]
            base = starts[layer][0] + table[name] if early else starts[layer][1] + table[name] - table["p_in"]
            for b in range(out.shape[2] // WIDE):
                out[layer, :, b * WIDE : (b + 1) * WIDE] = share[base + b * height : base + (b + 1) * height, :].astype(jnp.float32)
        base = starts[layer][1] + end - table["p_in"]
        small = share[base : base + 16, 0:128].astype(jnp.float32)
        gains[layer] = small[0:5, :shard]
        taps[layer] = small[5 : 5 + taps.shape[1], :shard]
    at = starts[layers]
    low, tall = enc.shape[0], pred.shape[0]
    enc[:, :WIDE] = share[at : at + low, :].astype(jnp.float32)
    at += lift(low)
    pred[:, :WIDE] = share[at : at + tall, :].astype(jnp.float32)
    at += lift(tall)
    for b in range(tok.shape[1] // WIDE):
        tok[:, b * WIDE : (b + 1) * WIDE] = share[at : at + tall, :].astype(jnp.float32)
        at += lift(tall)
    enc[:, WIDE:] = share[at : at + low, 0:128].astype(jnp.float32)
    pred[:, WIDE:] = share[at : at + tall, 128:256].astype(jnp.float32)
    dur[...] = share[at : at + tall, 256:384].astype(jnp.float32)[:, : dur.shape[1]]


def unpack(layers, table, end, dims, shares, like):
    ends = []
    for share in shares:
        ends.append(share.shape[0] + (ends[-1] if ends else 0))
    return pl.pallas_call(
        partial(unpack_kernel, layers, table, end, dims, tuple(ends)),
        in_specs=[VMEM_SPEC] * len(shares),
        out_specs=[VMEM_SPEC] * len(like),
        out_shape=[sds(x.shape) for x in like],
        compiler_params=pltpu.CompilerParams(vmem_limit_bytes=48 << 20),
        name="unpack_grads",
    )(*shares)


def cut(whole, sizes, offset=0):
    parts = []
    for size in sizes:
        parts.append(whole[..., offset : offset + size, :])
        offset += size
    return parts


def from_blocks(part, cols, rows):
    n, height, _ = part.shape
    blocks = cols // WIDE
    return jnp.swapaxes(part.reshape(n, blocks, height // blocks, WIDE)[:, :, :rows], 1, 2).reshape(-1, cols)


def joint_inputs_kernel(base, x_ref, pred_ref, whole, low_ref, enc_t, pred_t, w_t, w_enc, w_pred, w_cat, sems):
    n = whole.shape[0]
    joint = w_enc.shape[1]
    low, tall = w_enc.shape[0] // n, w_pred.shape[0] // n
    vocab = w_cat.shape[1] - 128
    first = base + low + tall
    rest = first + tall * (vocab // WIDE)

    def spread(at, height, dst, cols, lanes, sem):
        def one(s, carry):
            pltpu.make_async_copy(
                whole.at[s, pl.ds(at, height), lanes], dst.at[pl.ds(pl.multiple_of(s * height, 16), height), cols], sem
            ).start()
            return carry

        lax.fori_loop(0, n, one, 0)

    every = pl.ds(0, WIDE)
    spread(base, low, w_enc, every, every, sems.at[0])
    spread(rest, low, w_enc, pl.ds(WIDE, 128), pl.ds(0, 128), sems.at[0])
    spread(base + low, tall, w_pred, every, every, sems.at[1])
    spread(rest, tall, w_pred, pl.ds(WIDE, 128), pl.ds(128, 128), sems.at[1])
    for b in range(vocab // WIDE):
        spread(first + b * tall, tall, w_cat, pl.ds(b * WIDE, WIDE), every, sems.at[2])
    spread(rest, tall, w_cat, pl.ds(vocab, 128), pl.ds(256, 128), sems.at[2])
    low_ref[...] = x_ref[...].astype(jnp.bfloat16)
    pltpu.make_async_copy(w_enc, w_enc, sems.at[0]).wait()
    enc_t[...] = nn(low_ref[...], w_enc[...]).T
    pltpu.make_async_copy(w_pred, w_pred, sems.at[1]).wait()
    pred = nn(pred_ref[...], w_pred[...])
    for g in range(pred_t.shape[0]):
        pred_t[g] = pred[g * 8 : (g + 1) * 8, :].T
    pltpu.make_async_copy(w_cat, w_cat, sems.at[2]).wait()
    w_t[...] = w_cat[...].T


def joint_inputs(x, pred_low, whole, base, joint, vocab):
    rows, width = x.shape
    groups = pred_low.shape[0] // 8
    return pl.pallas_call(
        partial(joint_inputs_kernel, base),
        in_specs=[VMEM_SPEC, VMEM_SPEC, ANY_SPEC],
        out_specs=[VMEM_SPEC] * 7,
        out_shape=[sds((rows, width), BF16), sds((joint, rows)), sds((groups, joint, 8)), sds((vocab + 128, joint), BF16),
                   sds((width, joint), BF16), sds((joint, joint), BF16), sds((joint, vocab + 128), BF16)],
        scratch_shapes=[pltpu.SemaphoreType.DMA((3,))],
        compiler_params=pltpu.CompilerParams(vmem_limit_bytes=48 << 20),
        name="joint_inputs",
    )(x, pred_low, whole)


def joint_outputs_kernel(genc_t, gpred_t, gtok, gdur, low_ref, pred_ref, w_enc, gx, pack, g_low, gp):
    n = pack.shape[0]
    joint = w_enc.shape[1]
    low, tall = w_enc.shape[0] // n, joint // n
    g_low[...] = genc_t[...].T.astype(jnp.bfloat16)
    gx[...] = nt(g_low[...], w_enc[...])
    g_enc = tn(low_ref[...], g_low[...]).astype(jnp.bfloat16)
    real = lax.broadcasted_iota(jnp.int32, (8, joint), 0) < GROUP
    for g in range(gpred_t.shape[0]):
        gp[g * 8 : (g + 1) * 8, :] = jnp.where(real, gpred_t[g].T, 0.0)
    g_pred = tn(pred_ref[...], gp[...].astype(jnp.bfloat16)).astype(jnp.bfloat16)
    blocks = gtok.shape[1] // WIDE
    rest = low + tall * (1 + blocks)
    for s in range(n):
        mine = slice(s * tall, (s + 1) * tall)
        pack[s, 0:low, :] = g_enc[s * low : (s + 1) * low, :WIDE]
        pack[s, low : low + tall, :] = g_pred[mine, :WIDE]
        for b in range(blocks):
            at = low + tall * (1 + b)
            pack[s, at : at + tall, :] = gtok[mine, b * WIDE : (b + 1) * WIDE]
        pack[s, rest : rest + low, 0:128] = g_enc[s * low : (s + 1) * low, WIDE:]
        if tall > low:
            pack[s, rest + low : rest + tall, 0:128] = jnp.zeros((tall - low, 128), jnp.bfloat16)
        pack[s, rest : rest + tall, 128:256] = g_pred[mine, WIDE:]
        pack[s, rest : rest + tall, 256:384] = gdur[mine, :]
        pack[s, rest : rest + tall, 384:] = jnp.zeros((tall, WIDE - 384), jnp.bfloat16)
        if pack.shape[1] > rest + tall:
            pack[s, rest + tall :, :] = jnp.zeros((pack.shape[1] - rest - tall, WIDE), jnp.bfloat16)


def joint_outputs(genc_t, gpred_t, gtok, gdur, low, pred_low, w_enc, n):
    rows, width = low.shape
    joint = w_enc.shape[1]
    count = width // n + (joint // n) * (2 + gtok.shape[1] // WIDE)
    return pl.pallas_call(
        joint_outputs_kernel,
        in_specs=[VMEM_SPEC] * 7,
        out_specs=[VMEM_SPEC] * 2,
        out_shape=[sds((rows, width)), sds((n, tiled(count), WIDE), BF16)],
        scratch_shapes=[pltpu.VMEM((rows, joint), BF16), pltpu.VMEM((pred_low.shape[0], joint), F32)],
        compiler_params=pltpu.CompilerParams(vmem_limit_bytes=48 << 20),
        name="joint_outputs",
    )(genc_t, gpred_t, gtok, gdur, low, pred_low, w_enc)


def unpack_joint(whole, first, sizes, w_enc, w_pred, vocab):
    enc, pred, tok, rest = cut(whole, sizes, first)
    joint = w_enc.shape[1]
    low = w_enc.shape[0]
    tall = w_pred.shape[0]
    w_enc = jnp.concatenate([enc[:, :low], rest[:, :low, : joint - WIDE]], 2).reshape(-1, joint)
    w_pred = jnp.concatenate([pred[:, :tall], rest[:, :tall, 128 : 128 + joint - WIDE]], 2).reshape(-1, joint)
    return w_enc, w_pred, from_blocks(tok, vocab, tall), rest[:, :tall, 256:384].reshape(-1, 128)


def grow(part):
    short = lift(part.shape[1]) - part.shape[1]
    return jnp.pad(part, ((0, 0), (0, short), (0, 0))) if short else part


def pack_joint_grads(g_enc, g_pred, g_tok, g_dur, n):
    def shards(grad):
        return grow(grad.astype(jnp.bfloat16).reshape(n, -1, grad.shape[1]))
    g_enc, g_pred, g_tok, g_dur = shards(g_enc), shards(g_pred), shards(g_tok), shards(g_dur)
    tall = g_pred.shape[1]
    rest = jnp.concatenate(
        [
            jnp.pad(g_enc[:, :, WIDE:], ((0, 0), (0, tall - g_enc.shape[1]), (0, 0))),
            g_pred[:, :, WIDE:],
            g_dur,
            jnp.zeros((n, tall, 128), jnp.bfloat16),
        ],
        2,
    )
    parts = [g_enc[:, :, :WIDE], g_pred[:, :, :WIDE]]
    parts += [g_tok[:, :, b : b + WIDE] for b in range(0, g_tok.shape[2], WIDE)] + [rest]
    rows = sum(p.shape[1] for p in parts)
    return jnp.concatenate(parts + [jnp.zeros((n, tiled(rows) - rows, WIDE), jnp.bfloat16)], 1)


def matmul(left, right):
    return jnp.dot(left, right, preferred_element_type=jnp.float32)


def contract_rows(left, right):
    return lax.dot_general(
        left, right, (((0,), (0,)), ((), ())), preferred_element_type=jnp.float32
    )


def contract_cols(left, right):
    return lax.dot_general(
        left, right, (((1,), (1,)), ((), ())), preferred_element_type=jnp.float32
    )


def local(
    frames_in,
    frame_lengths,
    label_ids,
    label_lengths,
    pred_states,
    norm_gains,
    first_in,
    first_out,
    attend_joint,
    attend_out,
    point_in,
    depth_taps,
    batch_gain,
    batch_bias,
    point_out,
    second_in,
    second_out,
    enc_weight,
    pred_weight,
    token_weight,
    duration_weight,
):
    utts, frames, width = frames_in.shape
    slots = pred_states.shape[1]
    rows = utts * frames
    layers = norm_gains.shape[0]
    n = lax.axis_size("fsdp")
    ff = first_in.shape[2]
    mats = {
        "f_in": first_in, "f_out": first_out, "w_joint": attend_joint, "w_proj": attend_out,
        "p_in": point_in, "p_out": point_out, "s_in": second_in, "s_out": second_out,
    }
    table, end = offsets(n, width, ff)
    shard = width // n
    sizes = joint_sizes(enc_weight, pred_weight, token_weight)
    vocab = token_weight.shape[1]
    arrays = [mats[name] for name in PLACE]
    arrays += [norm_gains, depth_taps, batch_gain, batch_bias, enc_weight, pred_weight, token_weight, duration_weight]
    resid = frames_in.reshape(rows, width)
    whole, records, tables, joint_at = forward(frame_lengths, resid, arrays, layers, ff, sizes, 1)
    held = [{name: spot[0] for name, spot in t.items()} for t in tables]
    starts_of = [resid] + [record[10] for record in records]
    resid = starts_of[-1]
    joint = enc_weight.shape[1]
    groups = slots // GROUP
    durs = duration_weight.shape[1]
    aligned = joint % (16 * n) == 0 and width % (16 * n) == 0
    pred_low = pred_states.reshape(utts * groups, GROUP, joint)
    pred_low = jnp.pad(pred_low, ((0, 0), (0, 8 - GROUP), (0, 0))).reshape(-1, joint)
    if aligned:
        out_low, enc_t, pred_t, w_cat_t, w_enc, _, w_cat = joint_inputs(resid, pred_low, whole, joint_at, joint, vocab)
    else:
        w_enc, w_pred, w_tok, w_dur = unpack_joint(whole, joint_at, sizes, enc_weight, pred_weight, vocab)
        out_low = resid.astype(jnp.bfloat16)
        enc_t = matmul(out_low, w_enc).T
        pred_t = jnp.swapaxes(matmul(pred_low, w_pred).reshape(utts * groups, 8, joint), 1, 2)
        w_cat = jnp.concatenate([w_tok, w_dur], 1)
        w_cat_t = w_cat.T
    labels_ext = jnp.concatenate([label_ids, jnp.zeros((utts, 1), jnp.int32)], 1)
    feats, expd = joint_forward(enc_t, pred_t, labels_ext, w_cat_t, vocab, durs, frames)
    lat_grads, scores = lattice(feats[: 2 + durs], frame_lengths, label_lengths, slots)
    log_prob = scores[:utts, 0]
    utt_loss = -log_prob / frame_lengths.astype(jnp.float32)
    grad_enc_t, grad_pred_t, grad_tok, grad_dur_w = joint_backward(
        enc_t, pred_t, labels_ext, w_cat, feats, lat_grads, expd, vocab, durs, frames
    )
    if aligned:
        grad, joint_grads = joint_outputs(grad_enc_t, grad_pred_t, grad_tok, grad_dur_w, out_low, pred_low, w_enc, n)
    else:
        grad_pred_rows = jnp.swapaxes(grad_pred_t[:, :, :GROUP], 1, 2)
        grad_pred_rows = jnp.pad(grad_pred_rows, ((0, 0), (0, 8 - GROUP), (0, 0))).reshape(-1, joint)
        grad_enc_low = grad_enc_t.T.astype(jnp.bfloat16)
        grad = contract_cols(grad_enc_low, w_enc)
        grad_w_enc = contract_rows(out_low, grad_enc_low)
        grad_w_pred = contract_rows(pred_low, grad_pred_rows.astype(jnp.bfloat16))
        joint_grads = pack_joint_grads(grad_w_enc, grad_w_pred, grad_tok, grad_dur_w, n)

    def whole_of(source):
        return (source, 0, source.shape[1] // TILE)

    waiting = [whole_of(joint_grads)]
    shares = []
    starts = [None] * layers + [0]
    at = joint_grads.shape[1]
    bn_grads = [None] * layers
    for layer in reversed(range(layers)):
        x0 = starts_of[layer]
        y1, h1, y2, qkv, ctx, gates, depthwise, y3, h2, y4, result, pooled, small = records[layer]
        args = (grad, y4, y3, depthwise, pooled, small, whole, h2, ff, held[layer])
        g3, db, grads_one, sums, late_gains = back_one(*args)
        if layer == layers - 1:
            ride, later = waiting + [whole_of(grads_one)], []
        else:
            ride, later = waiting, [whole_of(grads_one)]
        args = (frame_lengths, x0, y1, y2, gates, qkv, ctx, depthwise, db, g3, pooled, sums, late_gains)
        (grad, grads_two, sums), share = back_two(*args, small, whole, h1, ff, held[layer], ride, 20 + layer)
        shares.append(share)
        waiting = later + [whole_of(grads_two)]
        starts[layer] = (at, at + grads_one.shape[1])
        at += grads_one.shape[1] + grads_two.shape[1]
        bn_grads[layer] = (sums[4:8].reshape(width), sums[0:4].reshape(width))
    shares.append(scatter(waiting, 4))
    grads = unpack(
        layers,
        table,
        end,
        (starts, width, joint),
        shares,
        [norm_gains, first_in, first_out, attend_joint, attend_out, point_in, depth_taps, point_out, second_in, second_out,
         enc_weight, pred_weight, token_weight, duration_weight],
    )
    offset = lax.axis_index("fsdp") * shard
    gain_piece = lax.dynamic_slice_in_dim(jnp.stack([g[0] for g in bn_grads]), offset, shard, 1)
    bias_piece = lax.dynamic_slice_in_dim(jnp.stack([g[1] for g in bn_grads]), offset, shard, 1)
    return (
        utt_loss,
        grad.reshape(utts, frames, width),
        *grads[:7],
        gain_piece,
        bias_piece,
        *grads[7:],
    )


def solution(mesh):
    placed = (
        P(("dp", "fsdp"), None, None),
        P(("dp", "fsdp")),
        P(("dp", "fsdp"), None),
        P(("dp", "fsdp")),
        P(("dp", "fsdp"), None, None),
        P(None, None, "fsdp"),
        P(None, "fsdp", None),
        P(None, "fsdp", None),
        P(None, "fsdp", None),
        P(None, "fsdp", None),
        P(None, "fsdp", None),
        P(None, None, "fsdp"),
        P(None, "fsdp"),
        P(None, "fsdp"),
        P(None, "fsdp", None),
        P(None, "fsdp", None),
        P(None, "fsdp", None),
        P("fsdp", None),
        P("fsdp", None),
        P("fsdp", None),
        P("fsdp", None),
    )
    return jax.shard_map(
        local,
        mesh=mesh,
        in_specs=placed,
        out_specs=(
            P(("dp", "fsdp")),
            P(("dp", "fsdp"), None, None),
            P(None, None, "fsdp"),
            P(None, "fsdp", None),
            P(None, "fsdp", None),
            P(None, "fsdp", None),
            P(None, "fsdp", None),
            P(None, "fsdp", None),
            P(None, None, "fsdp"),
            P(None, "fsdp"),
            P(None, "fsdp"),
            P(None, "fsdp", None),
            P(None, "fsdp", None),
            P(None, "fsdp", None),
            P("fsdp", None),
            P("fsdp", None),
            P("fsdp", None),
            P("fsdp", None),
        ),
        check_vma=False,
    )
```

```python
from functools import partial, reduce

import jax
import jax.numpy as jnp
from jax import lax
from jax.experimental import pallas as pl
from jax.experimental.pallas import tpu as pltpu
from jax.sharding import PartitionSpec as P

HEADS = 8


EPS = 1e-05
MASKED = -1000000000.0
NEG = -1e30


def lattice_kernel(slots, feats_ref, tlen_ref, ulen_ref, grads_ref, prob_ref, s_ref, l_ref, ls_ref, a_ref, b_ref, init_ref):
    utts = tlen_ref.shape[0]
    frames = feats_ref.shape[2]
    rows = feats_ref.shape[1]
    wide = frames + 128
    reach = feats_ref.shape[0] - 3
    diags = frames + slots
    pad = 8
    total = a_ref.shape[0]
    body = wide

    def skew(x, sign):
        k = lax.broadcasted_iota(jnp.int32, x.shape, 0) % 32
        for bit in range(5):
            step = 1 << bit
            x = jnp.where((k // step) % 2 == 1, pltpu.roll(x, step if sign > 0 else wide - step, 1), x)
        return x

    def to_diag(x):
        x = jnp.concatenate([x, jnp.zeros((rows, 128), jnp.float32)], 1)
        x = skew(x, 1)
        x = jnp.concatenate([x, jnp.zeros((128 - rows, wide), jnp.float32)], 0)
        return x.T

    lane = lax.broadcasted_iota(jnp.int32, (wide, 128), 1)
    diag = lax.broadcasted_iota(jnp.int32, (wide, 128), 0)
    k_of = lane % 32
    t_of = diag - k_of
    t_len = jnp.full((wide, 128), -1, jnp.int32)
    u_len = jnp.full((wide, 128), -1, jnp.int32)
    for u in range(utts):
        mine = (lane // 32) == u
        t_len = jnp.where(mine, tlen_ref[u], t_len)
        u_len = jnp.where(mine, ulen_ref[u], u_len)
    blank = to_diag(feats_ref[0])
    label = to_diag(feats_ref[1])
    edge = jnp.full((pad, 128), NEG, jnp.float32)
    real = (t_of >= 0)
    for ref in (s_ref, l_ref, ls_ref):
        for e in range(ref.shape[0]):
            ref[e, 0:pad, :] = edge
            ref[e, pad + wide:, :] = jnp.full((ref.shape[1] - pad - wide, 128), NEG, jnp.float32)
    for e in range(reach + 1):
        dur = to_diag(feats_ref[2 + e])
        if e > 0:
            keep = real & (k_of <= u_len) & ((t_of + e < t_len) | ((t_of + e == t_len) & (k_of == u_len)))
            s_ref[e - 1, pad:pad + wide, :] = jnp.where(keep, blank + dur, NEG)
        keep = real & (k_of < u_len) & (t_of + e < t_len)
        lab = jnp.where(keep, label + dur, NEG)
        l_ref[e, pad:pad + wide, :] = lab
        ls_ref[e, pad:pad + wide, :] = pltpu.roll(lab, 1, 1)
    init_ref[pad:pad + wide, :] = jnp.where((t_of == t_len) & (k_of == u_len), 0.0, NEG)
    a_ref[...] = jnp.full(a_ref.shape, NEG, jnp.float32)
    b_ref[...] = jnp.full(b_ref.shape, NEG, jnp.float32)

    first = jnp.where((lax.broadcasted_iota(jnp.int32, (1, 128), 1) % 32 == 0)
                      & (lax.broadcasted_iota(jnp.int32, (1, 128), 1) < 32 * utts), 0.0, NEG)

    a_ref[pl.ds(pad, 1), :] = first
    last = diags

    def tree(parts, op):
        while len(parts) > 1:
            parts = [op(parts[i], parts[i + 1]) if i + 1 < len(parts) else parts[i] for i in range(0, len(parts), 2)]
        return parts[0]

    def older(hist, rolled, edge_s, edge_l):
        terms = [hist[e - 2] + edge_s(e) for e in range(2, reach + 1)]
        terms += [rolled[e - 1] + edge_l(e) for e in range(1, reach + 1)]
        top = tree(terms, jnp.maximum)
        return top, tree([jnp.exp(x - top) for x in terms], jnp.add)

    def newest(old, one, two):
        top = jnp.maximum(jnp.maximum(one, two), old[0])
        total = (jnp.exp(one - top) + jnp.exp(two - top)) + old[1] * jnp.exp(old[0] - top)
        return jnp.maximum(top + jnp.log(total), NEG)

    def step(i, carry):
        ha, hra, olda, hb, hrb, oldb = carry
        row = pad + i
        rowb = pad + last - i
        nexta = older(ha, hra, lambda e: s_ref[e - 1, pl.ds(row + 1 - e, 1), :], lambda e: ls_ref[e, pl.ds(row - e, 1), :])
        nextb = older(hb, hrb, lambda e: s_ref[e - 1, pl.ds(rowb - 1, 1), :], lambda e: l_ref[e, pl.ds(rowb - 1, 1), :])
        a = newest(olda, ha[0] + s_ref[0, pl.ds(row - 1, 1), :], hra[0] + ls_ref[0, pl.ds(row - 1, 1), :])
        b = newest(oldb, hb[0] + s_ref[0, pl.ds(rowb, 1), :], hrb[0] + l_ref[0, pl.ds(rowb, 1), :])
        b = jnp.maximum(b, init_ref[pl.ds(rowb, 1), :])
        a_ref[pl.ds(row, 1), :] = a
        b_ref[pl.ds(rowb, 1), :] = b
        ra = pltpu.roll(a, 1, 1)
        rb = pltpu.roll(b, 127, 1)
        return ((a,) + ha[:-1], (ra,) + hra[:-1], nexta, (b,) + hb[:-1], (rb,) + hrb[:-1], nextb)

    b0 = init_ref[pl.ds(pad + last, 1), :]
    b_ref[pl.ds(pad + last, 1), :] = b0
    none = a_ref[pl.ds(0, 1), :]
    first = a_ref[pl.ds(pad, 1), :]
    ha = (first,) + (none,) * (reach - 2)
    hra = (pltpu.roll(first, 1, 1),) + (none,) * (reach - 1)
    hb = (b0,) + (none,) * (reach - 2)
    hrb = (pltpu.roll(b0, 127, 1),) + (none,) * (reach - 1)
    empty = (none, none - none)
    lax.fori_loop(1, last + 1, step, (ha, hra, empty, hb, hrb, empty), unroll=4)

    zrow = b_ref[pl.ds(pad, 1), :]
    lane1 = lax.broadcasted_iota(jnp.int32, (1, 128), 1)
    z = jnp.zeros((1, 128), jnp.float32)
    for u in range(utts):
        zu = jnp.max(jnp.where(lane1 == 32 * u, zrow, 2 * NEG), axis=1, keepdims=True)
        z = jnp.where(lane1 // 32 == u, zu, z)
        prob_ref[pl.ds(u, 1), :] = jnp.broadcast_to(zu, (1, 128))

    def from_diag(x):
        x = x.T[:rows]
        return skew(x, -1)[:, :frames]

    a = a_ref[pad:pad + wide, :] - z
    g_blank = jnp.zeros((wide, 128), jnp.float32)
    g_label = jnp.zeros((wide, 128), jnp.float32)
    for e in range(reach + 1):
        bb = b_ref[pad + e + 1: pad + e + 1 + wide, :]
        pl_ = jnp.exp(a + l_ref[e, pad:pad + wide, :] + pltpu.roll(bb, 127, 1))
        g_label = g_label - pl_
        g = -pl_
        if e > 0:
            ps = jnp.exp(a + s_ref[e - 1, pad:pad + wide, :] + b_ref[pad + e: pad + e + wide, :])
            g_blank = g_blank - ps
            g = g - ps
        grads_ref[2 + e] = from_diag(g)
    grads_ref[0] = from_diag(g_blank)
    grads_ref[1] = from_diag(g_label)


def lattice(feats, t_len, u_len, slots):
    _, rows, frames = feats.shape
    wide = frames + 128
    total = wide + 16
    reach = feats.shape[0] - 3
    return pl.pallas_call(
        partial(lattice_kernel, slots),
        out_shape=(jax.ShapeDtypeStruct(feats.shape, jnp.float32), jax.ShapeDtypeStruct((8, 128), jnp.float32)),
        in_specs=[pl.BlockSpec(memory_space=pltpu.VMEM), pl.BlockSpec(memory_space=pltpu.SMEM), pl.BlockSpec(memory_space=pltpu.SMEM)],
        out_specs=(pl.BlockSpec(memory_space=pltpu.VMEM),) * 2,
        scratch_shapes=[pltpu.VMEM((reach, total, 128), jnp.float32), pltpu.VMEM((reach + 1, total, 128), jnp.float32),
                        pltpu.VMEM((reach + 1, total, 128), jnp.float32), pltpu.VMEM((total, 128), jnp.float32),
                        pltpu.VMEM((total, 128), jnp.float32), pltpu.VMEM((total, 128), jnp.float32)],
        compiler_params=pltpu.CompilerParams(vmem_limit_bytes=48 << 20),
        name="lattice",
    )(feats, t_len, u_len)


GROUP=5
CHUNK=256

def nn(a,b): return jnp.dot(a,b,preferred_element_type=jnp.float32)
def nt(a,b): return lax.dot_general(a,b,(((1,),(1,)),((),())),preferred_element_type=jnp.float32)

def fold8(x, op):
    parts=[x[i:i+8] for i in range(0,x.shape[0],8)]
    while len(parts)>1:
        parts=[op(parts[i],parts[i+1]) if i+1<len(parts) else parts[i] for i in range(0,len(parts),2)]
    return parts[0]

def joint_fwd_kernel(groups, durs, labels_ref, enc_ref, pred_ref, wt_ref, feats_ref, p_ref, tok_ref):
    step=pl.program_id(0)
    vocab=p_ref.shape[2]
    u=step//groups
    g=step%groups
    for j in range(GROUP):
        k=g*GROUP+j
        hid=jnp.tanh(enc_ref[...]+pred_ref[0,:,j:j+1]).astype(jnp.bfloat16)
        tops=[]
        for c in range(0,vocab,CHUNK):
            t=nn(wt_ref[c:c+CHUNK,:],hid)
            tok_ref[j%2,c:c+CHUNK,:]=t
            tops.append(fold8(t,jnp.maximum))
        dl=nn(wt_ref[vocab:,:],hid)[:8]
        top=jnp.max(reduce(jnp.maximum,tops),0,keepdims=True)
        sums=[]
        for c in range(0,vocab,CHUNK):
            e=jnp.exp(tok_ref[j%2,c:c+CHUNK,:]-top)
            p_ref[0,j,c:c+CHUNK,:]=e.astype(jnp.bfloat16)
            sums.append(fold8(e,jnp.add))
        total=jnp.sum(reduce(jnp.add,sums),0,keepdims=True)
        lse=top+jnp.log(total)
        row=u*32+k
        feats_ref[0,pl.ds(row,1),:]=tok_ref[j%2,0:1,:]-lse
        feats_ref[1,pl.ds(row,1),:]=tok_ref[j%2,pl.ds(labels_ref[u,k],1),:]-lse
        real=lax.broadcasted_iota(jnp.int32,dl.shape,0)<durs
        dtop=jnp.max(jnp.where(real,dl,-1e30),0,keepdims=True)
        dlse=dtop+jnp.log(jnp.sum(jnp.where(real,jnp.exp(dl-dtop),0.0),0,keepdims=True))
        dlp=dl-dlse
        for e in range(durs):
            feats_ref[2+e,pl.ds(row,1),:]=dlp[e:e+1]
        feats_ref[2+durs,pl.ds(row,1),:]=1.0/total

def joint_forward(enc_t, pred_t, labels, w_t, vocab, durs, frames):
    joint, rows=enc_t.shape
    utts,slots=labels.shape
    groups=slots//GROUP
    return pl.pallas_call(
        partial(joint_fwd_kernel,groups,durs),
        grid=(utts*groups,),
        in_specs=[pl.BlockSpec(memory_space=pltpu.SMEM),
            pl.BlockSpec((joint,frames),lambda s:(0,s//groups)),
            pl.BlockSpec((1,joint,8),lambda s:(s,0,0)),
            pl.BlockSpec(w_t.shape,lambda s:(0,0))],
        out_specs=[pl.BlockSpec((3+durs,utts*32,frames),lambda s:(0,0,0)),
            pl.BlockSpec((1,GROUP,vocab,frames),lambda s:(s,0,0,0))],
        out_shape=[jax.ShapeDtypeStruct((3+durs,utts*32,frames),jnp.float32),
            jax.ShapeDtypeStruct((utts*groups,GROUP,vocab,frames),jnp.bfloat16)],
        scratch_shapes=[pltpu.VMEM((2,vocab,frames),jnp.float32)],
        compiler_params=pltpu.CompilerParams(vmem_limit_bytes=50<<20),
        name="joint_forward",
    )(labels,enc_t,pred_t,w_t)

def joint_bwd_kernel(groups, durs, labels_ref, enc_ref, pred_ref, w_ref, feats_ref, grads_ref, p_ref, genc_ref, gpred_ref, gtok_ref, gdur_ref, h_ref, d_ref, acc_ref, th_ref):
    step=pl.program_id(0)
    vocab=p_ref.shape[2]
    frames=p_ref.shape[3]
    u=step//groups
    g=step%groups

    @pl.when(step==0)
    def _():
        acc_ref[...]=jnp.zeros_like(acc_ref)
    @pl.when(g==0)
    def _():
        genc_ref[...]=jnp.zeros_like(genc_ref)
    for j in range(GROUP):
        k=g*GROUP+j
        row=u*32+k
        cols=slice(j*frames,(j+1)*frames)
        th=jnp.tanh(enc_ref[...]+pred_ref[0,:,j:j+1])
        h_ref[:,cols]=th.astype(jnp.bfloat16)
        th_ref[...]=th
        gb=grads_ref[0,pl.ds(row,1),:]
        gl=grads_ref[1,pl.ds(row,1),:]
        scale=-(gb+gl)*feats_ref[2+durs,pl.ds(row,1),:]
        for c in range(0,vocab,CHUNK):
            d_ref[c:c+CHUNK,cols]=(p_ref[0,j,c:c+CHUNK,:].astype(jnp.float32)*scale).astype(jnp.bfloat16)
        label=labels_ref[u,k]
        def fix(base):
            v=p_ref[0,j,pl.ds(base,16),:].astype(jnp.float32)*scale
            at=lax.broadcasted_iota(jnp.int32,v.shape,0)+base
            v=v+jnp.where(at==0,gb,0.0)+jnp.where(at==label,gl,0.0)
            d_ref[pl.ds(base,16),cols]=v.astype(jnp.bfloat16)
        fix(0)
        fix(pl.multiple_of((label//16)*16,16))
        gd=[grads_ref[2+e,pl.ds(row,1),:] for e in range(durs)]
        gsum=reduce(jnp.add,gd)
        at=lax.broadcasted_iota(jnp.int32,(16,frames),0)
        dd=jnp.zeros((16,frames),jnp.float32)
        for e in range(durs):
            dd=jnp.where(at==e,gd[e]-gsum*jnp.exp(feats_ref[2+e,pl.ds(row,1),:]),dd)
        d_ref[vocab:vocab+16,cols]=dd.astype(jnp.bfloat16)
        d_ref[vocab+16:,cols]=jnp.zeros((d_ref.shape[0]-vocab-16,frames),jnp.bfloat16)
        dh=nn(w_ref[...],d_ref[:,cols])
        th=th_ref[...]
        dp=dh*(1.0-th*th)
        genc_ref[...]+=dp
        gpred_ref[0,:,j:j+1]=jnp.sum(dp,1,keepdims=True)
    acc_ref[...]+=nt(h_ref[...],d_ref[...])
    @pl.when(step==pl.num_programs(0)-1)
    def _():
        gtok_ref[...]=acc_ref[:,:vocab].astype(jnp.bfloat16)
        gdur_ref[...]=acc_ref[:,vocab:].astype(jnp.bfloat16)

def joint_backward(enc_t, pred_t, labels, w, feats, grads, p, vocab, durs, frames):
    joint, rows=enc_t.shape
    utts,slots=labels.shape
    groups=slots//GROUP
    full=lambda a: pl.BlockSpec(a.shape,lambda s:(0,)*a.ndim)
    return pl.pallas_call(
        partial(joint_bwd_kernel,groups,durs),
        grid=(utts*groups,),
        in_specs=[pl.BlockSpec(memory_space=pltpu.SMEM),
            pl.BlockSpec((joint,frames),lambda s:(0,s//groups)),
            pl.BlockSpec((1,joint,8),lambda s:(s,0,0)),
            full(w),full(feats),full(grads),
            pl.BlockSpec((1,GROUP,vocab,frames),lambda s:(s,0,0,0))],
        out_specs=[pl.BlockSpec((joint,frames),lambda s:(0,s//groups)),
            pl.BlockSpec((1,joint,8),lambda s:(s,0,0)),
            pl.BlockSpec((joint,vocab),lambda s:(0,0)),
            pl.BlockSpec((joint,128),lambda s:(0,0))],
        out_shape=[jax.ShapeDtypeStruct((joint,rows),jnp.float32),
            jax.ShapeDtypeStruct((utts*groups,joint,8),jnp.float32),
            jax.ShapeDtypeStruct((joint,vocab),jnp.bfloat16),
            jax.ShapeDtypeStruct((joint,128),jnp.bfloat16)],
        scratch_shapes=[pltpu.VMEM((joint,GROUP*frames),jnp.bfloat16),
            pltpu.VMEM((vocab+128,GROUP*frames),jnp.bfloat16),
            pltpu.VMEM((joint,vocab+128),jnp.float32),pltpu.VMEM((joint,frames),jnp.float32)],
        compiler_params=pltpu.CompilerParams(vmem_limit_bytes=56<<20),
        name="joint_backward",
    )(labels,enc_t,pred_t,w,feats,grads,p)


MESH=pl.DeviceIdType.MESH
QA = QB = 16
HALF = 2 * QA + QB
TILE = 2 * HALF


def place():
    dp=lax.axis_index("dp"); fs=lax.axis_index("fsdp")
    return dp, fs, dp//2, dp%2, fs//2, fs%2

def greet(n1, dp, fs, a, c, i1, i2):
    barrier=pltpu.get_barrier_semaphore()
    for d in range(1,n1):
        pl.semaphore_signal(barrier,inc=1,device_id=(dp,lax.rem(i1+d,n1)*2+i2),device_id_type=MESH)
    pl.semaphore_signal(barrier,inc=1,device_id=(dp,i1*2+1-i2),device_id_type=MESH)
    pl.semaphore_signal(barrier,inc=1,device_id=((1-a)*2+c,fs),device_id_type=MESH)
    pl.semaphore_signal(barrier,inc=1,device_id=(a*2+1-c,fs),device_id_type=MESH)
    pl.semaphore_wait(barrier,n1+2)

def remote(s, d, ss, rs, dev):
    return pltpu.make_async_remote_copy(src_ref=s,dst_ref=d,send_sem=ss,recv_sem=rs,device_id=dev,device_id_type=MESH)

def rows(base, size):
    return pl.ds(pl.multiple_of(base,16),size)

class Beats:
    def __init__(self, tick=None, total=0, sites=None):
        self.tick = tick
        self.total = total
        self.at = 0
        self.credit = 0.0
        self.scale = total / sites if sites else 1.0

    def grant(self, count):
        self.credit += count * self.scale
        steps = min(int(self.credit), self.total - self.at)
        self.credit -= int(self.credit)
        first = self.at
        self.at += steps
        return first, steps

    def span(self, low, high):
        def step(i, carry):
            self.tick(i)
            return carry

        lax.fori_loop(low, high, step, 0)

    def loop(self, sites, count=None):
        if self.tick is None:
            return lambda i: None
        first, steps = self.grant(sites)
        count = count or sites
        return lambda i: self.span(first + i * steps // count, first + (i + 1) * steps // count)

    def run(self, count):
        if self.tick is None:
            return
        first, steps = self.grant(count)
        if steps:
            self.span(first, first + steps)

    def until(self, step):
        if self.at < step:
            self.span(self.at, step)
            self.at = step

    def rest(self):
        self.until(self.total)


class ScatterEngine:
    def __init__(self, n1, plan, lag, srcs, out, own, gc, gx, gy, gz, gf, fin, lo, sc, rc, sx, rx, sy, ry, sz, rz, sf, rf, se, re, wo):
        dp, fs, a, c, i1, i2 = place()
        ypeer = (dp, i1 * 2 + 1 - i2)
        xpeer = ((1 - a) * 2 + c, fs)
        cpeer = (a * 2 + 1 - c, fs)
        tiles = sum(count for _, count in plan)
        main = rows(a * QA, QA + QB)
        middle = pl.ds(QA, QB)

        def quarter(aa):
            return rows(aa * (QA + QB), QA)

        def cwait(t):
            return remote(own.at[t], gc.at[t], sc.at[0], rc.at[t], cpeer)

        def xcopy(t):
            return remote(own.at[t, :, :, quarter(1 - a), :], gx.at[t], sx.at[0], rx.at[t], xpeer)

        def ycopy(t):
            return remote(own.at[t, :, 1 - i2, main, :], gy.at[t], sy.at[0], ry.at[t], ypeer)

        def zcopy(t, j):
            return remote(own.at[t, j, i2, main, :], gz.at[t, i1], sz.at[0], rz.at[t], (dp, j * 2 + i2))

        def zin(t):
            arrived = gz.at[t, pl.ds(0, n1 - 1)]
            return remote(arrived, arrived, sz.at[0], rz.at[t], ypeer)

        def fcopy(t):
            return remote(own.at[t, i1, i2, main, :], gf.at[t], sf.at[0], rf.at[t], xpeer)

        def ecopy(t):
            return remote(fin.at[t, c], fin.at[t, c], se.at[0], re.at[t], cpeer)

        def ein(t):
            return remote(fin.at[t, 1 - c], fin.at[t, 1 - c], se.at[0], re.at[t], cpeer)

        def store(t):
            return pltpu.make_async_copy(fin.at[t], out.at[t], wo.at[0])

        def stage_c(t):
            first = 0
            for src, (base, count) in zip(srcs, plan):

                @pl.when((t >= first) & (t < first + count))
                def _(src=src, skip=base - first):
                    at = (t + skip) * TILE
                    pltpu.make_async_copy(src.at[:, :, rows(at + c * HALF, HALF), :], own.at[t], lo.at[t]).start()
                    remote(src.at[:, :, rows(at + (1 - c) * HALF, HALF), :], gc.at[t], sc.at[0], rc.at[t], cpeer).start()

                first += count

        def stage_x(t):
            pltpu.make_async_copy(own.at[t], own.at[t], lo.at[t]).wait()
            cwait(t).wait_recv()
            own[t] = own[t] + gc[t]
            xcopy(t).start()

        def stage_y(t):
            xcopy(t).wait_recv()
            own[t, :, :, quarter(a), :] = own[t, :, :, quarter(a), :] + gx[t]
            ycopy(t).start()

        def stage_z(t):
            ycopy(t).wait_recv()
            own[t, :, i2, main, :] = own[t, :, i2, main, :] + gy[t]
            for d in range(1, n1):
                zcopy(t, lax.rem(i1 + d, n1)).start()

        def stage_f(t):
            total = own[t, i1, i2, main, :].astype(jnp.float32)
            zin(t).wait_recv()
            for d in range(1, n1):
                j = lax.rem(i1 + n1 - d, n1)
                total = total + gz[t, j].astype(jnp.float32)
            own[t, i1, i2, main, :] = total.astype(jnp.bfloat16)
            fcopy(t).start()

        def stage_e(t):
            fcopy(t).wait_recv()
            fin[t, c, quarter(a), :] = own[t, i1, i2, quarter(a), :]
            fin[t, c, quarter(1 - a), :] = gf[t, rows((1 - a) * QB, QA), :]
            fin[t, c, middle, :] = own[t, i1, i2, middle, :] + gf[t, rows(a * QA, QB), :]
            ecopy(t).start()

        def stage_o(t):
            ein(t).wait_recv()
            store(t).start()

        stages = (stage_c, stage_x, stage_y, stage_z, stage_f, stage_e, stage_o)

        def tick(tau):
            for place_of, stage in enumerate(stages):
                t = tau - place_of * lag

                @pl.when((t >= 0) & (t < tiles))
                def _(stage=stage, t=t):
                    stage(t)

        def finish():
            for sent, sem in (
                (own, sc), (gx, sx), (gy, sy), (gz.at[:, pl.ds(0, n1 - 1)], sz), (gf, sf), (fin.at[:, 0], se),
            ):
                remote(sent, sent, sem.at[0], rc.at[0], cpeer).wait_send()
            pltpu.make_async_copy(fin, fin, wo.at[0]).wait()

        self.tick = tick
        self.total = tiles + (len(stages) - 1) * lag
        self.finish = finish


def scatter_plan(sources):
    return tuple((first, count) for _, first, count in sources)


def scatter_scratch(n, tiles):
    n1 = n // 2
    dma = pltpu.SemaphoreType.DMA
    v = lambda *shape: pltpu.VMEM((tiles,) + shape + (WIDE,), jnp.bfloat16)
    one = dma((1,))
    each = dma((tiles,))
    return [
        v(n1, 2, HALF), v(n1, 2, HALF), v(n1, 2, QA), v(n1, QA + QB), v(n1, QA + QB), v(QA + QB), v(2, HALF),
        each, one, each, one, each, one, each, one, each, one, each, one, each, one,
    ]


def riding_kernel(kernel, counts, plan, lag, n1, sites, groups, *refs):
    n_in, n_out, n_scratch = counts
    k = len(plan)
    ins, refs = refs[:n_in], refs[n_in:]
    srcs, refs = refs[:k], refs[k:]
    outs, refs = refs[:n_out], refs[n_out:]
    share, refs = refs[0], refs[1:]
    scratch, refs = refs[:n_scratch], refs[n_scratch:]
    if groups:
        meet(groups, 2 * n1)()
    else:
        greet(n1, *place())
    engine = ScatterEngine(n1, plan, lag, srcs, share, *refs)
    beats = Beats(engine.tick, engine.total, sites)
    kernel(beats, *ins, *outs, *scratch)
    beats.rest()
    engine.finish()


def call(kernel, args, in_specs, out_specs, out_shape, scratch, name, ride=None, collective_id=None, sites=None, groups=0, lag=2):
    if not ride:
        return pl.pallas_call(
            partial(kernel, Beats()),
            in_specs=in_specs,
            out_specs=out_specs,
            out_shape=out_shape,
            scratch_shapes=scratch,
            compiler_params=pltpu.CompilerParams(vmem_limit_bytes=60 << 20),
            name=name,
        )(*args)
    n = lax.axis_size("fsdp")
    tiles = sum(count for _, _, count in ride)
    counts = (len(args), len(out_shape), len(scratch))
    *outs, share = pl.pallas_call(
        partial(riding_kernel, kernel, counts, scatter_plan(ride), lag, n // 2, sites, groups),
        in_specs=in_specs + [ANY_SPEC] * len(ride),
        out_specs=out_specs + [ANY_SPEC],
        out_shape=out_shape + [sds((tiles, 2, HALF, WIDE), BF16)],
        scratch_shapes=scratch + scatter_scratch(n, tiles),
        compiler_params=pltpu.CompilerParams(collective_id=collective_id, has_side_effects=True, vmem_limit_bytes=61 << 20),
        name=name + "_and_scatter",
    )(*args, *[grads.reshape(n // 2, 2, -1, WIDE) for grads, _, _ in ride])
    return outs, share.reshape(tiles * TILE, WIDE)


def idle_kernel(beats):
    pass


def scatter(ride, collective_id):
    return call(idle_kernel, [], [], [], [], [], "idle", ride, collective_id)[1]


def pooled(parts):
    counts = [x[8:9] for x in parts]
    count = sum(counts[1:], counts[0])
    mean = sum((x[0:4] * n for x, n in zip(parts[1:], counts[1:])), parts[0][0:4] * counts[0]) / count
    dev = jnp.zeros_like(mean)
    for x, n in zip(parts, counts):
        gap = x[0:4] - mean
        dev = dev + (x[4:8] + gap * gap * n)
    return mean, dev, count


CHUNK_ROWS = 128
PAIRS_AT_ONCE = 4
WIDE = 512
PLACE = ("p_out", "s_in", "s_out", "p_in", "w_proj", "w_joint", "f_in", "f_out")


def tn(a, b):
    return lax.dot_general(a, b, (((0,), (0,)), ((), ())), preferred_element_type=jnp.float32)


def row_loop(count, body, init=0):
    def step(i, carry):
        return body(pl.ds(pl.multiple_of(i * CHUNK_ROWS, CHUNK_ROWS), CHUNK_ROWS), i, carry)

    return lax.fori_loop(0, count // CHUNK_ROWS, step, init, unroll=count // CHUNK_ROWS)


def ln_parts(v):
    centred = v - jnp.mean(v, -1, keepdims=True)
    rstd = lax.rsqrt(jnp.mean(centred * centred, -1, keepdims=True) + EPS)
    return centred * rstd, rstd


def ln_back(v, gain, grad):
    hat, rstd = ln_parts(v)
    dy = grad * gain
    dv = rstd * (dy - jnp.mean(dy, -1, keepdims=True) - hat * jnp.mean(dy * hat, -1, keepdims=True))
    return dv, fold8(grad * hat, jnp.add)


def offsets(n, width, ff):
    low = width // n
    tall = ff // n
    sizes = {
        "p_out": low, "s_in": low * (ff // WIDE), "s_out": tall, "p_in": 2 * low,
        "w_proj": low, "w_joint": 3 * low, "f_in": low * (ff // WIDE), "f_out": tall,
    }
    table = {}
    at = 0
    for name in PLACE:
        table[name] = at
        at += sizes[name]
    return table, at


class Mover:
    def __init__(self, sems, used=0):
        self.sems = sems
        self.used = used
        self.pending = []

    def take(self):
        self.used += 1
        return self.sems.at[self.used - 1]

    def load(self, src, dst):
        cp = pltpu.make_async_copy(src, dst, self.take())
        cp.start()
        return cp

    def put(self, src, dst):
        cp = pltpu.make_async_copy(src, dst, self.take())
        cp.start()
        self.pending.append(cp)

    def load_weight(self, whole, at, dst):
        flat = len(whole.shape) == 3
        n = whole.shape[0] if flat else 2 * whole.shape[0]
        height = dst.shape[0] // n
        sem = self.take()

        def one(s, carry):
            for b in range(dst.shape[1] // WIDE):
                pltpu.make_async_copy(
                    (whole.at[s] if flat else whole.at[s // 2, s % 2]).at[pl.ds(at + b * height, height), :],
                    dst.at[pl.ds(pl.multiple_of(s * height, 16), height), pl.ds(b * WIDE, WIDE)],
                    sem,
                ).start()
            return carry

        lax.fori_loop(0, n, one, 0)
        return pltpu.make_async_copy(dst, dst, sem)

    def put_weight(self, src, grads, at):
        n = grads.shape[0]
        height = src.shape[0] // n
        sem = self.take()

        def one(s, carry):
            for b in range(src.shape[1] // WIDE):
                pltpu.make_async_copy(
                    src.at[pl.ds(pl.multiple_of(s * height, 16), height), pl.ds(b * WIDE, WIDE)],
                    grads.at[s, pl.ds(at + b * height, height), :],
                    sem,
                ).start()
            return carry

        lax.fori_loop(0, n, one, 0)
        self.pending.append(pltpu.make_async_copy(src, src, sem))

    def finish(self):
        for cp in self.pending:
            cp.wait()
        self.pending = []


def valid_rows_of(t_ref, frames, i):
    per = frames // CHUNK_ROWS
    t_len = t_ref[i // per]
    at = lax.broadcasted_iota(jnp.int32, (CHUNK_ROWS, 1), 0) + lax.rem(i, per) * CHUNK_ROWS
    return jnp.where(at < t_len, 1.0, 0.0)


def write_rows(out, base, vec):
    for i in range(vec.shape[1] // 128):
        out[base + i : base + i + 1, :] = vec[:, i * 128 : (i + 1) * 128]


def read_rows(ref, base, width):
    return jnp.concatenate([ref[base + i : base + i + 1, :] for i in range(width // 128)], 1)


def fill_gated(utts, frames, t_ref, r, gp):
    width = gp.shape[1]
    span = frames + 16
    per = frames // CHUNK_ROWS
    for u in range(utts):
        gp[u * span : u * span + 8, :] = jnp.zeros((8, width), jnp.float32)
        gp[u * span + 8 + frames : (u + 1) * span, :] = jnp.zeros((8, width), jnp.float32)

    def gate(rr, i, c):
        g = r[rr, :width] * jax.nn.sigmoid(r[rr, width:]) * valid_rows_of(t_ref, frames, i)
        at = (i // per) * span + 8 + lax.rem(i, per) * CHUNK_ROWS
        gp[pl.ds(pl.multiple_of(at, 8), CHUNK_ROWS), :] = g
        return c

    row_loop(utts * frames, gate)


def window(gp, frames, i):
    per = frames // CHUNK_ROWS
    at = (i // per) * (frames + 16) + lax.rem(i, per) * CHUNK_ROWS
    return gp[pl.ds(pl.multiple_of(at, 8), CHUNK_ROWS + 16), :]


def spread(gp, utts, frames, i, taps, flip=False):
    win = window(gp, frames, i)
    count = taps.shape[0]
    total = None
    for j in range(count):
        shift = 8 - count // 2 + (count - 1 - j if flip else j)
        term = win[shift : shift + CHUNK_ROWS] * taps[j : j + 1]
        total = term if total is None else total + term
    return total


def ffn_bwd(rows, v_ref, gain, w_in, w_out, h, loads, g_ref, gb, normed, dact, act, dh, dn, dw_in, dw_out, mover, grads, at_in, at_out, beats):
    def prepare(rr, i, c):
        normed[rr, :] = (ln_parts(v_ref[rr, :].astype(jnp.float32))[0] * gain).astype(jnp.bfloat16)
        gb[rr, :] = (0.5 * g_ref[rr, :]).astype(jnp.bfloat16)
        return c

    row_loop(rows, prepare)
    w_out[1].wait()
    for b in range(h.shape[0]):
        cols = slice(b * WIDE, (b + 1) * WIDE)
        dact[...] = nt(gb[...], w_out[0][cols, :])
        beats.run(1)
        loads[b].wait()

        def slope(rr, i, c):
            v = h[b, rr, :]
            sg = jax.nn.sigmoid(v)
            act[rr, :] = (v * sg).astype(jnp.bfloat16)
            dh[rr, cols] = (dact[rr, :] * (sg * (1.0 + v * (1.0 - sg)))).astype(jnp.bfloat16)
            return c

        row_loop(rows, slope)
        beats.run(1)
        dw_out[cols, :] = tn(act[...], gb[...]).astype(jnp.bfloat16)
        beats.run(1)
        dw_in[:, cols] = tn(normed[...], dh[:, cols]).astype(jnp.bfloat16)
        beats.run(1)
    mover.put_weight(dw_out, grads, at_out)
    mover.put_weight(dw_in, grads, at_in)
    w_in[1].wait()
    dn[...] = nt(dh[...], w_in[0][...])
    beats.run(2)

    def back(rr, i, total):
        dv, dg = ln_back(v_ref[rr, :].astype(jnp.float32), gain, dn[rr, :])
        g_ref[rr, :] = g_ref[rr, :] + dv
        return total + dg

    return row_loop(rows, back, jnp.zeros((8, g_ref.shape[1]), jnp.float32))


def down(folded):
    return jnp.sum(folded, 0, keepdims=True)


def back_one_kernel(table, held, beats, grad_ref, y4_ref, y3_ref, d_ref, pooled_ref, small, whole, h_hbm, g_out, db_out, grads, sums, gain_out,
                    w_pout, w_sin, w_sout, g, gb, normed, dact, act, dh, dn, dw_in, dw_out, dw_pout, h, db, sems):
    rows, width = g.shape
    mover = Mover(sems)
    gains = small[...]
    sout = mover.load_weight(whole, held["s_out"], w_sout)
    loads = [mover.load(h_hbm.at[b], h.at[b]) for b in range(h.shape[0])]
    sin = mover.load_weight(whole, held["s_in"], w_sin)
    wo = mover.load_weight(whole, held["p_out"], w_pout)
    beats.run(5)

    def first(rr, i, total):
        dv, dg = ln_back(y4_ref[rr, :], gains[4:5], grad_ref[rr, :])
        g[rr, :] = dv
        return total + dg

    gain4 = down(row_loop(rows, first, jnp.zeros((8, width), jnp.float32)))
    gain3 = down(ffn_bwd(rows, y3_ref, gains[3:4], (w_sin, sin), (w_sout, sout), h, loads, g, gb, normed, dact, act, dh, dn,
                         dw_in, dw_out, mover, grads, table["s_in"], table["s_out"], beats))
    mover.put(g, g_out)
    gain_out[...] = jnp.concatenate([gain3, gain4, jnp.zeros((6, width), jnp.float32)], 0)
    mean = read_rows(pooled_ref, 0, width)
    istd = lax.rsqrt(read_rows(pooled_ref, 4, width) / pooled_ref[8:9, 0:1] + EPS)

    def cast(rr, i, c):
        gb[rr, :] = g[rr, :].astype(jnp.bfloat16)
        return c

    row_loop(rows, cast)
    wo.wait()
    dact[...] = nt(gb[...], w_pout[...])
    beats.run(1)

    def bn(rr, i, totals):
        z = (d_ref[rr, :] - mean) * istd
        b = z * gains[14:15] + gains[15:16]
        sg = jax.nn.sigmoid(b)
        act[rr, :] = (b * sg).astype(jnp.bfloat16)
        db_chunk = dact[rr, :] * (sg * (1.0 + b * (1.0 - sg)))
        db[rr, :] = db_chunk
        return totals[0] + fold8(db_chunk, jnp.add), totals[1] + fold8(db_chunk * z, jnp.add)

    zero = jnp.zeros((8, width), jnp.float32)
    one, two = row_loop(rows, bn, (zero, zero))
    beats.run(2)
    mover.put(db, db_out)
    write_rows(sums, 0, down(one))
    write_rows(sums, 4, down(two))
    sums[8:16, :] = jnp.zeros((8, 128), jnp.float32)
    dw_pout[...] = tn(act[...], gb[...]).astype(jnp.bfloat16)
    mover.put_weight(dw_pout, grads, table["p_out"])
    mover.finish()


def back_two_kernel(utts, table, held, start, end, beats, t_ref, x_ref, y1_ref, y2_ref, r_ref, t_in, c_ref, d_ref, db_ref, g_in, pooled_ref, local_ref, late_ref, small, whole, h_hbm,
                    g_out, grads, sums_ref,
                    w_pin, w_proj, w_joint, w_fin, w_fout, g, gb, normed, dact, act, dh, dn, dw_pin, dw_proj, dw_joint, dw_in, dw_out, h, gp, dd, sm, sems, *meeting):
    rows, width = g.shape
    frames = rows // utts
    mover = Mover(sems)
    gains = small[...]
    wi = mover.load_weight(whole, held["p_in"], w_pin)
    wp = mover.load_weight(whole, held["w_proj"], w_proj)
    wj = mover.load_weight(whole, held["w_joint"], w_joint)
    fout = mover.load_weight(whole, held["f_out"], w_fout)
    loads = [mover.load(h_hbm.at[b], h.at[b]) for b in range(h.shape[0])]
    fin = mover.load_weight(whole, held["f_in"], w_fin)
    mean = read_rows(pooled_ref, 0, width)
    count = pooled_ref[8:9, 0:1]
    istd = lax.rsqrt(read_rows(pooled_ref, 4, width) / count + EPS)
    taps = gains[5:14]
    ntaps = taps.shape[0]
    span = frames + 16
    per = frames // CHUNK_ROWS
    dr = dh.at[:, pl.ds(0, 2 * width)]
    dt = dh.at[:, pl.ds(0, 3 * width)]
    beats.run(5)
    exchange = Exchange("sum", meeting[0].shape[0], meeting[1].shape[0], *meeting)
    exchange.begin(local_ref[...])
    fill_gated(utts, frames, t_ref, r_ref, gp)
    exchange.middle()
    beats.run(1)
    for u in range(utts):
        dd[u * span : u * span + 8, :] = jnp.zeros((8, width), jnp.float32)
        dd[u * span + 8 + frames : (u + 1) * span, :] = jnp.zeros((8, width), jnp.float32)

    sums_ref[...] = exchange.end()
    bias_sum = read_rows(sums_ref, 0, width)
    gain_sum = read_rows(sums_ref, 4, width)

    def bn(rr, i, c):
        z = (d_ref[rr, :] - mean) * istd
        v = gains[14:15] * istd * (db_ref[rr, :] - valid_rows_of(t_ref, frames, i) * (bias_sum + z * gain_sum) / count)
        at = (i // per) * span + 8 + lax.rem(i, per) * CHUNK_ROWS
        dd[pl.ds(pl.multiple_of(at, 8), CHUNK_ROWS), :] = v
        return c

    row_loop(rows, bn)

    def conv(rr, i, totals):
        dg = spread(dd, utts, frames, i, taps, True) * valid_rows_of(t_ref, frames, i)
        sg = jax.nn.sigmoid(r_ref[rr, width:])
        dr[rr, :width] = (dg * sg).astype(jnp.bfloat16)
        dr[rr, width:] = (dg * r_ref[rr, :width] * sg * (1.0 - sg)).astype(jnp.bfloat16)
        win = window(gp, frames, i)
        mine = window(dd, frames, i)[8 : 8 + CHUNK_ROWS]
        normed[rr, :] = (ln_parts(y2_ref[rr, :])[0] * gains[2:3]).astype(jnp.bfloat16)
        return tuple(
            totals[j] + fold8(win[8 - ntaps // 2 + j : 8 - ntaps // 2 + j + CHUNK_ROWS] * mine, jnp.add) for j in range(ntaps)
        )

    zero = jnp.zeros((8, width), jnp.float32)
    tap_grads = [down(x) for x in row_loop(rows, conv, (zero,) * ntaps)]
    beats.run(2)
    for b in range(2):
        cols = slice(b * width, (b + 1) * width)
        dw_pin[:, cols] = tn(normed[...], dr[:, cols]).astype(jnp.bfloat16)
    mover.put_weight(dw_pin, grads, table["p_in"] - start)
    beats.run(2)
    wi.wait()
    dn[...] = nt(dr[...], w_pin[...])
    beats.run(1)

    def back_conv(rr, i, total):
        dv, dg = ln_back(y2_ref[rr, :], gains[2:3], dn[rr, :])
        v = g_in[rr, :] + dv
        g[rr, :] = v
        gb[rr, :] = v.astype(jnp.bfloat16)
        normed[rr, :] = (ln_parts(y1_ref[rr, :])[0] * gains[1:2]).astype(jnp.bfloat16)
        return total + dg

    gain2 = down(row_loop(rows, back_conv, zero))
    dw_proj[...] = tn(c_ref[...], gb[...]).astype(jnp.bfloat16)
    mover.put_weight(dw_proj, grads, table["w_proj"] - start)
    beats.run(1)
    wp.wait()
    act[...] = nt(gb[...], w_proj[...]).astype(jnp.bfloat16)
    pairs = width // 128
    side = lax.broadcasted_iota(jnp.int32, (frames, 128), 1) < 64
    key_at = lax.broadcasted_iota(jnp.int32, (frames, 1), 0)
    turns = utts * pairs // PAIRS_AT_ONCE
    hook = beats.loop(utts * pairs, turns)

    def pair_step(m, carry):
        u = m // pairs
        base = lax.rem(m, pairs) * 128
        rr = pl.ds(pl.multiple_of(u * frames, frames), frames)
        at = [pl.ds(pl.multiple_of(base + b * width, 128), 128) for b in range(3)]
        bias = jnp.where(key_at < t_ref[u], 0.0, MASKED)
        q = t_in[rr, at[0]]
        k = t_in[rr, at[1]]
        v = t_in[rr, at[2]]
        dc = act[rr, at[0]]
        got = []
        for half in range(2):
            mine = side if half == 0 else ~side
            nothing = jnp.zeros_like(k)
            s = nt(jnp.where(mine, k, nothing), q) * 0.125 + bias
            p = jnp.exp(s - jnp.max(s, 0, keepdims=True))
            p = p * (1.0 / jnp.sum(p, 0, keepdims=True))
            dp = nt(jnp.where(mine, v, nothing), dc)
            ds = (p * (dp - jnp.sum(dp * p, 0, keepdims=True))).astype(jnp.bfloat16)
            got.append((tn(ds, k) * 0.125, nn(ds, q) * 0.125, nn(p.astype(jnp.bfloat16), dc)))
        for b in range(3):
            dt[rr, at[b]] = jnp.where(side, got[0][b], got[1][b]).astype(jnp.bfloat16)
        return carry

    def pair_turn(m, carry):
        hook(m)
        for i in range(PAIRS_AT_ONCE):
            carry = pair_step(m * PAIRS_AT_ONCE + i, carry)
        return carry

    lax.fori_loop(0, turns, pair_turn, 0)
    for b in range(3):
        cols = slice(b * width, (b + 1) * width)
        dw_joint[:, cols] = tn(normed[...], dt[:, cols]).astype(jnp.bfloat16)
    mover.put_weight(dw_joint, grads, table["w_joint"] - start)
    beats.run(2)
    wj.wait()
    dn[...] = nt(dt[...], w_joint[...])
    beats.run(1)

    def back_attend(rr, i, total):
        dv, dg = ln_back(y1_ref[rr, :], gains[1:2], dn[rr, :])
        g[rr, :] = g[rr, :] + dv
        return total + dg

    gain1 = down(row_loop(rows, back_attend, zero))
    gain0 = down(ffn_bwd(rows, x_ref, gains[0:1], (w_fin, fin), (w_fout, fout), h, loads, g, gb, normed, dact, act, dh, dn,
                         dw_in, dw_out, mover, grads, table["f_in"] - start, table["f_out"] - start, beats))
    mover.put(g, g_out)
    packed = jnp.concatenate([gain0, gain1, gain2, late_ref[0:2, :]] + tap_grads + [jnp.zeros((2, width), jnp.float32)], 0)
    n = grads.shape[0]
    low = width // n
    for s in range(n):
        sm[s] = jnp.concatenate([packed[:, s * low : (s + 1) * low], jnp.zeros((16, WIDE - low), jnp.float32)], 1).astype(jnp.bfloat16)
    mover.put(sm, grads.at[:, pl.ds(end - start, 16), :])
    mover.finish()


VMEM_SPEC = pl.BlockSpec(memory_space=pltpu.VMEM)
SMEM_SPEC = pl.BlockSpec(memory_space=pltpu.SMEM)
ANY_SPEC = pl.BlockSpec(memory_space=pl.ANY)
F32 = jnp.float32
BF16 = jnp.bfloat16


def sds(shape, dtype=jnp.float32):
    return jax.ShapeDtypeStruct(shape, dtype)


def tiled(count):
    return -(-count // TILE) * TILE


def back_one(grad, y4, y3, d, pooled, small, whole, h, ff, held, ride=None, collective_id=None):
    rows, width = grad.shape
    n = whole.shape[0]
    table, _ = offsets(n, width, ff)
    nb = ff // WIDE
    v = pltpu.VMEM
    return call(
        partial(back_one_kernel, table, held),
        (grad, y4, y3, d, pooled, small, whole, h),
        [VMEM_SPEC] * 6 + [ANY_SPEC] * 2,
        [ANY_SPEC] * 3 + [VMEM_SPEC] * 2,
        [sds((rows, width)), sds((rows, width)), sds((n, tiled(table["p_in"]), WIDE), BF16), sds((16, 128)), sds((8, width))],
        [v((width, width), BF16), v((width, ff), BF16), v((ff, width), BF16), v((rows, width), F32),
         v((rows, width), BF16), v((rows, width), BF16), v((rows, width), F32), v((rows, width), BF16),
         v((rows, ff), BF16), v((rows, width), F32), v((width, ff), BF16), v((ff, width), BF16),
         v((width, width), BF16), v((nb, rows, WIDE), F32), v((rows, width), F32), pltpu.SemaphoreType.DMA((16,))],
        "back_part_one",
        ride,
        collective_id,
        28,
    )


def back_two(t_len, x, y1, y2, r, t, c, d, db, g, pooled, sums, late, small, whole, h, ff, held, ride=None, collective_id=None):
    rows, width = d.shape
    utts = t_len.shape[0]
    n = whole.shape[0]
    table, end = offsets(n, width, ff)
    start = table["p_in"]
    nb = ff // WIDE
    v = pltpu.VMEM
    dma = pltpu.SemaphoreType.DMA
    groups = lax.axis_size("dp")
    pad_rows = utts * (rows // utts + 16)
    return call(
        partial(back_two_kernel, utts, table, held, start, end),
        (t_len, x, y1, y2, r, t, c, d, db, g, pooled, sums, late, small, whole, h),
        [SMEM_SPEC] + [VMEM_SPEC] * 13 + [ANY_SPEC] * 2,
        [ANY_SPEC] * 2 + [VMEM_SPEC],
        [sds((rows, width)), sds((n, tiled(end - start + 16), WIDE), BF16), sds((16, 128))],
        [v((width, 2 * width), BF16), v((width, width), BF16), v((width, 3 * width), BF16), v((width, ff), BF16),
         v((ff, width), BF16), v((rows, width), F32), v((rows, width), BF16), v((rows, width), BF16),
         v((rows, width), F32), v((rows, width), BF16), v((rows, ff), BF16), v((rows, width), F32),
         v((width, 2 * width), BF16), v((width, width), BF16), v((width, 3 * width), BF16), v((width, ff), BF16),
         v((ff, width), BF16), v((nb, rows, WIDE), F32), v((pad_rows, width), F32), v((pad_rows, width), F32),
         v((n, 16, WIDE), BF16), pltpu.SemaphoreType.DMA((20,)),
         v((groups, 16, 128), F32), v((n, 16, 128), F32), dma((groups,)), dma((groups,)), dma((n,)), dma((n,))],
        "back_part_two",
        ride,
        collective_id,
        44,
        groups,
    )


FIRST = ("small", "f_in", "f_out", "w_joint", "w_proj", "p_in", "p_out", "s_in", "s_out")


def gathered_rows(n, width, ff, layers):
    low = width // n
    tall = ff // n
    sizes = {
        "f_in": low * (ff // WIDE), "f_out": tall, "small": 16, "w_joint": 3 * low, "w_proj": low,
        "p_in": 2 * low, "p_out": low, "s_in": low * (ff // WIDE), "s_out": tall,
    }
    tables = []
    at = 0
    for layer in range(layers):
        table = {}
        for name in FIRST:
            table[name] = (at, at + sizes[name])
            at += sizes[name]
        tables.append(table)
    return tables, at


class GatherEngine:
    def __init__(self, n1, tiles, lag, packed, out, so, sz, rz, sy, ry, sx, rx, sc, rc):
        dp, fs, a, c, i1, i2 = place()
        ypeer = (dp, i1 * 2 + 1 - i2)
        xpeer = ((1 - a) * 2 + c, fs)
        cpeer = (a * 2 + 1 - c, fs)

        def main(t):
            return rows(t * TILE + c * HALF + a * QA, QA + QB)

        def quarter(t, aa):
            return rows(t * TILE + c * HALF + aa * (QA + QB), QA)

        def half(t, cc):
            return rows(t * TILE + cc * HALF, HALF)

        def local(t):
            return pltpu.make_async_copy(packed.at[main(t), :], out.at[i1, i2, main(t), :], so.at[t])

        def zcopy(t, j):
            return remote(packed.at[main(t), :], out.at[i1, i2, main(t), :], sz.at[0], rz.at[t], (dp, j * 2 + i2))

        def zin(t):
            arrived = out.at[pl.ds(0, n1 - 1), i2, main(t), :]
            return remote(arrived, arrived, sz.at[0], rz.at[t], ypeer)

        def ycopy(t):
            return remote(out.at[:, i2, main(t), :], out.at[:, i2, main(t), :], sy.at[0], ry.at[t], ypeer)

        def yin(t):
            return remote(out.at[:, i2, main(t), :], out.at[:, 1 - i2, main(t), :], sy.at[0], ry.at[t], ypeer)

        def xcopy(t):
            return remote(out.at[:, :, quarter(t, a), :], out.at[:, :, quarter(t, a), :], sx.at[0], rx.at[t], xpeer)

        def xin(t):
            return remote(out.at[:, :, quarter(t, a), :], out.at[:, :, quarter(t, 1 - a), :], sx.at[0], rx.at[t], xpeer)

        def ccopy(t):
            return remote(out.at[:, :, half(t, c), :], out.at[:, :, half(t, c), :], sc.at[0], rc.at[t], cpeer)

        def cin(t):
            return remote(out.at[:, :, half(t, c), :], out.at[:, :, half(t, 1 - c), :], sc.at[0], rc.at[t], cpeer)

        def stage_z(t):
            for d in range(1, n1):
                zcopy(t, lax.rem(i1 + d, n1)).start()
            local(t).start()

        def stage_y(t):
            local(t).wait()
            zin(t).wait_recv()
            ycopy(t).start()

        def stage_x(t):
            yin(t).wait_recv()
            xcopy(t).start()

        def stage_c(t):
            xin(t).wait_recv()
            ccopy(t).start()

        def stage_o(t):
            cin(t).wait_recv()

        stages = (stage_z, stage_y, stage_x, stage_c, stage_o)

        def tick(tau):
            for place_of, stage in enumerate(stages):
                t = tau - place_of * lag

                @pl.when((t >= 0) & (t < tiles))
                def _(stage=stage, t=t):
                    stage(t)

        def finish():
            every = pl.ds(0, n1)
            for peer, sem, far, near, height in (
                (ypeer, sz, pl.ds(0, n1 - 1), 0, QA + QB),
                (ypeer, sy, every, 0, QA + QB),
                (xpeer, sx, every, pl.ds(0, 2), QA),
                (cpeer, sc, every, pl.ds(0, 2), HALF),
            ):
                sent = out.at[far, near, pl.ds(0, tiles * height), :]
                remote(sent, sent, sem.at[0], rc.at[0], peer).wait_send()

        self.tick = tick
        self.total = tiles + (len(stages) - 1) * lag
        self.after = lambda end: -(-end // TILE) + (len(stages) - 1) * lag
        self.finish = finish


class Exchange:
    def __init__(self, kind, groups, n, near, far, s1, r1, s2, r2):
        self.kind = kind
        self.groups, self.n = groups, n
        self.near, self.far = near, far
        self.sems = (s1, r1, s2, r2)
        self.sent = []

    def merge(self, ref, members):
        if self.kind == "sum":
            total = ref[0]
            for i in range(1, members):
                total = total + ref[i]
            return total
        mean, dev, count = pooled([ref[i] for i in range(members)])
        return jnp.concatenate([mean, dev, jnp.broadcast_to(count, (8, 128))], 0)

    def begin(self, x):
        dp = lax.axis_index("dp")
        fs = lax.axis_index("fsdp")
        near, groups = self.near, self.groups
        s1, r1, s2, r2 = self.sems
        near[dp] = x
        for d in range(1, groups):
            cp = remote(near.at[dp], near.at[dp], s1.at[d], r1.at[dp], (lax.rem(dp + d, groups), fs))
            cp.start()
            self.sent.append(cp)

    def middle(self):
        dp = lax.axis_index("dp")
        fs = lax.axis_index("fsdp")
        near, far, groups, n = self.near, self.far, self.groups, self.n
        s1, r1, s2, r2 = self.sems
        for d in range(1, groups):
            other = lax.rem(dp + d, groups)
            remote(near.at[dp], near.at[other], s1.at[d], r1.at[other], (other, fs)).wait_recv()
        far[fs] = self.merge(near, groups)
        for d in range(1, n):
            cp = remote(far.at[fs], far.at[fs], s2.at[d], r2.at[fs], (dp, lax.rem(fs + d, n)))
            cp.start()
            self.sent.append(cp)

    def end(self):
        dp = lax.axis_index("dp")
        fs = lax.axis_index("fsdp")
        far, n = self.far, self.n
        s1, r1, s2, r2 = self.sems
        for d in range(1, n):
            other = lax.rem(fs + d, n)
            remote(far.at[fs], far.at[other], s2.at[d], r2.at[other], (dp, other)).wait_recv()
        for cp in self.sent:
            cp.wait_send()
        return self.merge(far, n)


def meet(groups, n):
    dp = lax.axis_index("dp")
    fs = lax.axis_index("fsdp")
    barrier = pltpu.get_barrier_semaphore()
    for d in range(1, groups):
        pl.semaphore_signal(barrier, inc=1, device_id=(lax.rem(dp + d, groups), fs), device_id_type=MESH)
    for d in range(1, n):
        pl.semaphore_signal(barrier, inc=1, device_id=(dp, lax.rem(fs + d, n)), device_id_type=MESH)
    return lambda: pl.semaphore_wait(barrier, groups + n - 2)


def pack_into(out, src, tables, joint_at, layers):
    for layer in range(layers):
        for name in FIRST:
            base, stop = tables[layer][name]
            if name == "small":
                small = [src["gains"][layer], src["taps"][layer], src["bn_gain"][layer : layer + 1, :], src["bn_bias"][layer : layer + 1, :]]
                small = jnp.concatenate([x.astype(jnp.float32) for x in small], 0)
                small = jnp.concatenate([small, jnp.zeros((16, WIDE - small.shape[1]), jnp.float32)], 1)
                out[base:stop, :] = small.astype(jnp.bfloat16)
                continue
            ref = src[name]
            height = ref.shape[1]
            for b in range(ref.shape[2] // WIDE):
                out[base + b * height : base + (b + 1) * height, :] = ref[layer, :, b * WIDE : (b + 1) * WIDE]
    enc, pred, tok, dur = src["enc"], src["pred"], src["tok"], src["dur"]
    low, tall = enc.shape[0], pred.shape[0]
    at = joint_at
    out[at : at + low, :] = enc[:, :WIDE]
    at += lift(low)
    out[at : at + tall, :] = pred[:, :WIDE]
    at += lift(tall)
    for b in range(tok.shape[1] // WIDE):
        out[at : at + tall, :] = tok[:, b * WIDE : (b + 1) * WIDE]
        at += lift(tall)
    out[at : at + low, 0:128] = enc[:, WIDE:]
    out[at : at + tall, 128:256] = pred[:, WIDE:]
    dur = dur[...].astype(jnp.float32)
    out[at : at + tall, 256:384] = jnp.concatenate([dur, jnp.zeros((tall, 128 - dur.shape[1]), jnp.float32)], 1).astype(jnp.bfloat16)


def ffn_fwd(rows, x_ref, gain, weights, names, normed, h, act, y, mover, h_out, beats):
    w_in = weights[names[0]]

    def prepare(r, i, c):
        normed[r, :] = (ln_parts(x_ref[r, :].astype(jnp.float32))[0] * gain).astype(jnp.bfloat16)
        return c

    row_loop(rows, prepare)
    w_in[1].wait()
    for b in range(h.shape[0]):
        h[b] = nn(normed[...], w_in[0][:, b * WIDE : (b + 1) * WIDE])
        mover.put(h.at[b], h_out.at[b])

        def swish(r, i, c):
            v = h[b, r, :]
            act[r, b * WIDE : (b + 1) * WIDE] = (v * jax.nn.sigmoid(v)).astype(jnp.bfloat16)
            return c

        row_loop(rows, swish)
        beats.run(1)
    w_out = weights[names[1]]
    w_out[1].wait()
    y[...] = x_ref[...].astype(jnp.float32) + 0.5 * nn(act[...], w_out[0][...])
    beats.run(1)


def part_one(utts, beats, mover, t_ref, x_ref, gains, weights, outs, scratch):
    y1_out, h_out, y2_out, t_out, c_out, r_out, d_out = outs
    y1, y2, normed, h, act, tq, ctx, r, gp, d = scratch
    rows, width = y1.shape
    frames = rows // utts
    ffn_fwd(rows, x_ref, gains[0:1], weights, ("f_in", "f_out"), normed, h, act, y1, mover, h_out, beats)
    mover.put(y1, y1_out)

    def prepare(rr, i, c):
        normed[rr, :] = (ln_parts(y1[rr, :])[0] * gains[1:2]).astype(jnp.bfloat16)
        return c

    row_loop(rows, prepare)
    w_joint = weights["w_joint"][0]
    weights["w_joint"][1].wait()
    for b in range(3):
        tq[:, b * width : (b + 1) * width] = nn(normed[...], w_joint[:, b * width : (b + 1) * width]).astype(jnp.bfloat16)
    mover.put(tq, t_out)
    beats.run(1)
    pairs = width // 128
    side = lax.broadcasted_iota(jnp.int32, (frames, 128), 1) < 64
    key_at = lax.broadcasted_iota(jnp.int32, (1, frames), 1)
    turns = utts * pairs // PAIRS_AT_ONCE
    hook = beats.loop(3, turns)

    def pair_step(m, carry):
        u = m // pairs
        base = lax.rem(m, pairs) * 128
        rr = pl.ds(pl.multiple_of(u * frames, frames), frames)
        bias = jnp.where(key_at < t_ref[u], 0.0, MASKED)
        q = tq[rr, pl.ds(pl.multiple_of(base, 128), 128)]
        k = tq[rr, pl.ds(pl.multiple_of(base + width, 128), 128)]
        v = tq[rr, pl.ds(pl.multiple_of(base + 2 * width, 128), 128)]
        got = []
        for half in range(2):
            mine = side if half == 0 else ~side
            s = nt(jnp.where(mine, q, jnp.zeros_like(q)), k) * 0.125 + bias
            p = jnp.exp(s - jnp.max(s, -1, keepdims=True))
            p = p * (1.0 / jnp.sum(p, -1, keepdims=True))
            got.append(nn(p.astype(jnp.bfloat16), v))
        ctx[rr, pl.ds(pl.multiple_of(base, 128), 128)] = jnp.where(side, got[0], got[1]).astype(jnp.bfloat16)
        return carry

    def pair_turn(m, carry):
        hook(m)
        for i in range(PAIRS_AT_ONCE):
            carry = pair_step(m * PAIRS_AT_ONCE + i, carry)
        return carry

    lax.fori_loop(0, turns, pair_turn, 0)
    mover.put(ctx, c_out)
    weights["w_proj"][1].wait()
    y2[...] = y1[...] + nn(ctx[...], weights["w_proj"][0][...])
    mover.put(y2, y2_out)

    def prepare_conv(rr, i, c):
        normed[rr, :] = (ln_parts(y2[rr, :])[0] * gains[2:3]).astype(jnp.bfloat16)
        return c

    row_loop(rows, prepare_conv)
    w_pin = weights["p_in"][0]
    weights["p_in"][1].wait()
    for b in range(2):
        r[:, b * width : (b + 1) * width] = nn(normed[...], w_pin[:, b * width : (b + 1) * width])
    mover.put(r, r_out)
    beats.run(1)
    fill_gated(utts, frames, t_ref, r, gp)
    taps = gains[5:14]

    def conv(rr, i, total):
        d_chunk = spread(gp, utts, frames, i, taps)
        d[rr, :] = d_chunk
        return total + fold8(d_chunk * valid_rows_of(t_ref, frames, i), jnp.add)

    total = row_loop(rows, conv, jnp.zeros((8, width), jnp.float32))
    mover.put(d, d_out)
    beats.run(1)
    count = t_ref[0]
    for u in range(1, utts):
        count = count + t_ref[u]
    count = count.astype(jnp.float32)
    mean = jnp.sum(total, 0, keepdims=True) / count

    def deviate(rr, i, total):
        gap = (d[rr, :] - mean) * valid_rows_of(t_ref, frames, i)
        return total + fold8(gap * gap, jnp.add)

    dev = jnp.sum(row_loop(rows, deviate, jnp.zeros((8, width), jnp.float32)), 0, keepdims=True)
    cut4 = lambda v: [v[:, i * 128 : (i + 1) * 128] for i in range(width // 128)]
    return jnp.concatenate(cut4(mean) + cut4(dev) + [jnp.full((8, 128), count, jnp.float32)], 0)


def part_two(beats, mover, pooled_ref, gains, weights, outs, scratch):
    y3_out, h_out, y4_out, x_out = outs
    d, y2, y3, normed, h, act, y4, x = scratch
    rows, width = y3.shape
    mean = read_rows(pooled_ref, 0, width)
    count = pooled_ref[8:9, 0:1]
    istd = lax.rsqrt(read_rows(pooled_ref, 4, width) / count + EPS)

    def bn(rr, i, c):
        b = (d[rr, :] - mean) * istd * gains[14:15] + gains[15:16]
        normed[rr, :] = (b * jax.nn.sigmoid(b)).astype(jnp.bfloat16)
        return c

    row_loop(rows, bn)
    weights["p_out"][1].wait()
    y3[...] = y2[...] + nn(normed[...], weights["p_out"][0][...])
    mover.put(y3, y3_out)
    ffn_fwd(rows, y3, gains[3:4], weights, ("s_in", "s_out"), normed, h, act, y4, mover, h_out, beats)
    mover.put(y4, y4_out)

    def last(rr, i, c):
        x[rr, :] = ln_parts(y4[rr, :])[0] * gains[4:5]
        return c

    row_loop(rows, last)
    mover.put(x, x_out)


def forward_kernel(utts, layers, n1, groups, tables, joint_at, tiles, lag, t_ref, frames_ref, *refs):
    n = 2 * n1
    names = PLACE + ("gains", "taps", "bn_gain", "bn_bias", "enc", "pred", "tok", "dur")
    src = dict(zip(names, refs))
    refs = refs[len(names) :]
    whole, refs = refs[0], refs[1:]
    layer_outs = []
    for layer in range(layers):
        layer_outs.append((refs[0:7], refs[7:11], refs[11], refs[12]))
        refs = refs[13:]
    buffers, refs = refs[:8], refs[8:]
    packed, smalls, y1, y2, normed, h, act, tq, ctx, r, gp, d, y3, y4, x, sems = refs[:16]
    refs = refs[16:]
    entered = meet(groups, n)
    pack_into(packed, src, tables, joint_at, layers)
    entered()
    engine = GatherEngine(n1, tiles, lag, packed, whole, *refs[:9])
    refs = refs[9:]
    beats = Beats(engine.tick, engine.total)
    held = dict(zip(("f_in", "f_out", "w_joint", "w_proj", "p_in", "p_out", "s_in", "s_out"), buffers))
    used = 0
    for layer in range(layers):
        table = tables[layer]
        mover = Mover(sems, used)

        def load(name):
            beats.until(engine.after(table[name][1]))
            return held[name], mover.load_weight(whole, table[name][0], held[name])

        weights = {"f_in": load("f_in")}
        small = mover.load(whole.at[:, :, pl.ds(table["small"][0], 16), :], smalls)
        small.wait()
        gains = None
        for s in range(n):
            part = smalls[s // 2, s % 2].astype(jnp.float32)
            part = part if s == 0 else pltpu.roll(part, s * (WIDE // n), 1)
            gains = part if gains is None else gains + part
        layer_outs[layer][3][...] = gains
        weights = Late(weights, load)
        first, second, pooled_out, _ = layer_outs[layer]
        source = frames_ref if layer == 0 else x
        stats = part_one(utts, beats, mover, t_ref, source, gains, weights, first, (y1, y2, normed, h, act, tq, ctx, r, gp, d))
        exchange = Exchange("pool", groups, n, *refs[:6])
        exchange.begin(stats)
        refs = refs[6:]
        for name in ("p_out", "s_in", "s_out"):
            weights.fetch(name)
        exchange.middle()
        beats.run(1)
        mover.finish()
        pooled_out[...] = exchange.end()
        part_two(beats, mover, pooled_out, gains, weights, second, (d, y2, y3, normed, h, act, y4, x))
        mover.finish()
        used = mover.used
    beats.rest()
    engine.finish()


class Late:
    def __init__(self, got, load):
        self.got = got
        self.load = load

    def fetch(self, name):
        if name not in self.got:
            self.got[name] = self.load(name)

    def __getitem__(self, name):
        self.fetch(name)
        return self.got[name]


def forward(t_len, frames_in, arrays, layers, ff, sizes, collective_id, lag=2):
    rows, width = frames_in.shape
    utts = t_len.shape[0]
    n = lax.axis_size("fsdp")
    groups = lax.axis_size("dp")
    n1 = n // 2
    tables, joint_at = gathered_rows(n, width, ff, layers)
    total = tiled(joint_at + sum(sizes))
    tiles = total // TILE
    nb = ff // WIDE
    v = pltpu.VMEM
    dma = pltpu.SemaphoreType.DMA
    big = sds((rows, width))
    one = [big, sds((nb, rows, WIDE)), big, sds((rows, 3 * width), BF16), sds((rows, width), BF16), sds((rows, 2 * width)), big]
    two = [big, sds((nb, rows, WIDE)), big, big]
    pad_rows = utts * (rows // utts + 16)
    outs = pl.pallas_call(
        partial(forward_kernel, utts, layers, n1, groups, tables, joint_at, tiles, lag),
        in_specs=[SMEM_SPEC] + [VMEM_SPEC] * (1 + len(arrays)),
        out_specs=[ANY_SPEC] + ([ANY_SPEC] * 11 + [VMEM_SPEC] * 2) * layers,
        out_shape=[sds((n1, 2, total, WIDE), BF16)] + (one + two + [sds((16, 128)), sds((16, width))]) * layers,
        scratch_shapes=[
            v((width, ff), BF16), v((ff, width), BF16), v((width, 3 * width), BF16), v((width, width), BF16), v((width, 2 * width), BF16),
            v((width, width), BF16), v((width, ff), BF16), v((ff, width), BF16),
            v((total, WIDE), BF16), v((n1, 2, 16, WIDE), BF16), v((rows, width), F32), v((rows, width), F32), v((rows, width), BF16),
            v((nb, rows, WIDE), F32), v((rows, ff), BF16), v((rows, 3 * width), BF16), v((rows, width), BF16), v((rows, 2 * width), F32),
            v((pad_rows, width), F32), v((rows, width), F32), v((rows, width), F32), v((rows, width), F32), v((rows, width), F32), dma((80,)),
            dma((tiles,)), dma((1,)), dma((tiles,)), dma((1,)), dma((tiles,)), dma((1,)), dma((tiles,)), dma((1,)), dma((tiles,)),
        ]
        + [v((groups, 16, 128), F32), v((n, 16, 128), F32), dma((groups,)), dma((groups,)), dma((n,)), dma((n,))] * layers,
        compiler_params=pltpu.CompilerParams(collective_id=collective_id, has_side_effects=True, vmem_limit_bytes=61 << 20),
        name="gather_and_forward",
    )(t_len, frames_in, *arrays)
    whole = outs[0].reshape(n, total, WIDE)
    return whole, [outs[1 + 13 * layer : 14 + 13 * layer] for layer in range(layers)], tables, joint_at


def lift(rows):
    return -(-rows // 16) * 16


def joint_sizes(w_enc, w_pred, w_tok):
    low, tall = lift(w_enc.shape[0]), lift(w_pred.shape[0])
    return [low, tall, tall * (w_tok.shape[1] // WIDE), tall]


class Joined:
    def __init__(self, parts, ends):
        self.parts = parts
        self.ends = ends

    def __getitem__(self, key):
        rows_of, cols = key
        got = []
        first = 0
        for part, last in zip(self.parts, self.ends):
            lo, hi = max(rows_of.start, first), min(rows_of.stop, last)
            if lo < hi:
                got.append(part[lo - first : hi - first, cols])
            first = last
        return got[0] if len(got) == 1 else jnp.concatenate(got, 0)


def unpack_kernel(layers, table, end, dims, ends, *refs):
    parts, refs = refs[: len(ends)], refs[len(ends) :]
    gains, f_in, f_out, w_joint, w_proj, p_in, taps, p_out, s_in, s_out, enc, pred, tok, dur = refs
    share = Joined(parts, ends)
    outs = {"f_in": f_in, "f_out": f_out, "w_joint": w_joint, "w_proj": w_proj, "p_in": p_in, "p_out": p_out, "s_in": s_in, "s_out": s_out}
    starts, width, joint = dims
    shard = gains.shape[2]
    for layer in range(layers):
        for name in PLACE:
            out = outs[name]
            height = out.shape[1]
            early = table[name] < table["p_in"]
            base = starts[layer][0] + table[name] if early else starts[layer][1] + table[name] - table["p_in"]
            for b in range(out.shape[2] // WIDE):
                out[layer, :, b * WIDE : (b + 1) * WIDE] = share[base + b * height : base + (b + 1) * height, :].astype(jnp.float32)
        base = starts[layer][1] + end - table["p_in"]
        small = share[base : base + 16, 0:128].astype(jnp.float32)
        gains[layer] = small[0:5, :shard]
        taps[layer] = small[5 : 5 + taps.shape[1], :shard]
    at = starts[layers]
    low, tall = enc.shape[0], pred.shape[0]
    enc[:, :WIDE] = share[at : at + low, :].astype(jnp.float32)
    at += lift(low)
    pred[:, :WIDE] = share[at : at + tall, :].astype(jnp.float32)
    at += lift(tall)
    for b in range(tok.shape[1] // WIDE):
        tok[:, b * WIDE : (b + 1) * WIDE] = share[at : at + tall, :].astype(jnp.float32)
        at += lift(tall)
    enc[:, WIDE:] = share[at : at + low, 0:128].astype(jnp.float32)
    pred[:, WIDE:] = share[at : at + tall, 128:256].astype(jnp.float32)
    dur[...] = share[at : at + tall, 256:384].astype(jnp.float32)[:, : dur.shape[1]]


def unpack(layers, table, end, dims, shares, like):
    ends = []
    for share in shares:
        ends.append(share.shape[0] + (ends[-1] if ends else 0))
    return pl.pallas_call(
        partial(unpack_kernel, layers, table, end, dims, tuple(ends)),
        in_specs=[VMEM_SPEC] * len(shares),
        out_specs=[VMEM_SPEC] * len(like),
        out_shape=[sds(x.shape) for x in like],
        compiler_params=pltpu.CompilerParams(vmem_limit_bytes=48 << 20),
        name="unpack_grads",
    )(*shares)


def cut(whole, sizes, offset=0):
    parts = []
    for size in sizes:
        parts.append(whole[..., offset : offset + size, :])
        offset += size
    return parts


def from_blocks(part, cols, rows):
    n, height, _ = part.shape
    blocks = cols // WIDE
    return jnp.swapaxes(part.reshape(n, blocks, height // blocks, WIDE)[:, :, :rows], 1, 2).reshape(-1, cols)


def joint_inputs_kernel(base, x_ref, pred_ref, whole, low_ref, enc_t, pred_t, w_t, w_enc, w_pred, w_cat, sems):
    n = whole.shape[0]
    joint = w_enc.shape[1]
    low, tall = w_enc.shape[0] // n, w_pred.shape[0] // n
    vocab = w_cat.shape[1] - 128
    first = base + low + tall
    rest = first + tall * (vocab // WIDE)

    def spread(at, height, dst, cols, lanes, sem):
        def one(s, carry):
            pltpu.make_async_copy(
                whole.at[s, pl.ds(at, height), lanes], dst.at[pl.ds(pl.multiple_of(s * height, 16), height), cols], sem
            ).start()
            return carry

        lax.fori_loop(0, n, one, 0)

    every = pl.ds(0, WIDE)
    spread(base, low, w_enc, every, every, sems.at[0])
    spread(rest, low, w_enc, pl.ds(WIDE, 128), pl.ds(0, 128), sems.at[0])
    spread(base + low, tall, w_pred, every, every, sems.at[1])
    spread(rest, tall, w_pred, pl.ds(WIDE, 128), pl.ds(128, 128), sems.at[1])
    for b in range(vocab // WIDE):
        spread(first + b * tall, tall, w_cat, pl.ds(b * WIDE, WIDE), every, sems.at[2])
    spread(rest, tall, w_cat, pl.ds(vocab, 128), pl.ds(256, 128), sems.at[2])
    low_ref[...] = x_ref[...].astype(jnp.bfloat16)
    pltpu.make_async_copy(w_enc, w_enc, sems.at[0]).wait()
    enc_t[...] = nn(low_ref[...], w_enc[...]).T
    pltpu.make_async_copy(w_pred, w_pred, sems.at[1]).wait()
    pred = nn(pred_ref[...], w_pred[...])
    for g in range(pred_t.shape[0]):
        pred_t[g] = pred[g * 8 : (g + 1) * 8, :].T
    pltpu.make_async_copy(w_cat, w_cat, sems.at[2]).wait()
    w_t[...] = w_cat[...].T


def joint_inputs(x, pred_low, whole, base, joint, vocab):
    rows, width = x.shape
    groups = pred_low.shape[0] // 8
    return pl.pallas_call(
        partial(joint_inputs_kernel, base),
        in_specs=[VMEM_SPEC, VMEM_SPEC, ANY_SPEC],
        out_specs=[VMEM_SPEC] * 7,
        out_shape=[sds((rows, width), BF16), sds((joint, rows)), sds((groups, joint, 8)), sds((vocab + 128, joint), BF16),
                   sds((width, joint), BF16), sds((joint, joint), BF16), sds((joint, vocab + 128), BF16)],
        scratch_shapes=[pltpu.SemaphoreType.DMA((3,))],
        compiler_params=pltpu.CompilerParams(vmem_limit_bytes=48 << 20),
        name="joint_inputs",
    )(x, pred_low, whole)


def joint_outputs_kernel(genc_t, gpred_t, gtok, gdur, low_ref, pred_ref, w_enc, gx, pack, g_low, gp):
    n = pack.shape[0]
    joint = w_enc.shape[1]
    low, tall = w_enc.shape[0] // n, joint // n
    g_low[...] = genc_t[...].T.astype(jnp.bfloat16)
    gx[...] = nt(g_low[...], w_enc[...])
    g_enc = tn(low_ref[...], g_low[...]).astype(jnp.bfloat16)
    real = lax.broadcasted_iota(jnp.int32, (8, joint), 0) < GROUP
    for g in range(gpred_t.shape[0]):
        gp[g * 8 : (g + 1) * 8, :] = jnp.where(real, gpred_t[g].T, 0.0)
    g_pred = tn(pred_ref[...], gp[...].astype(jnp.bfloat16)).astype(jnp.bfloat16)
    blocks = gtok.shape[1] // WIDE
    rest = low + tall * (1 + blocks)
    for s in range(n):
        mine = slice(s * tall, (s + 1) * tall)
        pack[s, 0:low, :] = g_enc[s * low : (s + 1) * low, :WIDE]
        pack[s, low : low + tall, :] = g_pred[mine, :WIDE]
        for b in range(blocks):
            at = low + tall * (1 + b)
            pack[s, at : at + tall, :] = gtok[mine, b * WIDE : (b + 1) * WIDE]
        pack[s, rest : rest + low, 0:128] = g_enc[s * low : (s + 1) * low, WIDE:]
        if tall > low:
            pack[s, rest + low : rest + tall, 0:128] = jnp.zeros((tall - low, 128), jnp.bfloat16)
        pack[s, rest : rest + tall, 128:256] = g_pred[mine, WIDE:]
        pack[s, rest : rest + tall, 256:384] = gdur[mine, :]
        pack[s, rest : rest + tall, 384:] = jnp.zeros((tall, WIDE - 384), jnp.bfloat16)
        if pack.shape[1] > rest + tall:
            pack[s, rest + tall :, :] = jnp.zeros((pack.shape[1] - rest - tall, WIDE), jnp.bfloat16)


def joint_outputs(genc_t, gpred_t, gtok, gdur, low, pred_low, w_enc, n):
    rows, width = low.shape
    joint = w_enc.shape[1]
    count = width // n + (joint // n) * (2 + gtok.shape[1] // WIDE)
    return pl.pallas_call(
        joint_outputs_kernel,
        in_specs=[VMEM_SPEC] * 7,
        out_specs=[VMEM_SPEC] * 2,
        out_shape=[sds((rows, width)), sds((n, tiled(count), WIDE), BF16)],
        scratch_shapes=[pltpu.VMEM((rows, joint), BF16), pltpu.VMEM((pred_low.shape[0], joint), F32)],
        compiler_params=pltpu.CompilerParams(vmem_limit_bytes=48 << 20),
        name="joint_outputs",
    )(genc_t, gpred_t, gtok, gdur, low, pred_low, w_enc)


def unpack_joint(whole, first, sizes, w_enc, w_pred, vocab):
    enc, pred, tok, rest = cut(whole, sizes, first)
    joint = w_enc.shape[1]
    low = w_enc.shape[0]
    tall = w_pred.shape[0]
    w_enc = jnp.concatenate([enc[:, :low], rest[:, :low, : joint - WIDE]], 2).reshape(-1, joint)
    w_pred = jnp.concatenate([pred[:, :tall], rest[:, :tall, 128 : 128 + joint - WIDE]], 2).reshape(-1, joint)
    return w_enc, w_pred, from_blocks(tok, vocab, tall), rest[:, :tall, 256:384].reshape(-1, 128)


def grow(part):
    short = lift(part.shape[1]) - part.shape[1]
    return jnp.pad(part, ((0, 0), (0, short), (0, 0))) if short else part


def pack_joint_grads(g_enc, g_pred, g_tok, g_dur, n):
    def shards(grad):
        return grow(grad.astype(jnp.bfloat16).reshape(n, -1, grad.shape[1]))
    g_enc, g_pred, g_tok, g_dur = shards(g_enc), shards(g_pred), shards(g_tok), shards(g_dur)
    tall = g_pred.shape[1]
    rest = jnp.concatenate(
        [
            jnp.pad(g_enc[:, :, WIDE:], ((0, 0), (0, tall - g_enc.shape[1]), (0, 0))),
            g_pred[:, :, WIDE:],
            g_dur,
            jnp.zeros((n, tall, 128), jnp.bfloat16),
        ],
        2,
    )
    parts = [g_enc[:, :, :WIDE], g_pred[:, :, :WIDE]]
    parts += [g_tok[:, :, b : b + WIDE] for b in range(0, g_tok.shape[2], WIDE)] + [rest]
    rows = sum(p.shape[1] for p in parts)
    return jnp.concatenate(parts + [jnp.zeros((n, tiled(rows) - rows, WIDE), jnp.bfloat16)], 1)


def matmul(left, right):
    return jnp.dot(left, right, preferred_element_type=jnp.float32)


def contract_rows(left, right):
    return lax.dot_general(
        left, right, (((0,), (0,)), ((), ())), preferred_element_type=jnp.float32
    )


def contract_cols(left, right):
    return lax.dot_general(
        left, right, (((1,), (1,)), ((), ())), preferred_element_type=jnp.float32
    )


def local(
    frames_in,
    frame_lengths,
    label_ids,
    label_lengths,
    pred_states,
    norm_gains,
    first_in,
    first_out,
    attend_joint,
    attend_out,
    point_in,
    depth_taps,
    batch_gain,
    batch_bias,
    point_out,
    second_in,
    second_out,
    enc_weight,
    pred_weight,
    token_weight,
    duration_weight,
):
    utts, frames, width = frames_in.shape
    slots = pred_states.shape[1]
    rows = utts * frames
    layers = norm_gains.shape[0]
    n = lax.axis_size("fsdp")
    ff = first_in.shape[2]
    mats = {
        "f_in": first_in, "f_out": first_out, "w_joint": attend_joint, "w_proj": attend_out,
        "p_in": point_in, "p_out": point_out, "s_in": second_in, "s_out": second_out,
    }
    table, end = offsets(n, width, ff)
    shard = width // n
    sizes = joint_sizes(enc_weight, pred_weight, token_weight)
    vocab = token_weight.shape[1]
    arrays = [mats[name] for name in PLACE]
    arrays += [norm_gains, depth_taps, batch_gain, batch_bias, enc_weight, pred_weight, token_weight, duration_weight]
    resid = frames_in.reshape(rows, width)
    whole, records, tables, joint_at = forward(frame_lengths, resid, arrays, layers, ff, sizes, 1)
    held = [{name: spot[0] for name, spot in t.items()} for t in tables]
    starts_of = [resid] + [record[10] for record in records]
    resid = starts_of[-1]
    joint = enc_weight.shape[1]
    groups = slots // GROUP
    durs = duration_weight.shape[1]
    aligned = joint % (16 * n) == 0 and width % (16 * n) == 0
    pred_low = pred_states.reshape(utts * groups, GROUP, joint)
    pred_low = jnp.pad(pred_low, ((0, 0), (0, 8 - GROUP), (0, 0))).reshape(-1, joint)
    if aligned:
        out_low, enc_t, pred_t, w_cat_t, w_enc, _, w_cat = joint_inputs(resid, pred_low, whole, joint_at, joint, vocab)
    else:
        w_enc, w_pred, w_tok, w_dur = unpack_joint(whole, joint_at, sizes, enc_weight, pred_weight, vocab)
        out_low = resid.astype(jnp.bfloat16)
        enc_t = matmul(out_low, w_enc).T
        pred_t = jnp.swapaxes(matmul(pred_low, w_pred).reshape(utts * groups, 8, joint), 1, 2)
        w_cat = jnp.concatenate([w_tok, w_dur], 1)
        w_cat_t = w_cat.T
    labels_ext = jnp.concatenate([label_ids, jnp.zeros((utts, 1), jnp.int32)], 1)
    feats, expd = joint_forward(enc_t, pred_t, labels_ext, w_cat_t, vocab, durs, frames)
    lat_grads, scores = lattice(feats[: 2 + durs], frame_lengths, label_lengths, slots)
    log_prob = scores[:utts, 0]
    utt_loss = -log_prob / frame_lengths.astype(jnp.float32)
    grad_enc_t, grad_pred_t, grad_tok, grad_dur_w = joint_backward(
        enc_t, pred_t, labels_ext, w_cat, feats, lat_grads, expd, vocab, durs, frames
    )
    if aligned:
        grad, joint_grads = joint_outputs(grad_enc_t, grad_pred_t, grad_tok, grad_dur_w, out_low, pred_low, w_enc, n)
    else:
        grad_pred_rows = jnp.swapaxes(grad_pred_t[:, :, :GROUP], 1, 2)
        grad_pred_rows = jnp.pad(grad_pred_rows, ((0, 0), (0, 8 - GROUP), (0, 0))).reshape(-1, joint)
        grad_enc_low = grad_enc_t.T.astype(jnp.bfloat16)
        grad = contract_cols(grad_enc_low, w_enc)
        grad_w_enc = contract_rows(out_low, grad_enc_low)
        grad_w_pred = contract_rows(pred_low, grad_pred_rows.astype(jnp.bfloat16))
        joint_grads = pack_joint_grads(grad_w_enc, grad_w_pred, grad_tok, grad_dur_w, n)

    def whole_of(source):
        return (source, 0, source.shape[1] // TILE)

    waiting = [whole_of(joint_grads)]
    shares = []
    starts = [None] * layers + [0]
    at = joint_grads.shape[1]
    bn_grads = [None] * layers
    for layer in reversed(range(layers)):
        x0 = starts_of[layer]
        y1, h1, y2, qkv, ctx, gates, depthwise, y3, h2, y4, result, pooled, small = records[layer]
        args = (grad, y4, y3, depthwise, pooled, small, whole, h2, ff, held[layer])
        g3, db, grads_one, sums, late_gains = back_one(*args)
        if layer == layers - 1:
            ride, later = waiting + [whole_of(grads_one)], []
        else:
            ride, later = waiting, [whole_of(grads_one)]
        args = (frame_lengths, x0, y1, y2, gates, qkv, ctx, depthwise, db, g3, pooled, sums, late_gains)
        (grad, grads_two, sums), share = back_two(*args, small, whole, h1, ff, held[layer], ride, 20 + layer)
        shares.append(share)
        waiting = later + [whole_of(grads_two)]
        starts[layer] = (at, at + grads_one.shape[1])
        at += grads_one.shape[1] + grads_two.shape[1]
        bn_grads[layer] = (sums[4:8].reshape(width), sums[0:4].reshape(width))
    shares.append(scatter(waiting, 4))
    grads = unpack(
        layers,
        table,
        end,
        (starts, width, joint),
        shares,
        [norm_gains, first_in, first_out, attend_joint, attend_out, point_in, depth_taps, point_out, second_in, second_out,
         enc_weight, pred_weight, token_weight, duration_weight],
    )
    offset = lax.axis_index("fsdp") * shard
    gain_piece = lax.dynamic_slice_in_dim(jnp.stack([g[0] for g in bn_grads]), offset, shard, 1)
    bias_piece = lax.dynamic_slice_in_dim(jnp.stack([g[1] for g in bn_grads]), offset, shard, 1)
    return (
        utt_loss,
        grad.reshape(utts, frames, width),
        *grads[:7],
        gain_piece,
        bias_piece,
        *grads[7:],
    )


def solution(mesh):
    placed = (
        P(("dp", "fsdp"), None, None),
        P(("dp", "fsdp")),
        P(("dp", "fsdp"), None),
        P(("dp", "fsdp")),
        P(("dp", "fsdp"), None, None),
        P(None, None, "fsdp"),
        P(None, "fsdp", None),
        P(None, "fsdp", None),
        P(None, "fsdp", None),
        P(None, "fsdp", None),
        P(None, "fsdp", None),
        P(None, None, "fsdp"),
        P(None, "fsdp"),
        P(None, "fsdp"),
        P(None, "fsdp", None),
        P(None, "fsdp", None),
        P(None, "fsdp", None),
        P("fsdp", None),
        P("fsdp", None),
        P("fsdp", None),
        P("fsdp", None),
    )
    return jax.shard_map(
        local,
        mesh=mesh,
        in_specs=placed,
        out_specs=(
            P(("dp", "fsdp")),
            P(("dp", "fsdp"), None, None),
            P(None, None, "fsdp"),
            P(None, "fsdp", None),
            P(None, "fsdp", None),
            P(None, "fsdp", None),
            P(None, "fsdp", None),
            P(None, "fsdp", None),
            P(None, None, "fsdp"),
            P(None, "fsdp"),
            P(None, "fsdp"),
            P(None, "fsdp", None),
            P(None, "fsdp", None),
            P(None, "fsdp", None),
            P("fsdp", None),
            P("fsdp", None),
            P("fsdp", None),
            P("fsdp", None),
        ),
        check_vma=False,
    )
```
